32 devices in a mesh: dp: 8 (over z, y), tensor: 4 (over x, core).
Axes of the slice: x: 2, y: 2, z: 4, core: 2. Of those that a mesh axis runs over, the one named last changes fastest.
Arguments:
- tokens: bfloat16 [12608, 768], P('dp'), may hold values from -6 to 6
- ln1_gain: float32 [768], P('dp'), may hold values from 0.5 to 1.5
- ln1_bias: float32 [768], P('dp'), may hold values from -1 to 1
- w_qkv: float32 [768, 3, 768], P('dp', None, 'tensor'), may hold values from -0.21875 to 0.21875
- w_attn_out: float32 [768, 768], P('tensor', 'dp'), may hold values from -0.625 to 0.625
- ln2_gain: float32 [768], P('dp'), may hold values from 0.5 to 1.5
- ln2_bias: float32 [768], P('dp'), may hold values from -1 to 1
- router_weight: float32 [768, 8], P('dp'), may hold values from -0.15625 to 0.15625
- w_in: float32 [8, 768, 3072], P(None, 'dp', 'tensor'), may hold values from -0.21875 to 0.21875
- w_expert_out: float32 [8, 3072, 768], P(None, 'tensor', 'dp'), may hold values from -0.875 to 0.875
- router_noise: float32 [12608, 8], P('dp'), may hold values from -1.5 to 1.5
- routes: int32 [12608, 2], P('dp'), may hold values from 0 to 7, all different within a row; in each aligned block of 1576 rows (0 to 1575, 1576 to 3151, ...) at most 788 rows name the same one
- cotangent: bfloat16 [12608, 768], P('dp'), may hold values from -6 to 6
Outputs:
- output: bfloat16 [12608, 768], P('dp')
- d_tokens: bfloat16 [12608, 768], P('dp')
- g_ln1_gain: float32 [768], P('dp')
- g_ln1_bias: float32 [768], P('dp')
- g_w_qkv: float32 [768, 3, 768], P('dp', None, 'tensor')
- g_w_attn_out: float32 [768, 768], P('tensor', 'dp')
- g_ln2_gain: float32 [768], P('dp')
- g_ln2_bias: float32 [768], P('dp')
- g_router: float32 [768, 8], P('dp')
- g_w_in: float32 [8, 768, 3072], P(None, 'dp', 'tensor')
- g_w_expert_out: float32 [8, 3072, 768], P(None, 'tensor', 'dp')
The draws below stay inside these ranges and needn't reach their ends.
Inputs may be any that keep to these rules, and one draw needn't show every extreme that they name: `routes`: each row names 2 different experts; in the rows of one index of dp no expert is named more than 788 times, a bound that some block reaches.
All inputs are finite; a program needn't handle non-finite values.
Results may differ from the reference program's by a relative error of at most 0.023.
Values may be sent and summed in bfloat16 or wider, within the bound.
A program may use at most 320 MiB of HBM per device.

```python
import math
import jax
import jax.numpy as jnp
import numpy as np
from jax import lax

D = 768
HEADS = 12
HD = 64
FF = 3072
E = 8
TOP = 2
SEQ = 197
IMG_DEV = 8
TOK_DEV = 1576
TOKENS = 12608
CAP = 689
MOST = 788
N_DP = 8


def steps_of(rng, shape, shards, least, high):
    loudness, own = 1.0, jax.random.fold_in(rng, 6)
    for dim, shards_of in shards:
        steps = jnp.exp(jax.random.uniform(jax.random.fold_in(own, dim), (shards_of,), jnp.float32, least / len(shards), high / len(shards)))
        loudness = loudness * jnp.repeat(steps, shape[dim] // shards_of).reshape([-1 if axis == dim else 1 for axis in range(len(shape))])
    return loudness


def routed_block(own_key, own, number, rows, number_of, top, limit, skew):
    order = jax.random.permutation(own_key, number_of)
    heavy_load, common = load_shares(number_of, rows * top, limit, skew, True), load_shares(number_of, rows * top, limit, skew, False)
    places = jnp.arange(number_of)

    def named(sizes, rotation):
        used = int((sizes > 0).sum())
        fixed = max(1, used // 4)
        passed = fixed + (places - fixed + rotation * (used - fixed)) % max(1, number_of - fixed)
        return jnp.zeros((number_of,), jnp.int32).at[order[jnp.where(places < fixed, places, passed)]].set(jnp.asarray(sizes, jnp.int32))

    sizes = jnp.where(number % 4 == 0, named(heavy_load, number // 4), named(common, number - number // 4 - 1))
    mixed = jax.random.permutation(jax.random.fold_in(own, 3), number_of)
    donor, taker = mixed[0:number_of // 2 * 2:2], mixed[1:number_of // 2 * 2:2]
    room = jnp.minimum(sizes[donor] - 1, limit - sizes[taker]) // 2
    room = jnp.where((donor == order[0]) | (taker == order[0]) | (sizes[taker] == 0), 0, jnp.maximum(room, 0))
    passed = jax.random.randint(jax.random.fold_in(own, 4), (number_of // 2,), 0, 1 << 20) % (room + 1)
    sizes = sizes.at[donor].add(-passed).at[taker].add(passed)
    labels = jnp.searchsorted(jnp.cumsum(sizes), jnp.arange(rows * top), side="right").astype(jnp.int32)
    listing = labels.reshape(top, rows).T
    listing = listing[jax.random.permutation(jax.random.fold_in(own, 1), rows)]
    rotation = jax.random.randint(jax.random.fold_in(own, 2), (rows, 1), 0, top)
    return jnp.take_along_axis(listing, (jnp.arange(top)[None, :] + rotation) % top, axis=1)


def load_shares(number_of, total, most, slope, full):
    weights = [(1 << 20) // math.isqrt(grade ** slope) + 1 for grade in range(1, number_of + 1)]
    largest = most if full else min(most, max(-(-total // number_of), total * weights[0] // sum(weights)))
    least = 1 if total - largest >= number_of - 1 else 0
    holding, spare = [largest] + [least] * (number_of - 1), total - largest - least * (number_of - 1)
    while spare > 0:
        free = [i for i in range(1, number_of) if holding[i] < largest] or [i for i in range(1, number_of) if holding[i] < most]
        mass, remaining = sum([weights[i] for i in free]), spare
        for i in free:
            addition = min(most - holding[i], max(1, remaining * weights[i] // mass), spare)
            holding[i] = holding[i] + addition
            spare = spare - addition
    return np.array(holding)


def normal_values(key, extent, scale, most, cuts=(), kind=jnp.bfloat16):
    drawn = jax.random.normal(key, extent, jnp.float32) * scale
    if len(cuts) > 0:
        drawn = steps_of(key, extent, cuts, -0.22, 0.18) * drawn
    return jnp.clip(drawn, min=-most, max=most).astype(kind)


def setup_inputs(seed: int = 0) -> dict:
    seeds = jax.random.split(jax.random.key(seed), 14)
    tokens = normal_values(seeds[0], (TOKENS, D), 1.0, 6.0, ((0, 8),))
    ln1_gain = jnp.clip(1.0 + 0.1 * jax.random.normal(seeds[1], (D,), jnp.float32), 0.5, 1.5)
    ln1_bias = normal_values(seeds[2], (D,), 0.2, 1.0, ((0, 8),), jnp.float32)
    w_qkv = normal_values(seeds[3], (D, 3, HEADS * HD), D ** -0.5, 0.21875, ((0, 8), (2, 4)), jnp.float32)
    w_attn_out = normal_values(seeds[4], (HEADS * HD, D), (D // 8) ** -0.5, 0.625, ((0, 4), (1, 8)), jnp.float32)
    ln2_gain = jnp.clip(1.0 + 0.1 * jax.random.normal(seeds[5], (D,), jnp.float32), 0.5, 1.5)
    ln2_bias = normal_values(seeds[6], (D,), 0.2, 1.0, ((0, 8),), jnp.float32)
    router_weight = normal_values(seeds[7], (D, E), (2 * D) ** -0.5, 0.15625, ((0, 8),), jnp.float32)
    w_in = normal_values(seeds[8], (E, D, FF), D ** -0.5, 0.21875, ((1, 8), (2, 4)), jnp.float32)
    w_expert_out = normal_values(seeds[9], (E, FF, D), (FF // 64) ** -0.5, 0.875, ((1, 4), (2, 8)), jnp.float32)
    router_noise = normal_values(seeds[10], (TOKENS, E), 0.3, 1.5, ((0, 8),), jnp.float32)
    routes_keys = jax.random.split(jax.random.fold_in(seeds[11], 1), TOKENS // TOK_DEV)
    routes_turns = jax.random.permutation(jax.random.fold_in(seeds[11], 3), TOKENS // TOK_DEV)
    routes = jax.vmap(lambda own, number: routed_block(jax.random.fold_in(seeds[11], 2), own, number, TOK_DEV, E, TOP, MOST, 1))(routes_keys, routes_turns).reshape((TOKENS, TOP))
    cotangent = normal_values(seeds[12], (TOKENS, D), 1.0, 6.0, ((0, 8),))
    return {"tokens": tokens, "ln1_gain": ln1_gain, "ln1_bias": ln1_bias, "w_qkv": w_qkv, "w_attn_out": w_attn_out, "ln2_gain": ln2_gain, "ln2_bias": ln2_bias, "router_weight": router_weight, "w_in": w_in, "w_expert_out": w_expert_out, "router_noise": router_noise, "routes": routes, "cotangent": cotangent}


EPS = 1e-06
precise = lax.Precision.HIGHEST

@jax.custom_vjp
def low(v):
    return lax.optimization_barrier(v.astype(jnp.bfloat16)).astype(jnp.float32)

@jax.custom_vjp
def low_back(v):
    return v

def low_keep(v):
    return (low(v), None)

def low_pass(kept, grad):
    return (grad,)

def back_keep(v):
    return (v, None)

def back_low(kept, grad):
    return (low(grad),)
low.defvjp(low_keep, low_pass)
low_back.defvjp(back_keep, back_low)

def layer_norm(values, norm_gain, norm_bias):
    centred = values - lax.optimization_barrier(jnp.mean(values, axis=-1, keepdims=True))
    variance = lax.optimization_barrier(jnp.mean(centred * centred, axis=-1, keepdims=True))
    return centred * lax.rsqrt(variance + EPS) * norm_gain + norm_bias

def slot_table(routes):
    chosen = jnp.transpose(routes).reshape(-1).astype(jnp.int32)
    onehot = (chosen[:, None] == jnp.arange(E, dtype=jnp.int32)[None, :]).astype(jnp.int32)
    earlier = jnp.cumsum(onehot, axis=0) - onehot
    position = lax.optimization_barrier(jnp.sum(earlier * onehot, axis=1)).astype(jnp.int32)
    flat_slot = jnp.where(position < CAP, chosen * CAP + position, E * CAP)
    return jnp.transpose(flat_slot.reshape(TOP, routes.shape[0])).astype(jnp.int32)

def attend(packed):
    query = packed[:, :, 0]
    key_heads = packed[:, :, 1]
    value_heads = packed[:, :, 2]
    scores = jnp.einsum('bqhd,bkhd->bhqk', query, key_heads, precision=precise) * HD ** (-0.5)
    scores = low_back(scores)
    att_weights = low(jax.nn.softmax(scores, axis=-1))
    mixed = jnp.einsum('bhqk,bkhd->bqhd', att_weights, value_heads, precision=precise)
    return low_back(low(mixed))

def expert_block(normed_shard, slot_shard, gate_shard, expert_in_low, expert_out_low):
    token_count = normed_shard.shape[0]
    owners = jnp.broadcast_to(jnp.arange(token_count, dtype=jnp.int32)[:, None], slot_shard.shape).reshape(-1)
    slot_token = jnp.full((E * CAP + 1,), token_count, jnp.int32).at[slot_shard.reshape(-1)].set(owners)[:E * CAP]
    padded = jnp.concatenate([normed_shard, jnp.zeros((1, D), normed_shard.dtype)], axis=0)
    expert_rows = padded[slot_token].reshape(E, CAP, D)
    pre_act = low_back(jnp.einsum('ecd,edf->ecf', expert_rows, expert_in_low, precision=precise))
    hidden = low(jax.nn.gelu(pre_act, approximate=True))
    result = low_back(jnp.einsum('ecf,efd->ecd', hidden, expert_out_low, precision=precise))
    flat_result = jnp.concatenate([result.reshape(E * CAP, D), jnp.zeros((1, D), result.dtype)], axis=0)
    return lax.optimization_barrier(jnp.sum(gate_shard[:, :, None] * flat_result[slot_shard], axis=1))

def forward(tokens, ln1_gain, ln1_bias, w_qkv, w_attn_out, ln2_gain, ln2_bias, router_weight, w_in, w_expert_out, router_noise, route_onehot, slot_index):
    normed_one = low(layer_norm(tokens, low(ln1_gain), low(ln1_bias)))
    packed = jnp.dot(normed_one, low(w_qkv).reshape(D, 3 * HEADS * HD), precision=precise)
    packed = low_back(low(packed)).reshape(N_DP, IMG_DEV, SEQ, 3, HEADS, HD)
    mixed = lax.map(jax.checkpoint(attend), packed).reshape(TOKENS, HEADS * HD)
    attended = low_back(jnp.dot(mixed, low(w_attn_out), precision=precise))
    residual_mid = tokens + attended
    normed_two = low(layer_norm(residual_mid, low(ln2_gain), low(ln2_bias)))
    logits = low_back(jnp.dot(normed_two, low(router_weight), precision=precise) + router_noise)
    router_probs = jax.nn.softmax(logits, axis=-1)
    gates = lax.optimization_barrier(jnp.sum(router_probs[:, None, :] * route_onehot, axis=-1))
    expert_in_low = low(w_in)
    expert_out_low = low(w_expert_out)

    def one_shard(pack):
        return expert_block(pack[0], pack[1], pack[2], expert_in_low, expert_out_low)
    mixture = lax.map(jax.checkpoint(one_shard), (normed_two.reshape(N_DP, TOK_DEV, D), slot_index, gates.reshape(N_DP, TOK_DEV, TOP)))
    return residual_mid + mixture.reshape(TOKENS, D)

def reference(tokens, ln1_gain, ln1_bias, w_qkv, w_attn_out, ln2_gain, ln2_bias, router_weight, w_in, w_expert_out, router_noise, routes, cotangent):
    slot_index = jax.vmap(slot_table)(routes.reshape(N_DP, TOK_DEV, TOP))
    route_onehot = (routes[:, :, None] == jnp.arange(E, dtype=jnp.int32)[None, None, :]).astype(jnp.float32)

    def closed(tok_values, gain_one, bias_one, qkv_weight, out_weight, gain_two, bias_two, router_w, in_weight, out_expert):
        return forward(tok_values, gain_one, bias_one, qkv_weight, out_weight, gain_two, bias_two, router_w, in_weight, out_expert, router_noise, route_onehot, slot_index)
    output, pullback = jax.vjp(closed, tokens.astype(jnp.float32), ln1_gain, ln1_bias, w_qkv, w_attn_out, ln2_gain, ln2_bias, router_weight, w_in, w_expert_out)
    grads = pullback(cotangent.astype(jnp.float32))
    return (output.astype(jnp.bfloat16), grads[0].astype(jnp.bfloat16), grads[1], grads[2], grads[3], grads[4], grads[5], grads[6], grads[7], grads[8], grads[9])
```

```python
import functools

import jax
import jax.numpy as jnp
from jax import lax
from jax.experimental import pallas as pl
from jax.experimental.pallas import tpu as pltpu
from jax.sharding import PartitionSpec as P

D = 768
HD = 64
E = 8
TOP = 2
SEQ = 197
CAP = 689
PAD = 208
META = 200
TILE = 256
FFS = 768
EPS = 1e-06
VMEM_LIMIT = 60 * 1024 * 1024

F32 = jnp.float32
BF16 = jnp.bfloat16


def dot(a, b):
    return jnp.dot(a, b, preferred_element_type=F32)


def dot_nt(a, b):
    return lax.dot_general(a, b, (((1,), (1,)), ((), ())), preferred_element_type=F32)


def dot_tn(a, b):
    return lax.dot_general(a, b, (((0,), (0,)), ((), ())), preferred_element_type=F32)


def iota(shape, dim):
    return lax.broadcasted_iota(jnp.int32, shape, dim)


def normalise(values):
    centred = values - jnp.mean(values, axis=-1, keepdims=True)
    scale = lax.rsqrt(jnp.mean(centred * centred, axis=-1, keepdims=True) + EPS)
    return centred * scale, scale


def norm_back(grad, unit, scale, gain):
    g = grad * gain
    return scale * (
        g - jnp.mean(g, axis=-1, keepdims=True) - unit * jnp.mean(g * unit, axis=-1, keepdims=True)
    )


def attn_forward_kernel(
    x_ref, par_ref, wa_ref, wb_ref, noise_ref, keep_ref,
    chunk_ref, x1_ref, qkv_ref, o_ref, lse_ref, probs_ref,
):
    par = par_ref[...].astype(F32)
    x = x_ref[...].astype(F32)
    unit, _ = normalise(x)
    h1 = (unit * par[0:1] + par[1:2]).astype(BF16)
    acc = x
    lse = jnp.zeros((PAD, 128), F32)
    key_ok = iota((PAD, PAD), 1) < SEQ
    lane = iota((PAD, 128), 1)
    for r in range(4):
        w = wa_ref[r] if r < 2 else wb_ref[r - 2]
        qkv = dot(h1, w[:, : 9 * HD]).astype(BF16)
        qkv_ref[r] = qkv
        outs = []
        for h in range(3):
            q = qkv[:, h * HD : (h + 1) * HD]
            k = qkv[:, (3 + h) * HD : (4 + h) * HD]
            v = qkv[:, (6 + h) * HD : (7 + h) * HD]
            s = jnp.where(key_ok, dot_nt(q, k) * HD ** (-0.5), -1e30)
            top = jnp.max(s, axis=-1, keepdims=True)
            p = jnp.exp(s - top)
            total = jnp.sum(p, axis=-1, keepdims=True)
            outs.append(dot((p * (1.0 / total)).astype(BF16), v).astype(BF16))
            lse = jnp.where(lane == 3 * r + h, top + jnp.log(total), lse)
        o = jnp.concatenate(outs, axis=1)
        o_ref[r] = o
        acc = acc + dot_nt(o, w[:, 9 * HD :])
    lse_ref[...] = lse
    x1_ref[...] = acc
    unit2, _ = normalise(acc)
    h2 = (unit2 * par[2:3] + par[3:4]).astype(BF16)
    logits = dot_nt(par_ref[8:16, :], h2) + noise_ref[...]
    e = jnp.exp(logits - jnp.max(logits, axis=0, keepdims=True))
    probs = e / jnp.sum(e, axis=0, keepdims=True)
    probs_ref[...] = probs
    gates = jnp.where(keep_ref[...] > 0, probs, -1.0)
    chunk_ref[...] = h2
    tail = jnp.concatenate([gates, jnp.zeros((8, D - PAD), F32)], axis=1)
    low = h2[PAD - 16 :, :].astype(F32)
    chunk_ref[PAD - 16 :, :] = jnp.concatenate([low[:8], tail], axis=0).astype(BF16)


def attn_forward(x, par, wa, wb, noise, keep):
    vm = pl.BlockSpec(memory_space=pltpu.VMEM)
    return pl.pallas_call(
        attn_forward_kernel,
        out_shape=(
            jax.ShapeDtypeStruct((PAD, D), BF16),
            jax.ShapeDtypeStruct((PAD, D), F32),
            jax.ShapeDtypeStruct((4, PAD, 9 * HD), BF16),
            jax.ShapeDtypeStruct((4, PAD, 3 * HD), BF16),
            jax.ShapeDtypeStruct((PAD, 128), F32),
            jax.ShapeDtypeStruct((E, PAD), F32),
        ),
        in_specs=[vm] * 6,
        out_specs=(vm,) * 6,
        compiler_params=pltpu.CompilerParams(vmem_limit_bytes=VMEM_LIMIT),
        cost_estimate=pl.CostEstimate(flops=3 * 10**9, bytes_accessed=10**7, transcendentals=10**6),
        name="attn_forward",
    )(x, par, wa, wb, noise, keep)


def expert_kernel(nb, me_ref, *refs):
    h_in, dy_in = refs[:nb], refs[nb : 2 * nb]
    wa_ref, wb_ref = refs[2 * nb : 2 * nb + 2]
    outs = refs[2 * nb + 2 :]
    y_out, dx_out = outs[:nb], outs[nb : 2 * nb]
    rows_out, hid_out, tiles_ref = outs[2 * nb : 2 * nb + 3]
    (h, dy, y_t, dx_t, gate_s, slot_s, dgate_s, xs, dys, hid_s, rows_s, lo_s, hi_s, in_sem, out_sem, row_sem, hid_sem) = outs[2 * nb + 3 :]
    me = me_ref[0]
    loads = []
    for b in range(nb):
        for ref, table, c in ((h_in[b], h, 0), (dy_in[b], dy, 1)):
            copy = pltpu.make_async_copy(ref, table.at[b], in_sem.at[c, b])
            copy.start()
            loads.append(copy)
    y_t[...] = jnp.zeros_like(y_t)
    dx_t[...] = jnp.zeros_like(dx_t)
    dgate_s[...] = jnp.zeros_like(dgate_s)
    for copy in loads:
        copy.wait()

    row16 = iota((16, D), 0)
    for b in range(nb):
        meta = h[b, PAD - 16 : PAD, :].astype(F32)
        gate_s[b : b + 1, :] = jnp.sum(jnp.where(row16 == 8 + me, meta, 0.0), axis=0, keepdims=True)[:, :PAD]
    gates = gate_s[...]
    named = (gates >= 0) & (iota((nb, PAD), 1) < SEQ)
    ones = named.astype(F32).astype(BF16)
    upto = dot(ones, (iota((PAD, PAD), 0) <= iota((PAD, PAD), 1)).astype(F32).astype(BF16))
    count = dot(ones, jnp.ones((PAD, PAD), BF16)).astype(BF16)
    before = dot((iota((nb, nb), 0) > iota((nb, nb), 1)).astype(F32).astype(BF16), count)
    slot_s[...] = jnp.where(named, before + upto - 1.0, -1.0).astype(jnp.int32)
    ends = jnp.where(named, before + upto, before)
    for b in range(nb):
        lo_s[b] = jnp.max(before[b : b + 1, :]).astype(jnp.int32)
        hi_s[b] = jnp.max(ends[b : b + 1, :]).astype(jnp.int32)
    tiles = lax.div(hi_s[nb - 1] + TILE - 1, TILE)
    tiles_ref[0] = tiles

    def meets(b, first):
        return (lo_s[b] < first + TILE) & (hi_s[b] > first) & (hi_s[b] > lo_s[b])

    def place(b, first):
        return iota((TILE, PAD), 0) + first == slot_s[pl.ds(b, 1), :]

    def step(t, carry):
        first = t * TILE
        slot = lax.rem(t, 2)
        xs[...] = jnp.zeros_like(xs)
        dys[...] = jnp.zeros_like(dys)

        def collect(b, gcol):
            def one(gcol):
                hit = place(b, first)
                p = hit.astype(F32).astype(BF16)
                xs[...] += dot(p, h[b])
                dys[...] += dot(p, dy[b])
                return gcol + jnp.sum(jnp.where(hit, gate_s[pl.ds(b, 1), :], 0.0), axis=1, keepdims=True)

            return lax.cond(meets(b, first), one, lambda g: g, gcol)

        gcol = lax.fori_loop(0, nb, collect, jnp.zeros((TILE, 1), F32))

        def drain(s):
            pltpu.make_async_copy(rows_s.at[s], rows_out.at[:, pl.ds(0, TILE)], row_sem.at[s]).wait()
            pltpu.make_async_copy(hid_s.at[s], hid_out.at[:, pl.ds(0, TILE)], hid_sem.at[s]).wait()

        @pl.when(t >= 2)
        def _():
            drain(slot)

        x = xs[...].astype(BF16)
        g_rows = (dys[...] * gcol).astype(BF16)
        rows_s[slot, 0] = x
        rows_s[slot, 1] = g_rows
        y = jnp.zeros((TILE, D), F32)
        dx = jnp.zeros((TILE, D), F32)
        for r in range(4):
            w1, w2 = (wa_ref.at[r, 0], wa_ref.at[r, 1]) if r < 2 else (wb_ref.at[r - 2, 0], wb_ref.at[r - 2, 1])
            a = dot(x, w1[...])
            a2 = a * a
            th = jnp.tanh(0.7978845608028654 * a * (1.0 + 0.044715 * a2))
            half = 0.5 * (1.0 + th)
            hid = (a * half).astype(BF16)
            slope = half + 0.5 * a * (1.0 - th * th) * (0.7978845608028654 * (1.0 + 3 * 0.044715 * a2))
            da = (dot(g_rows, w2[...]) * slope).astype(BF16)
            y = y + dot_nt(hid, w2[...])
            dx = dx + dot_nt(da, w1[...])
            hid_s[slot, 0, :, r * FFS : (r + 1) * FFS] = da
            hid_s[slot, 1, :, r * FFS : (r + 1) * FFS] = hid
        at = pl.ds(pl.multiple_of(first, TILE), TILE)
        pltpu.make_async_copy(rows_s.at[slot], rows_out.at[:, at], row_sem.at[slot]).start()
        pltpu.make_async_copy(hid_s.at[slot], hid_out.at[:, at], hid_sem.at[slot]).start()
        dgate = jnp.sum(dys[...] * y, axis=1, keepdims=True)
        y_low = (y * gcol).astype(BF16)
        dx_low = dx.astype(BF16)

        def give(b, carry):
            @pl.when(meets(b, first))
            def _():
                hit = place(b, first)
                p = hit.astype(F32).astype(BF16)
                y_t[b] = y_t[b] + dot_tn(p, y_low).astype(BF16)
                dx_t[b] = dx_t[b] + dot_tn(p, dx_low).astype(BF16)
                dgate_s[pl.ds(b, 1), :] += jnp.sum(jnp.where(hit, dgate, 0.0), axis=0, keepdims=True)

            return carry

        lax.fori_loop(0, nb, give, 0)
        return carry

    lax.fori_loop(0, tiles, step, 0)
    for back in (1, 2):

        @pl.when(tiles >= back)
        def _():
            s = lax.rem(tiles - back, 2)
            pltpu.make_async_copy(rows_s.at[s], rows_out.at[:, pl.ds(0, TILE)], row_sem.at[s]).wait()
            pltpu.make_async_copy(hid_s.at[s], hid_out.at[:, pl.ds(0, TILE)], hid_sem.at[s]).wait()

    stores = []
    for b in range(nb):
        tail = dx_t[b, PAD - 16 : PAD, :].astype(F32)
        line = jnp.concatenate([dgate_s[b : b + 1, :], jnp.zeros((1, D - PAD), F32)], axis=1)
        dx_t[b, PAD - 16 : PAD, :] = (tail + jnp.where(row16 == 8 + me, line, 0.0)).astype(BF16)
        for table, ref, c in ((y_t, y_out[b], 0), (dx_t, dx_out[b], 1)):
            copy = pltpu.make_async_copy(table.at[b], ref, out_sem.at[c, b])
            copy.start()
            stores.append(copy)
    for copy in stores:
        copy.wait()


def expert_rows(nb):
    return -(-nb * SEQ // TILE) * TILE


def experts(me, h_blocks, dy_blocks, wa, wb):
    nb = len(h_blocks)
    rows = expert_rows(nb)
    hbm = pl.BlockSpec(memory_space=pl.ANY)
    vm = pl.BlockSpec(memory_space=pltpu.VMEM)
    sm = pl.BlockSpec(memory_space=pltpu.SMEM)
    block = jax.ShapeDtypeStruct((PAD, D), BF16)
    outs = pl.pallas_call(
        functools.partial(expert_kernel, nb),
        out_shape=[block] * (2 * nb)
        + [
            jax.ShapeDtypeStruct((2, rows, D), BF16),
            jax.ShapeDtypeStruct((2, rows, 4 * FFS), BF16),
            jax.ShapeDtypeStruct((1,), jnp.int32),
        ],
        in_specs=[sm] + [hbm] * (2 * nb) + [vm, vm],
        out_specs=[hbm] * (2 * nb + 2) + [sm],
        scratch_shapes=[
            pltpu.VMEM((nb, PAD, D), BF16),
            pltpu.VMEM((nb, PAD, D), BF16),
            pltpu.VMEM((nb, PAD, D), BF16),
            pltpu.VMEM((nb, PAD, D), BF16),
            pltpu.VMEM((nb, PAD), F32),
            pltpu.VMEM((nb, PAD), jnp.int32),
            pltpu.VMEM((nb, PAD), F32),
            pltpu.VMEM((TILE, D), F32),
            pltpu.VMEM((TILE, D), F32),
            pltpu.VMEM((2, 2, TILE, 4 * FFS), BF16),
            pltpu.VMEM((2, 2, TILE, D), BF16),
            pltpu.SMEM((nb,), jnp.int32),
            pltpu.SMEM((nb,), jnp.int32),
            pltpu.SemaphoreType.DMA((2, nb)),
            pltpu.SemaphoreType.DMA((2, nb)),
            pltpu.SemaphoreType.DMA((2,)),
            pltpu.SemaphoreType.DMA((2,)),
        ],
        compiler_params=pltpu.CompilerParams(vmem_limit_bytes=VMEM_LIMIT),
        cost_estimate=pl.CostEstimate(flops=30 * 10**9, bytes_accessed=4 * 10**7, transcendentals=4 * 10**6),
        name="experts",
    )(me.reshape(1), *h_blocks, *dy_blocks, wa, wb)
    return outs[:nb], outs[nb : 2 * nb], outs[2 * nb], outs[2 * nb + 1], outs[2 * nb + 2]


def expert_grad_kernel(tiles_ref, rows_ref, hid_ref, out_ref, acc):
    acc[...] = jnp.zeros_like(acc)

    def step(t, carry):
        at = pl.ds(pl.multiple_of(t * TILE, TILE), TILE)
        acc[...] += dot_tn(rows_ref[0, at, :], hid_ref[0, at, :])
        return carry

    lax.fori_loop(0, tiles_ref[0], step, 0)
    out_ref[0, 0] = acc[...].astype(BF16)


def expert_grads(tiles, rows, hid, base):
    n = rows.shape[1]
    return pl.pallas_call(
        expert_grad_kernel,
        grid_spec=pltpu.PrefetchScalarGridSpec(
            num_scalar_prefetch=1,
            grid=(2, 2),
            in_specs=[
                pl.BlockSpec((1, n, D), lambda k, s, _: (k, 0, 0)),
                pl.BlockSpec((1, n, FFS), lambda k, s, _: (k, 0, base + s)),
            ],
            out_specs=pl.BlockSpec((1, 1, D, FFS), lambda k, s, _: (s, k, 0, 0)),
            scratch_shapes=[pltpu.VMEM((D, FFS), F32)],
        ),
        out_shape=jax.ShapeDtypeStruct((2, 2, D, FFS), BF16),
        compiler_params=pltpu.CompilerParams(vmem_limit_bytes=VMEM_LIMIT),
        cost_estimate=pl.CostEstimate(flops=8 * 10**9, bytes_accessed=3 * 10**7, transcendentals=0),
        name="expert_grads",
    )(tiles, rows, hid)


def attn_backward_kernel(imgs, *refs):
    dh_in, x1_in, x_in, dy_in, probs_in, qkv_in, o_in, lse_in = (
        refs[i * imgs : (i + 1) * imgs] for i in range(8)
    )
    par_ref, wa_ref, wb_ref = refs[8 * imgs : 8 * imgs + 3]
    grads_ref, small_ref, dtok_ref = refs[8 * imgs + 3 : 8 * imgs + 6]
    dx1_s, low_s, h1_s, dh1_s, dqkv_s, o_s = refs[8 * imgs + 6 :]
    par = par_ref[...].astype(F32)
    router = par_ref[8:16, :]
    row_ok = iota((PAD, 1), 0) < SEQ
    lane_ok = iota((E, PAD), 1) < SEQ
    key_ok = iota((PAD, PAD), 1) < SEQ
    small2g = jnp.zeros((1, D), F32)
    small2b = jnp.zeros((1, D), F32)
    g_router = jnp.zeros((E, D), F32)
    for c in range(imgs):
        span = slice(c * PAD, (c + 1) * PAD)
        arrived = dh_in[c][...].astype(F32)
        dgate = arrived[PAD - 8 :, :PAD]
        probs = probs_in[c][...]
        dlogits = probs * (dgate - jnp.sum(probs * dgate, axis=0, keepdims=True))
        dlogits = jnp.where(lane_ok, dlogits, 0.0).astype(BF16)
        unit, scale = normalise(x1_in[c][...])
        h2 = (unit * par[2:3] + par[3:4]).astype(BF16)
        g_router = g_router + dot(dlogits, h2)
        dh2 = jnp.where(row_ok, arrived + dot_tn(dlogits, router), 0.0)
        small2g = small2g + jnp.sum(dh2 * unit, axis=0, keepdims=True)
        small2b = small2b + jnp.sum(dh2, axis=0, keepdims=True)
        dx1 = dy_in[c][...].astype(F32) + norm_back(dh2, unit, scale, par[2:3])
        dx1_s[span, :] = dx1
        low_s[span, :] = dx1.astype(BF16)
        unit1, _ = normalise(x_in[c][...].astype(F32))
        h1_s[span, :] = (unit1 * par[0:1] + par[1:2]).astype(BF16)
    low = low_s[...]
    h1 = h1_s[...]
    for r in range(4):
        w = wa_ref[r] if r < 2 else wb_ref[r - 2]
        dout = dot(low, w[:, 9 * HD :]).astype(BF16)
        for c in range(imgs):
            span = slice(c * PAD, (c + 1) * PAD)
            qkv = qkv_in[c][r]
            lse = lse_in[c][...]
            o_s[span, :] = o_in[c][r]
            dqs, dks, dvs = [], [], []
            for h in range(3):
                q = qkv[:, h * HD : (h + 1) * HD]
                k = qkv[:, (3 + h) * HD : (4 + h) * HD]
                v = qkv[:, (6 + h) * HD : (7 + h) * HD]
                do = dout[span, h * HD : (h + 1) * HD]
                s = dot_nt(q, k) * HD ** (-0.5)
                p = jnp.where(key_ok, jnp.exp(s - lse[:, 3 * r + h : 3 * r + h + 1]), 0.0)
                dvs.append(dot_tn(p.astype(BF16), do).astype(BF16))
                dp = dot_nt(do, v)
                ds = (p * (dp - jnp.sum(p * dp, axis=-1, keepdims=True))).astype(BF16)
                dqs.append((dot(ds, k) * HD ** (-0.5)).astype(BF16))
                dks.append((dot_tn(ds, q) * HD ** (-0.5)).astype(BF16))
            dqkv_s[span, :] = jnp.concatenate(dqs + dks + dvs, axis=1)
        dqkv = dqkv_s[...]
        part = dot_nt(dqkv, w[:, : 9 * HD])
        dh1_s[...] = part if r == 0 else dh1_s[...] + part
        grads_ref[r] = jnp.concatenate([dot_tn(h1, dqkv), dot_tn(low, o_s[...])], axis=1).astype(BF16)
    small1g = jnp.zeros((1, D), F32)
    small1b = jnp.zeros((1, D), F32)
    for c in range(imgs):
        span = slice(c * PAD, (c + 1) * PAD)
        dh1 = jnp.where(row_ok, dh1_s[span, :], 0.0)
        unit1, scale1 = normalise(x_in[c][...].astype(F32))
        small1g = small1g + jnp.sum(dh1 * unit1, axis=0, keepdims=True)
        small1b = small1b + jnp.sum(dh1, axis=0, keepdims=True)
        dtok_ref[c] = (dx1_s[span, :] + norm_back(dh1, unit1, scale1, par[0:1])).astype(BF16)
    small_ref[...] = jnp.concatenate(
        [small1g, small1b, small2g, small2b, jnp.zeros((4, D), F32), g_router], axis=0
    ).astype(BF16)


def attn_backward(dh, x1, x, dy, probs, qkv, o, lse, par, wa, wb):
    imgs = len(dh)
    vm = pl.BlockSpec(memory_space=pltpu.VMEM)
    rows = imgs * PAD
    return pl.pallas_call(
        functools.partial(attn_backward_kernel, imgs),
        out_shape=(
            jax.ShapeDtypeStruct((4, D, D), BF16),
            jax.ShapeDtypeStruct((16, D), BF16),
            jax.ShapeDtypeStruct((imgs, PAD, D), BF16),
        ),
        in_specs=[vm] * (8 * imgs + 3),
        out_specs=(vm,) * 3,
        scratch_shapes=[
            pltpu.VMEM((rows, D), F32),
            pltpu.VMEM((rows, D), BF16),
            pltpu.VMEM((rows, D), BF16),
            pltpu.VMEM((rows, D), F32),
            pltpu.VMEM((rows, 9 * HD), BF16),
            pltpu.VMEM((rows, 3 * HD), BF16),
        ],
        compiler_params=pltpu.CompilerParams(vmem_limit_bytes=VMEM_LIMIT),
        cost_estimate=pl.CostEstimate(flops=12 * 10**9, bytes_accessed=2 * 10**7, transcendentals=2 * 10**6),
        name="attn_backward",
    )(*dh, *x1, *x, *dy, *probs, *qkv, *o, *lse, par, wa, wb)


RING = (0, 2, 4, 6, 7, 5, 3, 1)


def ring_place(member):
    even = lax.rem(member, 2) == 0
    return jnp.where(even, lax.div(member, 2), E - 1 - lax.div(member, 2))


def ring_member(place):
    return jnp.where(place < E // 2, 2 * place, 2 * E - 1 - 2 * place)


class Mover:
    def __init__(self, n_dp):
        self.n_dp = n_dp
        self.groups = n_dp // E
        self.me = lax.axis_index("dp")
        self.member = lax.rem(self.me, E)
        self.group = lax.div(self.me, E)
        self.tensor = lax.axis_index("tensor")
        self.place = ring_place(self.member)
        bases = range(0, n_dp, E)
        self.ring = (
            [(b + RING[i], b + RING[(i + 1) % E]) for b in bases for i in range(E)],
            [(b + RING[(i + 1) % E], b + RING[i]) for b in bases for i in range(E)],
        )

    def along(self, value, way):
        return lax.ppermute(value, "dp", self.ring[way])

    def shift(self, value, by):
        perm = [(b + i, b + (i + by) % E) for b in range(0, self.n_dp, E) for i in range(E)]
        return lax.ppermute(value, "dp", perm)

    def shift_group(self, value, by):
        return lax.ppermute(value, "dp", [(k, (k + by * E) % self.n_dp) for k in range(self.n_dp)])

    def other(self, value, mask):
        return lax.ppermute(value, "tensor", [(k, k ^ mask) for k in range(4)])

    def behind(self, way, k):
        step = -k if way == 0 else k
        return ring_member(lax.rem(self.place + step + E, E))

    def ring_blocks(self, block, way):
        blocks = [block]
        for _ in range(E - 1):
            blocks.append(self.along(blocks[-1], way))
        return blocks

    def ring_sum(self, blocks, way):
        total = blocks[1]
        for k in range(2, E + 1):
            total = self.along(total, way)
            total = (total.astype(F32) + blocks[k % E].astype(F32)).astype(BF16)
        return total

    def both_ways(self, block):
        found = [(self.member, block)]
        ahead = back = block
        for k in range(1, E // 2 + 1):
            ahead = self.along(ahead, 0)
            found.append((self.behind(0, k), ahead))
            if k < E // 2:
                back = self.along(back, 1)
                found.append((self.behind(1, k), back))
        return found

    def sum_both_ways(self, block_for):
        def chain(way, steps):
            total = block_for(self.behind(1 - way, steps))
            for k in range(steps - 1, -1, -1):
                total = self.along(total, way)
                if k:
                    total = (total.astype(F32) + block_for(self.behind(1 - way, k)).astype(F32)).astype(BF16)
            return total

        ahead = chain(0, E // 2)
        back = chain(1, E // 2 - 1)
        return ahead.astype(F32) + back.astype(F32) + block_for(self.member).astype(F32)

    def all_groups(self, part, dim):
        if self.groups == 1:
            return part
        size = part.shape[dim]
        shape = part.shape[:dim] + (size * self.groups,) + part.shape[dim + 1 :]
        whole = lax.dynamic_update_slice_in_dim(jnp.zeros(shape, part.dtype), part, self.group * size, dim)
        for by in range(1, self.groups):
            came = lax.rem(self.group - by + self.groups, self.groups)
            whole = lax.dynamic_update_slice_in_dim(whole, self.shift_group(part, by), came * size, dim)
        return whole

    def sum_groups(self, whole, dim):
        if self.groups == 1:
            return whole
        size = whole.shape[dim] // self.groups
        total = lax.dynamic_slice_in_dim(whole, self.group * size, size, dim).astype(F32)
        for by in range(1, self.groups):
            to = lax.rem(self.group + by, self.groups)
            part = lax.dynamic_slice_in_dim(whole, to * size, size, dim)
            total = total + self.shift_group(part, by).astype(F32)
        return total.astype(whole.dtype)


def image_blocks(rows, tensor, imgs):
    first = tensor * (imgs * SEQ)
    return [
        jnp.pad(lax.dynamic_slice_in_dim(rows, first + c * SEQ, SEQ, 0), ((0, PAD - SEQ), (0, 0)))
        for c in range(imgs)
    ]


def image_lanes(lanes, tensor, imgs):
    first = tensor * (imgs * SEQ)
    return [
        jnp.pad(lax.dynamic_slice_in_dim(lanes, first + c * SEQ, SEQ, 1), ((0, 0), (0, PAD - SEQ)))
        for c in range(imgs)
    ]


def kept_pairs(routes):
    chosen = jnp.transpose(routes).reshape(1, -1)
    named = (chosen == jnp.arange(E, dtype=jnp.int32)[:, None]).astype(jnp.int32)
    kept = named * (jnp.cumsum(named, axis=1) <= CAP)
    return jnp.sum(kept.reshape(E, TOP, -1), axis=1).astype(F32)


def body(
    n_dp,
    tokens,
    ln1_gain,
    ln1_bias,
    w_qkv,
    w_attn_out,
    ln2_gain,
    ln2_bias,
    router_weight,
    w_in,
    w_expert_out,
    router_noise,
    routes,
    cotangent,
):
    move = Mover(n_dp)
    token_count = tokens.shape[0]
    imgs = token_count // SEQ // 4
    d_own = w_qkv.shape[0]
    ways = [c % 2 for c in range(imgs)]

    pack = jnp.concatenate(
        [w_qkv[:, 0], w_qkv[:, 1], w_qkv[:, 2], jnp.transpose(w_attn_out)], axis=1
    ).astype(BF16)
    vectors = jnp.stack([ln1_gain, ln1_bias, ln2_gain, ln2_bias] + [jnp.zeros_like(ln1_gain)] * 4)
    small = jnp.concatenate([vectors, jnp.transpose(router_weight)], axis=0).astype(BF16)
    small = jnp.pad(small, ((0, 0), (0, D - d_own)))
    pack = jnp.concatenate([pack, small], axis=0)
    w_own = jnp.zeros((E * d_own, D), BF16)
    par = jnp.zeros((E, 16, d_own), BF16)
    for member, block in move.both_ways(pack):
        w_own = lax.dynamic_update_slice_in_dim(w_own, block[:d_own], member * d_own, 0)
        par = lax.dynamic_update_slice_in_dim(par, block[None, d_own:, :d_own], member, 0)
    w_own = move.all_groups(w_own, 0)
    par = move.all_groups(par, 0)
    par = jnp.transpose(par, (1, 0, 2)).reshape(16, D)
    wa = jnp.stack([w_own, move.other(w_own, 2)])
    wb = move.other(wa, 1)

    x = image_blocks(tokens, move.tensor, imgs)
    dy = image_blocks(cotangent, move.tensor, imgs)
    dy_ring = [move.ring_blocks(dy[c], ways[c]) for c in range(imgs)]
    out_rows = jnp.transpose(w_expert_out, (0, 2, 1))
    ew = jnp.zeros((2, E * d_own, FFS), BF16)
    for by in range(E):
        to = lax.rem(move.member + by, E)
        block = jnp.stack(
            [lax.dynamic_index_in_dim(w, to, 0, False).astype(BF16) for w in (w_in, out_rows)]
        )
        came = lax.rem(move.member - by + E, E)
        ew = lax.dynamic_update_slice_in_dim(ew, move.shift(block, by) if by else block, came * d_own, 1)
    ew = move.all_groups(ew, 1)
    ewa = jnp.stack([ew, move.other(ew, 2)])
    ewb = move.other(ewa, 1)

    keep = image_lanes(kept_pairs(routes), move.tensor, imgs)
    noise = image_lanes(jnp.transpose(router_noise), move.tensor, imgs)
    fwd = [attn_forward(x[c], par, wa, wb, noise[c], keep[c]) for c in range(imgs)]
    chunk, x1, qkv, o, lse, probs = (list(part) for part in zip(*fwd))

    h_ring = [move.ring_blocks(chunk[c], ways[c]) for c in range(imgs)]
    y, dh, rows, hid, tiles = experts(
        move.member, sum(h_ring, []), sum(dy_ring, []), ewa, ewb
    )
    dh_sum = [move.ring_sum(dh[c * E : (c + 1) * E], ways[c]) for c in range(imgs)]
    y_sum = [move.ring_sum(y[c * E : (c + 1) * E], ways[c]) for c in range(imgs)]
    grads_b = expert_grads(tiles, rows, hid, 2)
    grads_a = expert_grads(tiles, rows, hid, 0)
    pair = (grads_a.astype(F32) + move.other(grads_b, 1).astype(F32)).astype(BF16)
    g_exp = (pair[0].astype(F32) + move.other(pair[1], 2).astype(F32)).astype(BF16)
    g_exp = move.sum_groups(g_exp, 1)
    g_in = jnp.zeros((E, d_own, FFS), F32)
    g_out = jnp.zeros((E, d_own, FFS), F32)
    for by in range(E):
        to = lax.rem(move.member + by, E)
        block = lax.dynamic_slice_in_dim(g_exp, to * d_own, d_own, 1)
        came = lax.rem(move.member - by + E, E)
        block = (move.shift(block, by) if by else block).astype(F32)
        g_in = lax.dynamic_update_slice_in_dim(g_in, block[0:1], came, 0)
        g_out = lax.dynamic_update_slice_in_dim(g_out, block[1:2], came, 0)

    g_attn, g_small, d_tok = attn_backward(dh_sum, x1, x, dy, probs, qkv, o, lse, par, wa, wb)
    spread = jnp.transpose(g_small.reshape(16, n_dp, d_own), (1, 0, 2))
    spread = jnp.pad(spread, ((0, 0), (0, 0), (0, D - d_own)))
    packs = jnp.concatenate(
        [g_attn.reshape(4, n_dp, d_own, D), jnp.broadcast_to(spread[None], (4,) + spread.shape)], axis=2
    )
    pair = (packs[:2].astype(F32) + move.other(packs[2:], 1).astype(F32)).astype(BF16)
    packs = (pair[0].astype(F32) + move.other(pair[1], 2).astype(F32)).astype(BF16)
    packs = move.sum_groups(packs, 0)
    total = move.sum_both_ways(lambda member: lax.dynamic_index_in_dim(packs, member, 0, False))
    g_qkv = total[:d_own, : 9 * HD].reshape(d_own, 3, 3 * HD)
    g_attn_out = jnp.transpose(total[:d_own, 9 * HD :])
    g_small = total[d_own:, :d_own]

    def all_rows(blocks):
        own = jnp.concatenate([b[:SEQ] for b in blocks], axis=0)
        n = own.shape[0]
        two = jnp.stack([own, move.other(own, 2)])
        four = jnp.concatenate([two, move.other(two, 1)], axis=0)
        whole = jnp.zeros((4 * n, D), BF16)
        for at, mask in enumerate((0, 2, 1, 3)):
            whole = lax.dynamic_update_slice_in_dim(whole, four[at], (move.tensor ^ mask) * n, 0)
        return whole

    output = all_rows([(x1[c] + y_sum[c].astype(F32)).astype(BF16) for c in range(imgs)])
    d_tokens = all_rows([d_tok[c] for c in range(imgs)])
    return (
        output,
        d_tokens,
        g_small[0],
        g_small[1],
        g_qkv,
        g_attn_out,
        g_small[2],
        g_small[3],
        jnp.transpose(g_small[8:16]),
        g_in,
        jnp.transpose(g_out, (0, 2, 1)),
    )


def solution(mesh):
    in_specs = (
        P("dp", None),
        P("dp"),
        P("dp"),
        P("dp", None, "tensor"),
        P("tensor", "dp"),
        P("dp"),
        P("dp"),
        P("dp", None),
        P(None, "dp", "tensor"),
        P(None, "tensor", "dp"),
        P("dp", None),
        P("dp", None),
        P("dp", None),
    )
    out_specs = (
        P("dp", None),
        P("dp", None),
        P("dp"),
        P("dp"),
        P("dp", None, "tensor"),
        P("tensor", "dp"),
        P("dp"),
        P("dp"),
        P("dp", None),
        P(None, "dp", "tensor"),
        P(None, "tensor", "dp"),
    )
    return jax.shard_map(
        functools.partial(body, mesh.shape["dp"]),
        mesh=mesh,
        in_specs=in_specs,
        out_specs=out_specs,
        check_vma=False,
    )
```

```python
import functools

import jax
import jax.numpy as jnp
from jax import lax
from jax.experimental import pallas as pl
from jax.experimental.pallas import tpu as pltpu
from jax.sharding import PartitionSpec as P

D = 768
HD = 64
E = 8
TOP = 2
SEQ = 197
CAP = 689
PAD = 208
META = 200
TILE = 256
FFS = 768
EPS = 1e-06
VMEM_LIMIT = 60 * 1024 * 1024

F32 = jnp.float32
BF16 = jnp.bfloat16


def dot(a, b):
    return jnp.dot(a, b, preferred_element_type=F32)


def dot_nt(a, b):
    return lax.dot_general(a, b, (((1,), (1,)), ((), ())), preferred_element_type=F32)


def dot_tn(a, b):
    return lax.dot_general(a, b, (((0,), (0,)), ((), ())), preferred_element_type=F32)


def iota(shape, dim):
    return lax.broadcasted_iota(jnp.int32, shape, dim)


def normalise(values):
    centred = values - jnp.mean(values, axis=-1, keepdims=True)
    scale = lax.rsqrt(jnp.mean(centred * centred, axis=-1, keepdims=True) + EPS)
    return centred * scale, scale


def norm_back(grad, unit, scale, gain):
    g = grad * gain
    return scale * (
        g - jnp.mean(g, axis=-1, keepdims=True) - unit * jnp.mean(g * unit, axis=-1, keepdims=True)
    )


def load_attn_weights(order_ref, wa_ref, wb_ref, w_s, sem):
    rows = D // E
    copies = []
    for r in range(4):
        src = wa_ref if r < 2 else wb_ref
        for b in range(E):
            at = pl.ds(pl.multiple_of(order_ref[b] * rows, 16), rows)
            copies.append(pltpu.make_async_copy(src.at[r % 2, b, pl.ds(0, rows)], w_s.at[r, at], sem.at[r, b]))
            copies[-1].start()
    return [copies[r * E : (r + 1) * E] for r in range(4)]


def attn_forward_kernel(
    order_ref, x_ref, par_ref, wa_ref, wb_ref, noise_ref, keep_ref,
    chunk_ref, x1_ref, qkv_ref, o_ref, lse_ref, probs_ref,
    w_s, sem,
):
    copies = load_attn_weights(order_ref, wa_ref, wb_ref, w_s, sem)
    par = par_ref[...].astype(F32)
    x = x_ref[...].astype(F32)
    unit, _ = normalise(x)
    h1 = (unit * par[0:1] + par[1:2]).astype(BF16)
    acc = x
    lse = jnp.zeros((PAD, 128), F32)
    key_ok = iota((PAD, PAD), 1) < SEQ
    lane = iota((PAD, 128), 1)
    for r in range(4):
        for copy in copies[r]:
            copy.wait()
        w = w_s[r]
        qkv = dot(h1, w[:, : 9 * HD]).astype(BF16)
        qkv_ref[r] = qkv
        outs = []
        for h in range(3):
            q = qkv[:, h * HD : (h + 1) * HD]
            k = qkv[:, (3 + h) * HD : (4 + h) * HD]
            v = qkv[:, (6 + h) * HD : (7 + h) * HD]
            s = jnp.where(key_ok, dot_nt(q, k) * HD ** (-0.5), -1e30)
            top = jnp.max(s, axis=-1, keepdims=True)
            p = jnp.exp(s - top)
            total = jnp.sum(p, axis=-1, keepdims=True)
            outs.append(dot((p * (1.0 / total)).astype(BF16), v).astype(BF16))
            lse = jnp.where(lane == 3 * r + h, top + jnp.log(total), lse)
        o = jnp.concatenate(outs, axis=1)
        o_ref[r] = o
        acc = acc + dot_nt(o, w[:, 9 * HD :])
    lse_ref[...] = lse
    x1_ref[...] = acc
    unit2, _ = normalise(acc)
    h2 = (unit2 * par[2:3] + par[3:4]).astype(BF16)
    logits = dot_nt(par_ref[8:16, :], h2) + noise_ref[...]
    e = jnp.exp(logits - jnp.max(logits, axis=0, keepdims=True))
    probs = e / jnp.sum(e, axis=0, keepdims=True)
    probs_ref[...] = probs
    gates = jnp.where(keep_ref[...] > 0, probs, -1.0)
    chunk_ref[...] = h2
    tail = jnp.concatenate([gates, jnp.zeros((8, D - PAD), F32)], axis=1)
    low = h2[PAD - 16 :, :].astype(F32)
    chunk_ref[PAD - 16 :, :] = jnp.concatenate([low[:8], tail], axis=0).astype(BF16)


def attn_forward(order, x, par, wa, wb, noise, keep):
    vm = pl.BlockSpec(memory_space=pltpu.VMEM)
    hbm = pl.BlockSpec(memory_space=pl.ANY)
    sm = pl.BlockSpec(memory_space=pltpu.SMEM)
    return pl.pallas_call(
        attn_forward_kernel,
        out_shape=(
            jax.ShapeDtypeStruct((PAD, D), BF16),
            jax.ShapeDtypeStruct((PAD, D), F32),
            jax.ShapeDtypeStruct((4, PAD, 9 * HD), BF16),
            jax.ShapeDtypeStruct((4, PAD, 3 * HD), BF16),
            jax.ShapeDtypeStruct((PAD, 128), F32),
            jax.ShapeDtypeStruct((E, PAD), F32),
        ),
        in_specs=[sm, vm, vm, hbm, hbm, vm, vm],
        out_specs=(vm,) * 6,
        scratch_shapes=[pltpu.VMEM((4, D, D), BF16), pltpu.SemaphoreType.DMA((4, E))],
        compiler_params=pltpu.CompilerParams(vmem_limit_bytes=VMEM_LIMIT),
        cost_estimate=pl.CostEstimate(flops=3 * 10**9, bytes_accessed=10**7, transcendentals=10**6),
        name="attn_forward",
    )(order, x, par, wa, wb, noise, keep)


def expert_kernel(nb, who_ref, *refs):
    h_in = refs[:nb]
    dy_in, w_in = refs[nb], refs[nb + 1 : nb + 5]
    outs = refs[nb + 5 :]
    dx_out = outs[:nb]
    y_out, rows_out, hid_out, tiles_ref = outs[nb : nb + 4]
    (h, dy, y_t, dx_t, w_s, gate_s, slot_s, dgate_s, xs, dys, hid_s, rows_s, lo_s, hi_s, in_sem, out_sem, row_sem, hid_sem, w_sem) = outs[nb + 4 :]
    me = who_ref[nb]
    loads = []
    for b in range(nb):
        for ref, table, c in ((h_in[b], h, 0), (dy_in.at[who_ref[b]], dy, 1)):
            copy = pltpu.make_async_copy(ref, table.at[b], in_sem.at[c, b])
            copy.start()
            loads.append(copy)
    for b in range(E):
        at = pl.ds(pl.multiple_of(who_ref[nb + 1 + b] * (D // E), 16), D // E)
        for r in range(4):
            copy = pltpu.make_async_copy(w_in[r].at[b], w_s.at[r, :, at], w_sem.at[r, b])
            copy.start()
            loads.append(copy)
    y_t[...] = jnp.zeros_like(y_t)
    dx_t[...] = jnp.zeros_like(dx_t)
    dgate_s[...] = jnp.zeros_like(dgate_s)
    for copy in loads:
        copy.wait()

    row16 = iota((16, D), 0)
    for b in range(nb):
        meta = h[b, PAD - 16 : PAD, :].astype(F32)
        gate_s[b : b + 1, :] = jnp.sum(jnp.where(row16 == 8 + me, meta, 0.0), axis=0, keepdims=True)[:, :PAD]
    gates = gate_s[...]
    named = (gates >= 0) & (iota((nb, PAD), 1) < SEQ)
    ones = named.astype(F32).astype(BF16)
    upto = dot(ones, (iota((PAD, PAD), 0) <= iota((PAD, PAD), 1)).astype(F32).astype(BF16))
    count = dot(ones, jnp.ones((PAD, PAD), BF16)).astype(BF16)
    before = dot((iota((nb, nb), 0) > iota((nb, nb), 1)).astype(F32).astype(BF16), count)
    slot_s[...] = jnp.where(named, before + upto - 1.0, -1.0).astype(jnp.int32)
    ends = jnp.where(named, before + upto, before)
    for b in range(nb):
        lo_s[b] = jnp.max(before[b : b + 1, :]).astype(jnp.int32)
        hi_s[b] = jnp.max(ends[b : b + 1, :]).astype(jnp.int32)
    tiles = lax.div(hi_s[nb - 1] + TILE - 1, TILE)
    tiles_ref[0] = tiles

    def meets(b, first):
        return (lo_s[b] < first + TILE) & (hi_s[b] > first) & (hi_s[b] > lo_s[b])

    def place(b, first):
        return iota((TILE, PAD), 0) + first == slot_s[pl.ds(b, 1), :]

    def step(t, carry):
        first = t * TILE
        slot = lax.rem(t, 2)
        xs[...] = jnp.zeros_like(xs)
        dys[...] = jnp.zeros_like(dys)

        def collect(b, gcol):
            def one(gcol):
                hit = place(b, first)
                p = hit.astype(F32).astype(BF16)
                xs[...] += dot(p, h[b])
                dys[...] += dot(p, dy[b])
                return gcol + jnp.sum(jnp.where(hit, gate_s[pl.ds(b, 1), :], 0.0), axis=1, keepdims=True)

            return lax.cond(meets(b, first), one, lambda g: g, gcol)

        gcol = lax.fori_loop(0, nb, collect, jnp.zeros((TILE, 1), F32))

        def drain(s):
            pltpu.make_async_copy(rows_s.at[s], rows_out.at[:, pl.ds(0, TILE)], row_sem.at[s]).wait()
            pltpu.make_async_copy(hid_s.at[s], hid_out.at[:, pl.ds(0, TILE)], hid_sem.at[s]).wait()

        @pl.when(t >= 2)
        def _():
            drain(slot)

        x = xs[...].astype(BF16)
        g_rows = (dys[...] * gcol).astype(BF16)
        rows_s[slot, 0] = x
        rows_s[slot, 1] = g_rows
        y = jnp.zeros((TILE, D), F32)
        dx = jnp.zeros((TILE, D), F32)
        for r in range(4):
            w1, w2 = w_s.at[r, 0], w_s.at[r, 1]
            a = dot(x, w1[...])
            a2 = a * a
            th = jnp.tanh(0.7978845608028654 * a * (1.0 + 0.044715 * a2))
            half = 0.5 * (1.0 + th)
            hid = (a * half).astype(BF16)
            slope = half + 0.5 * a * (1.0 - th * th) * (0.7978845608028654 * (1.0 + 3 * 0.044715 * a2))
            da = (dot(g_rows, w2[...]) * slope).astype(BF16)
            y = y + dot_nt(hid, w2[...])
            dx = dx + dot_nt(da, w1[...])
            hid_s[slot, 0, :, r * FFS : (r + 1) * FFS] = da
            hid_s[slot, 1, :, r * FFS : (r + 1) * FFS] = hid
        at = pl.ds(pl.multiple_of(first, TILE), TILE)
        pltpu.make_async_copy(rows_s.at[slot], rows_out.at[:, at], row_sem.at[slot]).start()
        pltpu.make_async_copy(hid_s.at[slot], hid_out.at[:, at], hid_sem.at[slot]).start()
        dgate = jnp.sum(dys[...] * y, axis=1, keepdims=True)
        y_low = (y * gcol).astype(BF16)
        dx_low = dx.astype(BF16)

        def give(b, carry):
            @pl.when(meets(b, first))
            def _():
                hit = place(b, first)
                p = hit.astype(F32).astype(BF16)
                y_t[b] = y_t[b] + dot_tn(p, y_low).astype(BF16)
                dx_t[b] = dx_t[b] + dot_tn(p, dx_low).astype(BF16)
                dgate_s[pl.ds(b, 1), :] += jnp.sum(jnp.where(hit, dgate, 0.0), axis=0, keepdims=True)

            return carry

        lax.fori_loop(0, nb, give, 0)
        return carry

    lax.fori_loop(0, tiles, step, 0)
    for back in (1, 2):

        @pl.when(tiles >= back)
        def _():
            s = lax.rem(tiles - back, 2)
            pltpu.make_async_copy(rows_s.at[s], rows_out.at[:, pl.ds(0, TILE)], row_sem.at[s]).wait()
            pltpu.make_async_copy(hid_s.at[s], hid_out.at[:, pl.ds(0, TILE)], hid_sem.at[s]).wait()

    stores = []
    for b in range(nb):
        tail = dx_t[b, PAD - 16 : PAD, :].astype(F32)
        line = jnp.concatenate([dgate_s[b : b + 1, :], jnp.zeros((1, D - PAD), F32)], axis=1)
        dx_t[b, PAD - 16 : PAD, :] = (tail + jnp.where(row16 == 8 + me, line, 0.0)).astype(BF16)
        for table, ref, c in ((y_t, y_out.at[who_ref[b]], 0), (dx_t, dx_out[b], 1)):
            copy = pltpu.make_async_copy(table.at[b], ref, out_sem.at[c, b])
            copy.start()
            stores.append(copy)
    for copy in stores:
        copy.wait()


def expert_rows(nb):
    return -(-nb * SEQ // TILE) * TILE


def experts(who, h_blocks, dy_all, weights):
    nb = len(h_blocks)
    rows = expert_rows(nb)
    hbm = pl.BlockSpec(memory_space=pl.ANY)
    sm = pl.BlockSpec(memory_space=pltpu.SMEM)
    block = jax.ShapeDtypeStruct((PAD, D), BF16)
    outs = pl.pallas_call(
        functools.partial(expert_kernel, nb),
        out_shape=[block] * nb
        + [
            jax.ShapeDtypeStruct((nb, PAD, D), BF16),
            jax.ShapeDtypeStruct((2, rows, D), BF16),
            jax.ShapeDtypeStruct((2, rows, 4 * FFS), BF16),
            jax.ShapeDtypeStruct((1,), jnp.int32),
        ],
        in_specs=[sm] + [hbm] * (nb + 5),
        out_specs=[hbm] * (nb + 3) + [sm],
        scratch_shapes=[
            pltpu.VMEM((nb, PAD, D), BF16),
            pltpu.VMEM((nb, PAD, D), BF16),
            pltpu.VMEM((nb, PAD, D), BF16),
            pltpu.VMEM((nb, PAD, D), BF16),
            pltpu.VMEM((4, 2, D, FFS), BF16),
            pltpu.VMEM((nb, PAD), F32),
            pltpu.VMEM((nb, PAD), jnp.int32),
            pltpu.VMEM((nb, PAD), F32),
            pltpu.VMEM((TILE, D), F32),
            pltpu.VMEM((TILE, D), F32),
            pltpu.VMEM((2, 2, TILE, 4 * FFS), BF16),
            pltpu.VMEM((2, 2, TILE, D), BF16),
            pltpu.SMEM((nb,), jnp.int32),
            pltpu.SMEM((nb,), jnp.int32),
            pltpu.SemaphoreType.DMA((2, nb)),
            pltpu.SemaphoreType.DMA((2, nb)),
            pltpu.SemaphoreType.DMA((2,)),
            pltpu.SemaphoreType.DMA((2,)),
            pltpu.SemaphoreType.DMA((4, E)),
        ],
        compiler_params=pltpu.CompilerParams(vmem_limit_bytes=VMEM_LIMIT),
        cost_estimate=pl.CostEstimate(flops=30 * 10**9, bytes_accessed=4 * 10**7, transcendentals=4 * 10**6),
        name="experts",
    )(who, *h_blocks, dy_all, *weights)
    return outs[:nb], *outs[nb:]


def expert_grad_kernel(tiles_ref, rows_ref, hid_ref, out_ref, acc):
    acc[...] = jnp.zeros_like(acc)

    def step(t, carry):
        at = pl.ds(pl.multiple_of(t * TILE, TILE), TILE)
        acc[...] += dot_tn(rows_ref[0, at, :], hid_ref[0, at, :])
        return carry

    lax.fori_loop(0, tiles_ref[0], step, 0)
    out_ref[0] = acc[...].astype(BF16)


def expert_grads(tiles, rows, hid, kind, base):
    n = rows.shape[1]
    return pl.pallas_call(
        expert_grad_kernel,
        grid_spec=pltpu.PrefetchScalarGridSpec(
            num_scalar_prefetch=1,
            grid=(2,),
            in_specs=[
                pl.BlockSpec((1, n, D), lambda s, _: (kind, 0, 0)),
                pl.BlockSpec((1, n, FFS), lambda s, _: (kind, 0, base + s)),
            ],
            out_specs=pl.BlockSpec((1, D, FFS), lambda s, _: (s, 0, 0)),
            scratch_shapes=[pltpu.VMEM((D, FFS), F32)],
        ),
        out_shape=jax.ShapeDtypeStruct((2, D, FFS), BF16),
        compiler_params=pltpu.CompilerParams(vmem_limit_bytes=VMEM_LIMIT),
        cost_estimate=pl.CostEstimate(flops=4 * 10**9, bytes_accessed=15 * 10**6, transcendentals=0),
        name="expert_grads",
    )(tiles, rows, hid)


def unpack_kernel(who_ref, *refs):
    blocks, out_ref = refs[:E], refs[E]
    for by in range(E):
        out_ref[who_ref[by]] = blocks[by][...].astype(F32)


def unpack(who, blocks):
    vm = pl.BlockSpec(memory_space=pltpu.VMEM)
    return pl.pallas_call(
        unpack_kernel,
        out_shape=jax.ShapeDtypeStruct((E,) + blocks[0].shape, F32),
        in_specs=[pl.BlockSpec(memory_space=pltpu.SMEM)] + [vm] * E,
        out_specs=vm,
        compiler_params=pltpu.CompilerParams(vmem_limit_bytes=VMEM_LIMIT),
        cost_estimate=pl.CostEstimate(flops=10**6, bytes_accessed=4 * 10**6, transcendentals=0),
        name="unpack",
    )(who, *blocks)


def lay_out_kernel(imgs, at_ref, *refs):
    parts, out_ref, held, sem = refs[:4], refs[4], refs[5], refs[6]
    copies = [pltpu.make_async_copy(parts[s], held.at[s], sem.at[s]) for s in range(4)]
    for copy in copies:
        copy.start()
    for copy in copies:
        copy.wait()
    for i in range(4 * imgs):
        out_ref[i * SEQ : (i + 1) * SEQ, :] = held[at_ref[i // imgs], i % imgs, :SEQ, :]


def lay_out(at, parts):
    imgs = parts[0].shape[0]
    hbm = pl.BlockSpec(memory_space=pl.ANY)
    return pl.pallas_call(
        functools.partial(lay_out_kernel, imgs),
        out_shape=jax.ShapeDtypeStruct((4 * imgs * SEQ, D), BF16),
        in_specs=[pl.BlockSpec(memory_space=pltpu.SMEM)] + [hbm] * 4,
        out_specs=pl.BlockSpec(memory_space=pltpu.VMEM),
        scratch_shapes=[pltpu.VMEM((4, imgs, PAD, D), BF16), pltpu.SemaphoreType.DMA((4,))],
        compiler_params=pltpu.CompilerParams(vmem_limit_bytes=VMEM_LIMIT),
        cost_estimate=pl.CostEstimate(flops=10**6, bytes_accessed=5 * 10**6, transcendentals=0),
        name="lay_out",
    )(at, *parts)


def attn_backward_kernel(imgs, *refs):
    dh_in, x1_in, x_in, dy_in, probs_in, qkv_in, o_in, lse_in = (
        refs[i * imgs : (i + 1) * imgs] for i in range(8)
    )
    order_ref, par_ref, wa_ref, wb_ref = refs[8 * imgs : 8 * imgs + 4]
    packs, dtok_ref = refs[8 * imgs + 4 : 8 * imgs + 7], refs[8 * imgs + 7]
    dx1_s, low_s, h1_s, dh1_s, dqkv_s, o_s, w_s, sem = refs[8 * imgs + 8 :]
    n_dp, d_own = packs[0].shape[0], packs[0].shape[1] - 16
    copies = load_attn_weights(order_ref, wa_ref, wb_ref, w_s, sem)

    def pack_of(r):
        return packs[r] if r < 2 else packs[2].at[:, r - 2]

    par = par_ref[...].astype(F32)
    router = par_ref[8:16, :]
    row_ok = iota((PAD, 1), 0) < SEQ
    lane_ok = iota((E, PAD), 1) < SEQ
    key_ok = iota((PAD, PAD), 1) < SEQ
    small2g = jnp.zeros((1, D), F32)
    small2b = jnp.zeros((1, D), F32)
    g_router = jnp.zeros((E, D), F32)
    for c in range(imgs):
        span = slice(c * PAD, (c + 1) * PAD)
        arrived = dh_in[c][...].astype(F32)
        dgate = arrived[PAD - 8 :, :PAD]
        probs = probs_in[c][...]
        dlogits = probs * (dgate - jnp.sum(probs * dgate, axis=0, keepdims=True))
        dlogits = jnp.where(lane_ok, dlogits, 0.0).astype(BF16)
        unit, scale = normalise(x1_in[c][...])
        h2 = (unit * par[2:3] + par[3:4]).astype(BF16)
        g_router = g_router + dot(dlogits, h2)
        dh2 = jnp.where(row_ok, arrived + dot_tn(dlogits, router), 0.0)
        small2g = small2g + jnp.sum(dh2 * unit, axis=0, keepdims=True)
        small2b = small2b + jnp.sum(dh2, axis=0, keepdims=True)
        dx1 = dy_in[c][...].astype(F32) + norm_back(dh2, unit, scale, par[2:3])
        dx1_s[span, :] = dx1
        low_s[span, :] = dx1.astype(BF16)
        unit1, _ = normalise(x_in[c][...].astype(F32))
        h1_s[span, :] = (unit1 * par[0:1] + par[1:2]).astype(BF16)
    low = low_s[...]
    h1 = h1_s[...]
    for r in range(4):
        for copy in copies[r]:
            copy.wait()
        w = w_s[r]
        dout = dot(low, w[:, 9 * HD :]).astype(BF16)
        for c in range(imgs):
            span = slice(c * PAD, (c + 1) * PAD)
            qkv = qkv_in[c][r]
            lse = lse_in[c][...]
            o_s[span, :] = o_in[c][r]
            dqs, dks, dvs = [], [], []
            for h in range(3):
                q = qkv[:, h * HD : (h + 1) * HD]
                k = qkv[:, (3 + h) * HD : (4 + h) * HD]
                v = qkv[:, (6 + h) * HD : (7 + h) * HD]
                do = dout[span, h * HD : (h + 1) * HD]
                s = dot_nt(q, k) * HD ** (-0.5)
                p = jnp.where(key_ok, jnp.exp(s - lse[:, 3 * r + h : 3 * r + h + 1]), 0.0)
                dvs.append(dot_tn(p.astype(BF16), do).astype(BF16))
                dp = dot_nt(do, v)
                ds = (p * (dp - jnp.sum(p * dp, axis=-1, keepdims=True))).astype(BF16)
                dqs.append((dot(ds, k) * HD ** (-0.5)).astype(BF16))
                dks.append((dot_tn(ds, q) * HD ** (-0.5)).astype(BF16))
            dqkv_s[span, :] = jnp.concatenate(dqs + dks + dvs, axis=1)
        dqkv = dqkv_s[...]
        part = dot_nt(dqkv, w[:, : 9 * HD])
        dh1_s[...] = part if r == 0 else dh1_s[...] + part
        grad = jnp.concatenate([dot_tn(h1, dqkv), dot_tn(low, o_s[...])], axis=1).astype(BF16)
        for i in range(n_dp):
            pack_of(r)[i, :d_own, :] = grad[i * d_own : (i + 1) * d_own]
    small1g = jnp.zeros((1, D), F32)
    small1b = jnp.zeros((1, D), F32)
    for c in range(imgs):
        span = slice(c * PAD, (c + 1) * PAD)
        dh1 = jnp.where(row_ok, dh1_s[span, :], 0.0)
        unit1, scale1 = normalise(x_in[c][...].astype(F32))
        small1g = small1g + jnp.sum(dh1 * unit1, axis=0, keepdims=True)
        small1b = small1b + jnp.sum(dh1, axis=0, keepdims=True)
        dtok_ref[c] = (dx1_s[span, :] + norm_back(dh1, unit1, scale1, par[0:1])).astype(BF16)
    small = jnp.concatenate([small1g, small1b, small2g, small2b, jnp.zeros((4, D), F32), g_router], axis=0)
    for i in range(n_dp):
        line = jnp.concatenate([small[:, i * d_own : (i + 1) * d_own], jnp.zeros((16, D - d_own), F32)], axis=1)
        for r in range(4):
            pack_of(r)[i, d_own:, :] = line.astype(BF16)


def attn_backward(dh, x1, x, dy, probs, qkv, o, lse, order, par, wa, wb, n_dp):
    imgs = len(dh)
    hbm = pl.BlockSpec(memory_space=pl.ANY)
    sm = pl.BlockSpec(memory_space=pltpu.SMEM)
    pack = (n_dp, D // n_dp + 16, D)
    vm = pl.BlockSpec(memory_space=pltpu.VMEM)
    rows = imgs * PAD
    return pl.pallas_call(
        functools.partial(attn_backward_kernel, imgs),
        out_shape=(
            jax.ShapeDtypeStruct(pack, BF16),
            jax.ShapeDtypeStruct(pack, BF16),
            jax.ShapeDtypeStruct((n_dp, 2) + pack[1:], BF16),
            jax.ShapeDtypeStruct((imgs, PAD, D), BF16),
        ),
        in_specs=[vm] * (8 * imgs) + [sm, vm, hbm, hbm],
        out_specs=(vm,) * 4,
        scratch_shapes=[
            pltpu.VMEM((rows, D), F32),
            pltpu.VMEM((rows, D), BF16),
            pltpu.VMEM((rows, D), BF16),
            pltpu.VMEM((rows, D), F32),
            pltpu.VMEM((rows, 9 * HD), BF16),
            pltpu.VMEM((rows, 3 * HD), BF16),
            pltpu.VMEM((4, D, D), BF16),
            pltpu.SemaphoreType.DMA((4, E)),
        ],
        compiler_params=pltpu.CompilerParams(vmem_limit_bytes=VMEM_LIMIT),
        cost_estimate=pl.CostEstimate(flops=12 * 10**9, bytes_accessed=2 * 10**7, transcendentals=2 * 10**6),
        name="attn_backward",
    )(*dh, *x1, *x, *dy, *probs, *qkv, *o, *lse, order, par, wa, wb)


RING = (0, 2, 4, 6, 7, 5, 3, 1)


def ring_place(member):
    even = lax.rem(member, 2) == 0
    return jnp.where(even, lax.div(member, 2), E - 1 - lax.div(member, 2))


def ring_member(place):
    return jnp.where(place < E // 2, 2 * place, 2 * E - 1 - 2 * place)


class Mover:
    def __init__(self, n_dp):
        self.n_dp = n_dp
        self.groups = n_dp // E
        self.me = lax.axis_index("dp")
        self.member = lax.rem(self.me, E)
        self.group = lax.div(self.me, E)
        self.tensor = lax.axis_index("tensor")
        self.place = ring_place(self.member)
        bases = range(0, n_dp, E)
        self.ring = (
            [(b + RING[i], b + RING[(i + 1) % E]) for b in bases for i in range(E)],
            [(b + RING[(i + 1) % E], b + RING[i]) for b in bases for i in range(E)],
        )

    def along(self, value, way):
        return lax.ppermute(value, "dp", self.ring[way])

    def shift(self, value, by):
        perm = [(b + i, b + (i + by) % E) for b in range(0, self.n_dp, E) for i in range(E)]
        return lax.ppermute(value, "dp", perm)

    def shift_group(self, value, by):
        return lax.ppermute(value, "dp", [(k, (k + by * E) % self.n_dp) for k in range(self.n_dp)])

    def other(self, value, mask):
        return lax.ppermute(value, "tensor", [(k, k ^ mask) for k in range(4)])

    def behind(self, way, k):
        step = -k if way == 0 else k
        return ring_member(lax.rem(self.place + step + E, E))

    def group_lists(self):
        if self.groups == 1:
            return None
        return [[b + i for i in range(E)] for b in range(0, self.n_dp, E)]

    def gather(self, value):
        return lax.all_gather(value, "dp", axis=0, tiled=False, axis_index_groups=self.group_lists())

    def scatter_sum(self, value):
        return lax.psum_scatter(
            value, "dp", scatter_dimension=0, tiled=False, axis_index_groups=self.group_lists()
        )

    def ring_blocks(self, block, way):
        blocks = [block]
        for _ in range(E - 1):
            blocks.append(self.along(blocks[-1], way))
        return blocks

    def ring_sum(self, blocks, way):
        total = blocks[1]
        for k in range(2, E + 1):
            total = self.along(total, way)
            total = (total.astype(F32) + blocks[k % E].astype(F32)).astype(BF16)
        return total

    def both_ways(self, block):
        found = [(self.member, block)]
        ahead = back = block
        for k in range(1, E // 2 + 1):
            ahead = self.along(ahead, 0)
            found.append((self.behind(0, k), ahead))
            if k < E // 2:
                back = self.along(back, 1)
                found.append((self.behind(1, k), back))
        return found

    def sum_both_ways(self, block_for):
        def chain(way, steps):
            total = block_for(self.behind(1 - way, steps)).astype(BF16)
            for k in range(steps - 1, -1, -1):
                total = self.along(total, way)
                if k:
                    total = (total.astype(F32) + block_for(self.behind(1 - way, k)).astype(F32)).astype(BF16)
            return total

        ahead = chain(0, E // 2)
        back = chain(1, E // 2 - 1)
        return ahead.astype(F32) + back.astype(F32) + block_for(self.member).astype(F32)

    def in_order(self, members, parts, d_own):
        if self.groups == 1:
            return jnp.stack(members), jnp.stack([jnp.stack(blocks) for blocks in parts])
        wholes = []
        for blocks in parts:
            rows = jnp.zeros((E * d_own,) + blocks[0].shape[1:], BF16)
            for member, block in zip(members, blocks):
                rows = lax.dynamic_update_slice_in_dim(rows, block[:d_own], member * d_own, 0)
            wholes.append(self.all_groups(rows, 0).reshape((E, D // E) + blocks[0].shape[1:]))
        return jnp.arange(E, dtype=jnp.int32), jnp.stack(wholes)

    def all_groups(self, part, dim):
        if self.groups == 1:
            return part
        size = part.shape[dim]
        shape = part.shape[:dim] + (size * self.groups,) + part.shape[dim + 1 :]
        whole = lax.dynamic_update_slice_in_dim(jnp.zeros(shape, part.dtype), part, self.group * size, dim)
        for by in range(1, self.groups):
            came = lax.rem(self.group - by + self.groups, self.groups)
            whole = lax.dynamic_update_slice_in_dim(whole, self.shift_group(part, by), came * size, dim)
        return whole

    def sum_groups(self, whole, dim):
        if self.groups == 1:
            return whole
        size = whole.shape[dim] // self.groups
        total = lax.dynamic_slice_in_dim(whole, self.group * size, size, dim).astype(F32)
        for by in range(1, self.groups):
            to = lax.rem(self.group + by, self.groups)
            part = lax.dynamic_slice_in_dim(whole, to * size, size, dim)
            total = total + self.shift_group(part, by).astype(F32)
        return total.astype(whole.dtype)


def after(value, *first):
    return lax.optimization_barrier((value, first))[0]


def _slot(tensor, t):
    apart = lax.bitwise_xor(tensor, t)
    return lax.div(apart, 2) + 2 * lax.rem(apart, 2)


def image_blocks(rows, tensor, imgs):
    first = tensor * (imgs * SEQ)
    return [
        jnp.pad(lax.dynamic_slice_in_dim(rows, first + c * SEQ, SEQ, 0), ((0, PAD - SEQ), (0, 0)))
        for c in range(imgs)
    ]


def image_lanes(lanes, tensor, imgs):
    first = tensor * (imgs * SEQ)
    return [
        jnp.pad(lax.dynamic_slice_in_dim(lanes, first + c * SEQ, SEQ, 1), ((0, 0), (0, PAD - SEQ)))
        for c in range(imgs)
    ]


def kept_pairs(routes):
    chosen = jnp.transpose(routes).reshape(1, -1)
    named = (chosen == jnp.arange(E, dtype=jnp.int32)[:, None]).astype(jnp.int32)
    kept = named * (jnp.cumsum(named, axis=1) <= CAP)
    return jnp.sum(kept.reshape(E, TOP, -1), axis=1).astype(F32)


def body(
    n_dp,
    tokens,
    ln1_gain,
    ln1_bias,
    w_qkv,
    w_attn_out,
    ln2_gain,
    ln2_bias,
    router_weight,
    w_in,
    w_expert_out,
    router_noise,
    routes,
    cotangent,
):
    move = Mover(n_dp)
    token_count = tokens.shape[0]
    imgs = token_count // SEQ // 4
    d_own = w_qkv.shape[0]
    ways = [c % 2 for c in range(imgs)]

    pack = jnp.concatenate(
        [w_qkv[:, 0], w_qkv[:, 1], w_qkv[:, 2], jnp.transpose(w_attn_out)], axis=1
    ).astype(BF16)
    vectors = jnp.stack([ln1_gain, ln1_bias, ln2_gain, ln2_bias] + [jnp.zeros_like(ln1_gain)] * 4)
    small = jnp.concatenate([vectors, jnp.transpose(router_weight)], axis=0).astype(BF16)
    small = jnp.pad(small, ((0, 0), (0, D - d_own)))
    pack = jnp.concatenate([pack, small], axis=0)
    found = move.both_ways(pack)
    par = jnp.zeros((E, 16, d_own), BF16)
    for member, block in found:
        par = lax.dynamic_update_slice_in_dim(par, block[None, d_own:, :d_own], member, 0)
    par = jnp.transpose(move.all_groups(par, 0), (1, 0, 2)).reshape(16, D)
    order, wa = move.in_order(
        [member for member, _ in found], [[b for _, b in found], [move.other(b, 2) for _, b in found]], d_own
    )
    wb = move.other(wa, 1)

    x = image_blocks(tokens, move.tensor, imgs)
    dy = image_blocks(cotangent, move.tensor, imgs)
    keep = image_lanes(kept_pairs(routes), move.tensor, imgs)
    noise = image_lanes(jnp.transpose(router_noise), move.tensor, imgs)
    out_rows = jnp.transpose(w_expert_out, (0, 2, 1))
    blocks = []
    for by in range(E):
        to = lax.rem(move.member + by, E)
        blocks.append(
            jnp.stack([lax.dynamic_index_in_dim(w, to, 0, False).astype(BF16) for w in (w_in, out_rows)])
        )
    blocks, dy_own, x, keep, noise, wb = lax.optimization_barrier((blocks, jnp.stack(dy), x, keep, noise, wb))
    dy_all = move.gather(dy_own)
    came = [lax.rem(move.member - by + E, E) for by in range(E)]
    blocks = [move.shift(blocks[by], by) if by else blocks[by] for by in range(E)]

    fwd = [attn_forward(order, x[c], par, wa, wb, noise[c], keep[c]) for c in range(imgs)]
    chunk, x1, qkv, o, lse, probs = (list(part) for part in zip(*fwd))

    blocks = after(blocks, chunk)
    e_order, e_own = move.in_order(came, [[b[kind] for b in blocks] for kind in range(2)], d_own)
    e_own = jnp.swapaxes(e_own, 0, 1)
    e_x = move.other(e_own, 2)
    weights = [e_own, e_x, move.other(e_own, 1), move.other(e_x, 1)]
    h_ring = [move.ring_blocks(chunk[c], ways[c]) for c in range(imgs)]
    who = [move.behind(ways[c], k) * imgs + c for c in range(imgs) for k in range(E)] + [move.member]
    who = jnp.concatenate([jnp.stack(who), e_order])
    dh, y_all, rows, hid, tiles = experts(who, sum(h_ring, []), dy_all.reshape(imgs * E, PAD, D), weights)
    dh = [dh[c * E : (c + 1) * E] for c in range(imgs)]
    dh_sum = [dh[c][1] for c in range(imgs)]
    g_work = {3: (1, 2), 4: (1, 0), 5: (0, 2), 6: (0, 0)}
    g_part = {}
    for k in range(2, E + 1):
        if k in g_work:
            part = expert_grads(tiles, rows, hid, *g_work[k])
            dh_sum, g_part[g_work[k]] = lax.optimization_barrier((dh_sum, part))
        for c in range(imgs):
            passed = move.along(dh_sum[c], ways[c])
            dh_sum[c] = (passed.astype(F32) + dh[c][k % E].astype(F32)).astype(BF16)
    y_all = after(y_all, dh_sum)
    y_sum = move.scatter_sum(y_all.reshape(E, imgs, PAD, D))
    g_exp = {}
    for kind in (1, 0):
        passed = move.other(g_part[kind, 2], 1).astype(F32)
        pair = [(g_part[kind, 0][s].astype(F32) + passed[s]).astype(BF16) for s in range(2)]
        total = (pair[0].astype(F32) + move.other(pair[1], 2).astype(F32)).astype(BF16)
        total = move.sum_groups(total, 0)
        blocks = []
        for by in range(E):
            to = lax.rem(move.member + by, E)
            block = lax.dynamic_slice_in_dim(total, to * d_own, d_own, 0)
            blocks.append(move.shift(block, by) if by else block)
        g_exp[kind] = blocks

    pack0, pack1, packs, d_tok = attn_backward(
        dh_sum, x1, x, dy, probs, qkv, o, lse, order, par, wa, wb, n_dp
    )
    passed = move.other(packs, 1)
    if move.groups > 1:
        pack0 = move.sum_groups((pack0.astype(F32) + passed[:, 0].astype(F32)).astype(BF16), 0)
        pack1 = move.sum_groups((pack1.astype(F32) + passed[:, 1].astype(F32)).astype(BF16), 0)
        passed = jnp.zeros((E, 2) + pack0.shape[1:], BF16)

    def pack_for(member):
        one, two = (lax.dynamic_index_in_dim(p, member, 0, False).astype(F32) for p in (pack0, pack1))
        came = lax.dynamic_index_in_dim(passed, member, 0, False).astype(F32)
        return one + came[0] + move.other((two + came[1]).astype(BF16), 2).astype(F32)

    total = move.sum_both_ways(pack_for)
    g_qkv = total[:d_own, : 9 * HD].reshape(d_own, 3, 3 * HD)
    g_attn_out = jnp.transpose(total[:d_own, 9 * HD :])
    g_small = total[d_own:, :d_own]

    at = jnp.stack([_slot(move.tensor, t) for t in range(4)])

    def all_rows(own):
        across = move.other(own, 2)
        return lay_out(at, [own, across, move.other(own, 1), move.other(across, 1)])

    d_tokens = all_rows(d_tok)
    output = all_rows((jnp.stack(x1) + y_sum.astype(F32)).astype(BF16))
    g_out, g_in = (unpack(jnp.stack(came), g_exp[kind]) for kind in (1, 0))
    return (
        output,
        d_tokens,
        g_small[0],
        g_small[1],
        g_qkv,
        g_attn_out,
        g_small[2],
        g_small[3],
        jnp.transpose(g_small[8:16]),
        g_in,
        jnp.transpose(g_out, (0, 2, 1)),
    )


def solution(mesh):
    in_specs = (
        P("dp", None),
        P("dp"),
        P("dp"),
        P("dp", None, "tensor"),
        P("tensor", "dp"),
        P("dp"),
        P("dp"),
        P("dp", None),
        P(None, "dp", "tensor"),
        P(None, "tensor", "dp"),
        P("dp", None),
        P("dp", None),
        P("dp", None),
    )
    out_specs = (
        P("dp", None),
        P("dp", None),
        P("dp"),
        P("dp"),
        P("dp", None, "tensor"),
        P("tensor", "dp"),
        P("dp"),
        P("dp"),
        P("dp", None),
        P(None, "dp", "tensor"),
        P(None, "tensor", "dp"),
    )
    return jax.shard_map(
        functools.partial(body, mesh.shape["dp"]),
        mesh=mesh,
        in_specs=in_specs,
        out_specs=out_specs,
        check_vma=False,
    )
```

```python
import functools

import jax
import jax.numpy as jnp
from jax import lax
from jax.experimental import pallas as pl
from jax.experimental.pallas import tpu as pltpu
from jax.sharding import PartitionSpec as P

D = 768
HD = 64
E = 8
TOP = 2
SEQ = 197
CAP = 689
PAD = 208
META = 200
TILE = 256
FFS = 768
EPS = 1e-06
VMEM_LIMIT = 60 * 1024 * 1024

F32 = jnp.float32
BF16 = jnp.bfloat16


def dot(a, b):
    return jnp.dot(a, b, preferred_element_type=F32)


def dot_nt(a, b):
    return lax.dot_general(a, b, (((1,), (1,)), ((), ())), preferred_element_type=F32)


def dot_tn(a, b):
    return lax.dot_general(a, b, (((0,), (0,)), ((), ())), preferred_element_type=F32)


def iota(shape, dim):
    return lax.broadcasted_iota(jnp.int32, shape, dim)


def normalise(values):
    centred = values - jnp.mean(values, axis=-1, keepdims=True)
    scale = lax.rsqrt(jnp.mean(centred * centred, axis=-1, keepdims=True) + EPS)
    return centred * scale, scale


def norm_back(grad, unit, scale, gain):
    g = grad * gain
    return scale * (
        g - jnp.mean(g, axis=-1, keepdims=True) - unit * jnp.mean(g * unit, axis=-1, keepdims=True)
    )


def params_of(w_own):
    return jnp.transpose(w_own[:, D:].astype(F32))[:16]


def attend(x, par, w_of, noise, keep, chunk_ref, x1_ref, qkv_ref, o_ref, lse_ref, probs_ref):
    x = x.astype(F32)
    unit, _ = normalise(x)
    h1 = (unit * par[0:1] + par[1:2]).astype(BF16)
    acc = x
    lse = jnp.zeros((PAD, 128), F32)
    key_ok = iota((PAD, PAD), 1) < SEQ
    lane = iota((PAD, 128), 1)
    for r in range(4):
        w = w_of(r)
        qkv = dot(h1, w[:, : 9 * HD]).astype(BF16)
        qkv_ref[r] = qkv
        outs = []
        for h in range(3):
            q = qkv[:, h * HD : (h + 1) * HD]
            k = qkv[:, (3 + h) * HD : (4 + h) * HD]
            v = qkv[:, (6 + h) * HD : (7 + h) * HD]
            s = jnp.where(key_ok, dot_nt(q, k) * HD ** (-0.5), -1e30)
            top = jnp.max(s, axis=-1, keepdims=True)
            p = jnp.exp(s - top)
            total = jnp.sum(p, axis=-1, keepdims=True)
            outs.append(dot((p * (1.0 / total)).astype(BF16), v).astype(BF16))
            lse = jnp.where(lane == 3 * r + h, top + jnp.log(total), lse)
        o = jnp.concatenate(outs, axis=1)
        o_ref[r] = o
        acc = acc + dot_nt(o, w[:, 9 * HD : D])
    lse_ref[...] = lse
    x1_ref[...] = acc
    unit2, _ = normalise(acc)
    h2 = (unit2 * par[2:3] + par[3:4]).astype(BF16)
    logits = dot_nt(par[8:16].astype(BF16), h2) + noise
    e = jnp.exp(logits - jnp.max(logits, axis=0, keepdims=True))
    probs = e / jnp.sum(e, axis=0, keepdims=True)
    probs_ref[...] = probs
    gates = jnp.where(keep > 0, probs, -1.0)
    chunk_ref[...] = h2
    tail = jnp.concatenate([gates, jnp.zeros((8, D - PAD), F32)], axis=1)
    low = h2[PAD - 16 :, :].astype(F32)
    chunk_ref[PAD - 16 :, :] = jnp.concatenate([low[:8], tail], axis=0).astype(BF16)


def attn_shapes(imgs):
    return (
        jax.ShapeDtypeStruct((imgs, PAD, D), F32),
        jax.ShapeDtypeStruct((imgs, 4, PAD, 9 * HD), BF16),
        jax.ShapeDtypeStruct((imgs, 4, PAD, 3 * HD), BF16),
        jax.ShapeDtypeStruct((imgs, PAD, 128), F32),
        jax.ShapeDtypeStruct((imgs, E, PAD), F32),
    )


def attn_forward_kernel(imgs, x_ref, w_ref, noise_ref, keep_ref, chunk_ref, *saved):
    par = params_of(w_ref[0])
    for c in range(imgs):
        attend(
            x_ref[c], par, lambda r: w_ref[r], noise_ref[c], keep_ref[c],
            chunk_ref.at[c], *(ref.at[c] for ref in saved),
        )


def attn_forward(x, w, noise, keep):
    imgs = x.shape[0]
    vm = pl.BlockSpec(memory_space=pltpu.VMEM)
    return pl.pallas_call(
        functools.partial(attn_forward_kernel, imgs),
        out_shape=(jax.ShapeDtypeStruct((imgs, PAD, D), BF16),) + attn_shapes(imgs),
        in_specs=[vm] * 4,
        out_specs=(vm,) * 6,
        compiler_params=pltpu.CompilerParams(vmem_limit_bytes=VMEM_LIMIT),
        cost_estimate=pl.CostEstimate(flops=6 * 10**9, bytes_accessed=10**7, transcendentals=2 * 10**6),
        name="attn_forward",
    )(x, w, noise, keep)


def ring_place(member):
    odd = lax.rem(member, 2)
    half = lax.div(member, 2)
    return half + odd * (E - 1 - 2 * half)


def ring_member(place):
    late = lax.div(place, E // 2)
    return 2 * place + late * (2 * E - 1 - 4 * place)


class Peers:
    def __init__(self):
        dp = lax.axis_index("dp")
        tensor = lax.axis_index("tensor")
        self.member = lax.rem(dp, E)
        self.base = dp - self.member
        self.place = ring_place(self.member)
        self.across = {"tensor": lax.rem(tensor + 2, 4)}
        self.core = {"tensor": tensor + 1 - 2 * lax.rem(tensor, 2)}
        self.next = ({"dp": self.base + self.behind(1, 1)}, {"dp": self.base + self.behind(0, 1)})
        self.sends = []

    def behind(self, way, k):
        step = E - k if way == 0 else k
        return ring_member(lax.rem(self.place + step, E))

    def ahead(self, by):
        return lax.rem(self.member + by, E)

    def came(self, by):
        return lax.rem(self.member + E - by, E)

    def meet(self):
        barrier = pltpu.get_barrier_semaphore()
        others = [{"dp": self.base + self.ahead(by)} for by in range(1, E)] + [self.across, self.core]
        for device in others:
            pl.semaphore_signal(barrier, inc=1, device_id=device, device_id_type=pl.DeviceIdType.MESH)
        pl.semaphore_wait(barrier, len(others))

    def send(self, src, dst, sems, at, device):
        copy = pltpu.make_async_remote_copy(
            src_ref=src,
            dst_ref=dst,
            send_sem=sems[0].at[at],
            recv_sem=sems[1].at[at],
            device_id=device,
            device_id_type=pl.DeviceIdType.MESH,
        )
        copy.start()
        self.sends.append(copy)
        return copy


def front_kernel(
    imgs, pack_ref, ew_ref, dy_ref, x_ref, noise_ref, keep_ref,
    h_out, dy_out, ew_out, w_out, x1_ref, qkv_ref, o_ref, lse_ref, probs_ref,
    w_s, chunk_s, p_s, p_r, px_s, px_r, pc_s, pc_r, d_s, d_r, h_s, h_r, e_s, e_r, ex_s, ex_r, ec_s, ec_r, local,
):
    peers = Peers()
    member = peers.member
    d_own = pack_ref.shape[0]
    half = E // 2
    peers.meet()

    def rows(of):
        return pl.ds(pl.multiple_of(of * d_own, 16), d_own)

    locals_ = [pltpu.make_async_copy(pack_ref, w_s.at[0, rows(member)], local.at[0])]
    locals_[0].start()

    ring, px, pc = {}, {}, {}

    def pass_pack(number, of, src, way=None, k=None):
        if way is not None:
            ring[way, k] = peers.send(src, w_s.at[0, rows(of)], (p_s, p_r), (way, k), peers.next[way])
        px[number] = peers.send(src, w_s.at[1, rows(of)], (px_s, px_r), number, peers.across)
        pc[0, number] = peers.send(src, w_s.at[2, rows(of)], (pc_s, pc_r), (0, number), peers.core)

    arrivals = [(0, k) if i == 0 else (1, k) for k in range(1, half + 1) for i in range(2 if k < half else 1)]
    owners = [member] + [peers.behind(way, k) for way, k in arrivals]
    ring[0, 0] = peers.send(pack_ref, w_s.at[0, rows(member)], (p_s, p_r), (0, 0), peers.next[0])
    pass_pack(0, member, pack_ref, 1, 0)

    def pass_x(number):
        px[number].wait_recv()
        at = rows(owners[number])
        pc[1, number] = peers.send(w_s.at[1, at], w_s.at[3, at], (pc_s, pc_r), (1, number), peers.core)

    for number, (way, k) in enumerate(arrivals, 1):
        ring[way, k - 1].wait_recv()
        of = owners[number]
        last = half if way == 0 else half - 1
        pass_pack(number, of, w_s.at[0, rows(of)], way if k < last else None, k)
        if number >= 2:
            pass_x(number - 2)

    e_copy = {}
    for by in range(1, E):
        to = peers.ahead(by)
        e_copy[by] = peers.send(ew_ref.at[to], ew_out.at[0, member], (e_s, e_r), by, {"dp": peers.base + to})

    d_ring, h_ring = {}, {}

    def row_ring(c, k, src, out, kept, sems):
        at = peers.behind(c % 2, k) * imgs + c if k else member * imgs + c
        kept[c, k] = peers.send(src if k == 0 else out.at[at], out.at[at], sems, (c, k), peers.next[c % 2])

    for c in range(imgs):
        row_ring(c, 0, dy_ref.at[c], dy_out, d_ring, (d_s, d_r))
    for number in range(len(arrivals) - 1, len(arrivals) + 1):
        pass_x(number)

    ex, ec = {}, {}

    def pass_e(by):
        if by:
            e_copy[by].wait_recv()
        of = peers.came(by)
        src = ew_out.at[0, of] if by else ew_ref.at[member]
        ex[by] = peers.send(src, ew_out.at[1, of], (ex_s, ex_r), by, peers.across)
        ec[0, by] = peers.send(src, ew_out.at[2, of], (ec_s, ec_r), (0, by), peers.core)

    def pass_ex(by):
        ex[by].wait_recv()
        of = peers.came(by)
        ec[1, by] = peers.send(ew_out.at[1, of], ew_out.at[3, of], (ec_s, ec_r), (1, by), peers.core)

    for number in range(E):
        pc[0, number].wait_recv()
        pc[1, number].wait_recv()
    locals_[0].wait()
    pass_e(0)
    keepers = [
        pltpu.make_async_copy(w_s, w_out, local.at[1]),
        pltpu.make_async_copy(ew_ref.at[member], ew_out.at[0, member], local.at[2]),
    ] + [
        pltpu.make_async_copy(dy_ref.at[c], dy_out.at[member * imgs + c], local.at[3 + c]) for c in range(imgs)
    ]
    for copy in keepers:
        copy.start()

    par = params_of(w_s[0])
    for c in range(imgs):
        attend(
            x_ref[c], par, lambda r: w_s[r], noise_ref[c], keep_ref[c],
            chunk_s.at[c], *(ref.at[c] for ref in (x1_ref, qkv_ref, o_ref, lse_ref, probs_ref)),
        )
        row_ring(c, 0, chunk_s.at[c], h_out, h_ring, (h_s, h_r))
        keepers.append(
            pltpu.make_async_copy(chunk_s.at[c], h_out.at[member * imgs + c], local.at[3 + imgs + c])
        )
        keepers[-1].start()
        if c == 0:
            for i in range(imgs):
                d_ring[i, 0].wait_recv()
                row_ring(i, 1, None, dy_out, d_ring, (d_s, d_r))

    for k in range(1, E):
        for c in range(imgs):
            h_ring[c, k - 1].wait_recv()
            if k < E - 1:
                row_ring(c, k, None, h_out, h_ring, (h_s, h_r))
        if k < E - 1:
            for c in range(imgs):
                d_ring[c, k].wait_recv()
                if k + 1 < E - 1:
                    row_ring(c, k + 1, None, dy_out, d_ring, (d_s, d_r))
        for by in {2: (1, 7), 3: (2, 6), 4: (3, 5), 5: (4,)}.get(k, ()):
            pass_e(by)
        for by in {2: (0,), 3: (1, 7), 4: (2, 6), 5: (3, 5), 6: (4,)}.get(k, ()):
            pass_ex(by)
    for by in range(E):
        ec[0, by].wait_recv()
        ec[1, by].wait_recv()
    for copy in keepers:
        copy.wait()
    for copy in peers.sends:
        copy.wait_send()


def front(pack, ew, dy, x, noise, keep):
    imgs = x.shape[0]
    d_own = pack.shape[0]
    vm = pl.BlockSpec(memory_space=pltpu.VMEM)
    hbm = pl.BlockSpec(memory_space=pl.ANY)
    table = jax.ShapeDtypeStruct((E * imgs, PAD, D), BF16)
    dma = pltpu.SemaphoreType.DMA
    return pl.pallas_call(
        functools.partial(front_kernel, imgs),
        out_shape=(
            table,
            table,
            jax.ShapeDtypeStruct((4, E, 2, d_own, FFS), BF16),
            jax.ShapeDtypeStruct((4, E * d_own, D + 128), BF16),
        )
        + attn_shapes(imgs),
        in_specs=[vm, hbm, hbm, vm, vm, vm],
        out_specs=(hbm,) * 4 + (vm,) * 5,
        scratch_shapes=[
            pltpu.VMEM((4, E * d_own, D + 128), BF16),
            pltpu.VMEM((imgs, PAD, D), BF16),
            dma((2, 4)), dma((2, 4)), dma((E,)), dma((E,)), dma((2, E)), dma((2, E)),
            dma((imgs, E - 1)), dma((imgs, E - 1)), dma((imgs, E - 1)), dma((imgs, E - 1)),
            dma((E,)), dma((E,)), dma((E,)), dma((E,)), dma((2, E)), dma((2, E)),
            dma((3 + 2 * imgs,)),
        ],
        compiler_params=pltpu.CompilerParams(
            vmem_limit_bytes=VMEM_LIMIT, collective_id=0, has_side_effects=True
        ),
        cost_estimate=pl.CostEstimate(flops=6 * 10**9, bytes_accessed=10**8, transcendentals=2 * 10**6),
        name="front",
    )(pack, ew, dy, x, noise, keep)


def expert_kernel(nb, who_ref, *refs):
    h_in, dy_in, w_in = refs[:3]
    outs = refs[3:]
    dx_out, y_out, rows_out, hid_out, tiles_ref = outs[:5]
    (h, dy, y_t, dx_t, w_s, gate_s, slot_s, dgate_s, xs, dys, hid_s, rows_s, lo_s, hi_s, in_sem, out_sem, row_sem, hid_sem, w_sem) = outs[5:]
    me = who_ref[0]
    loads = [
        pltpu.make_async_copy(h_in, h, in_sem.at[0]),
        pltpu.make_async_copy(dy_in, dy, in_sem.at[1]),
    ]
    for b in range(E):
        at = pl.ds(b * (D // E), D // E)
        for r in range(4):
            loads.append(pltpu.make_async_copy(w_in.at[r, b], w_s.at[r, :, at], w_sem.at[r, b]))
    for copy in loads:
        copy.start()
    y_t[...] = jnp.zeros_like(y_t)
    dx_t[...] = jnp.zeros_like(dx_t)
    dgate_s[...] = jnp.zeros_like(dgate_s)
    for copy in loads:
        copy.wait()

    row16 = iota((16, D), 0)
    for b in range(nb):
        meta = h[b, PAD - 16 : PAD, :].astype(F32)
        gate_s[b : b + 1, :] = jnp.sum(jnp.where(row16 == 8 + me, meta, 0.0), axis=0, keepdims=True)[:, :PAD]
    gates = gate_s[...]
    named = (gates >= 0) & (iota((nb, PAD), 1) < SEQ)
    ones = named.astype(F32).astype(BF16)
    upto = dot(ones, (iota((PAD, PAD), 0) <= iota((PAD, PAD), 1)).astype(F32).astype(BF16))
    count = dot(ones, jnp.ones((PAD, PAD), BF16)).astype(BF16)
    before = dot((iota((nb, nb), 0) > iota((nb, nb), 1)).astype(F32).astype(BF16), count)
    slot_s[...] = jnp.where(named, before + upto - 1.0, -1.0).astype(jnp.int32)
    ends = jnp.where(named, before + upto, before)
    for b in range(nb):
        lo_s[b] = jnp.max(before[b : b + 1, :]).astype(jnp.int32)
        hi_s[b] = jnp.max(ends[b : b + 1, :]).astype(jnp.int32)
    tiles = lax.div(hi_s[nb - 1] + TILE - 1, TILE)
    tiles_ref[0] = tiles

    def meets(b, first):
        return (lo_s[b] < first + TILE) & (hi_s[b] > first) & (hi_s[b] > lo_s[b])

    def place(b, first):
        return iota((TILE, PAD), 0) + first == slot_s[pl.ds(b, 1), :]

    def step(t, carry):
        first = t * TILE
        slot = lax.rem(t, 2)
        xs[...] = jnp.zeros_like(xs)
        dys[...] = jnp.zeros_like(dys)

        def collect(b, gcol):
            def one(gcol):
                hit = place(b, first)
                p = hit.astype(F32).astype(BF16)
                xs[...] += dot(p, h[b])
                dys[...] += dot(p, dy[b])
                return gcol + jnp.sum(jnp.where(hit, gate_s[pl.ds(b, 1), :], 0.0), axis=1, keepdims=True)

            return lax.cond(meets(b, first), one, lambda g: g, gcol)

        gcol = lax.fori_loop(0, nb, collect, jnp.zeros((TILE, 1), F32))

        def drain(s):
            pltpu.make_async_copy(rows_s.at[s], rows_out.at[:, pl.ds(0, TILE)], row_sem.at[s]).wait()
            pltpu.make_async_copy(hid_s.at[s], hid_out.at[:, pl.ds(0, TILE)], hid_sem.at[s]).wait()

        @pl.when(t >= 2)
        def _():
            drain(slot)

        x = xs[...].astype(BF16)
        g_rows = (dys[...] * gcol).astype(BF16)
        rows_s[slot, 0] = x
        rows_s[slot, 1] = g_rows
        y = jnp.zeros((TILE, D), F32)
        dx = jnp.zeros((TILE, D), F32)
        for r in range(4):
            w1, w2 = w_s.at[r, 0], w_s.at[r, 1]
            a = dot(x, w1[...])
            a2 = a * a
            th = jnp.tanh(0.7978845608028654 * a * (1.0 + 0.044715 * a2))
            half = 0.5 * (1.0 + th)
            hid = (a * half).astype(BF16)
            slope = half + 0.5 * a * (1.0 - th * th) * (0.7978845608028654 * (1.0 + 3 * 0.044715 * a2))
            da = (dot(g_rows, w2[...]) * slope).astype(BF16)
            y = y + dot_nt(hid, w2[...])
            dx = dx + dot_nt(da, w1[...])
            hid_s[slot, 0, :, r * FFS : (r + 1) * FFS] = da
            hid_s[slot, 1, :, r * FFS : (r + 1) * FFS] = hid
        at = pl.ds(pl.multiple_of(first, TILE), TILE)
        pltpu.make_async_copy(rows_s.at[slot], rows_out.at[:, at], row_sem.at[slot]).start()
        pltpu.make_async_copy(hid_s.at[slot], hid_out.at[:, at], hid_sem.at[slot]).start()
        dgate = jnp.sum(dys[...] * y, axis=1, keepdims=True)
        y_low = (y * gcol).astype(BF16)
        dx_low = dx.astype(BF16)

        def give(b, carry):
            @pl.when(meets(b, first))
            def _():
                hit = place(b, first)
                p = hit.astype(F32).astype(BF16)
                y_t[b] = y_t[b] + dot_tn(p, y_low).astype(BF16)
                dx_t[b] = dx_t[b] + dot_tn(p, dx_low).astype(BF16)
                dgate_s[pl.ds(b, 1), :] += jnp.sum(jnp.where(hit, dgate, 0.0), axis=0, keepdims=True)

            return carry

        lax.fori_loop(0, nb, give, 0)
        return carry

    lax.fori_loop(0, tiles, step, 0)
    for back in (1, 2):

        @pl.when(tiles >= back)
        def _():
            s = lax.rem(tiles - back, 2)
            pltpu.make_async_copy(rows_s.at[s], rows_out.at[:, pl.ds(0, TILE)], row_sem.at[s]).wait()
            pltpu.make_async_copy(hid_s.at[s], hid_out.at[:, pl.ds(0, TILE)], hid_sem.at[s]).wait()

    for b in range(nb):
        tail = dx_t[b, PAD - 16 : PAD, :].astype(F32)
        line = jnp.concatenate([dgate_s[b : b + 1, :], jnp.zeros((1, D - PAD), F32)], axis=1)
        dx_t[b, PAD - 16 : PAD, :] = (tail + jnp.where(row16 == 8 + me, line, 0.0)).astype(BF16)
    stores = [
        pltpu.make_async_copy(dx_t, dx_out, out_sem.at[0]),
        pltpu.make_async_copy(y_t, y_out, out_sem.at[1]),
    ]
    for copy in stores:
        copy.start()
    for copy in stores:
        copy.wait()


def expert_rows(nb):
    return -(-nb * SEQ // TILE) * TILE


def experts(member, h_all, dy_all, weights):
    nb = h_all.shape[0]
    rows = expert_rows(nb)
    hbm = pl.BlockSpec(memory_space=pl.ANY)
    sm = pl.BlockSpec(memory_space=pltpu.SMEM)
    table = jax.ShapeDtypeStruct((nb, PAD, D), BF16)
    return pl.pallas_call(
        functools.partial(expert_kernel, nb),
        out_shape=[
            table,
            table,
            jax.ShapeDtypeStruct((2, rows, D), BF16),
            jax.ShapeDtypeStruct((2, rows, 4 * FFS), BF16),
            jax.ShapeDtypeStruct((1,), jnp.int32),
        ],
        in_specs=[sm, hbm, hbm, hbm],
        out_specs=[hbm] * 4 + [sm],
        scratch_shapes=[
            pltpu.VMEM((nb, PAD, D), BF16),
            pltpu.VMEM((nb, PAD, D), BF16),
            pltpu.VMEM((nb, PAD, D), BF16),
            pltpu.VMEM((nb, PAD, D), BF16),
            pltpu.VMEM((4, 2, D, FFS), BF16),
            pltpu.VMEM((nb, PAD), F32),
            pltpu.VMEM((nb, PAD), jnp.int32),
            pltpu.VMEM((nb, PAD), F32),
            pltpu.VMEM((TILE, D), F32),
            pltpu.VMEM((TILE, D), F32),
            pltpu.VMEM((2, 2, TILE, 4 * FFS), BF16),
            pltpu.VMEM((2, 2, TILE, D), BF16),
            pltpu.SMEM((nb,), jnp.int32),
            pltpu.SMEM((nb,), jnp.int32),
            pltpu.SemaphoreType.DMA((2,)),
            pltpu.SemaphoreType.DMA((2,)),
            pltpu.SemaphoreType.DMA((2,)),
            pltpu.SemaphoreType.DMA((2,)),
            pltpu.SemaphoreType.DMA((4, E)),
        ],
        compiler_params=pltpu.CompilerParams(vmem_limit_bytes=VMEM_LIMIT),
        cost_estimate=pl.CostEstimate(flops=30 * 10**9, bytes_accessed=4 * 10**7, transcendentals=4 * 10**6),
        name="experts",
    )(member.reshape(1), h_all, dy_all, weights)


def expert_grad_kernel(tiles_ref, rows_ref, hid_ref, out_ref, acc):
    acc[...] = jnp.zeros_like(acc)

    def step(t, carry):
        at = pl.ds(pl.multiple_of(t * TILE, TILE), TILE)
        acc[...] += dot_tn(rows_ref[0, at, :], hid_ref[0, at, :])
        return carry

    lax.fori_loop(0, tiles_ref[0], step, 0)
    out_ref[0] = acc[...].astype(BF16)


def expert_grads(tiles, rows, hid, kind, base):
    n = rows.shape[1]
    return pl.pallas_call(
        expert_grad_kernel,
        grid_spec=pltpu.PrefetchScalarGridSpec(
            num_scalar_prefetch=1,
            grid=(2,),
            in_specs=[
                pl.BlockSpec((1, n, D), lambda s, _: (kind, 0, 0)),
                pl.BlockSpec((1, n, FFS), lambda s, _: (kind, 0, base + s)),
            ],
            out_specs=pl.BlockSpec((1, D, FFS), lambda s, _: (s, 0, 0)),
            scratch_shapes=[pltpu.VMEM((D, FFS), F32)],
        ),
        out_shape=jax.ShapeDtypeStruct((2, D, FFS), BF16),
        compiler_params=pltpu.CompilerParams(vmem_limit_bytes=VMEM_LIMIT),
        cost_estimate=pl.CostEstimate(flops=4 * 10**9, bytes_accessed=15 * 10**6, transcendentals=0),
        name="expert_grads",
    )(tiles, rows, hid)


def unpack_kernel(who_ref, *refs):
    blocks, out_ref = refs[:E], refs[E]
    for by in range(E):
        out_ref[who_ref[by]] = blocks[by][...].astype(F32)


def unpack(who, blocks):
    vm = pl.BlockSpec(memory_space=pltpu.VMEM)
    return pl.pallas_call(
        unpack_kernel,
        out_shape=jax.ShapeDtypeStruct((E,) + blocks[0].shape, F32),
        in_specs=[pl.BlockSpec(memory_space=pltpu.SMEM)] + [vm] * E,
        out_specs=vm,
        compiler_params=pltpu.CompilerParams(vmem_limit_bytes=VMEM_LIMIT),
        cost_estimate=pl.CostEstimate(flops=10**6, bytes_accessed=4 * 10**6, transcendentals=0),
        name="unpack",
    )(who, *blocks)


def lay_out_kernel(imgs, at_ref, *refs):
    parts, out_ref, held, sem = refs[:4], refs[4], refs[5], refs[6]
    copies = [pltpu.make_async_copy(parts[s], held.at[s], sem.at[s]) for s in range(4)]
    for copy in copies:
        copy.start()
    for copy in copies:
        copy.wait()
    for i in range(4 * imgs):
        out_ref[i * SEQ : (i + 1) * SEQ, :] = held[at_ref[i // imgs], i % imgs, :SEQ, :]


def lay_out(at, parts):
    imgs = parts[0].shape[0]
    hbm = pl.BlockSpec(memory_space=pl.ANY)
    return pl.pallas_call(
        functools.partial(lay_out_kernel, imgs),
        out_shape=jax.ShapeDtypeStruct((4 * imgs * SEQ, D), BF16),
        in_specs=[pl.BlockSpec(memory_space=pltpu.SMEM)] + [hbm] * 4,
        out_specs=pl.BlockSpec(memory_space=pltpu.VMEM),
        scratch_shapes=[pltpu.VMEM((4, imgs, PAD, D), BF16), pltpu.SemaphoreType.DMA((4,))],
        compiler_params=pltpu.CompilerParams(vmem_limit_bytes=VMEM_LIMIT),
        cost_estimate=pl.CostEstimate(flops=10**6, bytes_accessed=5 * 10**6, transcendentals=0),
        name="lay_out",
    )(at, *parts)


def attn_backward_kernel(imgs, *refs):
    dh_in = refs[:imgs]
    x1_in, x_in, dy_in, probs_in, qkv_in, o_in, lse_in, w_ref = refs[imgs : imgs + 8]
    packs, dtok_ref = refs[imgs + 8 : imgs + 11], refs[imgs + 11]
    dx1_s, low_s, h1_s, dh1_s, dqkv_s, o_s = refs[imgs + 12 :]
    n_dp, d_own = packs[0].shape[0], packs[0].shape[1] - 16

    def pack_of(r):
        return packs[r] if r < 2 else packs[2].at[:, r - 2]

    par = params_of(w_ref[0])
    router = par[8:16].astype(BF16)
    row_ok = iota((PAD, 1), 0) < SEQ
    lane_ok = iota((E, PAD), 1) < SEQ
    key_ok = iota((PAD, PAD), 1) < SEQ
    small2g = jnp.zeros((1, D), F32)
    small2b = jnp.zeros((1, D), F32)
    g_router = jnp.zeros((E, D), F32)
    for c in range(imgs):
        span = slice(c * PAD, (c + 1) * PAD)
        arrived = dh_in[c][...].astype(F32)
        dgate = arrived[PAD - 8 :, :PAD]
        probs = probs_in[c]
        dlogits = probs * (dgate - jnp.sum(probs * dgate, axis=0, keepdims=True))
        dlogits = jnp.where(lane_ok, dlogits, 0.0).astype(BF16)
        unit, scale = normalise(x1_in[c])
        h2 = (unit * par[2:3] + par[3:4]).astype(BF16)
        g_router = g_router + dot(dlogits, h2)
        dh2 = jnp.where(row_ok, arrived + dot_tn(dlogits, router), 0.0)
        small2g = small2g + jnp.sum(dh2 * unit, axis=0, keepdims=True)
        small2b = small2b + jnp.sum(dh2, axis=0, keepdims=True)
        dx1 = dy_in[c].astype(F32) + norm_back(dh2, unit, scale, par[2:3])
        dx1_s[span, :] = dx1
        low_s[span, :] = dx1.astype(BF16)
        unit1, _ = normalise(x_in[c].astype(F32))
        h1_s[span, :] = (unit1 * par[0:1] + par[1:2]).astype(BF16)
    low = low_s[...]
    h1 = h1_s[...]
    for r in range(4):
        w = w_ref[r]
        dout = dot(low, w[:, 9 * HD : D]).astype(BF16)
        for c in range(imgs):
            span = slice(c * PAD, (c + 1) * PAD)
            qkv = qkv_in[c, r]
            lse = lse_in[c]
            o_s[span, :] = o_in[c, r]
            dqs, dks, dvs = [], [], []
            for h in range(3):
                q = qkv[:, h * HD : (h + 1) * HD]
                k = qkv[:, (3 + h) * HD : (4 + h) * HD]
                v = qkv[:, (6 + h) * HD : (7 + h) * HD]
                do = dout[span, h * HD : (h + 1) * HD]
                s = dot_nt(q, k) * HD ** (-0.5)
                p = jnp.where(key_ok, jnp.exp(s - lse[:, 3 * r + h : 3 * r + h + 1]), 0.0)
                dvs.append(dot_tn(p.astype(BF16), do).astype(BF16))
                dp = dot_nt(do, v)
                ds = (p * (dp - jnp.sum(p * dp, axis=-1, keepdims=True))).astype(BF16)
                dqs.append((dot(ds, k) * HD ** (-0.5)).astype(BF16))
                dks.append((dot_tn(ds, q) * HD ** (-0.5)).astype(BF16))
            dqkv_s[span, :] = jnp.concatenate(dqs + dks + dvs, axis=1)
        dqkv = dqkv_s[...]
        part = dot_nt(dqkv, w[:, : 9 * HD])
        dh1_s[...] = part if r == 0 else dh1_s[...] + part
        grad = jnp.concatenate([dot_tn(h1, dqkv), dot_tn(low, o_s[...])], axis=1).astype(BF16)
        for i in range(n_dp):
            pack_of(r)[i, :d_own, :] = grad[i * d_own : (i + 1) * d_own]
    small1g = jnp.zeros((1, D), F32)
    small1b = jnp.zeros((1, D), F32)
    for c in range(imgs):
        span = slice(c * PAD, (c + 1) * PAD)
        dh1 = jnp.where(row_ok, dh1_s[span, :], 0.0)
        unit1, scale1 = normalise(x_in[c].astype(F32))
        small1g = small1g + jnp.sum(dh1 * unit1, axis=0, keepdims=True)
        small1b = small1b + jnp.sum(dh1, axis=0, keepdims=True)
        dtok_ref[c] = (dx1_s[span, :] + norm_back(dh1, unit1, scale1, par[0:1])).astype(BF16)
    small = jnp.concatenate([small1g, small1b, small2g, small2b, jnp.zeros((4, D), F32), g_router], axis=0)
    for i in range(n_dp):
        line = jnp.concatenate([small[:, i * d_own : (i + 1) * d_own], jnp.zeros((16, D - d_own), F32)], axis=1)
        for r in range(4):
            pack_of(r)[i, d_own:, :] = line.astype(BF16)


def attn_backward(dh, saved, w, n_dp):
    imgs = len(dh)
    pack = (n_dp, D // n_dp + 16, D)
    vm = pl.BlockSpec(memory_space=pltpu.VMEM)
    rows = imgs * PAD
    return pl.pallas_call(
        functools.partial(attn_backward_kernel, imgs),
        out_shape=(
            jax.ShapeDtypeStruct(pack, BF16),
            jax.ShapeDtypeStruct(pack, BF16),
            jax.ShapeDtypeStruct((n_dp, 2) + pack[1:], BF16),
            jax.ShapeDtypeStruct((imgs, PAD, D), BF16),
        ),
        in_specs=[vm] * (imgs + 8),
        out_specs=(vm,) * 4,
        scratch_shapes=[
            pltpu.VMEM((rows, D), F32),
            pltpu.VMEM((rows, D), BF16),
            pltpu.VMEM((rows, D), BF16),
            pltpu.VMEM((rows, D), F32),
            pltpu.VMEM((rows, 9 * HD), BF16),
            pltpu.VMEM((rows, 3 * HD), BF16),
        ],
        compiler_params=pltpu.CompilerParams(vmem_limit_bytes=VMEM_LIMIT),
        cost_estimate=pl.CostEstimate(flops=12 * 10**9, bytes_accessed=2 * 10**7, transcendentals=2 * 10**6),
        name="attn_backward",
    )(*dh, *saved, w)


RING = (0, 2, 4, 6, 7, 5, 3, 1)


class Mover:
    def __init__(self, n_dp):
        self.n_dp = n_dp
        self.groups = n_dp // E
        self.me = lax.axis_index("dp")
        self.member = lax.rem(self.me, E)
        self.group = lax.div(self.me, E)
        self.tensor = lax.axis_index("tensor")
        self.place = ring_place(self.member)
        bases = range(0, n_dp, E)
        self.ring = (
            [(b + RING[i], b + RING[(i + 1) % E]) for b in bases for i in range(E)],
            [(b + RING[(i + 1) % E], b + RING[i]) for b in bases for i in range(E)],
        )

    def along(self, value, way):
        return lax.ppermute(value, "dp", self.ring[way])

    def shift(self, value, by):
        perm = [(b + i, b + (i + by) % E) for b in range(0, self.n_dp, E) for i in range(E)]
        return lax.ppermute(value, "dp", perm)

    def shift_group(self, value, by):
        return lax.ppermute(value, "dp", [(k, (k + by * E) % self.n_dp) for k in range(self.n_dp)])

    def other(self, value, mask):
        return lax.ppermute(value, "tensor", [(k, k ^ mask) for k in range(4)])

    def behind(self, way, k):
        step = -k if way == 0 else k
        return ring_member(lax.rem(self.place + step + E, E))

    def group_lists(self):
        if self.groups == 1:
            return None
        return [[b + i for i in range(E)] for b in range(0, self.n_dp, E)]

    def gather(self, value):
        return lax.all_gather(value, "dp", axis=0, tiled=False, axis_index_groups=self.group_lists())

    def scatter_sum(self, value):
        return lax.psum_scatter(
            value, "dp", scatter_dimension=0, tiled=False, axis_index_groups=self.group_lists()
        )

    def front(self, pack, ew, dy, x, noise, keep):
        own = lax.all_gather(pack, "dp", axis=0, tiled=True)
        two = jnp.stack([own, self.other(own, 2)])
        w = jnp.concatenate([two, self.other(two, 1)], axis=0)
        blocks = jnp.zeros((2, E * pack.shape[0], FFS), BF16)
        for by in range(E):
            to = lax.rem(self.member + by, E)
            block = lax.dynamic_index_in_dim(ew, to, 0, False)
            came = lax.rem(self.member - by + E, E)
            block = self.shift(block, by) if by else block
            blocks = lax.dynamic_update_slice_in_dim(blocks, block, came * pack.shape[0], 1)
        blocks = self.all_groups(blocks, 1)
        blocks = jnp.swapaxes(blocks.reshape(2, E, D // E, FFS), 0, 1)
        two = jnp.stack([blocks, self.other(blocks, 2)])
        weights = jnp.concatenate([two, self.other(two, 1)], axis=0)
        chunk, *saved = attn_forward(x, w, noise, keep)
        table = (E * x.shape[0], PAD, D)
        return self.gather(chunk).reshape(table), self.gather(dy).reshape(table), weights, w, *saved

    def sum_both_ways(self, block_for):
        def chain(way, steps):
            total = block_for(self.behind(1 - way, steps)).astype(BF16)
            for k in range(steps - 1, -1, -1):
                total = self.along(total, way)
                if k:
                    total = (total.astype(F32) + block_for(self.behind(1 - way, k)).astype(F32)).astype(BF16)
            return total

        ahead = chain(0, E // 2)
        back = chain(1, E // 2 - 1)
        return ahead.astype(F32) + back.astype(F32) + block_for(self.member).astype(F32)

    def all_groups(self, part, dim):
        if self.groups == 1:
            return part
        size = part.shape[dim]
        shape = part.shape[:dim] + (size * self.groups,) + part.shape[dim + 1 :]
        whole = lax.dynamic_update_slice_in_dim(jnp.zeros(shape, part.dtype), part, self.group * size, dim)
        for by in range(1, self.groups):
            came = lax.rem(self.group - by + self.groups, self.groups)
            whole = lax.dynamic_update_slice_in_dim(whole, self.shift_group(part, by), came * size, dim)
        return whole

    def sum_groups(self, whole, dim):
        if self.groups == 1:
            return whole
        size = whole.shape[dim] // self.groups
        total = lax.dynamic_slice_in_dim(whole, self.group * size, size, dim).astype(F32)
        for by in range(1, self.groups):
            to = lax.rem(self.group + by, self.groups)
            part = lax.dynamic_slice_in_dim(whole, to * size, size, dim)
            total = total + self.shift_group(part, by).astype(F32)
        return total.astype(whole.dtype)


def after(value, *first):
    return lax.optimization_barrier((value, first))[0]


def _slot(tensor, t):
    apart = lax.bitwise_xor(tensor, t)
    return lax.div(apart, 2) + 2 * lax.rem(apart, 2)


def image_blocks(rows, tensor, imgs):
    first = tensor * (imgs * SEQ)
    return [
        jnp.pad(lax.dynamic_slice_in_dim(rows, first + c * SEQ, SEQ, 0), ((0, PAD - SEQ), (0, 0)))
        for c in range(imgs)
    ]


def image_lanes(lanes, tensor, imgs):
    first = tensor * (imgs * SEQ)
    return [
        jnp.pad(lax.dynamic_slice_in_dim(lanes, first + c * SEQ, SEQ, 1), ((0, 0), (0, PAD - SEQ)))
        for c in range(imgs)
    ]


def kept_pairs(routes):
    chosen = jnp.transpose(routes).reshape(1, -1)
    named = (chosen == jnp.arange(E, dtype=jnp.int32)[:, None]).astype(jnp.int32)
    kept = named * (jnp.cumsum(named, axis=1) <= CAP)
    return jnp.sum(kept.reshape(E, TOP, -1), axis=1).astype(F32)


def body(
    n_dp,
    tokens,
    ln1_gain,
    ln1_bias,
    w_qkv,
    w_attn_out,
    ln2_gain,
    ln2_bias,
    router_weight,
    w_in,
    w_expert_out,
    router_noise,
    routes,
    cotangent,
):
    move = Mover(n_dp)
    token_count = tokens.shape[0]
    imgs = token_count // SEQ // 4
    d_own = w_qkv.shape[0]
    ways = [c % 2 for c in range(imgs)]

    vectors = jnp.stack([ln1_gain, ln1_bias, ln2_gain, ln2_bias] + [jnp.zeros_like(ln1_gain)] * 4, axis=1)
    pack = jnp.concatenate(
        [w_qkv[:, 0], w_qkv[:, 1], w_qkv[:, 2], jnp.transpose(w_attn_out), vectors, router_weight], axis=1
    )
    pack = jnp.pad(pack, ((0, 0), (0, 128 - 16))).astype(BF16)
    ew = jnp.stack([w_in, jnp.transpose(w_expert_out, (0, 2, 1))], axis=1).astype(BF16)
    x = jnp.stack(image_blocks(tokens, move.tensor, imgs))
    dy = jnp.stack(image_blocks(cotangent, move.tensor, imgs))
    keep = jnp.stack(image_lanes(kept_pairs(routes), move.tensor, imgs))
    noise = jnp.stack(image_lanes(jnp.transpose(router_noise), move.tensor, imgs))
    if move.groups == 1:
        h_all, dy_all, weights, w, *saved = front(pack, ew, dy, x, noise, keep)
    else:
        h_all, dy_all, weights, w, *saved = move.front(pack, ew, dy, x, noise, keep)
    x1, qkv, o, lse, probs = saved

    dh, y_all, rows, hid, tiles = experts(move.member, h_all, dy_all, weights)

    def dh_for(c, k):
        return lax.dynamic_index_in_dim(dh, move.behind(ways[c], k) * imgs + c, 0, False)

    dh_sum = [dh_for(c, 1) for c in range(imgs)]
    g_work = {3: (1, 2), 4: (1, 0), 5: (0, 2), 6: (0, 0)}
    g_part = {}
    for k in range(2, E + 1):
        if k in g_work:
            part = expert_grads(tiles, rows, hid, *g_work[k])
            dh_sum, g_part[g_work[k]] = lax.optimization_barrier((dh_sum, part))
        for c in range(imgs):
            passed = move.along(dh_sum[c], ways[c])
            dh_sum[c] = (passed.astype(F32) + dh_for(c, k % E).astype(F32)).astype(BF16)
    y_all = after(y_all, dh_sum)
    y_sum = move.scatter_sum(y_all.reshape(E, imgs, PAD, D))
    g_exp = {}
    for kind in (1, 0):
        passed = move.other(g_part[kind, 2], 1).astype(F32)
        pair = [(g_part[kind, 0][s].astype(F32) + passed[s]).astype(BF16) for s in range(2)]
        total = (pair[0].astype(F32) + move.other(pair[1], 2).astype(F32)).astype(BF16)
        total = move.sum_groups(total, 0)
        blocks = []
        for by in range(E):
            to = lax.rem(move.member + by, E)
            block = lax.dynamic_slice_in_dim(total, to * d_own, d_own, 0)
            blocks.append(move.shift(block, by) if by else block)
        g_exp[kind] = blocks

    pack0, pack1, packs, d_tok = attn_backward(
        dh_sum, (x1, x, dy, probs, qkv, o, lse), w, n_dp
    )
    passed = move.other(packs, 1)
    if move.groups > 1:
        pack0 = move.sum_groups((pack0.astype(F32) + passed[:, 0].astype(F32)).astype(BF16), 0)
        pack1 = move.sum_groups((pack1.astype(F32) + passed[:, 1].astype(F32)).astype(BF16), 0)
        passed = jnp.zeros((E, 2) + pack0.shape[1:], BF16)

    def pack_for(member):
        one, two = (lax.dynamic_index_in_dim(p, member, 0, False).astype(F32) for p in (pack0, pack1))
        came = lax.dynamic_index_in_dim(passed, member, 0, False).astype(F32)
        return one + came[0] + move.other((two + came[1]).astype(BF16), 2).astype(F32)

    total = move.sum_both_ways(pack_for)
    g_qkv = total[:d_own, : 9 * HD].reshape(d_own, 3, 3 * HD)
    g_attn_out = jnp.transpose(total[:d_own, 9 * HD :])
    g_small = total[d_own:, :d_own]

    at = jnp.stack([_slot(move.tensor, t) for t in range(4)])

    def all_rows(own):
        across = move.other(own, 2)
        return lay_out(at, [own, across, move.other(own, 1), move.other(across, 1)])

    d_tokens = all_rows(d_tok)
    output = all_rows((x1 + y_sum.astype(F32)).astype(BF16))
    came = jnp.stack([lax.rem(move.member - by + E, E) for by in range(E)])
    g_out, g_in = (unpack(came, g_exp[kind]) for kind in (1, 0))
    return (
        output,
        d_tokens,
        g_small[0],
        g_small[1],
        g_qkv,
        g_attn_out,
        g_small[2],
        g_small[3],
        jnp.transpose(g_small[8:16]),
        g_in,
        jnp.transpose(g_out, (0, 2, 1)),
    )


def solution(mesh):
    in_specs = (
        P("dp", None),
        P("dp"),
        P("dp"),
        P("dp", None, "tensor"),
        P("tensor", "dp"),
        P("dp"),
        P("dp"),
        P("dp", None),
        P(None, "dp", "tensor"),
        P(None, "tensor", "dp"),
        P("dp", None),
        P("dp", None),
        P("dp", None),
    )
    out_specs = (
        P("dp", None),
        P("dp", None),
        P("dp"),
        P("dp"),
        P("dp", None, "tensor"),
        P("tensor", "dp"),
        P("dp"),
        P("dp"),
        P("dp", None),
        P(None, "dp", "tensor"),
        P(None, "tensor", "dp"),
    )
    return jax.shard_map(
        functools.partial(body, mesh.shape["dp"]),
        mesh=mesh,
        in_specs=in_specs,
        out_specs=out_specs,
        check_vma=False,
    )
```

```python
import functools

import jax
import jax.numpy as jnp
from jax import lax
from jax.experimental import pallas as pl
from jax.experimental.pallas import tpu as pltpu
from jax.sharding import PartitionSpec as P

D = 768
HD = 64
E = 8
TOP = 2
SEQ = 197
CAP = 689
PAD = 208
META = 200
TILE = 256
FFS = 768
EPS = 1e-06
VMEM_LIMIT = 62 * 1024 * 1024

F32 = jnp.float32
BF16 = jnp.bfloat16


def dot(a, b):
    return jnp.dot(a, b, preferred_element_type=F32)


def dot_nt(a, b):
    return lax.dot_general(a, b, (((1,), (1,)), ((), ())), preferred_element_type=F32)


def dot_tn(a, b):
    return lax.dot_general(a, b, (((0,), (0,)), ((), ())), preferred_element_type=F32)


def iota(shape, dim):
    return lax.broadcasted_iota(jnp.int32, shape, dim)


def normalise(values):
    centred = values - jnp.mean(values, axis=-1, keepdims=True)
    scale = lax.rsqrt(jnp.mean(centred * centred, axis=-1, keepdims=True) + EPS)
    return centred * scale, scale


def norm_back(grad, unit, scale, gain):
    g = grad * gain
    return scale * (
        g - jnp.mean(g, axis=-1, keepdims=True) - unit * jnp.mean(g * unit, axis=-1, keepdims=True)
    )


def params_of(w_own):
    return jnp.transpose(w_own[:, D:].astype(F32))[:16]


def attend(x, par, w_of, noise, keep, chunk_ref, x1_ref, qkv_ref, o_ref, lse_ref, probs_ref):
    x = x.astype(F32)
    unit, _ = normalise(x)
    h1 = (unit * par[0:1] + par[1:2]).astype(BF16)
    acc = x
    lse = jnp.zeros((PAD, 128), F32)
    key_ok = iota((PAD, PAD), 1) < SEQ
    lane = iota((PAD, 128), 1)
    for r in range(4):
        w = w_of(r)
        qkv = dot(h1, w[:, : 9 * HD]).astype(BF16)
        qkv_ref[r] = qkv
        outs = []
        for h in range(3):
            q = qkv[:, h * HD : (h + 1) * HD]
            k = qkv[:, (3 + h) * HD : (4 + h) * HD]
            v = qkv[:, (6 + h) * HD : (7 + h) * HD]
            s = jnp.where(key_ok, dot_nt(q, k) * HD ** (-0.5), -1e30)
            top = jnp.max(s, axis=-1, keepdims=True)
            p = jnp.exp(s - top)
            total = jnp.sum(p, axis=-1, keepdims=True)
            outs.append(dot((p * (1.0 / total)).astype(BF16), v).astype(BF16))
            lse = jnp.where(lane == 3 * r + h, top + jnp.log(total), lse)
        o = jnp.concatenate(outs, axis=1)
        o_ref[r] = o
        acc = acc + dot_nt(o, w[:, 9 * HD : D])
    lse_ref[...] = lse
    x1_ref[...] = acc
    unit2, _ = normalise(acc)
    h2 = (unit2 * par[2:3] + par[3:4]).astype(BF16)
    logits = dot_nt(par[8:16].astype(BF16), h2) + noise
    e = jnp.exp(logits - jnp.max(logits, axis=0, keepdims=True))
    probs = e / jnp.sum(e, axis=0, keepdims=True)
    probs_ref[...] = probs
    gates = jnp.where(keep > 0, probs, -1.0)
    chunk_ref[...] = h2
    tail = jnp.concatenate([gates, jnp.zeros((8, D - PAD), F32)], axis=1)
    low = h2[PAD - 16 :, :].astype(F32)
    chunk_ref[PAD - 16 :, :] = jnp.concatenate([low[:8], tail], axis=0).astype(BF16)


def attn_shapes(imgs):
    return (
        jax.ShapeDtypeStruct((imgs, PAD, D), F32),
        jax.ShapeDtypeStruct((imgs, 4, PAD, 9 * HD), BF16),
        jax.ShapeDtypeStruct((imgs, 4, PAD, 3 * HD), BF16),
        jax.ShapeDtypeStruct((imgs, PAD, 128), F32),
        jax.ShapeDtypeStruct((imgs, E, PAD), F32),
    )


def attn_forward_kernel(imgs, x_ref, w_ref, noise_ref, keep_ref, chunk_ref, *saved):
    par = params_of(w_ref[0])
    for c in range(imgs):
        attend(
            x_ref[c], par, lambda r: w_ref[r], noise_ref[c], keep_ref[c],
            chunk_ref.at[c], *(ref.at[c] for ref in saved),
        )


def attn_forward(x, w, noise, keep):
    imgs = x.shape[0]
    vm = pl.BlockSpec(memory_space=pltpu.VMEM)
    return pl.pallas_call(
        functools.partial(attn_forward_kernel, imgs),
        out_shape=(jax.ShapeDtypeStruct((imgs, PAD, D), BF16),) + attn_shapes(imgs),
        in_specs=[vm] * 4,
        out_specs=(vm,) * 6,
        compiler_params=pltpu.CompilerParams(vmem_limit_bytes=VMEM_LIMIT),
        cost_estimate=pl.CostEstimate(flops=6 * 10**9, bytes_accessed=10**7, transcendentals=2 * 10**6),
        name="attn_forward",
    )(x, w, noise, keep)


def ring_place(member):
    odd = lax.rem(member, 2)
    half = lax.div(member, 2)
    return half + odd * (E - 1 - 2 * half)


def ring_member(place):
    late = lax.div(place, E // 2)
    return 2 * place + late * (2 * E - 1 - 4 * place)


class Peers:
    def __init__(self):
        dp = lax.axis_index("dp")
        tensor = lax.axis_index("tensor")
        self.member = lax.rem(dp, E)
        self.base = dp - self.member
        self.place = ring_place(self.member)
        self.across = {"tensor": lax.rem(tensor + 2, 4)}
        self.core = {"tensor": tensor + 1 - 2 * lax.rem(tensor, 2)}
        self.next = ({"dp": self.base + self.behind(1, 1)}, {"dp": self.base + self.behind(0, 1)})
        self.sends = []

    def behind(self, way, k):
        step = E - k if way == 0 else k
        return ring_member(lax.rem(self.place + step, E))

    def ahead(self, by):
        return lax.rem(self.member + by, E)

    def came(self, by):
        return lax.rem(self.member + E - by, E)

    def meet(self):
        barrier = pltpu.get_barrier_semaphore()
        others = [{"dp": self.base + self.ahead(by)} for by in range(1, E)] + [self.across, self.core]
        for device in others:
            pl.semaphore_signal(barrier, inc=1, device_id=device, device_id_type=pl.DeviceIdType.MESH)
        pl.semaphore_wait(barrier, len(others))

    def send(self, src, dst, sems, at, device):
        copy = pltpu.make_async_remote_copy(
            src_ref=src,
            dst_ref=dst,
            send_sem=sems[0].at[at],
            recv_sem=sems[1].at[at],
            device_id=device,
            device_id_type=pl.DeviceIdType.MESH,
        )
        copy.start()
        self.sends.append(copy)
        return copy


def expert_step(x, dy, gate, w_ref, g_ref, y_ref, dx_ref):
    weight = jnp.maximum(gate, 0.0)
    d_rows = (dy.astype(F32) * weight).astype(BF16)

    def hidden(r, carry):
        w1 = w_ref[r, :, 0].reshape(D, FFS)
        w2 = w_ref[r, :, 1].reshape(D, FFS)
        a = dot(x, w1)
        a2 = a * a
        th = jnp.tanh(0.7978845608028654 * a * (1.0 + 0.044715 * a2))
        half = 0.5 * (1.0 + th)
        hid = (a * half).astype(BF16)
        slope = half + 0.5 * a * (1.0 - th * th) * (0.7978845608028654 * (1.0 + 3 * 0.044715 * a2))
        da = (dot(d_rows, w2) * slope).astype(BF16)
        y_ref[...] += dot_nt(hid, w2)
        dx_ref[...] += dot_nt(da, w1)
        g_ref[r, 0] += dot_tn(x, da)
        g_ref[r, 1] += dot_tn(d_rows, hid)
        return carry

    y_ref[...] = jnp.zeros_like(y_ref)
    dx_ref[...] = jnp.zeros_like(dx_ref)
    lax.fori_loop(0, 4, hidden, 0)
    y = y_ref[...]
    dgate = jnp.where(gate >= 0, jnp.sum(dy.astype(F32) * y, axis=1, keepdims=True), 0.0)
    return (y * weight).astype(BF16), dx_ref[...], dgate


def front_kernel(
    imgs, pack_ref, ew_ref, dy_ref, x_ref, noise_ref, keep_ref,
    h_out, dy_out, t_in, g_out, sums_out, w_out, x1_ref, qkv_ref, o_ref, lse_ref, probs_ref,
    w_s, chunk_s, we_s, g_s, xs, dys, y_s, dx_s, t_s, pass_s, g_low,
    p_s, p_r, px_s, px_r, pc_s, pc_r, d_s, d_r, h_s, h_r, e_s, e_r, ex_s, ex_r, ec_s, ec_r, t_ss, t_r, local, stage, g_sem,
):
    peers = Peers()
    member = peers.member
    d_own = pack_ref.shape[0]
    half = E // 2
    peers.meet()

    def rows(of):
        return pl.ds(pl.multiple_of(of * d_own, 16), d_own)

    own_pack = pltpu.make_async_copy(pack_ref, w_s.at[0, rows(member)], local.at[0])
    own_pack.start()

    ring, px, pc = {}, {}, {}

    def pass_pack(number, of, src, way=None, k=None):
        if way is not None:
            ring[way, k] = peers.send(src, w_s.at[0, rows(of)], (p_s, p_r), (way, k), peers.next[way])
        px[number] = peers.send(src, w_s.at[1, rows(of)], (px_s, px_r), number, peers.across)
        pc[0, number] = peers.send(src, w_s.at[2, rows(of)], (pc_s, pc_r), (0, number), peers.core)

    arrivals = [(0, k) if i == 0 else (1, k) for k in range(1, half + 1) for i in range(2 if k < half else 1)]
    owners = [member] + [peers.behind(way, k) for way, k in arrivals]
    ring[0, 0] = peers.send(pack_ref, w_s.at[0, rows(member)], (p_s, p_r), (0, 0), peers.next[0])
    pass_pack(0, member, pack_ref, 1, 0)

    def pass_x(number):
        px[number].wait_recv()
        at = rows(owners[number])
        pc[1, number] = peers.send(w_s.at[1, at], w_s.at[3, at], (pc_s, pc_r), (1, number), peers.core)

    for number, (way, k) in enumerate(arrivals, 1):
        ring[way, k - 1].wait_recv()
        of = owners[number]
        last = half if way == 0 else half - 1
        pass_pack(number, of, w_s.at[0, rows(of)], way if k < last else None, k)
        if number >= 2:
            pass_x(number - 2)

    e_copy = {}
    for by in range(1, E):
        to = peers.ahead(by)
        e_copy[by] = peers.send(ew_ref.at[to], we_s.at[0, member], (e_s, e_r), by, {"dp": peers.base + to})

    def block_at(c, k):
        return peers.behind(c % 2, k) * imgs + c

    def row_copy(out, sems, c, k, src=None):
        at = block_at(c, k)
        return pltpu.make_async_remote_copy(
            src_ref=out.at[at] if src is None else src,
            dst_ref=out.at[at],
            send_sem=sems[0].at[c, k],
            recv_sem=sems[1].at[c, k],
            device_id=peers.next[c % 2],
            device_id_type=pl.DeviceIdType.MESH,
        )

    h_sems, d_sems = (h_s, h_r), (d_s, d_r)
    for c in range(imgs):
        row_copy(dy_out, d_sems, c, 0, dy_ref.at[c]).start()
    for number in range(len(arrivals) - 1, len(arrivals) + 1):
        pass_x(number)

    ex, ec = {}, {}

    def pass_e(by):
        if by:
            e_copy[by].wait_recv()
        of = peers.came(by)
        src = we_s.at[0, of] if by else ew_ref.at[member]
        ex[by] = peers.send(src, we_s.at[1, of], (ex_s, ex_r), by, peers.across)
        ec[0, by] = peers.send(src, we_s.at[2, of], (ec_s, ec_r), (0, by), peers.core)

    def pass_ex(by):
        ex[by].wait_recv()
        of = peers.came(by)
        ec[1, by] = peers.send(we_s.at[1, of], we_s.at[3, of], (ec_s, ec_r), (1, by), peers.core)

    for number in range(E):
        pc[0, number].wait_recv()
        pc[1, number].wait_recv()
    own_pack.wait()
    pass_e(0)
    keepers = [
        pltpu.make_async_copy(w_s, w_out, local.at[1]),
        pltpu.make_async_copy(ew_ref.at[member], we_s.at[0, member], local.at[2]),
    ] + [
        pltpu.make_async_copy(dy_ref.at[c], dy_out.at[member * imgs + c], local.at[3 + c]) for c in range(imgs)
    ]
    for copy in keepers:
        copy.start()

    par = params_of(w_s[0])
    for c in range(imgs):
        attend(
            x_ref[c], par, lambda r: w_s[r], noise_ref[c], keep_ref[c],
            chunk_s.at[c], *(ref.at[c] for ref in (x1_ref, qkv_ref, o_ref, lse_ref, probs_ref)),
        )
        row_copy(h_out, h_sems, c, 0, chunk_s.at[c]).start()
        keepers.append(
            pltpu.make_async_copy(chunk_s.at[c], h_out.at[member * imgs + c], local.at[3 + imgs + c])
        )
        keepers[-1].start()

    far = (1, 7, 2, 6, 3, 5, 4)
    for i, by in enumerate(far):
        pass_e(by)
        if i >= 1:
            pass_ex((0, *far)[i - 1])
    g_s[...] = jnp.zeros_like(g_s)
    for by in (0, *far)[len(far) - 1 :]:
        pass_ex(by)
    for by in range(E):
        ec[0, by].wait_recv()
        ec[1, by].wait_recv()
    for copy in keepers:
        copy.wait()

    row16 = iota((16, D), 0)
    eye = iota((PAD, PAD), 0) == iota((PAD, PAD), 1)

    def sum_copy(flow, c, k):
        return pltpu.make_async_remote_copy(
            src_ref=pass_s.at[lax.rem(k, 2), flow, c],
            dst_ref=t_in.at[k - 1, flow, c],
            send_sem=t_ss.at[flow, c, k - 1],
            recv_sem=t_r.at[flow, c, k - 1],
            device_id=peers.next[c % 2],
            device_id_type=pl.DeviceIdType.MESH,
        )

    own_sums = pltpu.make_async_copy(pass_s.at[0], t_in.at[E - 1], local.at[0])

    def fetch_sums(k):
        copies = []
        for flow in range(2):
            for c in range(imgs):
                sum_copy(flow, c, k - 1).wait_recv()
                copies.append(pltpu.make_async_copy(t_in.at[k - 2, flow, c], t_s.at[flow, c], stage.at[flow, c]))
                copies[-1].start()
        for copy in copies:
            copy.wait()

    def step(k, carry):
        for c in range(imgs):
            for out, sems in ((h_out, h_sems), (dy_out, d_sems)):

                @pl.when(k > 0)
                def _():
                    row_copy(out, sems, c, k - 1).wait_recv()

                @pl.when((k > 0) & (k < E - 1))
                def _():
                    row_copy(out, sems, c, k).start()

        loads = []
        for c in range(imgs):
            for i, (out, held) in enumerate(((h_out, xs), (dy_out, dys))):
                loads.append(pltpu.make_async_copy(out.at[block_at(c, k)], held.at[c], stage.at[i, c]))
                loads[-1].start()
        for copy in loads:
            copy.wait()
        columns = []
        for c in range(imgs):
            meta = xs[c, PAD - 16 :, :].astype(F32)
            line = jnp.sum(jnp.where(row16 == 8 + member, meta, 0.0), axis=0, keepdims=True)[:, :PAD]
            columns.append(jnp.sum(jnp.where(eye, line, 0.0), axis=1, keepdims=True))
        y, dx, dgate = expert_step(
            xs[...].reshape(imgs * PAD, D), dys[...].reshape(imgs * PAD, D), jnp.concatenate(columns, axis=0),
            we_s, g_s, y_s, dx_s,
        )
        slot = lax.rem(k, 2)

        @pl.when(k >= 3)
        def _():
            for flow in range(2):
                for c in range(imgs):
                    sum_copy(flow, c, k - 2).wait_send()

        for c in range(imgs):
            span = slice(c * PAD, (c + 1) * PAD)
            line = jnp.sum(jnp.where(eye, dgate[span], 0.0), axis=0, keepdims=True)
            line = jnp.concatenate([line, jnp.zeros((1, D - PAD), F32)], axis=1)
            tail = dx[span][PAD - 16 :] + jnp.where(row16 == 8 + member, line, 0.0)
            pass_s[slot, 0, c] = jnp.concatenate([dx[span][: PAD - 16], tail], axis=0).astype(BF16)
            pass_s[slot, 1, c] = y[span]

        @pl.when(k == 0)
        def _():
            own_sums.start()
            own_sums.wait()

        @pl.when(k >= 2)
        def _():
            fetch_sums(k)
            pass_s[slot] = (pass_s[slot].astype(F32) + t_s[...].astype(F32)).astype(BF16)

        @pl.when(k >= 1)
        def _():
            for flow in range(2):
                for c in range(imgs):
                    sum_copy(flow, c, k).start()

        return carry

    lax.fori_loop(0, E, step, 0)

    for i in range(8):
        r, kind = i // 2, i % 2
        if i >= 2:
            pltpu.make_async_copy(g_low.at[i % 2], g_out.at[r, :, kind], g_sem.at[i % 2]).wait()
        g_low[i % 2] = g_s[r, kind].astype(BF16).reshape(E, d_own, FFS)
        pltpu.make_async_copy(g_low.at[i % 2], g_out.at[r, :, kind], g_sem.at[i % 2]).start()
    fetch_sums(E)
    for c in range(imgs):
        for flow in range(2):
            sum_copy(flow, c, E - 2).wait_send()
    own_sums = pltpu.make_async_copy(t_in.at[E - 1], pass_s.at[0], local.at[0])
    own_sums.start()
    own_sums.wait()
    sums_out[...] = (pass_s[0].astype(F32) + t_s[...].astype(F32)).astype(BF16)
    for i in range(2):
        pltpu.make_async_copy(g_low.at[i], g_out.at[3, :, i], g_sem.at[i]).wait()
    for c in range(imgs):
        for flow in range(2):
            sum_copy(flow, c, E - 1).wait_send()
        for k in range(E - 1):
            row_copy(h_out, h_sems, c, k).wait_send()
            row_copy(dy_out, d_sems, c, k).wait_send()
    for copy in peers.sends:
        copy.wait_send()


def front(pack, ew, dy, x, noise, keep):
    imgs = x.shape[0]
    d_own = pack.shape[0]
    vm = pl.BlockSpec(memory_space=pltpu.VMEM)
    hbm = pl.BlockSpec(memory_space=pl.ANY)
    table = jax.ShapeDtypeStruct((E * imgs, PAD, D), BF16)
    dma = pltpu.SemaphoreType.DMA
    pair = (2, imgs, PAD, D)
    return pl.pallas_call(
        functools.partial(front_kernel, imgs),
        out_shape=(
            table,
            table,
            jax.ShapeDtypeStruct((E,) + pair, BF16),
            jax.ShapeDtypeStruct((4, E, 2, d_own, FFS), BF16),
            jax.ShapeDtypeStruct(pair, BF16),
            jax.ShapeDtypeStruct((4, E * d_own, D + 128), BF16),
        )
        + attn_shapes(imgs),
        in_specs=[vm, hbm, hbm, vm, vm, vm],
        out_specs=(hbm,) * 4 + (vm, hbm) + (vm,) * 5,
        scratch_shapes=[
            pltpu.VMEM((4, E * d_own, D + 128), BF16),
            pltpu.VMEM((imgs, PAD, D), BF16),
            pltpu.VMEM((4, E, 2, d_own, FFS), BF16),
            pltpu.VMEM((4, 2, D, FFS), F32),
            pltpu.VMEM((imgs, PAD, D), BF16),
            pltpu.VMEM((imgs, PAD, D), BF16),
            pltpu.VMEM((imgs * PAD, D), F32),
            pltpu.VMEM((imgs * PAD, D), F32),
            pltpu.VMEM(pair, BF16),
            pltpu.VMEM((2,) + pair, BF16),
            pltpu.VMEM((2, E, d_own, FFS), BF16),
            dma((2, 4)), dma((2, 4)), dma((E,)), dma((E,)), dma((2, E)), dma((2, E)),
            dma((imgs, E - 1)), dma((imgs, E - 1)), dma((imgs, E - 1)), dma((imgs, E - 1)),
            dma((E,)), dma((E,)), dma((E,)), dma((E,)), dma((2, E)), dma((2, E)),
            dma((2, imgs, E - 1)), dma((2, imgs, E - 1)),
            dma((3 + 2 * imgs,)), dma((2, imgs)), dma((2,)),
        ],
        compiler_params=pltpu.CompilerParams(
            vmem_limit_bytes=VMEM_LIMIT, collective_id=0, has_side_effects=True
        ),
        cost_estimate=pl.CostEstimate(flops=10**11, bytes_accessed=10**8, transcendentals=2 * 10**7),
        name="front",
    )(pack, ew, dy, x, noise, keep)


def expert_kernel(nb, who_ref, *refs):
    h_in, dy_in, w_in = refs[:3]
    outs = refs[3:]
    dx_out, y_out, rows_out, hid_out, tiles_ref = outs[:5]
    (h, dy, y_t, dx_t, w_s, gate_s, slot_s, dgate_s, xs, dys, hid_s, rows_s, lo_s, hi_s, in_sem, out_sem, row_sem, hid_sem, w_sem) = outs[5:]
    me = who_ref[0]
    loads = [
        pltpu.make_async_copy(h_in, h, in_sem.at[0]),
        pltpu.make_async_copy(dy_in, dy, in_sem.at[1]),
    ]
    for b in range(E):
        at = pl.ds(b * (D // E), D // E)
        for r in range(4):
            loads.append(pltpu.make_async_copy(w_in.at[r, b], w_s.at[r, :, at], w_sem.at[r, b]))
    for copy in loads:
        copy.start()
    y_t[...] = jnp.zeros_like(y_t)
    dx_t[...] = jnp.zeros_like(dx_t)
    dgate_s[...] = jnp.zeros_like(dgate_s)
    for copy in loads:
        copy.wait()

    row16 = iota((16, D), 0)
    for b in range(nb):
        meta = h[b, PAD - 16 : PAD, :].astype(F32)
        gate_s[b : b + 1, :] = jnp.sum(jnp.where(row16 == 8 + me, meta, 0.0), axis=0, keepdims=True)[:, :PAD]
    gates = gate_s[...]
    named = (gates >= 0) & (iota((nb, PAD), 1) < SEQ)
    ones = named.astype(F32).astype(BF16)
    upto = dot(ones, (iota((PAD, PAD), 0) <= iota((PAD, PAD), 1)).astype(F32).astype(BF16))
    count = dot(ones, jnp.ones((PAD, PAD), BF16)).astype(BF16)
    before = dot((iota((nb, nb), 0) > iota((nb, nb), 1)).astype(F32).astype(BF16), count)
    slot_s[...] = jnp.where(named, before + upto - 1.0, -1.0).astype(jnp.int32)
    ends = jnp.where(named, before + upto, before)
    for b in range(nb):
        lo_s[b] = jnp.max(before[b : b + 1, :]).astype(jnp.int32)
        hi_s[b] = jnp.max(ends[b : b + 1, :]).astype(jnp.int32)
    tiles = lax.div(hi_s[nb - 1] + TILE - 1, TILE)
    tiles_ref[0] = tiles

    def meets(b, first):
        return (lo_s[b] < first + TILE) & (hi_s[b] > first) & (hi_s[b] > lo_s[b])

    def place(b, first):
        return iota((TILE, PAD), 0) + first == slot_s[pl.ds(b, 1), :]

    def step(t, carry):
        first = t * TILE
        slot = lax.rem(t, 2)
        xs[...] = jnp.zeros_like(xs)
        dys[...] = jnp.zeros_like(dys)

        def collect(b, gcol):
            def one(gcol):
                hit = place(b, first)
                p = hit.astype(F32).astype(BF16)
                xs[...] += dot(p, h[b])
                dys[...] += dot(p, dy[b])
                return gcol + jnp.sum(jnp.where(hit, gate_s[pl.ds(b, 1), :], 0.0), axis=1, keepdims=True)

            return lax.cond(meets(b, first), one, lambda g: g, gcol)

        gcol = lax.fori_loop(0, nb, collect, jnp.zeros((TILE, 1), F32))

        def drain(s):
            pltpu.make_async_copy(rows_s.at[s], rows_out.at[:, pl.ds(0, TILE)], row_sem.at[s]).wait()
            pltpu.make_async_copy(hid_s.at[s], hid_out.at[:, pl.ds(0, TILE)], hid_sem.at[s]).wait()

        @pl.when(t >= 2)
        def _():
            drain(slot)

        x = xs[...].astype(BF16)
        g_rows = (dys[...] * gcol).astype(BF16)
        rows_s[slot, 0] = x
        rows_s[slot, 1] = g_rows
        y = jnp.zeros((TILE, D), F32)
        dx = jnp.zeros((TILE, D), F32)
        for r in range(4):
            w1, w2 = w_s.at[r, 0], w_s.at[r, 1]
            a = dot(x, w1[...])
            a2 = a * a
            th = jnp.tanh(0.7978845608028654 * a * (1.0 + 0.044715 * a2))
            half = 0.5 * (1.0 + th)
            hid = (a * half).astype(BF16)
            slope = half + 0.5 * a * (1.0 - th * th) * (0.7978845608028654 * (1.0 + 3 * 0.044715 * a2))
            da = (dot(g_rows, w2[...]) * slope).astype(BF16)
            y = y + dot_nt(hid, w2[...])
            dx = dx + dot_nt(da, w1[...])
            hid_s[slot, 0, :, r * FFS : (r + 1) * FFS] = da
            hid_s[slot, 1, :, r * FFS : (r + 1) * FFS] = hid
        at = pl.ds(pl.multiple_of(first, TILE), TILE)
        pltpu.make_async_copy(rows_s.at[slot], rows_out.at[:, at], row_sem.at[slot]).start()
        pltpu.make_async_copy(hid_s.at[slot], hid_out.at[:, at], hid_sem.at[slot]).start()
        dgate = jnp.sum(dys[...] * y, axis=1, keepdims=True)
        y_low = (y * gcol).astype(BF16)
        dx_low = dx.astype(BF16)

        def give(b, carry):
            @pl.when(meets(b, first))
            def _():
                hit = place(b, first)
                p = hit.astype(F32).astype(BF16)
                y_t[b] = y_t[b] + dot_tn(p, y_low).astype(BF16)
                dx_t[b] = dx_t[b] + dot_tn(p, dx_low).astype(BF16)
                dgate_s[pl.ds(b, 1), :] += jnp.sum(jnp.where(hit, dgate, 0.0), axis=0, keepdims=True)

            return carry

        lax.fori_loop(0, nb, give, 0)
        return carry

    lax.fori_loop(0, tiles, step, 0)
    for back in (1, 2):

        @pl.when(tiles >= back)
        def _():
            s = lax.rem(tiles - back, 2)
            pltpu.make_async_copy(rows_s.at[s], rows_out.at[:, pl.ds(0, TILE)], row_sem.at[s]).wait()
            pltpu.make_async_copy(hid_s.at[s], hid_out.at[:, pl.ds(0, TILE)], hid_sem.at[s]).wait()

    for b in range(nb):
        tail = dx_t[b, PAD - 16 : PAD, :].astype(F32)
        line = jnp.concatenate([dgate_s[b : b + 1, :], jnp.zeros((1, D - PAD), F32)], axis=1)
        dx_t[b, PAD - 16 : PAD, :] = (tail + jnp.where(row16 == 8 + me, line, 0.0)).astype(BF16)
    stores = [
        pltpu.make_async_copy(dx_t, dx_out, out_sem.at[0]),
        pltpu.make_async_copy(y_t, y_out, out_sem.at[1]),
    ]
    for copy in stores:
        copy.start()
    for copy in stores:
        copy.wait()


def expert_rows(nb):
    return -(-nb * SEQ // TILE) * TILE


def experts(member, h_all, dy_all, weights):
    nb = h_all.shape[0]
    rows = expert_rows(nb)
    hbm = pl.BlockSpec(memory_space=pl.ANY)
    sm = pl.BlockSpec(memory_space=pltpu.SMEM)
    table = jax.ShapeDtypeStruct((nb, PAD, D), BF16)
    return pl.pallas_call(
        functools.partial(expert_kernel, nb),
        out_shape=[
            table,
            table,
            jax.ShapeDtypeStruct((2, rows, D), BF16),
            jax.ShapeDtypeStruct((2, rows, 4 * FFS), BF16),
            jax.ShapeDtypeStruct((1,), jnp.int32),
        ],
        in_specs=[sm, hbm, hbm, hbm],
        out_specs=[hbm] * 4 + [sm],
        scratch_shapes=[
            pltpu.VMEM((nb, PAD, D), BF16),
            pltpu.VMEM((nb, PAD, D), BF16),
            pltpu.VMEM((nb, PAD, D), BF16),
            pltpu.VMEM((nb, PAD, D), BF16),
            pltpu.VMEM((4, 2, D, FFS), BF16),
            pltpu.VMEM((nb, PAD), F32),
            pltpu.VMEM((nb, PAD), jnp.int32),
            pltpu.VMEM((nb, PAD), F32),
            pltpu.VMEM((TILE, D), F32),
            pltpu.VMEM((TILE, D), F32),
            pltpu.VMEM((2, 2, TILE, 4 * FFS), BF16),
            pltpu.VMEM((2, 2, TILE, D), BF16),
            pltpu.SMEM((nb,), jnp.int32),
            pltpu.SMEM((nb,), jnp.int32),
            pltpu.SemaphoreType.DMA((2,)),
            pltpu.SemaphoreType.DMA((2,)),
            pltpu.SemaphoreType.DMA((2,)),
            pltpu.SemaphoreType.DMA((2,)),
            pltpu.SemaphoreType.DMA((4, E)),
        ],
        compiler_params=pltpu.CompilerParams(vmem_limit_bytes=VMEM_LIMIT),
        cost_estimate=pl.CostEstimate(flops=30 * 10**9, bytes_accessed=4 * 10**7, transcendentals=4 * 10**6),
        name="experts",
    )(member.reshape(1), h_all, dy_all, weights)


def expert_grad_kernel(tiles_ref, rows_ref, hid_ref, out_ref, acc):
    acc[...] = jnp.zeros_like(acc)

    def step(t, carry):
        at = pl.ds(pl.multiple_of(t * TILE, TILE), TILE)
        acc[...] += dot_tn(rows_ref[0, at, :], hid_ref[0, at, :])
        return carry

    lax.fori_loop(0, tiles_ref[0], step, 0)
    out_ref[0] = acc[...].astype(BF16)


def expert_grads(tiles, rows, hid, kind, base):
    n = rows.shape[1]
    return pl.pallas_call(
        expert_grad_kernel,
        grid_spec=pltpu.PrefetchScalarGridSpec(
            num_scalar_prefetch=1,
            grid=(2,),
            in_specs=[
                pl.BlockSpec((1, n, D), lambda s, _: (kind, 0, 0)),
                pl.BlockSpec((1, n, FFS), lambda s, _: (kind, 0, base + s)),
            ],
            out_specs=pl.BlockSpec((1, D, FFS), lambda s, _: (s, 0, 0)),
            scratch_shapes=[pltpu.VMEM((D, FFS), F32)],
        ),
        out_shape=jax.ShapeDtypeStruct((2, D, FFS), BF16),
        compiler_params=pltpu.CompilerParams(vmem_limit_bytes=VMEM_LIMIT),
        cost_estimate=pl.CostEstimate(flops=4 * 10**9, bytes_accessed=15 * 10**6, transcendentals=0),
        name="expert_grads",
    )(tiles, rows, hid)


def unpack_kernel(who_ref, *refs):
    blocks, (in_ref, out_ref) = refs[:E], refs[E:]
    for by in range(E):
        in_ref[who_ref[by]] = blocks[by][0].astype(F32)
        out_ref[who_ref[by]] = blocks[by][1].astype(F32)


def unpack(who, blocks):
    vm = pl.BlockSpec(memory_space=pltpu.VMEM)
    whole = jax.ShapeDtypeStruct((E,) + blocks[0].shape[1:], F32)
    return pl.pallas_call(
        unpack_kernel,
        out_shape=(whole, whole),
        in_specs=[pl.BlockSpec(memory_space=pltpu.SMEM)] + [vm] * E,
        out_specs=(vm, vm),
        compiler_params=pltpu.CompilerParams(vmem_limit_bytes=VMEM_LIMIT),
        cost_estimate=pl.CostEstimate(flops=10**6, bytes_accessed=7 * 10**6, transcendentals=0),
        name="unpack",
    )(who, *blocks)


def lay_out_kernel(imgs, at_ref, *refs):
    parts, out_ref, held, sem = refs[:4], refs[4], refs[5], refs[6]
    copies = [pltpu.make_async_copy(parts[s], held.at[s], sem.at[s]) for s in range(4)]
    for copy in copies:
        copy.start()
    for copy in copies:
        copy.wait()
    for i in range(4 * imgs):
        out_ref[i * SEQ : (i + 1) * SEQ, :] = held[at_ref[i // imgs], i % imgs, :SEQ, :]


def lay_out(at, parts):
    imgs = parts[0].shape[0]
    hbm = pl.BlockSpec(memory_space=pl.ANY)
    return pl.pallas_call(
        functools.partial(lay_out_kernel, imgs),
        out_shape=jax.ShapeDtypeStruct((4 * imgs * SEQ, D), BF16),
        in_specs=[pl.BlockSpec(memory_space=pltpu.SMEM)] + [hbm] * 4,
        out_specs=pl.BlockSpec(memory_space=pltpu.VMEM),
        scratch_shapes=[pltpu.VMEM((4, imgs, PAD, D), BF16), pltpu.SemaphoreType.DMA((4,))],
        compiler_params=pltpu.CompilerParams(vmem_limit_bytes=VMEM_LIMIT),
        cost_estimate=pl.CostEstimate(flops=10**6, bytes_accessed=5 * 10**6, transcendentals=0),
        name="lay_out",
    )(at, *parts)


def attn_backward_kernel(imgs, *refs):
    dh_in = refs[:imgs]
    x1_in, x_in, dy_in, probs_in, qkv_in, o_in, lse_in, w_ref = refs[imgs : imgs + 8]
    packs, dtok_ref = refs[imgs + 8 : imgs + 11], refs[imgs + 11]
    dx1_s, low_s, h1_s, dh1_s, dqkv_s, o_s = refs[imgs + 12 :]
    n_dp, d_own = packs[0].shape[0], packs[0].shape[1] - 16

    def pack_of(r):
        return packs[r] if r < 2 else packs[2].at[:, r - 2]

    par = params_of(w_ref[0])
    router = par[8:16].astype(BF16)
    row_ok = iota((PAD, 1), 0) < SEQ
    lane_ok = iota((E, PAD), 1) < SEQ
    key_ok = iota((PAD, PAD), 1) < SEQ
    small2g = jnp.zeros((1, D), F32)
    small2b = jnp.zeros((1, D), F32)
    g_router = jnp.zeros((E, D), F32)
    for c in range(imgs):
        span = slice(c * PAD, (c + 1) * PAD)
        arrived = dh_in[c][...].astype(F32)
        dgate = arrived[PAD - 8 :, :PAD]
        probs = probs_in[c]
        dlogits = probs * (dgate - jnp.sum(probs * dgate, axis=0, keepdims=True))
        dlogits = jnp.where(lane_ok, dlogits, 0.0).astype(BF16)
        unit, scale = normalise(x1_in[c])
        h2 = (unit * par[2:3] + par[3:4]).astype(BF16)
        g_router = g_router + dot(dlogits, h2)
        dh2 = jnp.where(row_ok, arrived + dot_tn(dlogits, router), 0.0)
        small2g = small2g + jnp.sum(dh2 * unit, axis=0, keepdims=True)
        small2b = small2b + jnp.sum(dh2, axis=0, keepdims=True)
        dx1 = dy_in[c].astype(F32) + norm_back(dh2, unit, scale, par[2:3])
        dx1_s[span, :] = dx1
        low_s[span, :] = dx1.astype(BF16)
        unit1, _ = normalise(x_in[c].astype(F32))
        h1_s[span, :] = (unit1 * par[0:1] + par[1:2]).astype(BF16)
    low = low_s[...]
    h1 = h1_s[...]
    for r in range(4):
        w = w_ref[r]
        dout = dot(low, w[:, 9 * HD : D]).astype(BF16)
        for c in range(imgs):
            span = slice(c * PAD, (c + 1) * PAD)
            qkv = qkv_in[c, r]
            lse = lse_in[c]
            o_s[span, :] = o_in[c, r]
            dqs, dks, dvs = [], [], []
            for h in range(3):
                q = qkv[:, h * HD : (h + 1) * HD]
                k = qkv[:, (3 + h) * HD : (4 + h) * HD]
                v = qkv[:, (6 + h) * HD : (7 + h) * HD]
                do = dout[span, h * HD : (h + 1) * HD]
                s = dot_nt(q, k) * HD ** (-0.5)
                p = jnp.where(key_ok, jnp.exp(s - lse[:, 3 * r + h : 3 * r + h + 1]), 0.0)
                dvs.append(dot_tn(p.astype(BF16), do).astype(BF16))
                dp = dot_nt(do, v)
                ds = (p * (dp - jnp.sum(p * dp, axis=-1, keepdims=True))).astype(BF16)
                dqs.append((dot(ds, k) * HD ** (-0.5)).astype(BF16))
                dks.append((dot_tn(ds, q) * HD ** (-0.5)).astype(BF16))
            dqkv_s[span, :] = jnp.concatenate(dqs + dks + dvs, axis=1)
        dqkv = dqkv_s[...]
        part = dot_nt(dqkv, w[:, : 9 * HD])
        dh1_s[...] = part if r == 0 else dh1_s[...] + part
        grad = jnp.concatenate([dot_tn(h1, dqkv), dot_tn(low, o_s[...])], axis=1).astype(BF16)
        for i in range(n_dp):
            pack_of(r)[i, :d_own, :] = grad[i * d_own : (i + 1) * d_own]
    small1g = jnp.zeros((1, D), F32)
    small1b = jnp.zeros((1, D), F32)
    for c in range(imgs):
        span = slice(c * PAD, (c + 1) * PAD)
        dh1 = jnp.where(row_ok, dh1_s[span, :], 0.0)
        unit1, scale1 = normalise(x_in[c].astype(F32))
        small1g = small1g + jnp.sum(dh1 * unit1, axis=0, keepdims=True)
        small1b = small1b + jnp.sum(dh1, axis=0, keepdims=True)
        dtok_ref[c] = (dx1_s[span, :] + norm_back(dh1, unit1, scale1, par[0:1])).astype(BF16)
    small = jnp.concatenate([small1g, small1b, small2g, small2b, jnp.zeros((4, D), F32), g_router], axis=0)
    for i in range(n_dp):
        line = jnp.concatenate([small[:, i * d_own : (i + 1) * d_own], jnp.zeros((16, D - d_own), F32)], axis=1)
        for r in range(4):
            pack_of(r)[i, d_own:, :] = line.astype(BF16)


def attn_backward(dh, saved, w, n_dp):
    imgs = len(dh)
    pack = (n_dp, D // n_dp + 16, D)
    vm = pl.BlockSpec(memory_space=pltpu.VMEM)
    rows = imgs * PAD
    return pl.pallas_call(
        functools.partial(attn_backward_kernel, imgs),
        out_shape=(
            jax.ShapeDtypeStruct(pack, BF16),
            jax.ShapeDtypeStruct(pack, BF16),
            jax.ShapeDtypeStruct((n_dp, 2) + pack[1:], BF16),
            jax.ShapeDtypeStruct((imgs, PAD, D), BF16),
        ),
        in_specs=[vm] * (imgs + 8),
        out_specs=(vm,) * 4,
        scratch_shapes=[
            pltpu.VMEM((rows, D), F32),
            pltpu.VMEM((rows, D), BF16),
            pltpu.VMEM((rows, D), BF16),
            pltpu.VMEM((rows, D), F32),
            pltpu.VMEM((rows, 9 * HD), BF16),
            pltpu.VMEM((rows, 3 * HD), BF16),
        ],
        compiler_params=pltpu.CompilerParams(vmem_limit_bytes=VMEM_LIMIT),
        cost_estimate=pl.CostEstimate(flops=12 * 10**9, bytes_accessed=2 * 10**7, transcendentals=2 * 10**6),
        name="attn_backward",
    )(*dh, *saved, w)


RING = (0, 2, 4, 6, 7, 5, 3, 1)


class Mover:
    def __init__(self, n_dp):
        self.n_dp = n_dp
        self.groups = n_dp // E
        self.me = lax.axis_index("dp")
        self.member = lax.rem(self.me, E)
        self.group = lax.div(self.me, E)
        self.tensor = lax.axis_index("tensor")
        self.place = ring_place(self.member)
        bases = range(0, n_dp, E)
        self.ring = (
            [(b + RING[i], b + RING[(i + 1) % E]) for b in bases for i in range(E)],
            [(b + RING[(i + 1) % E], b + RING[i]) for b in bases for i in range(E)],
        )

    def along(self, value, way):
        return lax.ppermute(value, "dp", self.ring[way])

    def shift(self, value, by):
        perm = [(b + i, b + (i + by) % E) for b in range(0, self.n_dp, E) for i in range(E)]
        return lax.ppermute(value, "dp", perm)

    def shift_group(self, value, by):
        return lax.ppermute(value, "dp", [(k, (k + by * E) % self.n_dp) for k in range(self.n_dp)])

    def other(self, value, mask):
        return lax.ppermute(value, "tensor", [(k, k ^ mask) for k in range(4)])

    def behind(self, way, k):
        step = -k if way == 0 else k
        return ring_member(lax.rem(self.place + step + E, E))

    def group_lists(self):
        if self.groups == 1:
            return None
        return [[b + i for i in range(E)] for b in range(0, self.n_dp, E)]

    def gather(self, value):
        return lax.all_gather(value, "dp", axis=0, tiled=False, axis_index_groups=self.group_lists())

    def scatter_sum(self, value):
        return lax.psum_scatter(
            value, "dp", scatter_dimension=0, tiled=False, axis_index_groups=self.group_lists()
        )

    def front(self, pack, ew, dy, x, noise, keep):
        own = lax.all_gather(pack, "dp", axis=0, tiled=True)
        two = jnp.stack([own, self.other(own, 2)])
        w = jnp.concatenate([two, self.other(two, 1)], axis=0)
        blocks = jnp.zeros((2, E * pack.shape[0], FFS), BF16)
        for by in range(E):
            to = lax.rem(self.member + by, E)
            block = lax.dynamic_index_in_dim(ew, to, 0, False)
            came = lax.rem(self.member - by + E, E)
            block = self.shift(block, by) if by else block
            blocks = lax.dynamic_update_slice_in_dim(blocks, block, came * pack.shape[0], 1)
        blocks = self.all_groups(blocks, 1)
        blocks = jnp.swapaxes(blocks.reshape(2, E, D // E, FFS), 0, 1)
        two = jnp.stack([blocks, self.other(blocks, 2)])
        weights = jnp.concatenate([two, self.other(two, 1)], axis=0)
        chunk, *saved = attn_forward(x, w, noise, keep)
        table = (E * x.shape[0], PAD, D)
        dh, y, rows, hid, tiles = experts(
            self.member, self.gather(chunk).reshape(table), self.gather(dy).reshape(table), weights
        )
        sums = [self.scatter_sum(t.reshape((E,) + chunk.shape)) for t in (dh, y)]
        g = [jnp.concatenate([expert_grads(tiles, rows, hid, kind, base) for base in (0, 2)]) for kind in (0, 1)]
        g = jnp.stack([part.reshape(4, E, D // E, FFS) for part in g], axis=2)
        return g, jnp.stack(sums), w, *saved

    def sum_both_ways(self, block_for):
        def chain(way, steps):
            total = block_for(self.behind(1 - way, steps)).astype(BF16)
            for k in range(steps - 1, -1, -1):
                total = self.along(total, way)
                if k:
                    total = (total.astype(F32) + block_for(self.behind(1 - way, k)).astype(F32)).astype(BF16)
            return total

        ahead = chain(0, E // 2)
        back = chain(1, E // 2 - 1)
        return ahead.astype(F32) + back.astype(F32) + block_for(self.member).astype(F32)

    def all_groups(self, part, dim):
        if self.groups == 1:
            return part
        size = part.shape[dim]
        shape = part.shape[:dim] + (size * self.groups,) + part.shape[dim + 1 :]
        whole = lax.dynamic_update_slice_in_dim(jnp.zeros(shape, part.dtype), part, self.group * size, dim)
        for by in range(1, self.groups):
            came = lax.rem(self.group - by + self.groups, self.groups)
            whole = lax.dynamic_update_slice_in_dim(whole, self.shift_group(part, by), came * size, dim)
        return whole

    def sum_groups(self, whole, dim):
        if self.groups == 1:
            return whole
        size = whole.shape[dim] // self.groups
        total = lax.dynamic_slice_in_dim(whole, self.group * size, size, dim).astype(F32)
        for by in range(1, self.groups):
            to = lax.rem(self.group + by, self.groups)
            part = lax.dynamic_slice_in_dim(whole, to * size, size, dim)
            total = total + self.shift_group(part, by).astype(F32)
        return total.astype(whole.dtype)


def after(value, *first):
    return lax.optimization_barrier((value, first))[0]


def _slot(tensor, t):
    apart = lax.bitwise_xor(tensor, t)
    return lax.div(apart, 2) + 2 * lax.rem(apart, 2)


def image_blocks(rows, tensor, imgs):
    first = tensor * (imgs * SEQ)
    return [
        jnp.pad(lax.dynamic_slice_in_dim(rows, first + c * SEQ, SEQ, 0), ((0, PAD - SEQ), (0, 0)))
        for c in range(imgs)
    ]


def image_lanes(lanes, tensor, imgs):
    first = tensor * (imgs * SEQ)
    return [
        jnp.pad(lax.dynamic_slice_in_dim(lanes, first + c * SEQ, SEQ, 1), ((0, 0), (0, PAD - SEQ)))
        for c in range(imgs)
    ]


def kept_pairs(routes):
    chosen = jnp.transpose(routes).reshape(1, -1)
    named = (chosen == jnp.arange(E, dtype=jnp.int32)[:, None]).astype(jnp.int32)
    kept = named * (jnp.cumsum(named, axis=1) <= CAP)
    return jnp.sum(kept.reshape(E, TOP, -1), axis=1).astype(F32)


def body(
    n_dp,
    tokens,
    ln1_gain,
    ln1_bias,
    w_qkv,
    w_attn_out,
    ln2_gain,
    ln2_bias,
    router_weight,
    w_in,
    w_expert_out,
    router_noise,
    routes,
    cotangent,
):
    move = Mover(n_dp)
    token_count = tokens.shape[0]
    imgs = token_count // SEQ // 4
    d_own = w_qkv.shape[0]
    ways = [c % 2 for c in range(imgs)]

    vectors = jnp.stack([ln1_gain, ln1_bias, ln2_gain, ln2_bias] + [jnp.zeros_like(ln1_gain)] * 4, axis=1)
    pack = jnp.concatenate(
        [w_qkv[:, 0], w_qkv[:, 1], w_qkv[:, 2], jnp.transpose(w_attn_out), vectors, router_weight], axis=1
    )
    pack = jnp.pad(pack, ((0, 0), (0, 128 - 16))).astype(BF16)
    ew = jnp.stack([w_in, jnp.transpose(w_expert_out, (0, 2, 1))], axis=1).astype(BF16)
    x = jnp.stack(image_blocks(tokens, move.tensor, imgs))
    dy = jnp.stack(image_blocks(cotangent, move.tensor, imgs))
    keep = jnp.stack(image_lanes(kept_pairs(routes), move.tensor, imgs))
    noise = jnp.stack(image_lanes(jnp.transpose(router_noise), move.tensor, imgs))
    if move.groups == 1:
        _, _, _, g_low, sums, w, *saved = front(pack, ew, dy, x, noise, keep)
    else:
        g_low, sums, w, *saved = move.front(pack, ew, dy, x, noise, keep)
    x1, qkv, o, lse, probs = saved
    dh_sum, y_sum = sums[0], sums[1]

    passed = move.other(g_low[2:], 1)
    pair = [(g_low[s].astype(F32) + passed[s].astype(F32)).astype(BF16) for s in range(2)]
    total = (pair[0].astype(F32) + move.other(pair[1], 2).astype(F32)).astype(BF16)
    if move.groups > 1:
        total = jnp.swapaxes(total, 1, 2).reshape(D, 2, FFS)
        total = jnp.swapaxes(move.sum_groups(total, 0).reshape(E, d_own, 2, FFS), 1, 2)
    g_exp = []
    for by in range(E):
        to = lax.rem(move.member + by, E)
        block = lax.dynamic_index_in_dim(total, to, 0, False)
        g_exp.append(move.shift(block, by) if by else block)

    pack0, pack1, packs, d_tok = attn_backward(
        [dh_sum[c] for c in range(imgs)], (x1, x, dy, probs, qkv, o, lse), w, n_dp
    )
    passed = move.other(packs, 1)
    if move.groups > 1:
        pack0 = move.sum_groups((pack0.astype(F32) + passed[:, 0].astype(F32)).astype(BF16), 0)
        pack1 = move.sum_groups((pack1.astype(F32) + passed[:, 1].astype(F32)).astype(BF16), 0)
        passed = jnp.zeros((E, 2) + pack0.shape[1:], BF16)

    def pack_for(member):
        one, two = (lax.dynamic_index_in_dim(p, member, 0, False).astype(F32) for p in (pack0, pack1))
        came = lax.dynamic_index_in_dim(passed, member, 0, False).astype(F32)
        return one + came[0] + move.other((two + came[1]).astype(BF16), 2).astype(F32)

    total = move.sum_both_ways(pack_for)
    g_qkv = total[:d_own, : 9 * HD].reshape(d_own, 3, 3 * HD)
    g_attn_out = jnp.transpose(total[:d_own, 9 * HD :])
    g_small = total[d_own:, :d_own]

    at = jnp.stack([_slot(move.tensor, t) for t in range(4)])

    def all_rows(own):
        across = move.other(own, 2)
        return lay_out(at, [own, across, move.other(own, 1), move.other(across, 1)])

    d_tokens = all_rows(d_tok)
    output = all_rows((x1 + y_sum.astype(F32)).astype(BF16))
    came = jnp.stack([lax.rem(move.member - by + E, E) for by in range(E)])
    g_in, g_out = unpack(came, g_exp)
    return (
        output,
        d_tokens,
        g_small[0],
        g_small[1],
        g_qkv,
        g_attn_out,
        g_small[2],
        g_small[3],
        jnp.transpose(g_small[8:16]),
        g_in,
        jnp.transpose(g_out, (0, 2, 1)),
    )


def solution(mesh):
    in_specs = (
        P("dp", None),
        P("dp"),
        P("dp"),
        P("dp", None, "tensor"),
        P("tensor", "dp"),
        P("dp"),
        P("dp"),
        P("dp", None),
        P(None, "dp", "tensor"),
        P(None, "tensor", "dp"),
        P("dp", None),
        P("dp", None),
        P("dp", None),
    )
    out_specs = (
        P("dp", None),
        P("dp", None),
        P("dp"),
        P("dp"),
        P("dp", None, "tensor"),
        P("tensor", "dp"),
        P("dp"),
        P("dp"),
        P("dp", None),
        P(None, "dp", "tensor"),
        P(None, "tensor", "dp"),
    )
    return jax.shard_map(
        functools.partial(body, mesh.shape["dp"]),
        mesh=mesh,
        in_specs=in_specs,
        out_specs=out_specs,
        check_vma=False,
    )
```

```python
import functools

import jax
import jax.numpy as jnp
from jax import lax
from jax.experimental import pallas as pl
from jax.experimental.pallas import tpu as pltpu
from jax.sharding import PartitionSpec as P

D = 768
HD = 64
E = 8
TOP = 2
SEQ = 197
CAP = 689
PAD = 208
META = 200
TILE = 256
FFS = 768
EPS = 1e-06
VMEM_LIMIT = 62 * 1024 * 1024

F32 = jnp.float32
BF16 = jnp.bfloat16


def dot(a, b):
    return jnp.dot(a, b, preferred_element_type=F32)


def dot_nt(a, b):
    return lax.dot_general(a, b, (((1,), (1,)), ((), ())), preferred_element_type=F32)


def dot_tn(a, b):
    return lax.dot_general(a, b, (((0,), (0,)), ((), ())), preferred_element_type=F32)


def iota(shape, dim):
    return lax.broadcasted_iota(jnp.int32, shape, dim)


def normalise(values):
    centred = values - jnp.mean(values, axis=-1, keepdims=True)
    scale = lax.rsqrt(jnp.mean(centred * centred, axis=-1, keepdims=True) + EPS)
    return centred * scale, scale


def norm_back(grad, unit, scale, gain):
    g = grad * gain
    return scale * (
        g - jnp.mean(g, axis=-1, keepdims=True) - unit * jnp.mean(g * unit, axis=-1, keepdims=True)
    )


def params_of(w_own):
    return jnp.transpose(w_own[:, D:].astype(F32))[:16]


def attend(x, par, w_of, noise, keep, chunk_ref, x1_ref, qkv_ref, o_ref, lse_ref, probs_ref):
    x = x.astype(F32)
    unit, _ = normalise(x)
    h1 = (unit * par[0:1] + par[1:2]).astype(BF16)
    acc = x
    lse = jnp.zeros((PAD, 128), F32)
    key_ok = iota((PAD, PAD), 1) < SEQ
    lane = iota((PAD, 128), 1)
    for r in range(4):
        w = w_of(r)
        qkv = dot(h1, w[:, : 9 * HD]).astype(BF16)
        qkv_ref[r] = qkv
        outs = []
        for h in range(3):
            q = qkv[:, h * HD : (h + 1) * HD]
            k = qkv[:, (3 + h) * HD : (4 + h) * HD]
            v = qkv[:, (6 + h) * HD : (7 + h) * HD]
            s = jnp.where(key_ok, dot_nt(q, k) * HD ** (-0.5), -1e30)
            top = jnp.max(s, axis=-1, keepdims=True)
            p = jnp.exp(s - top)
            total = jnp.sum(p, axis=-1, keepdims=True)
            outs.append(dot((p * (1.0 / total)).astype(BF16), v).astype(BF16))
            lse = jnp.where(lane == 3 * r + h, top + jnp.log(total), lse)
        o = jnp.concatenate(outs, axis=1)
        o_ref[r] = o
        acc = acc + dot_nt(o, w[:, 9 * HD : D])
    lse_ref[...] = lse
    x1_ref[...] = acc
    unit2, _ = normalise(acc)
    h2 = (unit2 * par[2:3] + par[3:4]).astype(BF16)
    logits = dot_nt(par[8:16].astype(BF16), h2) + noise
    e = jnp.exp(logits - jnp.max(logits, axis=0, keepdims=True))
    probs = e / jnp.sum(e, axis=0, keepdims=True)
    probs_ref[...] = probs
    gates = jnp.where(keep > 0, probs, -1.0)
    chunk_ref[...] = h2
    tail = jnp.concatenate([gates, jnp.zeros((8, D - PAD), F32)], axis=1)
    low = h2[PAD - 16 :, :].astype(F32)
    chunk_ref[PAD - 16 :, :] = jnp.concatenate([low[:8], tail], axis=0).astype(BF16)


def attn_shapes(imgs):
    return (
        jax.ShapeDtypeStruct((imgs, PAD, D), F32),
        jax.ShapeDtypeStruct((imgs, 4, PAD, 9 * HD), BF16),
        jax.ShapeDtypeStruct((imgs, 4, PAD, 3 * HD), BF16),
        jax.ShapeDtypeStruct((imgs, PAD, 128), F32),
        jax.ShapeDtypeStruct((imgs, E, PAD), F32),
    )


def attn_forward_kernel(imgs, x_ref, w_ref, noise_ref, keep_ref, chunk_ref, *saved):
    par = params_of(w_ref[0])
    for c in range(imgs):
        attend(
            x_ref[c], par, lambda r: w_ref[r], noise_ref[c], keep_ref[c],
            chunk_ref.at[c], *(ref.at[c] for ref in saved),
        )


def attn_forward(x, w, noise, keep):
    imgs = x.shape[0]
    vm = pl.BlockSpec(memory_space=pltpu.VMEM)
    return pl.pallas_call(
        functools.partial(attn_forward_kernel, imgs),
        out_shape=(jax.ShapeDtypeStruct((imgs, PAD, D), BF16),) + attn_shapes(imgs),
        in_specs=[vm] * 4,
        out_specs=(vm,) * 6,
        compiler_params=pltpu.CompilerParams(vmem_limit_bytes=VMEM_LIMIT),
        cost_estimate=pl.CostEstimate(flops=6 * 10**9, bytes_accessed=10**7, transcendentals=2 * 10**6),
        name="attn_forward",
    )(x, w, noise, keep)


def ring_place(member):
    odd = lax.rem(member, 2)
    half = lax.div(member, 2)
    return half + odd * (E - 1 - 2 * half)


def ring_member(place):
    late = lax.div(place, E // 2)
    return 2 * place + late * (2 * E - 1 - 4 * place)


class Peers:
    def __init__(self):
        dp = lax.axis_index("dp")
        tensor = lax.axis_index("tensor")
        self.member = lax.rem(dp, E)
        self.base = dp - self.member
        self.place = ring_place(self.member)
        self.across = {"tensor": lax.rem(tensor + 2, 4)}
        self.core = {"tensor": tensor + 1 - 2 * lax.rem(tensor, 2)}
        self.next = ({"dp": self.base + self.behind(1, 1)}, {"dp": self.base + self.behind(0, 1)})
        self.sends = []

    def behind(self, way, k):
        step = E - k if way == 0 else k
        return ring_member(lax.rem(self.place + step, E))

    def ahead(self, by):
        return lax.rem(self.member + by, E)

    def came(self, by):
        return lax.rem(self.member + E - by, E)

    def meet(self):
        barrier = pltpu.get_barrier_semaphore()
        others = [{"dp": self.base + self.ahead(by)} for by in range(1, E)] + [self.across, self.core]
        for device in others:
            pl.semaphore_signal(barrier, inc=1, device_id=device, device_id_type=pl.DeviceIdType.MESH)
        pl.semaphore_wait(barrier, len(others))

    def send(self, src, dst, sems, at, device):
        copy = pltpu.make_async_remote_copy(
            src_ref=src,
            dst_ref=dst,
            send_sem=sems[0].at[at],
            recv_sem=sems[1].at[at],
            device_id=device,
            device_id_type=pl.DeviceIdType.MESH,
        )
        copy.start()
        self.sends.append(copy)
        return copy


def expert_step(x, dy, gate, w_ref, g_ref, y_ref, dx_ref):
    weight = jnp.maximum(gate, 0.0)
    d_rows = (dy.astype(F32) * weight).astype(BF16)

    def hidden(r, carry):
        w1 = w_ref[r, :, 0].reshape(D, FFS)
        w2 = w_ref[r, :, 1].reshape(D, FFS)
        a = dot(x, w1)
        a2 = a * a
        th = jnp.tanh(0.7978845608028654 * a * (1.0 + 0.044715 * a2))
        half = 0.5 * (1.0 + th)
        hid = (a * half).astype(BF16)
        slope = half + 0.5 * a * (1.0 - th * th) * (0.7978845608028654 * (1.0 + 3 * 0.044715 * a2))
        da = (dot(d_rows, w2) * slope).astype(BF16)
        y_ref[...] += dot_nt(hid, w2)
        dx_ref[...] += dot_nt(da, w1)
        g_ref[r, 0] += dot_tn(x, da)
        g_ref[r, 1] += dot_tn(d_rows, hid)
        return carry

    y_ref[...] = jnp.zeros_like(y_ref)
    dx_ref[...] = jnp.zeros_like(dx_ref)
    lax.fori_loop(0, 4, hidden, 0)
    y = y_ref[...]
    dgate = jnp.where(gate >= 0, jnp.sum(dy.astype(F32) * y, axis=1, keepdims=True), 0.0)
    return (y * weight).astype(BF16), dx_ref[...], dgate


def front_kernel(
    imgs, pack_ref, ew_ref, dy_ref, x_ref, noise_ref, keep_ref,
    h_out, dy_out, t_in, g_out, sums_out, w_out, x1_ref, qkv_ref, o_ref, lse_ref, probs_ref,
    w_s, chunk_s, we_s, g_s, xs, dys, y_s, dx_s, t_s, pass_s, g_low,
    p_s, p_r, px_s, px_r, pc_s, pc_r, d_s, d_r, h_s, h_r, e_s, e_r, ex_s, ex_r, ec_s, ec_r, t_ss, t_r, local, stage, g_sem,
):
    peers = Peers()
    member = peers.member
    d_own = pack_ref.shape[0]
    half = E // 2
    peers.meet()

    def rows(of):
        return pl.ds(pl.multiple_of(of * d_own, 16), d_own)

    own_pack = pltpu.make_async_copy(pack_ref, w_s.at[0, rows(member)], local.at[0])
    own_pack.start()

    ring, px, pc = {}, {}, {}

    def pass_pack(number, of, src, way=None, k=None):
        if way is not None:
            ring[way, k] = peers.send(src, w_s.at[0, rows(of)], (p_s, p_r), (way, k), peers.next[way])
        px[number] = peers.send(src, w_s.at[1, rows(of)], (px_s, px_r), number, peers.across)
        pc[0, number] = peers.send(src, w_s.at[2, rows(of)], (pc_s, pc_r), (0, number), peers.core)

    arrivals = [(0, k) if i == 0 else (1, k) for k in range(1, half + 1) for i in range(2 if k < half else 1)]
    owners = [member] + [peers.behind(way, k) for way, k in arrivals]
    ring[0, 0] = peers.send(pack_ref, w_s.at[0, rows(member)], (p_s, p_r), (0, 0), peers.next[0])
    pass_pack(0, member, pack_ref, 1, 0)

    def pass_x(number):
        px[number].wait_recv()
        at = rows(owners[number])
        pc[1, number] = peers.send(w_s.at[1, at], w_s.at[3, at], (pc_s, pc_r), (1, number), peers.core)

    for number, (way, k) in enumerate(arrivals, 1):
        ring[way, k - 1].wait_recv()
        of = owners[number]
        last = half if way == 0 else half - 1
        pass_pack(number, of, w_s.at[0, rows(of)], way if k < last else None, k)
        if number >= 2:
            pass_x(number - 2)

    e_copy = {}
    for by in range(1, E):
        to = peers.ahead(by)
        e_copy[by] = peers.send(ew_ref.at[to], we_s.at[0, member], (e_s, e_r), by, {"dp": peers.base + to})

    def block_at(c, k):
        return peers.behind(c % 2, k) * imgs + c

    def row_copy(out, sems, c, k, src=None):
        at = block_at(c, k)
        return pltpu.make_async_remote_copy(
            src_ref=out.at[at] if src is None else src,
            dst_ref=out.at[at],
            send_sem=sems[0].at[c, k],
            recv_sem=sems[1].at[c, k],
            device_id=peers.next[c % 2],
            device_id_type=pl.DeviceIdType.MESH,
        )

    h_sems, d_sems = (h_s, h_r), (d_s, d_r)
    for c in range(imgs):
        row_copy(dy_out, d_sems, c, 0, dy_ref.at[c]).start()
    for number in range(len(arrivals) - 1, len(arrivals) + 1):
        pass_x(number)

    ex, ec = {}, {}

    def pass_e(by):
        if by:
            e_copy[by].wait_recv()
        of = peers.came(by)
        src = we_s.at[0, of] if by else ew_ref.at[member]
        ex[by] = peers.send(src, we_s.at[1, of], (ex_s, ex_r), by, peers.across)
        ec[0, by] = peers.send(src, we_s.at[2, of], (ec_s, ec_r), (0, by), peers.core)

    def pass_ex(by):
        ex[by].wait_recv()
        of = peers.came(by)
        ec[1, by] = peers.send(we_s.at[1, of], we_s.at[3, of], (ec_s, ec_r), (1, by), peers.core)

    for number in range(E):
        pc[0, number].wait_recv()
        pc[1, number].wait_recv()
    own_pack.wait()
    pass_e(0)
    keepers = [
        pltpu.make_async_copy(w_s, w_out, local.at[1]),
        pltpu.make_async_copy(ew_ref.at[member], we_s.at[0, member], local.at[2]),
    ] + [
        pltpu.make_async_copy(dy_ref.at[c], dy_out.at[member * imgs + c], local.at[3 + c]) for c in range(imgs)
    ]
    for copy in keepers:
        copy.start()

    par = params_of(w_s[0])
    for c in range(imgs):
        attend(
            x_ref[c], par, lambda r: w_s[r], noise_ref[c], keep_ref[c],
            chunk_s.at[c], *(ref.at[c] for ref in (x1_ref, qkv_ref, o_ref, lse_ref, probs_ref)),
        )
        row_copy(h_out, h_sems, c, 0, chunk_s.at[c]).start()
        keepers.append(
            pltpu.make_async_copy(chunk_s.at[c], h_out.at[member * imgs + c], local.at[3 + imgs + c])
        )
        keepers[-1].start()

    far = (1, 7, 2, 6, 3, 5, 4)
    for i, by in enumerate(far):
        pass_e(by)
        if i >= 1:
            pass_ex((0, *far)[i - 1])
    g_s[...] = jnp.zeros_like(g_s)
    for by in (0, *far)[len(far) - 1 :]:
        pass_ex(by)
    for by in range(E):
        ec[0, by].wait_recv()
        ec[1, by].wait_recv()
    for copy in keepers:
        copy.wait()

    row16 = iota((16, D), 0)
    eye = iota((PAD, PAD), 0) == iota((PAD, PAD), 1)

    def sum_copy(flow, c, k):
        return pltpu.make_async_remote_copy(
            src_ref=pass_s.at[lax.rem(k, 2), flow, c],
            dst_ref=t_in.at[k - 1, flow, c],
            send_sem=t_ss.at[flow, c, k - 1],
            recv_sem=t_r.at[flow, c, k - 1],
            device_id=peers.next[c % 2],
            device_id_type=pl.DeviceIdType.MESH,
        )

    own_sums = pltpu.make_async_copy(pass_s.at[0], t_in.at[E - 1], local.at[0])

    def fetch_sums(k):
        copies = []
        for flow in range(2):
            for c in range(imgs):
                sum_copy(flow, c, k - 1).wait_recv()
                copies.append(pltpu.make_async_copy(t_in.at[k - 2, flow, c], t_s.at[flow, c], stage.at[flow, c]))
                copies[-1].start()
        for copy in copies:
            copy.wait()

    def step(k, carry):
        for c in range(imgs):
            for out, sems in ((h_out, h_sems), (dy_out, d_sems)):

                @pl.when(k > 0)
                def _():
                    row_copy(out, sems, c, k - 1).wait_recv()

                @pl.when((k > 0) & (k < E - 1))
                def _():
                    row_copy(out, sems, c, k).start()

        loads = []
        for c in range(imgs):
            for i, (out, held) in enumerate(((h_out, xs), (dy_out, dys))):
                loads.append(pltpu.make_async_copy(out.at[block_at(c, k)], held.at[c], stage.at[i, c]))
                loads[-1].start()
        for copy in loads:
            copy.wait()
        columns = []
        for c in range(imgs):
            meta = xs[c, PAD - 16 :, :].astype(F32)
            line = jnp.sum(jnp.where(row16 == 8 + member, meta, 0.0), axis=0, keepdims=True)[:, :PAD]
            columns.append(jnp.sum(jnp.where(eye, line, 0.0), axis=1, keepdims=True))
        y, dx, dgate = expert_step(
            xs[...].reshape(imgs * PAD, D), dys[...].reshape(imgs * PAD, D), jnp.concatenate(columns, axis=0),
            we_s, g_s, y_s, dx_s,
        )
        slot = lax.rem(k, 2)

        @pl.when(k >= 3)
        def _():
            for flow in range(2):
                for c in range(imgs):
                    sum_copy(flow, c, k - 2).wait_send()

        for c in range(imgs):
            span = slice(c * PAD, (c + 1) * PAD)
            line = jnp.sum(jnp.where(eye, dgate[span], 0.0), axis=0, keepdims=True)
            line = jnp.concatenate([line, jnp.zeros((1, D - PAD), F32)], axis=1)
            tail = dx[span][PAD - 16 :] + jnp.where(row16 == 8 + member, line, 0.0)
            pass_s[slot, 0, c] = jnp.concatenate([dx[span][: PAD - 16], tail], axis=0).astype(BF16)
            pass_s[slot, 1, c] = y[span]

        @pl.when(k == 0)
        def _():
            own_sums.start()
            own_sums.wait()

        @pl.when(k >= 2)
        def _():
            fetch_sums(k)
            pass_s[slot] = (pass_s[slot].astype(F32) + t_s[...].astype(F32)).astype(BF16)

        @pl.when(k >= 1)
        def _():
            for flow in range(2):
                for c in range(imgs):
                    sum_copy(flow, c, k).start()

        return carry

    lax.fori_loop(0, E, step, 0)

    for i in range(8):
        r, kind = i // 2, i % 2
        if i >= 2:
            pltpu.make_async_copy(g_low.at[i % 2], g_out.at[r, :, kind], g_sem.at[i % 2]).wait()
        g_low[i % 2] = g_s[r, kind].astype(BF16).reshape(E, d_own, FFS)
        pltpu.make_async_copy(g_low.at[i % 2], g_out.at[r, :, kind], g_sem.at[i % 2]).start()
    fetch_sums(E)
    for c in range(imgs):
        for flow in range(2):
            sum_copy(flow, c, E - 2).wait_send()
    own_sums = pltpu.make_async_copy(t_in.at[E - 1], pass_s.at[0], local.at[0])
    own_sums.start()
    own_sums.wait()
    sums_out[...] = (pass_s[0].astype(F32) + t_s[...].astype(F32)).astype(BF16)
    for i in range(2):
        pltpu.make_async_copy(g_low.at[i], g_out.at[3, :, i], g_sem.at[i]).wait()
    for c in range(imgs):
        for flow in range(2):
            sum_copy(flow, c, E - 1).wait_send()
        for k in range(E - 1):
            row_copy(h_out, h_sems, c, k).wait_send()
            row_copy(dy_out, d_sems, c, k).wait_send()
    for copy in peers.sends:
        copy.wait_send()


def front(pack, ew, dy, x, noise, keep):
    imgs = x.shape[0]
    d_own = pack.shape[0]
    vm = pl.BlockSpec(memory_space=pltpu.VMEM)
    hbm = pl.BlockSpec(memory_space=pl.ANY)
    table = jax.ShapeDtypeStruct((E * imgs, PAD, D), BF16)
    dma = pltpu.SemaphoreType.DMA
    pair = (2, imgs, PAD, D)
    return pl.pallas_call(
        functools.partial(front_kernel, imgs),
        out_shape=(
            table,
            table,
            jax.ShapeDtypeStruct((E,) + pair, BF16),
            jax.ShapeDtypeStruct((4, E, 2, d_own, FFS), BF16),
            jax.ShapeDtypeStruct(pair, BF16),
            jax.ShapeDtypeStruct((4, E * d_own, D + 128), BF16),
        )
        + attn_shapes(imgs),
        in_specs=[vm, hbm, hbm, vm, vm, vm],
        out_specs=(hbm,) * 4 + (vm, hbm) + (vm,) * 5,
        scratch_shapes=[
            pltpu.VMEM((4, E * d_own, D + 128), BF16),
            pltpu.VMEM((imgs, PAD, D), BF16),
            pltpu.VMEM((4, E, 2, d_own, FFS), BF16),
            pltpu.VMEM((4, 2, D, FFS), F32),
            pltpu.VMEM((imgs, PAD, D), BF16),
            pltpu.VMEM((imgs, PAD, D), BF16),
            pltpu.VMEM((imgs * PAD, D), F32),
            pltpu.VMEM((imgs * PAD, D), F32),
            pltpu.VMEM(pair, BF16),
            pltpu.VMEM((2,) + pair, BF16),
            pltpu.VMEM((2, E, d_own, FFS), BF16),
            dma((2, 4)), dma((2, 4)), dma((E,)), dma((E,)), dma((2, E)), dma((2, E)),
            dma((imgs, E - 1)), dma((imgs, E - 1)), dma((imgs, E - 1)), dma((imgs, E - 1)),
            dma((E,)), dma((E,)), dma((E,)), dma((E,)), dma((2, E)), dma((2, E)),
            dma((2, imgs, E - 1)), dma((2, imgs, E - 1)),
            dma((3 + 2 * imgs,)), dma((2, imgs)), dma((2,)),
        ],
        compiler_params=pltpu.CompilerParams(
            vmem_limit_bytes=VMEM_LIMIT, collective_id=0, has_side_effects=True
        ),
        cost_estimate=pl.CostEstimate(flops=10**11, bytes_accessed=10**8, transcendentals=2 * 10**7),
        name="front",
    )(pack, ew, dy, x, noise, keep)


def expert_kernel(nb, who_ref, *refs):
    h_in, dy_in, w_in = refs[:3]
    outs = refs[3:]
    dx_out, y_out, rows_out, hid_out, tiles_ref = outs[:5]
    (h, dy, y_t, dx_t, w_s, gate_s, slot_s, dgate_s, xs, dys, hid_s, rows_s, lo_s, hi_s, in_sem, out_sem, row_sem, hid_sem, w_sem) = outs[5:]
    me = who_ref[0]
    loads = [
        pltpu.make_async_copy(h_in, h, in_sem.at[0]),
        pltpu.make_async_copy(dy_in, dy, in_sem.at[1]),
    ]
    for b in range(E):
        at = pl.ds(b * (D // E), D // E)
        for r in range(4):
            loads.append(pltpu.make_async_copy(w_in.at[r, b], w_s.at[r, :, at], w_sem.at[r, b]))
    for copy in loads:
        copy.start()
    y_t[...] = jnp.zeros_like(y_t)
    dx_t[...] = jnp.zeros_like(dx_t)
    dgate_s[...] = jnp.zeros_like(dgate_s)
    for copy in loads:
        copy.wait()

    row16 = iota((16, D), 0)
    for b in range(nb):
        meta = h[b, PAD - 16 : PAD, :].astype(F32)
        gate_s[b : b + 1, :] = jnp.sum(jnp.where(row16 == 8 + me, meta, 0.0), axis=0, keepdims=True)[:, :PAD]
    gates = gate_s[...]
    named = (gates >= 0) & (iota((nb, PAD), 1) < SEQ)
    ones = named.astype(F32).astype(BF16)
    upto = dot(ones, (iota((PAD, PAD), 0) <= iota((PAD, PAD), 1)).astype(F32).astype(BF16))
    count = dot(ones, jnp.ones((PAD, PAD), BF16)).astype(BF16)
    before = dot((iota((nb, nb), 0) > iota((nb, nb), 1)).astype(F32).astype(BF16), count)
    slot_s[...] = jnp.where(named, before + upto - 1.0, -1.0).astype(jnp.int32)
    ends = jnp.where(named, before + upto, before)
    for b in range(nb):
        lo_s[b] = jnp.max(before[b : b + 1, :]).astype(jnp.int32)
        hi_s[b] = jnp.max(ends[b : b + 1, :]).astype(jnp.int32)
    tiles = lax.div(hi_s[nb - 1] + TILE - 1, TILE)
    tiles_ref[0] = tiles

    def meets(b, first):
        return (lo_s[b] < first + TILE) & (hi_s[b] > first) & (hi_s[b] > lo_s[b])

    def place(b, first):
        return iota((TILE, PAD), 0) + first == slot_s[pl.ds(b, 1), :]

    def step(t, carry):
        first = t * TILE
        slot = lax.rem(t, 2)
        xs[...] = jnp.zeros_like(xs)
        dys[...] = jnp.zeros_like(dys)

        def collect(b, gcol):
            def one(gcol):
                hit = place(b, first)
                p = hit.astype(F32).astype(BF16)
                xs[...] += dot(p, h[b])
                dys[...] += dot(p, dy[b])
                return gcol + jnp.sum(jnp.where(hit, gate_s[pl.ds(b, 1), :], 0.0), axis=1, keepdims=True)

            return lax.cond(meets(b, first), one, lambda g: g, gcol)

        gcol = lax.fori_loop(0, nb, collect, jnp.zeros((TILE, 1), F32))

        def drain(s):
            pltpu.make_async_copy(rows_s.at[s], rows_out.at[:, pl.ds(0, TILE)], row_sem.at[s]).wait()
            pltpu.make_async_copy(hid_s.at[s], hid_out.at[:, pl.ds(0, TILE)], hid_sem.at[s]).wait()

        @pl.when(t >= 2)
        def _():
            drain(slot)

        x = xs[...].astype(BF16)
        g_rows = (dys[...] * gcol).astype(BF16)
        rows_s[slot, 0] = x
        rows_s[slot, 1] = g_rows
        y = jnp.zeros((TILE, D), F32)
        dx = jnp.zeros((TILE, D), F32)
        for r in range(4):
            w1, w2 = w_s.at[r, 0], w_s.at[r, 1]
            a = dot(x, w1[...])
            a2 = a * a
            th = jnp.tanh(0.7978845608028654 * a * (1.0 + 0.044715 * a2))
            half = 0.5 * (1.0 + th)
            hid = (a * half).astype(BF16)
            slope = half + 0.5 * a * (1.0 - th * th) * (0.7978845608028654 * (1.0 + 3 * 0.044715 * a2))
            da = (dot(g_rows, w2[...]) * slope).astype(BF16)
            y = y + dot_nt(hid, w2[...])
            dx = dx + dot_nt(da, w1[...])
            hid_s[slot, 0, :, r * FFS : (r + 1) * FFS] = da
            hid_s[slot, 1, :, r * FFS : (r + 1) * FFS] = hid
        at = pl.ds(pl.multiple_of(first, TILE), TILE)
        pltpu.make_async_copy(rows_s.at[slot], rows_out.at[:, at], row_sem.at[slot]).start()
        pltpu.make_async_copy(hid_s.at[slot], hid_out.at[:, at], hid_sem.at[slot]).start()
        dgate = jnp.sum(dys[...] * y, axis=1, keepdims=True)
        y_low = (y * gcol).astype(BF16)
        dx_low = dx.astype(BF16)

        def give(b, carry):
            @pl.when(meets(b, first))
            def _():
                hit = place(b, first)
                p = hit.astype(F32).astype(BF16)
                y_t[b] = y_t[b] + dot_tn(p, y_low).astype(BF16)
                dx_t[b] = dx_t[b] + dot_tn(p, dx_low).astype(BF16)
                dgate_s[pl.ds(b, 1), :] += jnp.sum(jnp.where(hit, dgate, 0.0), axis=0, keepdims=True)

            return carry

        lax.fori_loop(0, nb, give, 0)
        return carry

    lax.fori_loop(0, tiles, step, 0)
    for back in (1, 2):

        @pl.when(tiles >= back)
        def _():
            s = lax.rem(tiles - back, 2)
            pltpu.make_async_copy(rows_s.at[s], rows_out.at[:, pl.ds(0, TILE)], row_sem.at[s]).wait()
            pltpu.make_async_copy(hid_s.at[s], hid_out.at[:, pl.ds(0, TILE)], hid_sem.at[s]).wait()

    for b in range(nb):
        tail = dx_t[b, PAD - 16 : PAD, :].astype(F32)
        line = jnp.concatenate([dgate_s[b : b + 1, :], jnp.zeros((1, D - PAD), F32)], axis=1)
        dx_t[b, PAD - 16 : PAD, :] = (tail + jnp.where(row16 == 8 + me, line, 0.0)).astype(BF16)
    stores = [
        pltpu.make_async_copy(dx_t, dx_out, out_sem.at[0]),
        pltpu.make_async_copy(y_t, y_out, out_sem.at[1]),
    ]
    for copy in stores:
        copy.start()
    for copy in stores:
        copy.wait()


def expert_rows(nb):
    return -(-nb * SEQ // TILE) * TILE


def experts(member, h_all, dy_all, weights):
    nb = h_all.shape[0]
    rows = expert_rows(nb)
    hbm = pl.BlockSpec(memory_space=pl.ANY)
    sm = pl.BlockSpec(memory_space=pltpu.SMEM)
    table = jax.ShapeDtypeStruct((nb, PAD, D), BF16)
    return pl.pallas_call(
        functools.partial(expert_kernel, nb),
        out_shape=[
            table,
            table,
            jax.ShapeDtypeStruct((2, rows, D), BF16),
            jax.ShapeDtypeStruct((2, rows, 4 * FFS), BF16),
            jax.ShapeDtypeStruct((1,), jnp.int32),
        ],
        in_specs=[sm, hbm, hbm, hbm],
        out_specs=[hbm] * 4 + [sm],
        scratch_shapes=[
            pltpu.VMEM((nb, PAD, D), BF16),
            pltpu.VMEM((nb, PAD, D), BF16),
            pltpu.VMEM((nb, PAD, D), BF16),
            pltpu.VMEM((nb, PAD, D), BF16),
            pltpu.VMEM((4, 2, D, FFS), BF16),
            pltpu.VMEM((nb, PAD), F32),
            pltpu.VMEM((nb, PAD), jnp.int32),
            pltpu.VMEM((nb, PAD), F32),
            pltpu.VMEM((TILE, D), F32),
            pltpu.VMEM((TILE, D), F32),
            pltpu.VMEM((2, 2, TILE, 4 * FFS), BF16),
            pltpu.VMEM((2, 2, TILE, D), BF16),
            pltpu.SMEM((nb,), jnp.int32),
            pltpu.SMEM((nb,), jnp.int32),
            pltpu.SemaphoreType.DMA((2,)),
            pltpu.SemaphoreType.DMA((2,)),
            pltpu.SemaphoreType.DMA((2,)),
            pltpu.SemaphoreType.DMA((2,)),
            pltpu.SemaphoreType.DMA((4, E)),
        ],
        compiler_params=pltpu.CompilerParams(vmem_limit_bytes=VMEM_LIMIT),
        cost_estimate=pl.CostEstimate(flops=30 * 10**9, bytes_accessed=4 * 10**7, transcendentals=4 * 10**6),
        name="experts",
    )(member.reshape(1), h_all, dy_all, weights)


def expert_grad_kernel(tiles_ref, rows_ref, hid_ref, out_ref, acc):
    acc[...] = jnp.zeros_like(acc)

    def step(t, carry):
        at = pl.ds(pl.multiple_of(t * TILE, TILE), TILE)
        acc[...] += dot_tn(rows_ref[0, at, :], hid_ref[0, at, :])
        return carry

    lax.fori_loop(0, tiles_ref[0], step, 0)
    out_ref[0] = acc[...].astype(BF16)


def expert_grads(tiles, rows, hid, kind, base):
    n = rows.shape[1]
    return pl.pallas_call(
        expert_grad_kernel,
        grid_spec=pltpu.PrefetchScalarGridSpec(
            num_scalar_prefetch=1,
            grid=(2,),
            in_specs=[
                pl.BlockSpec((1, n, D), lambda s, _: (kind, 0, 0)),
                pl.BlockSpec((1, n, FFS), lambda s, _: (kind, 0, base + s)),
            ],
            out_specs=pl.BlockSpec((1, D, FFS), lambda s, _: (s, 0, 0)),
            scratch_shapes=[pltpu.VMEM((D, FFS), F32)],
        ),
        out_shape=jax.ShapeDtypeStruct((2, D, FFS), BF16),
        compiler_params=pltpu.CompilerParams(vmem_limit_bytes=VMEM_LIMIT),
        cost_estimate=pl.CostEstimate(flops=4 * 10**9, bytes_accessed=15 * 10**6, transcendentals=0),
        name="expert_grads",
    )(tiles, rows, hid)


def unpack_kernel(who_ref, *refs):
    blocks, (in_ref, out_ref) = refs[:E], refs[E:]
    for by in range(E):
        in_ref[who_ref[by]] = blocks[by][0].astype(F32)
        out_ref[who_ref[by]] = blocks[by][1].astype(F32)


def unpack(who, blocks):
    vm = pl.BlockSpec(memory_space=pltpu.VMEM)
    whole = jax.ShapeDtypeStruct((E,) + blocks[0].shape[1:], F32)
    return pl.pallas_call(
        unpack_kernel,
        out_shape=(whole, whole),
        in_specs=[pl.BlockSpec(memory_space=pltpu.SMEM)] + [vm] * E,
        out_specs=(vm, vm),
        compiler_params=pltpu.CompilerParams(vmem_limit_bytes=VMEM_LIMIT),
        cost_estimate=pl.CostEstimate(flops=10**6, bytes_accessed=7 * 10**6, transcendentals=0),
        name="unpack",
    )(who, *blocks)


def lay_out_kernel(imgs, at_ref, *refs):
    parts, out_ref, held, sem = refs[:4], refs[4], refs[5], refs[6]
    copies = [pltpu.make_async_copy(parts[s], held.at[s], sem.at[s]) for s in range(4)]
    for copy in copies:
        copy.start()
    for copy in copies:
        copy.wait()
    for i in range(4 * imgs):
        out_ref[i * SEQ : (i + 1) * SEQ, :] = held[at_ref[i // imgs], i % imgs, :SEQ, :]


def lay_out(at, parts):
    imgs = parts[0].shape[0]
    hbm = pl.BlockSpec(memory_space=pl.ANY)
    return pl.pallas_call(
        functools.partial(lay_out_kernel, imgs),
        out_shape=jax.ShapeDtypeStruct((4 * imgs * SEQ, D), BF16),
        in_specs=[pl.BlockSpec(memory_space=pltpu.SMEM)] + [hbm] * 4,
        out_specs=pl.BlockSpec(memory_space=pltpu.VMEM),
        scratch_shapes=[pltpu.VMEM((4, imgs, PAD, D), BF16), pltpu.SemaphoreType.DMA((4,))],
        compiler_params=pltpu.CompilerParams(vmem_limit_bytes=VMEM_LIMIT),
        cost_estimate=pl.CostEstimate(flops=10**6, bytes_accessed=5 * 10**6, transcendentals=0),
        name="lay_out",
    )(at, *parts)


class Backward:
    def __init__(self, imgs, dh_of, saved, w_ref, dx1_s, low_s, h1_s, dh1_s, dqkv_s, o_s):
        self.imgs, self.dh_of, self.saved, self.w_ref = imgs, dh_of, saved, w_ref
        self.dx1_s, self.low_s, self.h1_s, self.dh1_s, self.dqkv_s, self.o_s = dx1_s, low_s, h1_s, dh1_s, dqkv_s, o_s
        self.par = params_of(w_ref[0])
        self.row_ok = iota((PAD, 1), 0) < SEQ
        self.started = False

    def span(self, c):
        return slice(c * PAD, (c + 1) * PAD)

    def first(self):
        x1_in, x_in, dy_in, probs_in = self.saved[:4]
        par, row_ok = self.par, self.row_ok
        lane_ok = iota((E, PAD), 1) < SEQ
        router = par[8:16].astype(BF16)
        gain = jnp.zeros((1, D), F32)
        bias = jnp.zeros((1, D), F32)
        g_router = jnp.zeros((E, D), F32)
        for c in range(self.imgs):
            arrived = self.dh_of(c).astype(F32)
            dgate = arrived[PAD - 8 :, :PAD]
            probs = probs_in[c]
            dlogits = probs * (dgate - jnp.sum(probs * dgate, axis=0, keepdims=True))
            dlogits = jnp.where(lane_ok, dlogits, 0.0).astype(BF16)
            unit, scale = normalise(x1_in[c])
            h2 = (unit * par[2:3] + par[3:4]).astype(BF16)
            g_router = g_router + dot(dlogits, h2)
            dh2 = jnp.where(row_ok, arrived + dot_tn(dlogits, router), 0.0)
            gain = gain + jnp.sum(dh2 * unit, axis=0, keepdims=True)
            bias = bias + jnp.sum(dh2, axis=0, keepdims=True)
            dx1 = dy_in[c].astype(F32) + norm_back(dh2, unit, scale, par[2:3])
            self.dx1_s[self.span(c), :] = dx1
            self.low_s[self.span(c), :] = dx1.astype(BF16)
            unit1, _ = normalise(x_in[c].astype(F32))
            self.h1_s[self.span(c), :] = (unit1 * par[0:1] + par[1:2]).astype(BF16)
        self.small2 = [gain, bias, jnp.zeros((4, D), F32), g_router]

    def heads(self, r):
        qkv_in, o_in, lse_in = self.saved[4:]
        key_ok = iota((PAD, PAD), 1) < SEQ
        low, h1, w = self.low_s[...], self.h1_s[...], self.w_ref[r]
        dout = dot(low, w[:, 9 * HD : D]).astype(BF16)
        for c in range(self.imgs):
            qkv = qkv_in[c, r]
            lse = lse_in[c]
            self.o_s[self.span(c), :] = o_in[c, r]
            dqs, dks, dvs = [], [], []
            for h in range(3):
                q = qkv[:, h * HD : (h + 1) * HD]
                k = qkv[:, (3 + h) * HD : (4 + h) * HD]
                v = qkv[:, (6 + h) * HD : (7 + h) * HD]
                do = dout[self.span(c), h * HD : (h + 1) * HD]
                s = dot_nt(q, k) * HD ** (-0.5)
                p = jnp.where(key_ok, jnp.exp(s - lse[:, 3 * r + h : 3 * r + h + 1]), 0.0)
                dvs.append(dot_tn(p.astype(BF16), do).astype(BF16))
                dp = dot_nt(do, v)
                ds = (p * (dp - jnp.sum(p * dp, axis=-1, keepdims=True))).astype(BF16)
                dqs.append((dot(ds, k) * HD ** (-0.5)).astype(BF16))
                dks.append((dot_tn(ds, q) * HD ** (-0.5)).astype(BF16))
            self.dqkv_s[self.span(c), :] = jnp.concatenate(dqs + dks + dvs, axis=1)
        dqkv = self.dqkv_s[...]
        part = dot_nt(dqkv, w[:, : 9 * HD])
        self.dh1_s[...] = self.dh1_s[...] + part if self.started else part
        self.started = True
        return jnp.concatenate([dot_tn(h1, dqkv), dot_tn(low, self.o_s[...])], axis=1).astype(BF16)

    def last(self, dtok_ref):
        x_in = self.saved[1]
        gain = jnp.zeros((1, D), F32)
        bias = jnp.zeros((1, D), F32)
        for c in range(self.imgs):
            dh1 = jnp.where(self.row_ok, self.dh1_s[self.span(c), :], 0.0)
            unit, scale = normalise(x_in[c].astype(F32))
            gain = gain + jnp.sum(dh1 * unit, axis=0, keepdims=True)
            bias = bias + jnp.sum(dh1, axis=0, keepdims=True)
            dtok_ref[c] = (self.dx1_s[self.span(c), :] + norm_back(dh1, unit, scale, self.par[0:1])).astype(BF16)
        return jnp.concatenate([gain, bias] + self.small2, axis=0)


def small_block(small, i, d_own):
    line = jnp.concatenate([small[:, i * d_own : (i + 1) * d_own], jnp.zeros((16, D - d_own), F32)], axis=1)
    return line.astype(BF16)


def backward_scratch(imgs):
    rows = imgs * PAD
    return [
        pltpu.VMEM((rows, D), F32),
        pltpu.VMEM((rows, D), BF16),
        pltpu.VMEM((rows, D), BF16),
        pltpu.VMEM((rows, D), F32),
        pltpu.VMEM((rows, 9 * HD), BF16),
        pltpu.VMEM((rows, 3 * HD), BF16),
    ]


def attn_backward_kernel(imgs, *refs):
    dh_in, saved, w_ref = refs[:imgs], refs[imgs : imgs + 7], refs[imgs + 7]
    packs, dtok_ref = refs[imgs + 8 : imgs + 11], refs[imgs + 11]
    n_dp, d_own = packs[0].shape[0], packs[0].shape[1] - 16
    back = Backward(imgs, lambda c: dh_in[c][...], saved, w_ref, *refs[imgs + 12 :])

    def pack_of(r):
        return packs[r] if r < 2 else packs[2].at[:, r - 2]

    back.first()
    for r in range(4):
        grad = back.heads(r)
        for i in range(n_dp):
            pack_of(r)[i, :d_own, :] = grad[i * d_own : (i + 1) * d_own]
    small = back.last(dtok_ref)
    for i in range(n_dp):
        for r in range(4):
            pack_of(r)[i, d_own:, :] = small_block(small, i, d_own)


def attn_backward(dh, saved, w, n_dp):
    imgs = len(dh)
    pack = (n_dp, D // n_dp + 16, D)
    vm = pl.BlockSpec(memory_space=pltpu.VMEM)
    return pl.pallas_call(
        functools.partial(attn_backward_kernel, imgs),
        out_shape=(
            jax.ShapeDtypeStruct(pack, BF16),
            jax.ShapeDtypeStruct(pack, BF16),
            jax.ShapeDtypeStruct((n_dp, 2) + pack[1:], BF16),
            jax.ShapeDtypeStruct((imgs, PAD, D), BF16),
        ),
        in_specs=[vm] * (imgs + 8),
        out_specs=(vm,) * 4,
        scratch_shapes=backward_scratch(imgs),
        compiler_params=pltpu.CompilerParams(vmem_limit_bytes=VMEM_LIMIT),
        cost_estimate=pl.CostEstimate(flops=12 * 10**9, bytes_accessed=2 * 10**7, transcendentals=2 * 10**6),
        name="attn_backward",
    )(*dh, *saved, w)


def back_kernel(
    imgs, g_low, sums_ref, x1_ref, x_ref, dy_ref, probs_ref, qkv_ref, o_ref, lse_ref, w_ref,
    g_out, out_all, dtok_all, total_ref,
    ga_s, gc_s, gx_s, pk_s, pkc_s, pkr_s, sm_s, smr_s, cs_s, cr_s, fs_s, fr_s, or_s, dt_s,
    dx1_s, low_s, h1_s, dh1_s, dqkv_s, o_s,
    gc_ss, gc_r, gx_ss, gx_r, ga_ss, ga_r, pk_ss, pk_r, sm_ss, sm_r, c_ss, c_r, f_ss, f_r, row_ss, row_r, local,
):
    peers = Peers()
    member = peers.member
    tensor = lax.axis_index("tensor")
    d_own = g_low.shape[3]
    peers.meet()
    loads = []

    def here(src, dst):
        copy = pltpu.make_async_copy(src, dst, local.at[len(loads)])
        copy.start()
        loads.append(copy)
        return copy

    def give_rows(kind, src, whole):
        here(src, whole.at[tensor])
        across = peers.send(src, whole.at[tensor], (row_ss, row_r), (kind, 0), peers.across)
        core = peers.send(src, whole.at[tensor], (row_ss, row_r), (kind, 1), peers.core)

        def onwards():
            across.wait_recv()
            other = lax.rem(tensor + 2, 4)
            copy = peers.send(whole.at[other], whole.at[other], (row_ss, row_r), (kind, 2), peers.core)
            return core, copy

        return onwards

    for c in range(imgs):
        or_s[c] = (x1_ref[c] + sums_ref[1, c].astype(F32)).astype(BF16)
    out_rows = give_rows(0, or_s, out_all)

    g_core = [
        peers.send(g_low.at[2 + s], gc_s.at[s], (gc_ss, gc_r), s, peers.core) for s in (1, 0)
    ][::-1]
    g_load = [here(g_low.at[s], ga_s.at[s]) for s in (1, 0)][::-1]
    order = (4, 3, 5, 2, 6, 1, 7, 0)
    gx = {}

    def pass_across():
        g_core[1].wait_recv()
        g_load[1].wait()
        for by in order:
            to = peers.ahead(by)
            ga_s[1, to] = (ga_s[1, to].astype(F32) + gc_s[1, to].astype(F32)).astype(BF16)
            gx[by] = peers.send(ga_s.at[1, to], gx_s.at[to], (gx_ss, gx_r), by, peers.across)
        g_core[0].wait_recv()
        g_load[0].wait()

    ga = {}

    def pass_home(by):
        gx[by].wait_recv()
        to = peers.ahead(by)
        part = ga_s[0, to].astype(F32) + gc_s[0, to].astype(F32)
        ga_s[0, to] = (part + gx_s[to].astype(F32)).astype(BF16)
        if by:
            device = {"dp": peers.base + to}
            ga[by] = peers.send(ga_s.at[0, to], g_out.at[member], (ga_ss, ga_r), by, device)
        else:
            here(ga_s.at[0, to], g_out.at[member])

    saved = (x1_ref, x_ref, dy_ref, probs_ref, qkv_ref, o_ref, lse_ref)
    back = Backward(imgs, lambda c: sums_ref[0, c], saved, w_ref, dx1_s, low_s, h1_s, dh1_s, dqkv_s, o_s)
    back.first()
    for r in (2, 3):
        grad = back.heads(r)
        for i in range(E):
            pkc_s[i, r - 2] = grad[i * d_own : (i + 1) * d_own]
        if r == 2:
            pass_across()
    pk_core = peers.send(pkc_s, pkr_s, (pk_ss, pk_r), 0, peers.core)
    out_rows = out_rows()
    for r in (0, 1):
        grad = back.heads(r)
        for i in range(E):
            pk_s[i, r, :d_own] = grad[i * d_own : (i + 1) * d_own]
        pass_home(order[r])
    small = back.last(dt_s)
    dtok_rows = give_rows(1, dt_s, dtok_all)
    for i in range(E):
        sm_s[i] = small_block(small, i, d_own)
    sm_core = peers.send(sm_s, smr_s, (sm_ss, sm_r), 0, peers.core)
    pk_core.wait_recv()
    sm_core.wait_recv()

    def term(of):
        weights = pk_s[of, :, :d_own].astype(F32) + pkr_s[of].astype(F32)
        both = sm_s[of].astype(F32) + smr_s[of].astype(F32)
        return jnp.concatenate([weights, jnp.broadcast_to(both[None], (2,) + both.shape)], axis=1)

    steps = (E // 2, E // 2 - 1)
    hops = {}

    def hop(way, i):
        value = term(peers.behind(1 - way, steps[way] - i))
        if i:
            hops[way, i - 1].wait_recv()
            value = value + cr_s[way, i - 1].astype(F32)
        cs_s[way, i] = value.astype(BF16)
        hops[way, i] = peers.send(cs_s.at[way, i], cr_s.at[way, i], (c_ss, c_r), (way, i), peers.next[way])

    for i in range(E // 2):
        hop(0, i)
        if i < steps[1]:
            hop(1, i)
        pass_home(order[2 + i])
    hops[1, steps[1] - 1].wait_recv()
    hops[0, steps[0] - 1].wait_recv()
    total = term(member) + cr_s[0, steps[0] - 1].astype(F32) + cr_s[1, steps[1] - 1].astype(F32)
    fs_s[...] = total[1].astype(BF16)
    final = peers.send(fs_s, fr_s, (f_ss, f_r), 0, peers.across)
    pass_home(order[6])
    pass_home(order[7])
    dtok_rows = dtok_rows()
    final.wait_recv()
    total_ref[...] = total[0] + fr_s[...].astype(F32)
    for by in range(1, E):
        ga[by].wait_recv()
    for copy in (*out_rows, *dtok_rows):
        copy.wait_recv()
    for copy in loads:
        if all(copy is not other for other in g_load):
            copy.wait()
    for copy in peers.sends:
        copy.wait_send()


def back(g_low, sums, saved, w):
    imgs = sums.shape[1]
    d_own = g_low.shape[3]
    vm = pl.BlockSpec(memory_space=pltpu.VMEM)
    hbm = pl.BlockSpec(memory_space=pl.ANY)
    dma = pltpu.SemaphoreType.DMA
    part = (E, 2, d_own, D)
    rows = (imgs, PAD, D)
    hop = (2, E // 2, 2, d_own + 16, D)
    return pl.pallas_call(
        functools.partial(back_kernel, imgs),
        out_shape=(
            jax.ShapeDtypeStruct(part, BF16),
            jax.ShapeDtypeStruct((4,) + rows, BF16),
            jax.ShapeDtypeStruct((4,) + rows, BF16),
            jax.ShapeDtypeStruct((d_own + 16, D), F32),
        ),
        in_specs=[hbm] + [vm] * 9,
        out_specs=(hbm, hbm, hbm, vm),
        scratch_shapes=[
            pltpu.VMEM((2,) + part, BF16),
            pltpu.VMEM((2,) + part, BF16),
            pltpu.VMEM(part, BF16),
            pltpu.VMEM((E, 2, d_own + 16, D), BF16),
            pltpu.VMEM(part, BF16),
            pltpu.VMEM(part, BF16),
            pltpu.VMEM((E, 16, D), BF16),
            pltpu.VMEM((E, 16, D), BF16),
            pltpu.VMEM(hop, BF16),
            pltpu.VMEM(hop, BF16),
            pltpu.VMEM((d_own + 16, D), BF16),
            pltpu.VMEM((d_own + 16, D), BF16),
            pltpu.VMEM(rows, BF16),
            pltpu.VMEM(rows, BF16),
            *backward_scratch(imgs),
            dma((2,)), dma((2,)), dma((E,)), dma((E,)), dma((E,)), dma((E,)), dma((1,)), dma((1,)),
            dma((1,)), dma((1,)), dma((2, E // 2)), dma((2, E // 2)), dma((1,)), dma((1,)), dma((2, 3)), dma((2, 3)),
            dma((5,)),
        ],
        compiler_params=pltpu.CompilerParams(
            vmem_limit_bytes=VMEM_LIMIT, collective_id=1, has_side_effects=True
        ),
        cost_estimate=pl.CostEstimate(flops=12 * 10**9, bytes_accessed=10**8, transcendentals=2 * 10**6),
        name="back",
    )(g_low, sums, *saved, w)


RING = (0, 2, 4, 6, 7, 5, 3, 1)


class Mover:
    def __init__(self, n_dp):
        self.n_dp = n_dp
        self.groups = n_dp // E
        self.me = lax.axis_index("dp")
        self.member = lax.rem(self.me, E)
        self.group = lax.div(self.me, E)
        self.tensor = lax.axis_index("tensor")
        self.place = ring_place(self.member)
        bases = range(0, n_dp, E)
        self.ring = (
            [(b + RING[i], b + RING[(i + 1) % E]) for b in bases for i in range(E)],
            [(b + RING[(i + 1) % E], b + RING[i]) for b in bases for i in range(E)],
        )

    def along(self, value, way):
        return lax.ppermute(value, "dp", self.ring[way])

    def shift(self, value, by):
        perm = [(b + i, b + (i + by) % E) for b in range(0, self.n_dp, E) for i in range(E)]
        return lax.ppermute(value, "dp", perm)

    def shift_group(self, value, by):
        return lax.ppermute(value, "dp", [(k, (k + by * E) % self.n_dp) for k in range(self.n_dp)])

    def other(self, value, mask):
        return lax.ppermute(value, "tensor", [(k, k ^ mask) for k in range(4)])

    def behind(self, way, k):
        step = -k if way == 0 else k
        return ring_member(lax.rem(self.place + step + E, E))

    def group_lists(self):
        if self.groups == 1:
            return None
        return [[b + i for i in range(E)] for b in range(0, self.n_dp, E)]

    def gather(self, value):
        return lax.all_gather(value, "dp", axis=0, tiled=False, axis_index_groups=self.group_lists())

    def scatter_sum(self, value):
        return lax.psum_scatter(
            value, "dp", scatter_dimension=0, tiled=False, axis_index_groups=self.group_lists()
        )

    def front(self, pack, ew, dy, x, noise, keep):
        own = lax.all_gather(pack, "dp", axis=0, tiled=True)
        two = jnp.stack([own, self.other(own, 2)])
        w = jnp.concatenate([two, self.other(two, 1)], axis=0)
        blocks = jnp.zeros((2, E * pack.shape[0], FFS), BF16)
        for by in range(E):
            to = lax.rem(self.member + by, E)
            block = lax.dynamic_index_in_dim(ew, to, 0, False)
            came = lax.rem(self.member - by + E, E)
            block = self.shift(block, by) if by else block
            blocks = lax.dynamic_update_slice_in_dim(blocks, block, came * pack.shape[0], 1)
        blocks = self.all_groups(blocks, 1)
        blocks = jnp.swapaxes(blocks.reshape(2, E, D // E, FFS), 0, 1)
        two = jnp.stack([blocks, self.other(blocks, 2)])
        weights = jnp.concatenate([two, self.other(two, 1)], axis=0)
        chunk, *saved = attn_forward(x, w, noise, keep)
        table = (E * x.shape[0], PAD, D)
        dh, y, rows, hid, tiles = experts(
            self.member, self.gather(chunk).reshape(table), self.gather(dy).reshape(table), weights
        )
        sums = [self.scatter_sum(t.reshape((E,) + chunk.shape)) for t in (dh, y)]
        g = [jnp.concatenate([expert_grads(tiles, rows, hid, kind, base) for base in (0, 2)]) for kind in (0, 1)]
        g = jnp.stack([part.reshape(4, E, D // E, FFS) for part in g], axis=2)
        return g, jnp.stack(sums), w, *saved

    def back(self, g_low, sums, saved, x, dy, w):
        x1, qkv, o, lse, probs = saved
        dh_sum, y_sum = sums[0], sums[1]
        imgs, d_own = x.shape[0], D // self.n_dp
        passed = self.other(g_low[2:], 1)
        pair = [(g_low[s].astype(F32) + passed[s].astype(F32)).astype(BF16) for s in range(2)]
        total = (pair[0].astype(F32) + self.other(pair[1], 2).astype(F32)).astype(BF16)
        if self.groups > 1:
            total = jnp.swapaxes(total, 1, 2).reshape(D, 2, FFS)
            total = jnp.swapaxes(self.sum_groups(total, 0).reshape(E, d_own, 2, FFS), 1, 2)
        g_exp = []
        for by in range(E):
            to = lax.rem(self.member + by, E)
            block = lax.dynamic_index_in_dim(total, to, 0, False)
            g_exp.append(self.shift(block, by) if by else block)

        pack0, pack1, packs, d_tok = attn_backward(
            [dh_sum[c] for c in range(imgs)], (x1, x, dy, probs, qkv, o, lse), w, self.n_dp
        )
        passed = self.other(packs, 1)
        if self.groups > 1:
            pack0 = self.sum_groups((pack0.astype(F32) + passed[:, 0].astype(F32)).astype(BF16), 0)
            pack1 = self.sum_groups((pack1.astype(F32) + passed[:, 1].astype(F32)).astype(BF16), 0)
            passed = jnp.zeros((E, 2) + pack0.shape[1:], BF16)

        def pack_for(member):
            one, two = (lax.dynamic_index_in_dim(p, member, 0, False).astype(F32) for p in (pack0, pack1))
            came = lax.dynamic_index_in_dim(passed, member, 0, False).astype(F32)
            return one + came[0] + self.other((two + came[1]).astype(BF16), 2).astype(F32)

        total = self.sum_both_ways(pack_for)
        at = jnp.stack([_slot(self.tensor, t) for t in range(4)])

        def all_rows(own):
            across = self.other(own, 2)
            return lay_out(at, [own, across, self.other(own, 1), self.other(across, 1)])

        d_tokens = all_rows(d_tok)
        output = all_rows((x1 + y_sum.astype(F32)).astype(BF16))
        came = jnp.stack([lax.rem(self.member - by + E, E) for by in range(E)])
        return output, d_tokens, *unpack(came, g_exp), total

    def sum_both_ways(self, block_for):
        def chain(way, steps):
            total = block_for(self.behind(1 - way, steps)).astype(BF16)
            for k in range(steps - 1, -1, -1):
                total = self.along(total, way)
                if k:
                    total = (total.astype(F32) + block_for(self.behind(1 - way, k)).astype(F32)).astype(BF16)
            return total

        ahead = chain(0, E // 2)
        back = chain(1, E // 2 - 1)
        return ahead.astype(F32) + back.astype(F32) + block_for(self.member).astype(F32)

    def all_groups(self, part, dim):
        if self.groups == 1:
            return part
        size = part.shape[dim]
        shape = part.shape[:dim] + (size * self.groups,) + part.shape[dim + 1 :]
        whole = lax.dynamic_update_slice_in_dim(jnp.zeros(shape, part.dtype), part, self.group * size, dim)
        for by in range(1, self.groups):
            came = lax.rem(self.group - by + self.groups, self.groups)
            whole = lax.dynamic_update_slice_in_dim(whole, self.shift_group(part, by), came * size, dim)
        return whole

    def sum_groups(self, whole, dim):
        if self.groups == 1:
            return whole
        size = whole.shape[dim] // self.groups
        total = lax.dynamic_slice_in_dim(whole, self.group * size, size, dim).astype(F32)
        for by in range(1, self.groups):
            to = lax.rem(self.group + by, self.groups)
            part = lax.dynamic_slice_in_dim(whole, to * size, size, dim)
            total = total + self.shift_group(part, by).astype(F32)
        return total.astype(whole.dtype)


def after(value, *first):
    return lax.optimization_barrier((value, first))[0]


def _slot(tensor, t):
    apart = lax.bitwise_xor(tensor, t)
    return lax.div(apart, 2) + 2 * lax.rem(apart, 2)


def image_blocks(rows, tensor, imgs):
    first = tensor * (imgs * SEQ)
    return [
        jnp.pad(lax.dynamic_slice_in_dim(rows, first + c * SEQ, SEQ, 0), ((0, PAD - SEQ), (0, 0)))
        for c in range(imgs)
    ]


def image_lanes(lanes, tensor, imgs):
    first = tensor * (imgs * SEQ)
    return [
        jnp.pad(lax.dynamic_slice_in_dim(lanes, first + c * SEQ, SEQ, 1), ((0, 0), (0, PAD - SEQ)))
        for c in range(imgs)
    ]


def kept_pairs(routes):
    chosen = jnp.transpose(routes).reshape(1, -1)
    named = (chosen == jnp.arange(E, dtype=jnp.int32)[:, None]).astype(jnp.int32)
    kept = named * (jnp.cumsum(named, axis=1) <= CAP)
    return jnp.sum(kept.reshape(E, TOP, -1), axis=1).astype(F32)


def body(
    n_dp,
    tokens,
    ln1_gain,
    ln1_bias,
    w_qkv,
    w_attn_out,
    ln2_gain,
    ln2_bias,
    router_weight,
    w_in,
    w_expert_out,
    router_noise,
    routes,
    cotangent,
):
    move = Mover(n_dp)
    token_count = tokens.shape[0]
    imgs = token_count // SEQ // 4
    d_own = w_qkv.shape[0]
    ways = [c % 2 for c in range(imgs)]

    vectors = jnp.stack([ln1_gain, ln1_bias, ln2_gain, ln2_bias] + [jnp.zeros_like(ln1_gain)] * 4, axis=1)
    pack = jnp.concatenate(
        [w_qkv[:, 0], w_qkv[:, 1], w_qkv[:, 2], jnp.transpose(w_attn_out), vectors, router_weight], axis=1
    )
    pack = jnp.pad(pack, ((0, 0), (0, 128 - 16))).astype(BF16)
    ew = jnp.stack([w_in, jnp.transpose(w_expert_out, (0, 2, 1))], axis=1).astype(BF16)
    x = jnp.stack(image_blocks(tokens, move.tensor, imgs))
    dy = jnp.stack(image_blocks(cotangent, move.tensor, imgs))
    keep = jnp.stack(image_lanes(kept_pairs(routes), move.tensor, imgs))
    noise = jnp.stack(image_lanes(jnp.transpose(router_noise), move.tensor, imgs))
    if move.groups == 1:
        _, _, _, g_low, sums, w, *saved = front(pack, ew, dy, x, noise, keep)
        x1, qkv, o, lse, probs = saved
        g_exp, output, d_tokens, total = back(g_low, sums, (x1, x, dy, probs, qkv, o, lse), w)
        g_in, g_out = g_exp[:, 0].astype(F32), g_exp[:, 1].astype(F32)
        output, d_tokens = (rows[:, :, :SEQ].reshape(token_count, D) for rows in (output, d_tokens))
    else:
        g_low, sums, w, *saved = move.front(pack, ew, dy, x, noise, keep)
        output, d_tokens, g_in, g_out, total = move.back(g_low, sums, saved, x, dy, w)
    g_qkv = total[:d_own, : 9 * HD].reshape(d_own, 3, 3 * HD)
    g_attn_out = jnp.transpose(total[:d_own, 9 * HD :])
    g_small = total[d_own:, :d_own]

    return (
        output,
        d_tokens,
        g_small[0],
        g_small[1],
        g_qkv,
        g_attn_out,
        g_small[2],
        g_small[3],
        jnp.transpose(g_small[8:16]),
        g_in,
        jnp.transpose(g_out, (0, 2, 1)),
    )


def solution(mesh):
    in_specs = (
        P("dp", None),
        P("dp"),
        P("dp"),
        P("dp", None, "tensor"),
        P("tensor", "dp"),
        P("dp"),
        P("dp"),
        P("dp", None),
        P(None, "dp", "tensor"),
        P(None, "tensor", "dp"),
        P("dp", None),
        P("dp", None),
        P("dp", None),
    )
    out_specs = (
        P("dp", None),
        P("dp", None),
        P("dp"),
        P("dp"),
        P("dp", None, "tensor"),
        P("tensor", "dp"),
        P("dp"),
        P("dp"),
        P("dp", None),
        P(None, "dp", "tensor"),
        P(None, "tensor", "dp"),
    )
    return jax.shard_map(
        functools.partial(body, mesh.shape["dp"]),
        mesh=mesh,
        in_specs=in_specs,
        out_specs=out_specs,
        check_vma=False,
    )
```

```python
import functools

import jax
import jax.numpy as jnp
from jax import lax
from jax.experimental import pallas as pl
from jax.experimental.pallas import tpu as pltpu
from jax.sharding import PartitionSpec as P

D = 768
HD = 64
E = 8
TOP = 2
SEQ = 197
CAP = 689
PAD = 208
META = 200
TILE = 256
FFS = 768
EPS = 1e-06
VMEM_LIMIT = 62 * 1024 * 1024

F32 = jnp.float32
BF16 = jnp.bfloat16


def dot(a, b):
    return jnp.dot(a, b, preferred_element_type=F32)


def dot_nt(a, b):
    return lax.dot_general(a, b, (((1,), (1,)), ((), ())), preferred_element_type=F32)


def dot_tn(a, b):
    return lax.dot_general(a, b, (((0,), (0,)), ((), ())), preferred_element_type=F32)


def iota(shape, dim):
    return lax.broadcasted_iota(jnp.int32, shape, dim)


def normalise(values):
    centred = values - jnp.mean(values, axis=-1, keepdims=True)
    scale = lax.rsqrt(jnp.mean(centred * centred, axis=-1, keepdims=True) + EPS)
    return centred * scale, scale


def norm_back(grad, unit, scale, gain):
    g = grad * gain
    return scale * (
        g - jnp.mean(g, axis=-1, keepdims=True) - unit * jnp.mean(g * unit, axis=-1, keepdims=True)
    )


def params_of(w_own):
    return jnp.transpose(w_own[:, D:].astype(F32))[:16]


def attend(x, par, w_of, noise, keep, chunk_ref, x1_ref, qkv_ref, o_ref, lse_ref, probs_ref):
    x = x.astype(F32)
    unit, _ = normalise(x)
    h1 = (unit * par[0:1] + par[1:2]).astype(BF16)
    acc = x
    lse = jnp.zeros((PAD, 128), F32)
    key_ok = iota((PAD, PAD), 1) < SEQ
    lane = iota((PAD, 128), 1)
    for r in range(4):
        w = w_of(r)
        qkv = dot(h1, w[:, : 9 * HD]).astype(BF16)
        qkv_ref[r] = qkv
        outs = []
        for h in range(3):
            q = qkv[:, h * HD : (h + 1) * HD]
            k = qkv[:, (3 + h) * HD : (4 + h) * HD]
            v = qkv[:, (6 + h) * HD : (7 + h) * HD]
            s = jnp.where(key_ok, dot_nt(q, k) * HD ** (-0.5), -1e30)
            top = jnp.max(s, axis=-1, keepdims=True)
            p = jnp.exp(s - top)
            total = jnp.sum(p, axis=-1, keepdims=True)
            outs.append(dot((p * (1.0 / total)).astype(BF16), v).astype(BF16))
            lse = jnp.where(lane == 3 * r + h, top + jnp.log(total), lse)
        o = jnp.concatenate(outs, axis=1)
        o_ref[r] = o
        acc = acc + dot_nt(o, w[:, 9 * HD : D])
    lse_ref[...] = lse
    x1_ref[...] = acc
    unit2, _ = normalise(acc)
    h2 = (unit2 * par[2:3] + par[3:4]).astype(BF16)
    logits = dot_nt(par[8:16].astype(BF16), h2) + noise
    e = jnp.exp(logits - jnp.max(logits, axis=0, keepdims=True))
    probs = e / jnp.sum(e, axis=0, keepdims=True)
    probs_ref[...] = probs
    gates = jnp.where(keep > 0, probs, -1.0)
    chunk_ref[...] = h2
    tail = jnp.concatenate([gates, jnp.zeros((8, D - PAD), F32)], axis=1)
    low = h2[PAD - 16 :, :].astype(F32)
    chunk_ref[PAD - 16 :, :] = jnp.concatenate([low[:8], tail], axis=0).astype(BF16)


def attn_shapes(imgs):
    return (
        jax.ShapeDtypeStruct((imgs, PAD, D), F32),
        jax.ShapeDtypeStruct((imgs, 4, PAD, 9 * HD), BF16),
        jax.ShapeDtypeStruct((imgs, 4, PAD, 3 * HD), BF16),
        jax.ShapeDtypeStruct((imgs, PAD, 128), F32),
        jax.ShapeDtypeStruct((imgs, E, PAD), F32),
    )


def attn_forward_kernel(imgs, x_ref, w_ref, noise_ref, keep_ref, chunk_ref, *saved):
    par = params_of(w_ref[0])
    for c in range(imgs):
        attend(
            x_ref[c], par, lambda r: w_ref[r], noise_ref[c], keep_ref[c],
            chunk_ref.at[c], *(ref.at[c] for ref in saved),
        )


def attn_forward(x, w, noise, keep):
    imgs = x.shape[0]
    vm = pl.BlockSpec(memory_space=pltpu.VMEM)
    return pl.pallas_call(
        functools.partial(attn_forward_kernel, imgs),
        out_shape=(jax.ShapeDtypeStruct((imgs, PAD, D), BF16),) + attn_shapes(imgs),
        in_specs=[vm] * 4,
        out_specs=(vm,) * 6,
        compiler_params=pltpu.CompilerParams(vmem_limit_bytes=VMEM_LIMIT),
        cost_estimate=pl.CostEstimate(flops=6 * 10**9, bytes_accessed=10**7, transcendentals=2 * 10**6),
        name="attn_forward",
    )(x, w, noise, keep)


def ring_place(member):
    odd = lax.rem(member, 2)
    half = lax.div(member, 2)
    return half + odd * (E - 1 - 2 * half)


def ring_member(place):
    late = lax.div(place, E // 2)
    return 2 * place + late * (2 * E - 1 - 4 * place)


class Peers:
    def __init__(self):
        dp = lax.axis_index("dp")
        tensor = lax.axis_index("tensor")
        self.member = lax.rem(dp, E)
        self.base = dp - self.member
        self.place = ring_place(self.member)
        self.across = {"tensor": lax.rem(tensor + 2, 4)}
        self.core = {"tensor": tensor + 1 - 2 * lax.rem(tensor, 2)}
        self.next = ({"dp": self.base + self.behind(1, 1)}, {"dp": self.base + self.behind(0, 1)})
        self.sends = []

    def behind(self, way, k):
        step = E - k if way == 0 else k
        return ring_member(lax.rem(self.place + step, E))

    def ahead(self, by):
        return lax.rem(self.member + by, E)

    def came(self, by):
        return lax.rem(self.member + E - by, E)

    def meet(self):
        barrier = pltpu.get_barrier_semaphore()
        others = [{"dp": self.base + self.ahead(by)} for by in range(1, E)] + [self.across, self.core]
        for device in others:
            pl.semaphore_signal(barrier, inc=1, device_id=device, device_id_type=pl.DeviceIdType.MESH)
        pl.semaphore_wait(barrier, len(others))

    def send(self, src, dst, sems, at, device):
        copy = pltpu.make_async_remote_copy(
            src_ref=src,
            dst_ref=dst,
            send_sem=sems[0].at[at],
            recv_sem=sems[1].at[at],
            device_id=device,
            device_id_type=pl.DeviceIdType.MESH,
        )
        copy.start()
        self.sends.append(copy)
        return copy


def expert_step(x, dy, gate, w_ref, g_ref, y_ref, dx_ref, meanwhile):
    weight = jnp.maximum(gate, 0.0)
    d_rows = (dy.astype(F32) * weight).astype(BF16)

    def hidden(r, carry):
        w1 = w_ref[r, :, 0].reshape(D, FFS)
        w2 = w_ref[r, :, 1].reshape(D, FFS)
        a = dot(x, w1)
        a2 = a * a
        th = jnp.tanh(0.7978845608028654 * a * (1.0 + 0.044715 * a2))
        half = 0.5 * (1.0 + th)
        hid = (a * half).astype(BF16)
        slope = half + 0.5 * a * (1.0 - th * th) * (0.7978845608028654 * (1.0 + 3 * 0.044715 * a2))
        da = (dot(d_rows, w2) * slope).astype(BF16)
        y_ref[...] += dot_nt(hid, w2)
        dx_ref[...] += dot_nt(da, w1)
        g_ref[r, 0] += dot_tn(x, da)
        g_ref[r, 1] += dot_tn(d_rows, hid)
        meanwhile(r)
        return carry

    y_ref[...] = jnp.zeros_like(y_ref)
    dx_ref[...] = jnp.zeros_like(dx_ref)
    lax.fori_loop(0, 4, hidden, 0)
    y = y_ref[...]
    dgate = jnp.where(gate >= 0, jnp.sum(dy.astype(F32) * y, axis=1, keepdims=True), 0.0)
    return (y * weight).astype(BF16), dx_ref[...], dgate


GIVEN, PASSED, DY_AT = (1, 3, 4, 6, 7), (1, 3), 2
NEXT_AT, SUMS_AT = 0, 3
HOPS_AT = ()


def front_kernel(
    imgs, pack_ref, ew_ref, dy_ref, x_ref, noise_ref, keep_ref,
    h_out, dy_out, t_in, y_out, g_out, sum_out, w_out, x1_ref, qkv_ref, o_ref, lse_ref, probs_ref,
    w_s, chunk_s, we_s, g_s, xs, dys, y_s, dx_s, t_s, own_s, y_low, pass_s, g_low,
    p_s, p_r, px_s, px_r, pc_s, pc_r, d_s, d_r, h_s, h_r, e_s, e_r, ex_s, ex_r, ec_s, ec_r, t_ss, t_r, local, stage, y_sem, g_sem,
):
    peers = Peers()
    member = peers.member
    d_own = pack_ref.shape[0]
    half = E // 2
    peers.meet()

    def rows(of):
        return pl.ds(pl.multiple_of(of * d_own, 16), d_own)

    own_pack = pltpu.make_async_copy(pack_ref, w_s.at[0, rows(member)], local.at[0])
    own_pack.start()

    ring, px, pc = {}, {}, {}

    def pass_pack(number, of, src, way=None, k=None):
        if way is not None:
            ring[way, k] = peers.send(src, w_s.at[0, rows(of)], (p_s, p_r), (way, k), peers.next[way])
        px[number] = peers.send(src, w_s.at[1, rows(of)], (px_s, px_r), number, peers.across)
        pc[0, number] = peers.send(src, w_s.at[2, rows(of)], (pc_s, pc_r), (0, number), peers.core)

    arrivals = [(0, k) if i == 0 else (1, k) for k in range(1, half + 1) for i in range(2 if k < half else 1)]
    owners = [member] + [peers.behind(way, k) for way, k in arrivals]

    def pass_x(number):
        px[number].wait_recv()
        at = rows(owners[number])
        pc[1, number] = peers.send(w_s.at[1, at], w_s.at[3, at], (pc_s, pc_r), (1, number), peers.core)

    far = (1, 7, 2, 6, 3, 5, 4)
    e_copy, ex, ec = {}, {}, {}

    def give_e(part):
        for by in part:
            to = peers.ahead(by)
            e_copy[by] = peers.send(ew_ref.at[to], we_s.at[0, member], (e_s, e_r), by, {"dp": peers.base + to})

    def pass_e(by):
        if by:
            e_copy[by].wait_recv()
        of = peers.came(by)
        src = we_s.at[0, of] if by else ew_ref.at[member]
        ex[by] = peers.send(src, we_s.at[1, of], (ex_s, ex_r), by, peers.across)
        ec[0, by] = peers.send(src, we_s.at[2, of], (ec_s, ec_r), (0, by), peers.core)

    def pass_ex(by):
        ex[by].wait_recv()
        of = peers.came(by)
        ec[1, by] = peers.send(we_s.at[1, of], we_s.at[3, of], (ec_s, ec_r), (1, by), peers.core)

    def block_at(c, k):
        return peers.behind(c % 2, k) * imgs + c

    def row_copy(out, sems, c, k, src=None):
        at = block_at(c, k)
        return pltpu.make_async_remote_copy(
            src_ref=out.at[at] if src is None else src,
            dst_ref=out.at[at],
            send_sem=sems[0].at[c, k],
            recv_sem=sems[1].at[c, k],
            device_id=peers.next[c % 2],
            device_id_type=pl.DeviceIdType.MESH,
        )

    h_sems, d_sems = (h_s, h_r), (d_s, d_r)

    def row_hop(k):
        for c in range(imgs):
            for out, sems in ((h_out, h_sems), (dy_out, d_sems)):
                row_copy(out, sems, c, k - 1).wait_recv()
                row_copy(out, sems, c, k).start()

    def give_dy():
        for c in range(imgs):
            row_copy(dy_out, d_sems, c, 0, dy_ref.at[c]).start()

    ring[0, 0] = peers.send(pack_ref, w_s.at[0, rows(member)], (p_s, p_r), (0, 0), peers.next[0])
    pass_pack(0, member, pack_ref, 1, 0)
    give_e(far[:GIVEN[0]])
    pass_e(0)
    if DY_AT == 0:
        give_dy()
    keepers = [
        pltpu.make_async_copy(ew_ref.at[member], we_s.at[0, member], local.at[2]),
    ] + [
        pltpu.make_async_copy(dy_ref.at[c], dy_out.at[member * imgs + c], local.at[3 + c]) for c in range(imgs)
    ]
    for copy in keepers:
        copy.start()
    for number, (way, k) in enumerate(arrivals, 1):
        ring[way, k - 1].wait_recv()
        of = owners[number]
        last = half if way == 0 else half - 1
        pass_pack(number, of, w_s.at[0, rows(of)], way if k < last else None, k)
        if number >= 2:
            pass_x(number - 2)
        if number == 4:
            give_e(far[GIVEN[0]:GIVEN[1]])
    give_e(far[GIVEN[1]:GIVEN[2]])
    if DY_AT == 1:
        give_dy()
    for number in range(len(arrivals) - 1, len(arrivals) + 1):
        pass_x(number)
    for number in range(E):
        pc[0, number].wait_recv()
        pc[1, number].wait_recv()
    own_pack.wait()
    keepers.append(pltpu.make_async_copy(w_s, w_out, local.at[1]))
    keepers[-1].start()

    par = params_of(w_s[0])
    done = 0
    for c in range(imgs):
        for by in far[done : PASSED[c]]:
            pass_e(by)
            pass_ex((0, *far)[done])
            done += 1
        attend(
            x_ref[c], par, lambda r: w_s[r], noise_ref[c], keep_ref[c],
            chunk_s.at[c], *(ref.at[c] for ref in (x1_ref, qkv_ref, o_ref, lse_ref, probs_ref)),
        )
        row_copy(h_out, h_sems, c, 0, chunk_s.at[c]).start()
        keepers.append(
            pltpu.make_async_copy(chunk_s.at[c], h_out.at[member * imgs + c], local.at[3 + imgs + c])
        )
        keepers[-1].start()
        give_e(far[GIVEN[2 + c]:GIVEN[3 + c]])
    if DY_AT == 2:
        give_dy()
    for i, by in enumerate(far):
        if i >= done:
            pass_e(by)
            pass_ex((0, *far)[i])
        if i in HOPS_AT:
            row_hop(1 + HOPS_AT.index(i))
    g_s[...] = jnp.zeros_like(g_s)
    pass_ex(far[-1])
    for by in range(E):
        ec[0, by].wait_recv()
        ec[1, by].wait_recv()
    for copy in keepers:
        copy.wait()

    row16 = iota((16, D), 0)
    eye = iota((PAD, PAD), 0) == iota((PAD, PAD), 1)

    def sum_copy(c, k):
        return pltpu.make_async_remote_copy(
            src_ref=pass_s.at[lax.rem(k, 2), c],
            dst_ref=t_in.at[k - 1, c],
            send_sem=t_ss.at[c, k - 1],
            recv_sem=t_r.at[c, k - 1],
            device_id=peers.next[c % 2],
            device_id_type=pl.DeviceIdType.MESH,
        )

    def sums_to_hand(k):
        return [pltpu.make_async_copy(t_in.at[k - 2, c], t_s.at[c], stage.at[2, c]) for c in range(imgs)]

    def rows_to_hand(k):
        slot = lax.rem(k, 2)
        return [
            pltpu.make_async_copy(out.at[block_at(c, k)], held.at[slot, c], stage.at[i, c])
            for c in range(imgs)
            for i, (out, held) in enumerate(((h_out, xs), (dy_out, dys)))
        ]

    def start(copies):
        for copy in copies:
            copy.start()

    def finish(copies):
        for copy in copies:
            copy.wait()

    def keep_y(k):
        return pltpu.make_async_copy(y_low, y_out.at[k], y_sem)

    def step(k, carry):
        slot = lax.rem(k, 2)
        finish(rows_to_hand(k))

        def meanwhile(r):
            for c in range(imgs):
                for out, sems in ((h_out, h_sems), (dy_out, d_sems)):

                    @pl.when((r == NEXT_AT) & (k >= len(HOPS_AT)) & (k < E - 1))
                    def _():
                        row_copy(out, sems, c, k).wait_recv()

                    @pl.when((r == NEXT_AT) & (k >= len(HOPS_AT)) & (k < E - 2))
                    def _():
                        row_copy(out, sems, c, k + 1).start()

            @pl.when((r == NEXT_AT) & (k < E - 1))
            def _():
                start(rows_to_hand(k + 1))

            @pl.when((r == SUMS_AT) & (k >= 2))
            def _():
                for c in range(imgs):
                    sum_copy(c, k - 1).wait_recv()
                start(sums_to_hand(k))

        columns = []
        for c in range(imgs):
            meta = xs[slot, c, PAD - 16 :, :].astype(F32)
            line = jnp.sum(jnp.where(row16 == 8 + member, meta, 0.0), axis=0, keepdims=True)[:, :PAD]
            columns.append(jnp.sum(jnp.where(eye, line, 0.0), axis=1, keepdims=True))
        y, dx, dgate = expert_step(
            xs[slot].reshape(imgs * PAD, D), dys[slot].reshape(imgs * PAD, D), jnp.concatenate(columns, axis=0),
            we_s, g_s, y_s, dx_s, meanwhile,
        )

        @pl.when(k >= 3)
        def _():
            for c in range(imgs):
                sum_copy(c, k - 2).wait_send()

        @pl.when(k >= 1)
        def _():
            keep_y(k - 1).wait()

        for c in range(imgs):
            span = slice(c * PAD, (c + 1) * PAD)
            line = jnp.sum(jnp.where(eye, dgate[span], 0.0), axis=0, keepdims=True)
            line = jnp.concatenate([line, jnp.zeros((1, D - PAD), F32)], axis=1)
            tail = dx[span][PAD - 16 :] + jnp.where(row16 == 8 + member, line, 0.0)
            pass_s[slot, c] = jnp.concatenate([dx[span][: PAD - 16], tail], axis=0).astype(BF16)
            y_low[c] = y[span]

        keep_y(k).start()

        @pl.when(k == 0)
        def _():
            own_s[...] = pass_s[0]

        @pl.when(k >= 2)
        def _():
            finish(sums_to_hand(k))
            pass_s[slot] = (pass_s[slot].astype(F32) + t_s[...].astype(F32)).astype(BF16)

        @pl.when(k >= 1)
        def _():
            for c in range(imgs):
                sum_copy(c, k).start()

        return carry

    start(rows_to_hand(0))
    lax.fori_loop(0, E, step, 0)

    for i in range(8):
        r, kind = i // 2, i % 2
        if i >= 2:
            pltpu.make_async_copy(g_low.at[i % 2], g_out.at[r, :, kind], g_sem.at[i % 2]).wait()
        g_low[i % 2] = g_s[r, kind].astype(BF16).reshape(E, d_own, FFS)
        pltpu.make_async_copy(g_low.at[i % 2], g_out.at[r, :, kind], g_sem.at[i % 2]).start()
    for c in range(imgs):
        sum_copy(c, E - 1).wait_recv()
    start(sums_to_hand(E))
    finish(sums_to_hand(E))
    sum_out[...] = (own_s[...].astype(F32) + t_s[...].astype(F32)).astype(BF16)
    keep_y(E - 1).wait()
    for i in range(2):
        pltpu.make_async_copy(g_low.at[i], g_out.at[3, :, i], g_sem.at[i]).wait()
    for c in range(imgs):
        sum_copy(c, E - 2).wait_send()
        sum_copy(c, E - 1).wait_send()
        for k in range(E - 1):
            row_copy(h_out, h_sems, c, k).wait_send()
            row_copy(dy_out, d_sems, c, k).wait_send()
    for copy in peers.sends:
        copy.wait_send()


def front(pack, ew, dy, x, noise, keep):
    imgs = x.shape[0]
    d_own = pack.shape[0]
    vm = pl.BlockSpec(memory_space=pltpu.VMEM)
    hbm = pl.BlockSpec(memory_space=pl.ANY)
    table = jax.ShapeDtypeStruct((E * imgs, PAD, D), BF16)
    dma = pltpu.SemaphoreType.DMA
    rows = (imgs, PAD, D)
    return pl.pallas_call(
        functools.partial(front_kernel, imgs),
        out_shape=(
            table,
            table,
            jax.ShapeDtypeStruct((E - 1,) + rows, BF16),
            jax.ShapeDtypeStruct((E,) + rows, BF16),
            jax.ShapeDtypeStruct((4, E, 2, d_own, FFS), BF16),
            jax.ShapeDtypeStruct(rows, BF16),
            jax.ShapeDtypeStruct((4, E * d_own, D + 128), BF16),
        )
        + attn_shapes(imgs),
        in_specs=[vm, hbm, hbm, vm, vm, vm],
        out_specs=(hbm,) * 5 + (vm, hbm) + (vm,) * 5,
        scratch_shapes=[
            pltpu.VMEM((4, E * d_own, D + 128), BF16),
            pltpu.VMEM((imgs, PAD, D), BF16),
            pltpu.VMEM((4, E, 2, d_own, FFS), BF16),
            pltpu.VMEM((4, 2, D, FFS), F32),
            pltpu.VMEM((2, imgs, PAD, D), BF16),
            pltpu.VMEM((2, imgs, PAD, D), BF16),
            pltpu.VMEM((imgs * PAD, D), F32),
            pltpu.VMEM((imgs * PAD, D), F32),
            pltpu.VMEM(rows, BF16),
            pltpu.VMEM(rows, BF16),
            pltpu.VMEM(rows, BF16),
            pltpu.VMEM((2,) + rows, BF16),
            pltpu.VMEM((2, E, d_own, FFS), BF16),
            dma((2, 4)), dma((2, 4)), dma((E,)), dma((E,)), dma((2, E)), dma((2, E)),
            dma((imgs, E - 1)), dma((imgs, E - 1)), dma((imgs, E - 1)), dma((imgs, E - 1)),
            dma((E,)), dma((E,)), dma((E,)), dma((E,)), dma((2, E)), dma((2, E)),
            dma((imgs, E - 1)), dma((imgs, E - 1)),
            dma((3 + 2 * imgs,)), dma((3, imgs)), dma(()), dma((2,)),
        ],
        compiler_params=pltpu.CompilerParams(
            vmem_limit_bytes=VMEM_LIMIT, collective_id=0, has_side_effects=True
        ),
        cost_estimate=pl.CostEstimate(flops=10**11, bytes_accessed=10**8, transcendentals=2 * 10**7),
        name="front",
    )(pack, ew, dy, x, noise, keep)


def expert_kernel(nb, who_ref, *refs):
    h_in, dy_in, w_in = refs[:3]
    outs = refs[3:]
    dx_out, y_out, rows_out, hid_out, tiles_ref = outs[:5]
    (h, dy, y_t, dx_t, w_s, gate_s, slot_s, dgate_s, xs, dys, hid_s, rows_s, lo_s, hi_s, in_sem, out_sem, row_sem, hid_sem, w_sem) = outs[5:]
    me = who_ref[0]
    loads = [
        pltpu.make_async_copy(h_in, h, in_sem.at[0]),
        pltpu.make_async_copy(dy_in, dy, in_sem.at[1]),
    ]
    for b in range(E):
        at = pl.ds(b * (D // E), D // E)
        for r in range(4):
            loads.append(pltpu.make_async_copy(w_in.at[r, b], w_s.at[r, :, at], w_sem.at[r, b]))
    for copy in loads:
        copy.start()
    y_t[...] = jnp.zeros_like(y_t)
    dx_t[...] = jnp.zeros_like(dx_t)
    dgate_s[...] = jnp.zeros_like(dgate_s)
    for copy in loads:
        copy.wait()

    row16 = iota((16, D), 0)
    for b in range(nb):
        meta = h[b, PAD - 16 : PAD, :].astype(F32)
        gate_s[b : b + 1, :] = jnp.sum(jnp.where(row16 == 8 + me, meta, 0.0), axis=0, keepdims=True)[:, :PAD]
    gates = gate_s[...]
    named = (gates >= 0) & (iota((nb, PAD), 1) < SEQ)
    ones = named.astype(F32).astype(BF16)
    upto = dot(ones, (iota((PAD, PAD), 0) <= iota((PAD, PAD), 1)).astype(F32).astype(BF16))
    count = dot(ones, jnp.ones((PAD, PAD), BF16)).astype(BF16)
    before = dot((iota((nb, nb), 0) > iota((nb, nb), 1)).astype(F32).astype(BF16), count)
    slot_s[...] = jnp.where(named, before + upto - 1.0, -1.0).astype(jnp.int32)
    ends = jnp.where(named, before + upto, before)
    for b in range(nb):
        lo_s[b] = jnp.max(before[b : b + 1, :]).astype(jnp.int32)
        hi_s[b] = jnp.max(ends[b : b + 1, :]).astype(jnp.int32)
    tiles = lax.div(hi_s[nb - 1] + TILE - 1, TILE)
    tiles_ref[0] = tiles

    def meets(b, first):
        return (lo_s[b] < first + TILE) & (hi_s[b] > first) & (hi_s[b] > lo_s[b])

    def place(b, first):
        return iota((TILE, PAD), 0) + first == slot_s[pl.ds(b, 1), :]

    def step(t, carry):
        first = t * TILE
        slot = lax.rem(t, 2)
        xs[...] = jnp.zeros_like(xs)
        dys[...] = jnp.zeros_like(dys)

        def collect(b, gcol):
            def one(gcol):
                hit = place(b, first)
                p = hit.astype(F32).astype(BF16)
                xs[...] += dot(p, h[b])
                dys[...] += dot(p, dy[b])
                return gcol + jnp.sum(jnp.where(hit, gate_s[pl.ds(b, 1), :], 0.0), axis=1, keepdims=True)

            return lax.cond(meets(b, first), one, lambda g: g, gcol)

        gcol = lax.fori_loop(0, nb, collect, jnp.zeros((TILE, 1), F32))

        def drain(s):
            pltpu.make_async_copy(rows_s.at[s], rows_out.at[:, pl.ds(0, TILE)], row_sem.at[s]).wait()
            pltpu.make_async_copy(hid_s.at[s], hid_out.at[:, pl.ds(0, TILE)], hid_sem.at[s]).wait()

        @pl.when(t >= 2)
        def _():
            drain(slot)

        x = xs[...].astype(BF16)
        g_rows = (dys[...] * gcol).astype(BF16)
        rows_s[slot, 0] = x
        rows_s[slot, 1] = g_rows
        y = jnp.zeros((TILE, D), F32)
        dx = jnp.zeros((TILE, D), F32)
        for r in range(4):
            w1, w2 = w_s.at[r, 0], w_s.at[r, 1]
            a = dot(x, w1[...])
            a2 = a * a
            th = jnp.tanh(0.7978845608028654 * a * (1.0 + 0.044715 * a2))
            half = 0.5 * (1.0 + th)
            hid = (a * half).astype(BF16)
            slope = half + 0.5 * a * (1.0 - th * th) * (0.7978845608028654 * (1.0 + 3 * 0.044715 * a2))
            da = (dot(g_rows, w2[...]) * slope).astype(BF16)
            y = y + dot_nt(hid, w2[...])
            dx = dx + dot_nt(da, w1[...])
            hid_s[slot, 0, :, r * FFS : (r + 1) * FFS] = da
            hid_s[slot, 1, :, r * FFS : (r + 1) * FFS] = hid
        at = pl.ds(pl.multiple_of(first, TILE), TILE)
        pltpu.make_async_copy(rows_s.at[slot], rows_out.at[:, at], row_sem.at[slot]).start()
        pltpu.make_async_copy(hid_s.at[slot], hid_out.at[:, at], hid_sem.at[slot]).start()
        dgate = jnp.sum(dys[...] * y, axis=1, keepdims=True)
        y_low = (y * gcol).astype(BF16)
        dx_low = dx.astype(BF16)

        def give(b, carry):
            @pl.when(meets(b, first))
            def _():
                hit = place(b, first)
                p = hit.astype(F32).astype(BF16)
                y_t[b] = y_t[b] + dot_tn(p, y_low).astype(BF16)
                dx_t[b] = dx_t[b] + dot_tn(p, dx_low).astype(BF16)
                dgate_s[pl.ds(b, 1), :] += jnp.sum(jnp.where(hit, dgate, 0.0), axis=0, keepdims=True)

            return carry

        lax.fori_loop(0, nb, give, 0)
        return carry

    lax.fori_loop(0, tiles, step, 0)
    for back in (1, 2):

        @pl.when(tiles >= back)
        def _():
            s = lax.rem(tiles - back, 2)
            pltpu.make_async_copy(rows_s.at[s], rows_out.at[:, pl.ds(0, TILE)], row_sem.at[s]).wait()
            pltpu.make_async_copy(hid_s.at[s], hid_out.at[:, pl.ds(0, TILE)], hid_sem.at[s]).wait()

    for b in range(nb):
        tail = dx_t[b, PAD - 16 : PAD, :].astype(F32)
        line = jnp.concatenate([dgate_s[b : b + 1, :], jnp.zeros((1, D - PAD), F32)], axis=1)
        dx_t[b, PAD - 16 : PAD, :] = (tail + jnp.where(row16 == 8 + me, line, 0.0)).astype(BF16)
    stores = [
        pltpu.make_async_copy(dx_t, dx_out, out_sem.at[0]),
        pltpu.make_async_copy(y_t, y_out, out_sem.at[1]),
    ]
    for copy in stores:
        copy.start()
    for copy in stores:
        copy.wait()


def expert_rows(nb):
    return -(-nb * SEQ // TILE) * TILE


def experts(member, h_all, dy_all, weights):
    nb = h_all.shape[0]
    rows = expert_rows(nb)
    hbm = pl.BlockSpec(memory_space=pl.ANY)
    sm = pl.BlockSpec(memory_space=pltpu.SMEM)
    table = jax.ShapeDtypeStruct((nb, PAD, D), BF16)
    return pl.pallas_call(
        functools.partial(expert_kernel, nb),
        out_shape=[
            table,
            table,
            jax.ShapeDtypeStruct((2, rows, D), BF16),
            jax.ShapeDtypeStruct((2, rows, 4 * FFS), BF16),
            jax.ShapeDtypeStruct((1,), jnp.int32),
        ],
        in_specs=[sm, hbm, hbm, hbm],
        out_specs=[hbm] * 4 + [sm],
        scratch_shapes=[
            pltpu.VMEM((nb, PAD, D), BF16),
            pltpu.VMEM((nb, PAD, D), BF16),
            pltpu.VMEM((nb, PAD, D), BF16),
            pltpu.VMEM((nb, PAD, D), BF16),
            pltpu.VMEM((4, 2, D, FFS), BF16),
            pltpu.VMEM((nb, PAD), F32),
            pltpu.VMEM((nb, PAD), jnp.int32),
            pltpu.VMEM((nb, PAD), F32),
            pltpu.VMEM((TILE, D), F32),
            pltpu.VMEM((TILE, D), F32),
            pltpu.VMEM((2, 2, TILE, 4 * FFS), BF16),
            pltpu.VMEM((2, 2, TILE, D), BF16),
            pltpu.SMEM((nb,), jnp.int32),
            pltpu.SMEM((nb,), jnp.int32),
            pltpu.SemaphoreType.DMA((2,)),
            pltpu.SemaphoreType.DMA((2,)),
            pltpu.SemaphoreType.DMA((2,)),
            pltpu.SemaphoreType.DMA((2,)),
            pltpu.SemaphoreType.DMA((4, E)),
        ],
        compiler_params=pltpu.CompilerParams(vmem_limit_bytes=VMEM_LIMIT),
        cost_estimate=pl.CostEstimate(flops=30 * 10**9, bytes_accessed=4 * 10**7, transcendentals=4 * 10**6),
        name="experts",
    )(member.reshape(1), h_all, dy_all, weights)


def expert_grad_kernel(tiles_ref, rows_ref, hid_ref, out_ref, acc):
    acc[...] = jnp.zeros_like(acc)

    def step(t, carry):
        at = pl.ds(pl.multiple_of(t * TILE, TILE), TILE)
        acc[...] += dot_tn(rows_ref[0, at, :], hid_ref[0, at, :])
        return carry

    lax.fori_loop(0, tiles_ref[0], step, 0)
    out_ref[0] = acc[...].astype(BF16)


def expert_grads(tiles, rows, hid, kind, base):
    n = rows.shape[1]
    return pl.pallas_call(
        expert_grad_kernel,
        grid_spec=pltpu.PrefetchScalarGridSpec(
            num_scalar_prefetch=1,
            grid=(2,),
            in_specs=[
                pl.BlockSpec((1, n, D), lambda s, _: (kind, 0, 0)),
                pl.BlockSpec((1, n, FFS), lambda s, _: (kind, 0, base + s)),
            ],
            out_specs=pl.BlockSpec((1, D, FFS), lambda s, _: (s, 0, 0)),
            scratch_shapes=[pltpu.VMEM((D, FFS), F32)],
        ),
        out_shape=jax.ShapeDtypeStruct((2, D, FFS), BF16),
        compiler_params=pltpu.CompilerParams(vmem_limit_bytes=VMEM_LIMIT),
        cost_estimate=pl.CostEstimate(flops=4 * 10**9, bytes_accessed=15 * 10**6, transcendentals=0),
        name="expert_grads",
    )(tiles, rows, hid)


def unpack_kernel(who_ref, *refs):
    blocks, (in_ref, out_ref) = refs[:E], refs[E:]
    for by in range(E):
        in_ref[who_ref[by]] = blocks[by][0].astype(F32)
        out_ref[who_ref[by]] = blocks[by][1].astype(F32)


def unpack(who, blocks):
    vm = pl.BlockSpec(memory_space=pltpu.VMEM)
    whole = jax.ShapeDtypeStruct((E,) + blocks[0].shape[1:], F32)
    return pl.pallas_call(
        unpack_kernel,
        out_shape=(whole, whole),
        in_specs=[pl.BlockSpec(memory_space=pltpu.SMEM)] + [vm] * E,
        out_specs=(vm, vm),
        compiler_params=pltpu.CompilerParams(vmem_limit_bytes=VMEM_LIMIT),
        cost_estimate=pl.CostEstimate(flops=10**6, bytes_accessed=7 * 10**6, transcendentals=0),
        name="unpack",
    )(who, *blocks)


def lay_out_kernel(imgs, at_ref, *refs):
    parts, out_ref, held, sem = refs[:4], refs[4], refs[5], refs[6]
    copies = [pltpu.make_async_copy(parts[s], held.at[s], sem.at[s]) for s in range(4)]
    for copy in copies:
        copy.start()
    for copy in copies:
        copy.wait()
    for i in range(4 * imgs):
        out_ref[i * SEQ : (i + 1) * SEQ, :] = held[at_ref[i // imgs], i % imgs, :SEQ, :]


def lay_out(at, parts):
    imgs = parts[0].shape[0]
    hbm = pl.BlockSpec(memory_space=pl.ANY)
    return pl.pallas_call(
        functools.partial(lay_out_kernel, imgs),
        out_shape=jax.ShapeDtypeStruct((4 * imgs * SEQ, D), BF16),
        in_specs=[pl.BlockSpec(memory_space=pltpu.SMEM)] + [hbm] * 4,
        out_specs=pl.BlockSpec(memory_space=pltpu.VMEM),
        scratch_shapes=[pltpu.VMEM((4, imgs, PAD, D), BF16), pltpu.SemaphoreType.DMA((4,))],
        compiler_params=pltpu.CompilerParams(vmem_limit_bytes=VMEM_LIMIT),
        cost_estimate=pl.CostEstimate(flops=10**6, bytes_accessed=5 * 10**6, transcendentals=0),
        name="lay_out",
    )(at, *parts)


class Backward:
    def __init__(self, imgs, dh_of, saved, w_ref, dx1_s, low_s, h1_s, dh1_s, dqkv_s, o_s):
        self.imgs, self.dh_of, self.saved, self.w_ref = imgs, dh_of, saved, w_ref
        self.dx1_s, self.low_s, self.h1_s, self.dh1_s, self.dqkv_s, self.o_s = dx1_s, low_s, h1_s, dh1_s, dqkv_s, o_s
        self.par = params_of(w_ref[0])
        self.row_ok = iota((PAD, 1), 0) < SEQ
        self.started = False

    def span(self, c):
        return slice(c * PAD, (c + 1) * PAD)

    def first(self):
        x1_in, x_in, dy_in, probs_in = self.saved[:4]
        par, row_ok = self.par, self.row_ok
        lane_ok = iota((E, PAD), 1) < SEQ
        router = par[8:16].astype(BF16)
        gain = jnp.zeros((1, D), F32)
        bias = jnp.zeros((1, D), F32)
        g_router = jnp.zeros((E, D), F32)
        for c in range(self.imgs):
            arrived = self.dh_of(c).astype(F32)
            dgate = arrived[PAD - 8 :, :PAD]
            probs = probs_in[c]
            dlogits = probs * (dgate - jnp.sum(probs * dgate, axis=0, keepdims=True))
            dlogits = jnp.where(lane_ok, dlogits, 0.0).astype(BF16)
            unit, scale = normalise(x1_in[c])
            h2 = (unit * par[2:3] + par[3:4]).astype(BF16)
            g_router = g_router + dot(dlogits, h2)
            dh2 = jnp.where(row_ok, arrived + dot_tn(dlogits, router), 0.0)
            gain = gain + jnp.sum(dh2 * unit, axis=0, keepdims=True)
            bias = bias + jnp.sum(dh2, axis=0, keepdims=True)
            dx1 = dy_in[c].astype(F32) + norm_back(dh2, unit, scale, par[2:3])
            self.dx1_s[self.span(c), :] = dx1
            self.low_s[self.span(c), :] = dx1.astype(BF16)
            unit1, _ = normalise(x_in[c].astype(F32))
            self.h1_s[self.span(c), :] = (unit1 * par[0:1] + par[1:2]).astype(BF16)
        self.small2 = [gain, bias, jnp.zeros((4, D), F32), g_router]

    def heads(self, r):
        qkv_in, o_in, lse_in = self.saved[4:]
        key_ok = iota((PAD, PAD), 1) < SEQ
        low, h1, w = self.low_s[...], self.h1_s[...], self.w_ref[r]
        dout = dot(low, w[:, 9 * HD : D]).astype(BF16)
        for c in range(self.imgs):
            qkv = qkv_in[c, r]
            lse = lse_in[c]
            self.o_s[self.span(c), :] = o_in[c, r]
            dqs, dks, dvs = [], [], []
            for h in range(3):
                q = qkv[:, h * HD : (h + 1) * HD]
                k = qkv[:, (3 + h) * HD : (4 + h) * HD]
                v = qkv[:, (6 + h) * HD : (7 + h) * HD]
                do = dout[self.span(c), h * HD : (h + 1) * HD]
                s = dot_nt(q, k) * HD ** (-0.5)
                p = jnp.where(key_ok, jnp.exp(s - lse[:, 3 * r + h : 3 * r + h + 1]), 0.0)
                dvs.append(dot_tn(p.astype(BF16), do).astype(BF16))
                dp = dot_nt(do, v)
                ds = (p * (dp - jnp.sum(p * dp, axis=-1, keepdims=True))).astype(BF16)
                dqs.append((dot(ds, k) * HD ** (-0.5)).astype(BF16))
                dks.append((dot_tn(ds, q) * HD ** (-0.5)).astype(BF16))
            self.dqkv_s[self.span(c), :] = jnp.concatenate(dqs + dks + dvs, axis=1)
        dqkv = self.dqkv_s[...]
        part = dot_nt(dqkv, w[:, : 9 * HD])
        self.dh1_s[...] = self.dh1_s[...] + part if self.started else part
        self.started = True
        return jnp.concatenate([dot_tn(h1, dqkv), dot_tn(low, self.o_s[...])], axis=1).astype(BF16)

    def last(self, dtok_ref):
        x_in = self.saved[1]
        gain = jnp.zeros((1, D), F32)
        bias = jnp.zeros((1, D), F32)
        for c in range(self.imgs):
            dh1 = jnp.where(self.row_ok, self.dh1_s[self.span(c), :], 0.0)
            unit, scale = normalise(x_in[c].astype(F32))
            gain = gain + jnp.sum(dh1 * unit, axis=0, keepdims=True)
            bias = bias + jnp.sum(dh1, axis=0, keepdims=True)
            dtok_ref[c] = (self.dx1_s[self.span(c), :] + norm_back(dh1, unit, scale, self.par[0:1])).astype(BF16)
        return jnp.concatenate([gain, bias] + self.small2, axis=0)


def small_block(small, i, d_own):
    line = jnp.concatenate([small[:, i * d_own : (i + 1) * d_own], jnp.zeros((16, D - d_own), F32)], axis=1)
    return line.astype(BF16)


def backward_scratch(imgs):
    rows = imgs * PAD
    return [
        pltpu.VMEM((rows, D), F32),
        pltpu.VMEM((rows, D), BF16),
        pltpu.VMEM((rows, D), BF16),
        pltpu.VMEM((rows, D), F32),
        pltpu.VMEM((rows, 9 * HD), BF16),
        pltpu.VMEM((rows, 3 * HD), BF16),
    ]


def attn_backward_kernel(imgs, *refs):
    dh_in, saved, w_ref = refs[:imgs], refs[imgs : imgs + 7], refs[imgs + 7]
    packs, dtok_ref = refs[imgs + 8 : imgs + 11], refs[imgs + 11]
    n_dp, d_own = packs[0].shape[0], packs[0].shape[1] - 16
    back = Backward(imgs, lambda c: dh_in[c][...], saved, w_ref, *refs[imgs + 12 :])

    def pack_of(r):
        return packs[r] if r < 2 else packs[2].at[:, r - 2]

    back.first()
    for r in range(4):
        grad = back.heads(r)
        for i in range(n_dp):
            pack_of(r)[i, :d_own, :] = grad[i * d_own : (i + 1) * d_own]
    small = back.last(dtok_ref)
    for i in range(n_dp):
        for r in range(4):
            pack_of(r)[i, d_own:, :] = small_block(small, i, d_own)


def attn_backward(dh, saved, w, n_dp):
    imgs = len(dh)
    pack = (n_dp, D // n_dp + 16, D)
    vm = pl.BlockSpec(memory_space=pltpu.VMEM)
    return pl.pallas_call(
        functools.partial(attn_backward_kernel, imgs),
        out_shape=(
            jax.ShapeDtypeStruct(pack, BF16),
            jax.ShapeDtypeStruct(pack, BF16),
            jax.ShapeDtypeStruct((n_dp, 2) + pack[1:], BF16),
            jax.ShapeDtypeStruct((imgs, PAD, D), BF16),
        ),
        in_specs=[vm] * (imgs + 8),
        out_specs=(vm,) * 4,
        scratch_shapes=backward_scratch(imgs),
        compiler_params=pltpu.CompilerParams(vmem_limit_bytes=VMEM_LIMIT),
        cost_estimate=pl.CostEstimate(flops=12 * 10**9, bytes_accessed=2 * 10**7, transcendentals=2 * 10**6),
        name="attn_backward",
    )(*dh, *saved, w)


def back_kernel(
    imgs, g_low, y_ref, dh_ref, x1_ref, x_ref, dy_ref, probs_ref, qkv_ref, o_ref, lse_ref, w_ref,
    out_all, dtok_all, g_out, total_ref,
    ga_s, gc_s, gx_s, pk_s, pkc_s, pkr_s, sm_s, smr_s, cs_s, cr_s, fs_s, fr_s, or_s, dt_s, y_s, yr_s,
    dx1_s, low_s, h1_s, dh1_s, dqkv_s, o_s,
    gc_ss, gc_r, gx_ss, gx_r, ga_ss, ga_r, pk_ss, pk_r, sm_ss, sm_r, c_ss, c_r, f_ss, f_r, row_ss, row_r, y_ss, y_r, local,
):
    peers = Peers()
    member = peers.member
    tensor = lax.axis_index("tensor")
    d_own = g_low.shape[3]
    peers.meet()
    loads = []

    def here(src, dst):
        copy = pltpu.make_async_copy(src, dst, local.at[len(loads)])
        copy.start()
        loads.append(copy)
        return copy

    def give_rows(kind, src, whole):
        here(src, whole.at[tensor])
        across = peers.send(src, whole.at[tensor], (row_ss, row_r), (kind, 0), peers.across)
        core = peers.send(src, whole.at[tensor], (row_ss, row_r), (kind, 1), peers.core)

        def onwards():
            across.wait_recv()
            other = lax.rem(tensor + 2, 4)
            copy = peers.send(whole.at[other], whole.at[other], (row_ss, row_r), (kind, 2), peers.core)
            return core, copy

        return onwards

    y_load = here(y_ref, y_s)
    y_sent = {}

    def y_hop(k):
        for c in range(imgs):
            if k == 1:
                src = y_s.at[1, c]
            else:
                y_sent[c, k - 1].wait_recv()
                src = yr_s.at[k - 2, c]
                src[...] = (src[...].astype(F32) + y_s[k, c].astype(F32)).astype(BF16)
            y_sent[c, k] = peers.send(src, yr_s.at[k - 1, c], (y_ss, y_r), (c, k - 1), peers.next[c % 2])

    def y_last():
        for c in range(imgs):
            y_sent[c, E - 1].wait_recv()
            total = yr_s[E - 2, c].astype(F32) + y_s[0, c].astype(F32)
            or_s[c] = (x1_ref[c] + total).astype(BF16)

    g_core = [
        peers.send(g_low.at[2 + s], gc_s.at[s], (gc_ss, gc_r), s, peers.core) for s in (1, 0)
    ][::-1]
    g_load = [here(g_low.at[s], ga_s.at[s]) for s in (1, 0)][::-1]
    y_load.wait()
    y_hop(1)
    order = (4, 3, 5, 2, 6, 1, 7, 0)
    gx = {}

    def pass_across():
        g_core[1].wait_recv()
        g_load[1].wait()
        for by in order:
            to = peers.ahead(by)
            ga_s[1, to] = (ga_s[1, to].astype(F32) + gc_s[1, to].astype(F32)).astype(BF16)
            gx[by] = peers.send(ga_s.at[1, to], gx_s.at[to], (gx_ss, gx_r), by, peers.across)
        g_core[0].wait_recv()
        g_load[0].wait()

    ga = {}

    def pass_home(by):
        gx[by].wait_recv()
        to = peers.ahead(by)
        part = ga_s[0, to].astype(F32) + gc_s[0, to].astype(F32)
        ga_s[0, to] = (part + gx_s[to].astype(F32)).astype(BF16)
        if by:
            device = {"dp": peers.base + to}
            ga[by] = peers.send(ga_s.at[0, to], g_out.at[member], (ga_ss, ga_r), by, device)
        else:
            here(ga_s.at[0, to], g_out.at[member])

    saved = (x1_ref, x_ref, dy_ref, probs_ref, qkv_ref, o_ref, lse_ref)
    back = Backward(imgs, lambda c: dh_ref[c], saved, w_ref, dx1_s, low_s, h1_s, dh1_s, dqkv_s, o_s)
    back.first()
    for r in (2, 3):
        grad = back.heads(r)
        for i in range(E):
            pkc_s[i, r - 2] = grad[i * d_own : (i + 1) * d_own]
        y_hop(r)
        if r == 2:
            pass_across()
    pk_core = peers.send(pkc_s, pkr_s, (pk_ss, pk_r), 0, peers.core)
    for r in (0, 1):
        grad = back.heads(r)
        for i in range(E):
            pk_s[i, r, :d_own] = grad[i * d_own : (i + 1) * d_own]
        y_hop(4 + r)
        pass_home(order[r])
    small = back.last(dt_s)
    dtok_rows = give_rows(1, dt_s, dtok_all)
    for i in range(E):
        sm_s[i] = small_block(small, i, d_own)
    sm_core = peers.send(sm_s, smr_s, (sm_ss, sm_r), 0, peers.core)
    pk_core.wait_recv()
    sm_core.wait_recv()

    def term(of):
        weights = pk_s[of, :, :d_own].astype(F32) + pkr_s[of].astype(F32)
        both = sm_s[of].astype(F32) + smr_s[of].astype(F32)
        return jnp.concatenate([weights, jnp.broadcast_to(both[None], (2,) + both.shape)], axis=1)

    steps = (E // 2, E // 2 - 1)
    hops = {}

    def hop(way, i):
        value = term(peers.behind(1 - way, steps[way] - i))
        if i:
            hops[way, i - 1].wait_recv()
            value = value + cr_s[way, i - 1].astype(F32)
        cs_s[way, i] = value.astype(BF16)
        hops[way, i] = peers.send(cs_s.at[way, i], cr_s.at[way, i], (c_ss, c_r), (way, i), peers.next[way])

    for i in range(E // 2):
        hop(0, i)
        if i < steps[1]:
            hop(1, i)
        if i < 2:
            y_hop(6 + i)
        if i == 2:
            y_last()
            out_rows = give_rows(0, or_s, out_all)
        pass_home(order[2 + i])
    hops[1, steps[1] - 1].wait_recv()
    hops[0, steps[0] - 1].wait_recv()
    total = term(member) + cr_s[0, steps[0] - 1].astype(F32) + cr_s[1, steps[1] - 1].astype(F32)
    fs_s[...] = total[1].astype(BF16)
    final = peers.send(fs_s, fr_s, (f_ss, f_r), 0, peers.across)
    pass_home(order[6])
    pass_home(order[7])
    dtok_rows = dtok_rows()
    out_rows = out_rows()
    final.wait_recv()
    total_ref[...] = total[0] + fr_s[...].astype(F32)
    for by in range(1, E):
        ga[by].wait_recv()
    for copy in (*out_rows, *dtok_rows):
        copy.wait_recv()
    for copy in loads:
        if all(copy is not other for other in (y_load, *g_load)):
            copy.wait()
    for copy in peers.sends:
        copy.wait_send()


def back(g_low, y, dh, saved, w):
    imgs = dh.shape[0]
    d_own = g_low.shape[3]
    vm = pl.BlockSpec(memory_space=pltpu.VMEM)
    hbm = pl.BlockSpec(memory_space=pl.ANY)
    dma = pltpu.SemaphoreType.DMA
    part = (E, 2, d_own, D)
    rows = (imgs, PAD, D)
    hop = (2, E // 2, 2, d_own + 16, D)
    return pl.pallas_call(
        functools.partial(back_kernel, imgs),
        out_shape=(
            jax.ShapeDtypeStruct((4,) + rows, BF16),
            jax.ShapeDtypeStruct((4,) + rows, BF16),
            jax.ShapeDtypeStruct(part, BF16),
            jax.ShapeDtypeStruct((d_own + 16, D), F32),
        ),
        in_specs=[hbm, hbm] + [vm] * 9,
        out_specs=(hbm, hbm, hbm, vm),
        scratch_shapes=[
            pltpu.VMEM((2,) + part, BF16),
            pltpu.VMEM((2,) + part, BF16),
            pltpu.VMEM(part, BF16),
            pltpu.VMEM((E, 2, d_own + 16, D), BF16),
            pltpu.VMEM(part, BF16),
            pltpu.VMEM(part, BF16),
            pltpu.VMEM((E, 16, D), BF16),
            pltpu.VMEM((E, 16, D), BF16),
            pltpu.VMEM(hop, BF16),
            pltpu.VMEM(hop, BF16),
            pltpu.VMEM((d_own + 16, D), BF16),
            pltpu.VMEM((d_own + 16, D), BF16),
            pltpu.VMEM(rows, BF16),
            pltpu.VMEM(rows, BF16),
            pltpu.VMEM((E,) + rows, BF16),
            pltpu.VMEM((E - 1,) + rows, BF16),
            *backward_scratch(imgs),
            dma((2,)), dma((2,)), dma((E,)), dma((E,)), dma((E,)), dma((E,)), dma((1,)), dma((1,)),
            dma((1,)), dma((1,)), dma((2, E // 2)), dma((2, E // 2)), dma((1,)), dma((1,)), dma((2, 3)), dma((2, 3)),
            dma((imgs, E - 1)), dma((imgs, E - 1)), dma((6,)),
        ],
        compiler_params=pltpu.CompilerParams(
            vmem_limit_bytes=VMEM_LIMIT, collective_id=1, has_side_effects=True
        ),
        cost_estimate=pl.CostEstimate(flops=12 * 10**9, bytes_accessed=10**8, transcendentals=2 * 10**6),
        name="back",
    )(g_low, y, dh, *saved, w)


def eye_of(n, lanes):
    return (iota((n, lanes), 0) == iota((n, lanes), 1)).astype(F32).astype(BF16)


def prepare_kernel(
    imgs, tensor_ref, tok_ref, cot_ref, qkv_ref, wo_ref, vec_ref, router_ref, win_ref, wout_ref, noise_ref, routes_ref,
    pack_ref, ew_ref, x_ref, dy_ref, keep_out, noise_out, keep_s,
):
    tensor = tensor_ref[0]
    d_own = wo_ref.shape[1]
    wo = dot_tn(wo_ref[...].astype(BF16), eye_of(3 * HD, 3 * HD)).astype(BF16)
    lines = jnp.concatenate([vec_ref[...], jnp.zeros((4, d_own), F32), router_ref[...]], axis=0).astype(BF16)
    lines = dot_tn(lines, eye_of(16, 128)).astype(BF16)
    pack_ref[...] = jnp.concatenate([qkv_ref[i].astype(BF16) for i in range(3)] + [wo, lines], axis=1)
    for e in range(E):
        ew_ref[e, 0] = win_ref[e].astype(BF16)
        ew_ref[e, 1] = wout_ref[e].astype(BF16)
    count = routes_ref.shape[1]
    earlier = (iota((count, count), 0) <= iota((count, count), 1)).astype(F32).astype(BF16)
    experts_ = iota((E, count), 0)
    before = jnp.zeros((E, 1), F32)
    keep = jnp.zeros((E, count), F32)
    for choice in range(TOP):
        named = experts_ == routes_ref[choice : choice + 1, :]
        upto = before + dot(named.astype(F32).astype(BF16), earlier)
        keep = keep + jnp.where(named & (upto <= CAP), 1.0, 0.0)
        before = upto[:, count - 1 :]
    keep_s[...] = keep
    for t in range(4):

        @pl.when(tensor == t)
        def _():
            for c in range(imgs):
                at = (t * imgs + c) * SEQ
                for src, dst in ((tok_ref, x_ref), (cot_ref, dy_ref)):
                    dst[c, :SEQ, :] = src[at : at + SEQ, :]
                    dst[c, SEQ:, :] = jnp.zeros((PAD - SEQ, D), BF16)
                for src, dst in ((keep_s, keep_out), (noise_ref, noise_out)):
                    dst[c] = jnp.concatenate([src[:, at : at + SEQ], jnp.zeros((E, PAD - SEQ), F32)], axis=1)


def prepare(tensor, imgs, tokens, cotangent, w_qkv, w_attn_out, vectors, router, w_in, w_out, noise, routes):
    vm = pl.BlockSpec(memory_space=pltpu.VMEM)
    d_own = w_attn_out.shape[1]
    rows = jax.ShapeDtypeStruct((imgs, PAD, D), BF16)
    lanes = jax.ShapeDtypeStruct((imgs, E, PAD), F32)
    return pl.pallas_call(
        functools.partial(prepare_kernel, imgs),
        out_shape=(
            jax.ShapeDtypeStruct((d_own, D + 128), BF16),
            jax.ShapeDtypeStruct((E, 2, d_own, FFS), BF16),
            rows,
            rows,
            lanes,
            lanes,
        ),
        in_specs=[pl.BlockSpec(memory_space=pltpu.SMEM)] + [vm] * 10,
        out_specs=(vm,) * 6,
        scratch_shapes=[pltpu.VMEM((E, tokens.shape[0]), F32)],
        compiler_params=pltpu.CompilerParams(vmem_limit_bytes=VMEM_LIMIT),
        cost_estimate=pl.CostEstimate(flops=10**8, bytes_accessed=15 * 10**6, transcendentals=0),
        name="prepare",
    )(tensor.reshape(1), tokens, cotangent, w_qkv, w_attn_out, vectors, router, w_in, w_out, noise, routes)


def finish_kernel(imgs, out_in, dtok_in, g_in, total_ref, out_ref, dtok_ref, gi_ref, go_ref, qkv_ref, wo_ref, small_ref, rows_s, g_s, sem):
    loads = [pltpu.make_async_copy(src, rows_s.at[i], sem.at[i]) for i, src in enumerate((out_in, dtok_in))]
    loads.append(pltpu.make_async_copy(g_in, g_s, sem.at[2]))
    for copy in loads:
        copy.start()
    d_own = gi_ref.shape[1]
    total = total_ref[...]
    for i in range(3):
        qkv_ref[i] = total[:d_own, i * 3 * HD : (i + 1) * 3 * HD]
    wo_ref[...] = jnp.transpose(total[:d_own, 9 * HD :])
    small_ref[...] = total[d_own:, :d_own]
    for which, dst in ((0, out_ref), (1, dtok_ref)):
        loads[which].wait()
        for i in range(4 * imgs):
            dst[i * SEQ : (i + 1) * SEQ, :] = rows_s[which, i // imgs, i % imgs, :SEQ, :]
    loads[2].wait()
    for e in range(E):
        gi_ref[e] = g_s[e, 0].astype(F32)
        go_ref[e] = g_s[e, 1].astype(F32)


def finish(out_all, dtok_all, g_exp, total):
    imgs = out_all.shape[1]
    d_own = g_exp.shape[2]
    vm = pl.BlockSpec(memory_space=pltpu.VMEM)
    hbm = pl.BlockSpec(memory_space=pl.ANY)
    rows = jax.ShapeDtypeStruct((4 * imgs * SEQ, D), BF16)
    grad = jax.ShapeDtypeStruct((E, d_own, FFS), F32)
    return pl.pallas_call(
        functools.partial(finish_kernel, imgs),
        out_shape=(
            rows,
            rows,
            grad,
            grad,
            jax.ShapeDtypeStruct((3, d_own, 3 * HD), F32),
            jax.ShapeDtypeStruct((3 * HD, d_own), F32),
            jax.ShapeDtypeStruct((16, d_own), F32),
        ),
        in_specs=[hbm, hbm, hbm, vm],
        out_specs=(vm,) * 7,
        scratch_shapes=[
            pltpu.VMEM((2, 4, imgs, PAD, D), BF16),
            pltpu.VMEM(g_exp.shape, BF16),
            pltpu.SemaphoreType.DMA((3,)),
        ],
        compiler_params=pltpu.CompilerParams(vmem_limit_bytes=VMEM_LIMIT),
        cost_estimate=pl.CostEstimate(flops=10**6, bytes_accessed=18 * 10**6, transcendentals=0),
        name="finish",
    )(out_all, dtok_all, g_exp, total)


RING = (0, 2, 4, 6, 7, 5, 3, 1)


class Mover:
    def __init__(self, n_dp):
        self.n_dp = n_dp
        self.groups = n_dp // E
        self.me = lax.axis_index("dp")
        self.member = lax.rem(self.me, E)
        self.group = lax.div(self.me, E)
        self.tensor = lax.axis_index("tensor")
        self.place = ring_place(self.member)
        bases = range(0, n_dp, E)
        self.ring = (
            [(b + RING[i], b + RING[(i + 1) % E]) for b in bases for i in range(E)],
            [(b + RING[(i + 1) % E], b + RING[i]) for b in bases for i in range(E)],
        )

    def along(self, value, way):
        return lax.ppermute(value, "dp", self.ring[way])

    def shift(self, value, by):
        perm = [(b + i, b + (i + by) % E) for b in range(0, self.n_dp, E) for i in range(E)]
        return lax.ppermute(value, "dp", perm)

    def shift_group(self, value, by):
        return lax.ppermute(value, "dp", [(k, (k + by * E) % self.n_dp) for k in range(self.n_dp)])

    def other(self, value, mask):
        return lax.ppermute(value, "tensor", [(k, k ^ mask) for k in range(4)])

    def behind(self, way, k):
        step = -k if way == 0 else k
        return ring_member(lax.rem(self.place + step + E, E))

    def group_lists(self):
        if self.groups == 1:
            return None
        return [[b + i for i in range(E)] for b in range(0, self.n_dp, E)]

    def gather(self, value):
        return lax.all_gather(value, "dp", axis=0, tiled=False, axis_index_groups=self.group_lists())

    def scatter_sum(self, value):
        return lax.psum_scatter(
            value, "dp", scatter_dimension=0, tiled=False, axis_index_groups=self.group_lists()
        )

    def front(self, pack, ew, dy, x, noise, keep):
        own = lax.all_gather(pack, "dp", axis=0, tiled=True)
        two = jnp.stack([own, self.other(own, 2)])
        w = jnp.concatenate([two, self.other(two, 1)], axis=0)
        blocks = jnp.zeros((2, E * pack.shape[0], FFS), BF16)
        for by in range(E):
            to = lax.rem(self.member + by, E)
            block = lax.dynamic_index_in_dim(ew, to, 0, False)
            came = lax.rem(self.member - by + E, E)
            block = self.shift(block, by) if by else block
            blocks = lax.dynamic_update_slice_in_dim(blocks, block, came * pack.shape[0], 1)
        blocks = self.all_groups(blocks, 1)
        blocks = jnp.swapaxes(blocks.reshape(2, E, D // E, FFS), 0, 1)
        two = jnp.stack([blocks, self.other(blocks, 2)])
        weights = jnp.concatenate([two, self.other(two, 1)], axis=0)
        chunk, *saved = attn_forward(x, w, noise, keep)
        table = (E * x.shape[0], PAD, D)
        dh, y, rows, hid, tiles = experts(
            self.member, self.gather(chunk).reshape(table), self.gather(dy).reshape(table), weights
        )
        sums = [self.scatter_sum(t.reshape((E,) + chunk.shape)) for t in (dh, y)]
        g = [jnp.concatenate([expert_grads(tiles, rows, hid, kind, base) for base in (0, 2)]) for kind in (0, 1)]
        g = jnp.stack([part.reshape(4, E, D // E, FFS) for part in g], axis=2)
        return g, jnp.stack(sums), w, *saved

    def back(self, g_low, sums, saved, x, dy, w):
        x1, qkv, o, lse, probs = saved
        dh_sum, y_sum = sums[0], sums[1]
        imgs, d_own = x.shape[0], D // self.n_dp
        passed = self.other(g_low[2:], 1)
        pair = [(g_low[s].astype(F32) + passed[s].astype(F32)).astype(BF16) for s in range(2)]
        total = (pair[0].astype(F32) + self.other(pair[1], 2).astype(F32)).astype(BF16)
        if self.groups > 1:
            total = jnp.swapaxes(total, 1, 2).reshape(D, 2, FFS)
            total = jnp.swapaxes(self.sum_groups(total, 0).reshape(E, d_own, 2, FFS), 1, 2)
        g_exp = []
        for by in range(E):
            to = lax.rem(self.member + by, E)
            block = lax.dynamic_index_in_dim(total, to, 0, False)
            g_exp.append(self.shift(block, by) if by else block)

        pack0, pack1, packs, d_tok = attn_backward(
            [dh_sum[c] for c in range(imgs)], (x1, x, dy, probs, qkv, o, lse), w, self.n_dp
        )
        passed = self.other(packs, 1)
        if self.groups > 1:
            pack0 = self.sum_groups((pack0.astype(F32) + passed[:, 0].astype(F32)).astype(BF16), 0)
            pack1 = self.sum_groups((pack1.astype(F32) + passed[:, 1].astype(F32)).astype(BF16), 0)
            passed = jnp.zeros((E, 2) + pack0.shape[1:], BF16)

        def pack_for(member):
            one, two = (lax.dynamic_index_in_dim(p, member, 0, False).astype(F32) for p in (pack0, pack1))
            came = lax.dynamic_index_in_dim(passed, member, 0, False).astype(F32)
            return one + came[0] + self.other((two + came[1]).astype(BF16), 2).astype(F32)

        total = self.sum_both_ways(pack_for)
        at = jnp.stack([_slot(self.tensor, t) for t in range(4)])

        def all_rows(own):
            across = self.other(own, 2)
            return lay_out(at, [own, across, self.other(own, 1), self.other(across, 1)])

        d_tokens = all_rows(d_tok)
        output = all_rows((x1 + y_sum.astype(F32)).astype(BF16))
        came = jnp.stack([lax.rem(self.member - by + E, E) for by in range(E)])
        return output, d_tokens, *unpack(came, g_exp), total

    def sum_both_ways(self, block_for):
        def chain(way, steps):
            total = block_for(self.behind(1 - way, steps)).astype(BF16)
            for k in range(steps - 1, -1, -1):
                total = self.along(total, way)
                if k:
                    total = (total.astype(F32) + block_for(self.behind(1 - way, k)).astype(F32)).astype(BF16)
            return total

        ahead = chain(0, E // 2)
        back = chain(1, E // 2 - 1)
        return ahead.astype(F32) + back.astype(F32) + block_for(self.member).astype(F32)

    def all_groups(self, part, dim):
        if self.groups == 1:
            return part
        size = part.shape[dim]
        shape = part.shape[:dim] + (size * self.groups,) + part.shape[dim + 1 :]
        whole = lax.dynamic_update_slice_in_dim(jnp.zeros(shape, part.dtype), part, self.group * size, dim)
        for by in range(1, self.groups):
            came = lax.rem(self.group - by + self.groups, self.groups)
            whole = lax.dynamic_update_slice_in_dim(whole, self.shift_group(part, by), came * size, dim)
        return whole

    def sum_groups(self, whole, dim):
        if self.groups == 1:
            return whole
        size = whole.shape[dim] // self.groups
        total = lax.dynamic_slice_in_dim(whole, self.group * size, size, dim).astype(F32)
        for by in range(1, self.groups):
            to = lax.rem(self.group + by, self.groups)
            part = lax.dynamic_slice_in_dim(whole, to * size, size, dim)
            total = total + self.shift_group(part, by).astype(F32)
        return total.astype(whole.dtype)


def after(value, *first):
    return lax.optimization_barrier((value, first))[0]


def _slot(tensor, t):
    apart = lax.bitwise_xor(tensor, t)
    return lax.div(apart, 2) + 2 * lax.rem(apart, 2)


def image_blocks(rows, tensor, imgs):
    first = tensor * (imgs * SEQ)
    return [
        jnp.pad(lax.dynamic_slice_in_dim(rows, first + c * SEQ, SEQ, 0), ((0, PAD - SEQ), (0, 0)))
        for c in range(imgs)
    ]


def image_lanes(lanes, tensor, imgs):
    first = tensor * (imgs * SEQ)
    return [
        jnp.pad(lax.dynamic_slice_in_dim(lanes, first + c * SEQ, SEQ, 1), ((0, 0), (0, PAD - SEQ)))
        for c in range(imgs)
    ]


def kept_pairs(routes):
    chosen = jnp.transpose(routes).reshape(1, -1)
    named = (chosen == jnp.arange(E, dtype=jnp.int32)[:, None]).astype(jnp.int32)
    kept = named * (jnp.cumsum(named, axis=1) <= CAP)
    return jnp.sum(kept.reshape(E, TOP, -1), axis=1).astype(F32)


def body(
    n_dp,
    tokens,
    ln1_gain,
    ln1_bias,
    w_qkv,
    w_attn_out,
    ln2_gain,
    ln2_bias,
    router_weight,
    w_in,
    w_expert_out,
    router_noise,
    routes,
    cotangent,
):
    move = Mover(n_dp)
    token_count = tokens.shape[0]
    imgs = token_count // SEQ // 4
    d_own = w_qkv.shape[0]
    ways = [c % 2 for c in range(imgs)]

    w_out = jnp.transpose(w_expert_out, (0, 2, 1))
    if move.groups == 1:
        pack, ew, x, dy, keep, noise = prepare(
            move.tensor, imgs, tokens, cotangent, jnp.transpose(w_qkv, (1, 0, 2)), w_attn_out,
            jnp.stack([ln1_gain, ln1_bias, ln2_gain, ln2_bias]), jnp.transpose(router_weight),
            w_in, w_out, jnp.transpose(router_noise), jnp.transpose(routes),
        )
        _, _, _, y, g_low, dh, w, *saved = front(pack, ew, dy, x, noise, keep)
        x1, qkv, o, lse, probs = saved
        output, d_tokens, g_in, g_out, g_qkv, g_attn_out, g_small = finish(
            *back(g_low, y, dh, (x1, x, dy, probs, qkv, o, lse), w)
        )
        g_qkv = jnp.transpose(g_qkv, (1, 0, 2))
    else:
        vectors = jnp.stack([ln1_gain, ln1_bias, ln2_gain, ln2_bias] + [jnp.zeros_like(ln1_gain)] * 4, axis=1)
        pack = jnp.concatenate(
            [w_qkv[:, 0], w_qkv[:, 1], w_qkv[:, 2], jnp.transpose(w_attn_out), vectors, router_weight], axis=1
        )
        pack = jnp.pad(pack, ((0, 0), (0, 128 - 16))).astype(BF16)
        ew = jnp.stack([w_in, jnp.transpose(w_expert_out, (0, 2, 1))], axis=1).astype(BF16)
        x = jnp.stack(image_blocks(tokens, move.tensor, imgs))
        dy = jnp.stack(image_blocks(cotangent, move.tensor, imgs))
        keep = jnp.stack(image_lanes(kept_pairs(routes), move.tensor, imgs))
        noise = jnp.stack(image_lanes(jnp.transpose(router_noise), move.tensor, imgs))
        g_low, sums, w, *saved = move.front(pack, ew, dy, x, noise, keep)
        output, d_tokens, g_in, g_out, total = move.back(g_low, sums, saved, x, dy, w)
        g_qkv = total[:d_own, : 9 * HD].reshape(d_own, 3, 3 * HD)
        g_attn_out = jnp.transpose(total[:d_own, 9 * HD :])
        g_small = total[d_own:, :d_own]
    return (
        output,
        d_tokens,
        g_small[0],
        g_small[1],
        g_qkv,
        g_attn_out,
        g_small[2],
        g_small[3],
        jnp.transpose(g_small[8:16]),
        g_in,
        jnp.transpose(g_out, (0, 2, 1)),
    )


def solution(mesh):
    in_specs = (
        P("dp", None),
        P("dp"),
        P("dp"),
        P("dp", None, "tensor"),
        P("tensor", "dp"),
        P("dp"),
        P("dp"),
        P("dp", None),
        P(None, "dp", "tensor"),
        P(None, "tensor", "dp"),
        P("dp", None),
        P("dp", None),
        P("dp", None),
    )
    out_specs = (
        P("dp", None),
        P("dp", None),
        P("dp"),
        P("dp"),
        P("dp", None, "tensor"),
        P("tensor", "dp"),
        P("dp"),
        P("dp"),
        P("dp", None),
        P(None, "dp", "tensor"),
        P(None, "tensor", "dp"),
    )
    return jax.shard_map(
        functools.partial(body, mesh.shape["dp"]),
        mesh=mesh,
        in_specs=in_specs,
        out_specs=out_specs,
        check_vma=False,
    )
```

```python
import functools

import jax
import jax.numpy as jnp
from jax import lax
from jax.experimental import pallas as pl
from jax.experimental.pallas import tpu as pltpu
from jax.sharding import PartitionSpec as P

D = 768
HD = 64
E = 8
TOP = 2
SEQ = 197
CAP = 689
PAD = 208
META = 200
TILE = 256
FFS = 768
EPS = 1e-06
VMEM_LIMIT = 62 * 1024 * 1024

F32 = jnp.float32
BF16 = jnp.bfloat16


def dot(a, b):
    return jnp.dot(a, b, preferred_element_type=F32)


def dot_nt(a, b):
    return lax.dot_general(a, b, (((1,), (1,)), ((), ())), preferred_element_type=F32)


def dot_tn(a, b):
    return lax.dot_general(a, b, (((0,), (0,)), ((), ())), preferred_element_type=F32)


def iota(shape, dim):
    return lax.broadcasted_iota(jnp.int32, shape, dim)


def normalise(values):
    centred = values - jnp.mean(values, axis=-1, keepdims=True)
    scale = lax.rsqrt(jnp.mean(centred * centred, axis=-1, keepdims=True) + EPS)
    return centred * scale, scale


def norm_back(grad, unit, scale, gain):
    g = grad * gain
    return scale * (
        g - jnp.mean(g, axis=-1, keepdims=True) - unit * jnp.mean(g * unit, axis=-1, keepdims=True)
    )


def params_of(w_own):
    return jnp.transpose(w_own[:, D:].astype(F32))[:16]


def attend(x, par, w_of, noise, keep, chunk_ref, x1_ref, qkv_ref, o_ref, lse_ref, probs_ref):
    x = x.astype(F32)
    unit, _ = normalise(x)
    h1 = (unit * par[0:1] + par[1:2]).astype(BF16)
    acc = x
    lse = jnp.zeros((PAD, 128), F32)
    key_ok = iota((PAD, PAD), 1) < SEQ
    lane = iota((PAD, 128), 1)
    for r in range(4):
        w = w_of(r)
        qkv = dot(h1, w[:, : 9 * HD]).astype(BF16)
        qkv_ref[r] = qkv
        outs = []
        for h in range(3):
            q = qkv[:, h * HD : (h + 1) * HD]
            k = qkv[:, (3 + h) * HD : (4 + h) * HD]
            v = qkv[:, (6 + h) * HD : (7 + h) * HD]
            s = jnp.where(key_ok, dot_nt(q, k) * HD ** (-0.5), -1e30)
            top = jnp.max(s, axis=-1, keepdims=True)
            p = jnp.exp(s - top)
            total = jnp.sum(p, axis=-1, keepdims=True)
            outs.append(dot((p * (1.0 / total)).astype(BF16), v).astype(BF16))
            lse = jnp.where(lane == 3 * r + h, top + jnp.log(total), lse)
        o = jnp.concatenate(outs, axis=1)
        o_ref[r] = o
        acc = acc + dot_nt(o, w[:, 9 * HD : D])
    lse_ref[...] = lse
    x1_ref[...] = acc
    unit2, _ = normalise(acc)
    h2 = (unit2 * par[2:3] + par[3:4]).astype(BF16)
    logits = dot_nt(par[8:16].astype(BF16), h2) + noise
    e = jnp.exp(logits - jnp.max(logits, axis=0, keepdims=True))
    probs = e / jnp.sum(e, axis=0, keepdims=True)
    probs_ref[...] = probs
    gates = jnp.where(keep > 0, probs, -1.0)
    chunk_ref[...] = h2
    tail = jnp.concatenate([gates, jnp.zeros((8, D - PAD), F32)], axis=1)
    low = h2[PAD - 16 :, :].astype(F32)
    chunk_ref[PAD - 16 :, :] = jnp.concatenate([low[:8], tail], axis=0).astype(BF16)


def attn_shapes(imgs):
    return (
        jax.ShapeDtypeStruct((imgs, PAD, D), F32),
        jax.ShapeDtypeStruct((imgs, 4, PAD, 9 * HD), BF16),
        jax.ShapeDtypeStruct((imgs, 4, PAD, 3 * HD), BF16),
        jax.ShapeDtypeStruct((imgs, PAD, 128), F32),
        jax.ShapeDtypeStruct((imgs, E, PAD), F32),
    )


def attn_forward_kernel(imgs, x_ref, w_ref, noise_ref, keep_ref, chunk_ref, *saved):
    par = params_of(w_ref[0])
    for c in range(imgs):
        attend(
            x_ref[c], par, lambda r: w_ref[r], noise_ref[c], keep_ref[c],
            chunk_ref.at[c], *(ref.at[c] for ref in saved),
        )


def attn_forward(x, w, noise, keep):
    imgs = x.shape[0]
    vm = pl.BlockSpec(memory_space=pltpu.VMEM)
    return pl.pallas_call(
        functools.partial(attn_forward_kernel, imgs),
        out_shape=(jax.ShapeDtypeStruct((imgs, PAD, D), BF16),) + attn_shapes(imgs),
        in_specs=[vm] * 4,
        out_specs=(vm,) * 6,
        compiler_params=pltpu.CompilerParams(vmem_limit_bytes=VMEM_LIMIT),
        cost_estimate=pl.CostEstimate(flops=6 * 10**9, bytes_accessed=10**7, transcendentals=2 * 10**6),
        name="attn_forward",
    )(x, w, noise, keep)


def ring_place(member):
    odd = lax.rem(member, 2)
    half = lax.div(member, 2)
    return half + odd * (E - 1 - 2 * half)


def ring_member(place):
    late = lax.div(place, E // 2)
    return 2 * place + late * (2 * E - 1 - 4 * place)


class Peers:
    def __init__(self):
        dp = lax.axis_index("dp")
        tensor = lax.axis_index("tensor")
        self.member = lax.rem(dp, E)
        self.base = dp - self.member
        self.place = ring_place(self.member)
        self.across = {"tensor": lax.rem(tensor + 2, 4)}
        self.core = {"tensor": tensor + 1 - 2 * lax.rem(tensor, 2)}
        self.next = ({"dp": self.base + self.behind(1, 1)}, {"dp": self.base + self.behind(0, 1)})
        self.sends = []

    def behind(self, way, k):
        step = E - k if way == 0 else k
        return ring_member(lax.rem(self.place + step, E))

    def ahead(self, by):
        return lax.rem(self.member + by, E)

    def came(self, by):
        return lax.rem(self.member + E - by, E)

    def meet(self):
        barrier = pltpu.get_barrier_semaphore()
        others = [{"dp": self.base + self.ahead(by)} for by in range(1, E)] + [self.across, self.core]
        for device in others:
            pl.semaphore_signal(barrier, inc=1, device_id=device, device_id_type=pl.DeviceIdType.MESH)
        pl.semaphore_wait(barrier, len(others))

    def send(self, src, dst, sems, at, device):
        copy = pltpu.make_async_remote_copy(
            src_ref=src,
            dst_ref=dst,
            send_sem=sems[0].at[at],
            recv_sem=sems[1].at[at],
            device_id=device,
            device_id_type=pl.DeviceIdType.MESH,
        )
        copy.start()
        self.sends.append(copy)
        return copy


def expert_step(x, dy, gate, w_ref, g_ref, y_ref, dx_ref, meanwhile):
    weight = jnp.maximum(gate, 0.0)
    d_rows = (dy.astype(F32) * weight).astype(BF16)

    def hidden(i, carry):
        r = 2 * lax.rem(i, 2) + lax.div(i, 2)
        w1 = w_ref[r, :, 0].reshape(D, FFS)
        w2 = w_ref[r, :, 1].reshape(D, FFS)
        a = dot(x, w1)
        a2 = a * a
        th = jnp.tanh(0.7978845608028654 * a * (1.0 + 0.044715 * a2))
        half = 0.5 * (1.0 + th)
        hid = (a * half).astype(BF16)
        slope = half + 0.5 * a * (1.0 - th * th) * (0.7978845608028654 * (1.0 + 3 * 0.044715 * a2))
        da = (dot(d_rows, w2) * slope).astype(BF16)
        y_ref[...] += dot_nt(hid, w2)
        dx_ref[...] += dot_nt(da, w1)
        g_ref[r, 0] += dot_tn(x, da)
        g_ref[r, 1] += dot_tn(d_rows, hid)
        meanwhile(i)
        return carry

    y_ref[...] = jnp.zeros_like(y_ref)
    dx_ref[...] = jnp.zeros_like(dx_ref)
    lax.fori_loop(0, 4, hidden, 0)
    y = y_ref[...]
    dgate = jnp.where(gate >= 0, jnp.sum(dy.astype(F32) * y, axis=1, keepdims=True), 0.0)
    return (y * weight).astype(BF16), dx_ref[...], dgate


GIVEN, PASSED, DY_AT = (1, 2, 4, 6, 7), (1, 3), 3
HOP0, PASSED_EX = 5, 4
NEXT_AT, SUMS_AT, Y_AT = 0, 3, 6
HOPS_AT = ()


def front_kernel(
    imgs, pack_ref, ew_ref, dy_ref, x_ref, noise_ref, keep_ref,
    h_out, dy_out, t_in, y_out, y_first, g_out, sum_out, w_out, x1_ref, qkv_ref, o_ref, lse_ref, probs_ref,
    w_s, chunk_s, we_s, g_s, xs, dys, y_s, dx_s, t_s, own_s, y_low, pass_s, g_low,
    p_s, p_r, px_s, px_r, pc_s, pc_r, d_s, d_r, h_s, h_r, e_s, e_r, ex_s, ex_r, ec_s, ec_r, t_ss, t_r, local, stage, y_sem, g_sem, yf_s, yf_r,
):
    peers = Peers()
    member = peers.member
    d_own = pack_ref.shape[0]
    half = E // 2
    peers.meet()

    def rows(of):
        return pl.ds(pl.multiple_of(of * d_own, 16), d_own)

    own_pack = pltpu.make_async_copy(pack_ref, w_s.at[0, rows(member)], local.at[0])
    own_pack.start()

    ring, px, pc = {}, {}, {}

    def pass_pack(number, of, src, way=None, k=None):
        if way is not None:
            ring[way, k] = peers.send(src, w_s.at[0, rows(of)], (p_s, p_r), (way, k), peers.next[way])
        px[number] = peers.send(src, w_s.at[1, rows(of)], (px_s, px_r), number, peers.across)
        pc[0, number] = peers.send(src, w_s.at[2, rows(of)], (pc_s, pc_r), (0, number), peers.core)

    arrivals = [(0, k) if i == 0 else (1, k) for k in range(1, half + 1) for i in range(2 if k < half else 1)]
    owners = [member] + [peers.behind(way, k) for way, k in arrivals]

    def pass_x(number):
        px[number].wait_recv()
        at = rows(owners[number])
        pc[1, number] = peers.send(w_s.at[1, at], w_s.at[3, at], (pc_s, pc_r), (1, number), peers.core)

    far = (1, 7, 2, 6, 3, 5, 4)
    e_copy, ex, ec = {}, {}, {}

    def give_e(part):
        for by in part:
            to = peers.ahead(by)
            e_copy[by] = peers.send(ew_ref.at[to], we_s.at[0, member], (e_s, e_r), by, {"dp": peers.base + to})

    def pass_e(by):
        if by:
            e_copy[by].wait_recv()
        of = peers.came(by)
        src = we_s.at[0, of] if by else ew_ref.at[member]
        ex[by] = peers.send(src, we_s.at[1, of], (ex_s, ex_r), by, peers.across)
        ec[0, by] = peers.send(src, we_s.at[2, of], (ec_s, ec_r), (0, by), peers.core)

    def slice_copy(to, of, sent, got, at, device):
        return pltpu.make_async_remote_copy(
            src_ref=we_s.at[0 if to == 1 else 1, of],
            dst_ref=we_s.at[to, of],
            send_sem=sent.at[at],
            recv_sem=got.at[at],
            device_id=device,
            device_id_type=pl.DeviceIdType.MESH,
        )

    def ex_core(by):
        return slice_copy(3, peers.came(by), ec_s, ec_r, (1, by), peers.core)

    def pass_ex(by):
        of = peers.came(by)
        slice_copy(1, of, ex_s, ex_r, by, peers.across).wait_recv()
        ex_core(by).start()

    def block_at(c, k):
        return peers.behind(c % 2, k) * imgs + c

    def row_copy(out, sems, c, k, src=None):
        at = block_at(c, k)
        return pltpu.make_async_remote_copy(
            src_ref=out.at[at] if src is None else src,
            dst_ref=out.at[at],
            send_sem=sems[0].at[c, k],
            recv_sem=sems[1].at[c, k],
            device_id=peers.next[c % 2],
            device_id_type=pl.DeviceIdType.MESH,
        )

    h_sems, d_sems = (h_s, h_r), (d_s, d_r)

    def row_hop(k):
        for c in range(imgs):
            for out, sems in ((h_out, h_sems), (dy_out, d_sems)):
                row_copy(out, sems, c, k - 1).wait_recv()
                row_copy(out, sems, c, k).start()

    def give_dy():
        for c in range(imgs):
            row_copy(dy_out, d_sems, c, 0, dy_ref.at[c]).start()

    ring[0, 0] = peers.send(pack_ref, w_s.at[0, rows(member)], (p_s, p_r), (0, 0), peers.next[0])
    pass_pack(0, member, pack_ref, 1, 0)
    give_e(far[:GIVEN[0]])
    pass_e(0)
    if DY_AT == 0:
        give_dy()
    keepers = [
        pltpu.make_async_copy(ew_ref.at[member], we_s.at[0, member], local.at[2]),
    ] + [
        pltpu.make_async_copy(dy_ref.at[c], dy_out.at[member * imgs + c], local.at[3 + c]) for c in range(imgs)
    ]
    for copy in keepers:
        copy.start()
    for number, (way, k) in enumerate(arrivals, 1):
        ring[way, k - 1].wait_recv()
        of = owners[number]
        last = half if way == 0 else half - 1
        pass_pack(number, of, w_s.at[0, rows(of)], way if k < last else None, k)
        if number >= 2:
            pass_x(number - 2)
        if number == 4:
            give_e(far[GIVEN[0]:GIVEN[1]])
    give_e(far[GIVEN[1]:GIVEN[2]])
    if DY_AT == 1:
        give_dy()
    for number in range(len(arrivals) - 1, len(arrivals) + 1):
        pass_x(number)
    for number in range(E):
        pc[0, number].wait_recv()
        pc[1, number].wait_recv()
    own_pack.wait()
    keepers.append(pltpu.make_async_copy(w_s, w_out, local.at[1]))
    keepers[-1].start()

    par = params_of(w_s[0])
    done = 0
    for c in range(imgs):
        for by in far[done : PASSED[c]]:
            pass_e(by)
            pass_ex((0, *far)[done])
            done += 1
        attend(
            x_ref[c], par, lambda r: w_s[r], noise_ref[c], keep_ref[c],
            chunk_s.at[c], *(ref.at[c] for ref in (x1_ref, qkv_ref, o_ref, lse_ref, probs_ref)),
        )
        if HOP0 == 0:
            row_copy(h_out, h_sems, c, 0, chunk_s.at[c]).start()
        keepers.append(
            pltpu.make_async_copy(chunk_s.at[c], h_out.at[member * imgs + c], local.at[3 + imgs + c])
        )
        keepers[-1].start()
        give_e(far[GIVEN[2 + c]:GIVEN[3 + c]])
    if DY_AT == 2:
        give_dy()

    def first_hops():
        for c in range(imgs):
            row_copy(h_out, h_sems, c, 0, chunk_s.at[c]).start()
        if DY_AT == 3:
            give_dy()

    for i, by in enumerate(far):
        if i >= done:
            pass_e(by)
            if i <= PASSED_EX:
                pass_ex((0, *far)[i])
        if HOP0 and i == HOP0:
            first_hops()
        if i in HOPS_AT:
            row_hop(1 + HOPS_AT.index(i))
    g_s[...] = jnp.zeros_like(g_s)
    for by in range(E):
        ec[0, by].wait_recv()
    for copy in keepers:
        copy.wait()

    row16 = iota((16, D), 0)
    eye = iota((PAD, PAD), 0) == iota((PAD, PAD), 1)

    def sum_copy(c, k):
        return pltpu.make_async_remote_copy(
            src_ref=pass_s.at[lax.rem(k, 2), c],
            dst_ref=t_in.at[k - 1, c],
            send_sem=t_ss.at[c, k - 1],
            recv_sem=t_r.at[c, k - 1],
            device_id=peers.next[c % 2],
            device_id_type=pl.DeviceIdType.MESH,
        )

    def sums_to_hand(k):
        return [pltpu.make_async_copy(t_in.at[k - 2, c], t_s.at[c], stage.at[2, c]) for c in range(imgs)]

    def rows_to_hand(k):
        slot = lax.rem(k, 2)
        return [
            pltpu.make_async_copy(out.at[block_at(c, k)], held.at[slot, c], stage.at[i, c])
            for c in range(imgs)
            for i, (out, held) in enumerate(((h_out, xs), (dy_out, dys)))
        ]

    def start(copies):
        for copy in copies:
            copy.start()

    def finish(copies):
        for copy in copies:
            copy.wait()

    def y_copy(c):
        return pltpu.make_async_remote_copy(
            src_ref=y_out.at[1, c],
            dst_ref=y_first.at[c],
            send_sem=yf_s.at[c],
            recv_sem=yf_r.at[c],
            device_id=peers.next[c % 2],
            device_id_type=pl.DeviceIdType.MESH,
        )

    def keep_y(k):
        return pltpu.make_async_copy(y_low, y_out.at[k], y_sem)

    def step(k, carry):
        slot = lax.rem(k, 2)
        finish(rows_to_hand(k))

        def meanwhile(r):
            @pl.when((r == 0) & (k == 0))
            def _():
                for by in far[PASSED_EX:]:
                    pass_ex(by)

            @pl.when((r == 1) & (k == 0))
            def _():
                for by in range(E):
                    ex_core(by).wait_recv()

            for c in range(imgs):
                for out, sems in ((h_out, h_sems), (dy_out, d_sems)):

                    @pl.when((r == NEXT_AT) & (k >= len(HOPS_AT)) & (k < E - 1))
                    def _():
                        row_copy(out, sems, c, k).wait_recv()

                    @pl.when((r == NEXT_AT) & (k >= len(HOPS_AT)) & (k < E - 2))
                    def _():
                        row_copy(out, sems, c, k + 1).start()

            @pl.when((r == NEXT_AT) & (k < E - 1))
            def _():
                start(rows_to_hand(k + 1))

            @pl.when((r == SUMS_AT) & (k >= 2))
            def _():
                for c in range(imgs):
                    sum_copy(c, k - 1).wait_recv()
                start(sums_to_hand(k))

        columns = []
        for c in range(imgs):
            meta = xs[slot, c, PAD - 16 :, :].astype(F32)
            line = jnp.sum(jnp.where(row16 == 8 + member, meta, 0.0), axis=0, keepdims=True)[:, :PAD]
            columns.append(jnp.sum(jnp.where(eye, line, 0.0), axis=1, keepdims=True))
        y, dx, dgate = expert_step(
            xs[slot].reshape(imgs * PAD, D), dys[slot].reshape(imgs * PAD, D), jnp.concatenate(columns, axis=0),
            we_s, g_s, y_s, dx_s, meanwhile,
        )

        @pl.when(k >= 3)
        def _():
            for c in range(imgs):
                sum_copy(c, k - 2).wait_send()

        @pl.when(k >= 1)
        def _():
            keep_y(k - 1).wait()

        for c in range(imgs):
            span = slice(c * PAD, (c + 1) * PAD)
            line = jnp.sum(jnp.where(eye, dgate[span], 0.0), axis=0, keepdims=True)
            line = jnp.concatenate([line, jnp.zeros((1, D - PAD), F32)], axis=1)
            tail = dx[span][PAD - 16 :] + jnp.where(row16 == 8 + member, line, 0.0)
            pass_s[slot, c] = jnp.concatenate([dx[span][: PAD - 16], tail], axis=0).astype(BF16)
            y_low[c] = y[span]

        keep_y(k).start()

        @pl.when(k == 0)
        def _():
            own_s[...] = pass_s[0]

        @pl.when(k >= 2)
        def _():
            finish(sums_to_hand(k))
            pass_s[slot] = (pass_s[slot].astype(F32) + t_s[...].astype(F32)).astype(BF16)

        @pl.when(k >= 1)
        def _():
            for c in range(imgs):
                sum_copy(c, k).start()

        @pl.when(k == Y_AT)
        def _():
            for c in range(imgs):
                y_copy(c).start()

        return carry

    start(rows_to_hand(0))
    lax.fori_loop(0, E, step, 0)

    for i in range(8):
        r, kind = i // 2, i % 2
        if i >= 2:
            pltpu.make_async_copy(g_low.at[i % 2], g_out.at[r, :, kind], g_sem.at[i % 2]).wait()
        g_low[i % 2] = g_s[r, kind].astype(BF16).reshape(E, d_own, FFS)
        pltpu.make_async_copy(g_low.at[i % 2], g_out.at[r, :, kind], g_sem.at[i % 2]).start()
    for c in range(imgs):
        sum_copy(c, E - 1).wait_recv()
    start(sums_to_hand(E))
    finish(sums_to_hand(E))
    sum_out[...] = (own_s[...].astype(F32) + t_s[...].astype(F32)).astype(BF16)
    keep_y(E - 1).wait()
    for c in range(imgs):
        y_copy(c).wait()
    for i in range(2):
        pltpu.make_async_copy(g_low.at[i], g_out.at[3, :, i], g_sem.at[i]).wait()
    for c in range(imgs):
        sum_copy(c, E - 2).wait_send()
        sum_copy(c, E - 1).wait_send()
        for k in range(E - 1):
            row_copy(h_out, h_sems, c, k).wait_send()
            row_copy(dy_out, d_sems, c, k).wait_send()
    for by in range(E):
        ex_core(by).wait_send()
    for copy in peers.sends:
        copy.wait_send()


def front(pack, ew, dy, x, noise, keep):
    imgs = x.shape[0]
    d_own = pack.shape[0]
    vm = pl.BlockSpec(memory_space=pltpu.VMEM)
    hbm = pl.BlockSpec(memory_space=pl.ANY)
    table = jax.ShapeDtypeStruct((E * imgs, PAD, D), BF16)
    dma = pltpu.SemaphoreType.DMA
    rows = (imgs, PAD, D)
    return pl.pallas_call(
        functools.partial(front_kernel, imgs),
        out_shape=(
            table,
            table,
            jax.ShapeDtypeStruct((E - 1,) + rows, BF16),
            jax.ShapeDtypeStruct((E,) + rows, BF16),
            jax.ShapeDtypeStruct(rows, BF16),
            jax.ShapeDtypeStruct((4, E, 2, d_own, FFS), BF16),
            jax.ShapeDtypeStruct(rows, BF16),
            jax.ShapeDtypeStruct((4, E * d_own, D + 128), BF16),
        )
        + attn_shapes(imgs),
        in_specs=[vm, hbm, hbm, vm, vm, vm],
        out_specs=(hbm,) * 6 + (vm, hbm) + (vm,) * 5,
        scratch_shapes=[
            pltpu.VMEM((4, E * d_own, D + 128), BF16),
            pltpu.VMEM((imgs, PAD, D), BF16),
            pltpu.VMEM((4, E, 2, d_own, FFS), BF16),
            pltpu.VMEM((4, 2, D, FFS), F32),
            pltpu.VMEM((2, imgs, PAD, D), BF16),
            pltpu.VMEM((2, imgs, PAD, D), BF16),
            pltpu.VMEM((imgs * PAD, D), F32),
            pltpu.VMEM((imgs * PAD, D), F32),
            pltpu.VMEM(rows, BF16),
            pltpu.VMEM(rows, BF16),
            pltpu.VMEM(rows, BF16),
            pltpu.VMEM((2,) + rows, BF16),
            pltpu.VMEM((2, E, d_own, FFS), BF16),
            dma((2, 4)), dma((2, 4)), dma((E,)), dma((E,)), dma((2, E)), dma((2, E)),
            dma((imgs, E - 1)), dma((imgs, E - 1)), dma((imgs, E - 1)), dma((imgs, E - 1)),
            dma((E,)), dma((E,)), dma((E,)), dma((E,)), dma((2, E)), dma((2, E)),
            dma((imgs, E - 1)), dma((imgs, E - 1)),
            dma((3 + 2 * imgs,)), dma((3, imgs)), dma(()), dma((2,)), dma((imgs,)), dma((imgs,)),
        ],
        compiler_params=pltpu.CompilerParams(
            vmem_limit_bytes=VMEM_LIMIT, collective_id=0, has_side_effects=True
        ),
        cost_estimate=pl.CostEstimate(flops=10**11, bytes_accessed=10**8, transcendentals=2 * 10**7),
        name="front",
    )(pack, ew, dy, x, noise, keep)


def expert_kernel(nb, who_ref, *refs):
    h_in, dy_in, w_in = refs[:3]
    outs = refs[3:]
    dx_out, y_out, rows_out, hid_out, tiles_ref = outs[:5]
    (h, dy, y_t, dx_t, w_s, gate_s, slot_s, dgate_s, xs, dys, hid_s, rows_s, lo_s, hi_s, in_sem, out_sem, row_sem, hid_sem, w_sem) = outs[5:]
    me = who_ref[0]
    loads = [
        pltpu.make_async_copy(h_in, h, in_sem.at[0]),
        pltpu.make_async_copy(dy_in, dy, in_sem.at[1]),
    ]
    for b in range(E):
        at = pl.ds(b * (D // E), D // E)
        for r in range(4):
            loads.append(pltpu.make_async_copy(w_in.at[r, b], w_s.at[r, :, at], w_sem.at[r, b]))
    for copy in loads:
        copy.start()
    y_t[...] = jnp.zeros_like(y_t)
    dx_t[...] = jnp.zeros_like(dx_t)
    dgate_s[...] = jnp.zeros_like(dgate_s)
    for copy in loads:
        copy.wait()

    row16 = iota((16, D), 0)
    for b in range(nb):
        meta = h[b, PAD - 16 : PAD, :].astype(F32)
        gate_s[b : b + 1, :] = jnp.sum(jnp.where(row16 == 8 + me, meta, 0.0), axis=0, keepdims=True)[:, :PAD]
    gates = gate_s[...]
    named = (gates >= 0) & (iota((nb, PAD), 1) < SEQ)
    ones = named.astype(F32).astype(BF16)
    upto = dot(ones, (iota((PAD, PAD), 0) <= iota((PAD, PAD), 1)).astype(F32).astype(BF16))
    count = dot(ones, jnp.ones((PAD, PAD), BF16)).astype(BF16)
    before = dot((iota((nb, nb), 0) > iota((nb, nb), 1)).astype(F32).astype(BF16), count)
    slot_s[...] = jnp.where(named, before + upto - 1.0, -1.0).astype(jnp.int32)
    ends = jnp.where(named, before + upto, before)
    for b in range(nb):
        lo_s[b] = jnp.max(before[b : b + 1, :]).astype(jnp.int32)
        hi_s[b] = jnp.max(ends[b : b + 1, :]).astype(jnp.int32)
    tiles = lax.div(hi_s[nb - 1] + TILE - 1, TILE)
    tiles_ref[0] = tiles

    def meets(b, first):
        return (lo_s[b] < first + TILE) & (hi_s[b] > first) & (hi_s[b] > lo_s[b])

    def place(b, first):
        return iota((TILE, PAD), 0) + first == slot_s[pl.ds(b, 1), :]

    def step(t, carry):
        first = t * TILE
        slot = lax.rem(t, 2)
        xs[...] = jnp.zeros_like(xs)
        dys[...] = jnp.zeros_like(dys)

        def collect(b, gcol):
            def one(gcol):
                hit = place(b, first)
                p = hit.astype(F32).astype(BF16)
                xs[...] += dot(p, h[b])
                dys[...] += dot(p, dy[b])
                return gcol + jnp.sum(jnp.where(hit, gate_s[pl.ds(b, 1), :], 0.0), axis=1, keepdims=True)

            return lax.cond(meets(b, first), one, lambda g: g, gcol)

        gcol = lax.fori_loop(0, nb, collect, jnp.zeros((TILE, 1), F32))

        def drain(s):
            pltpu.make_async_copy(rows_s.at[s], rows_out.at[:, pl.ds(0, TILE)], row_sem.at[s]).wait()
            pltpu.make_async_copy(hid_s.at[s], hid_out.at[:, pl.ds(0, TILE)], hid_sem.at[s]).wait()

        @pl.when(t >= 2)
        def _():
            drain(slot)

        x = xs[...].astype(BF16)
        g_rows = (dys[...] * gcol).astype(BF16)
        rows_s[slot, 0] = x
        rows_s[slot, 1] = g_rows
        y = jnp.zeros((TILE, D), F32)
        dx = jnp.zeros((TILE, D), F32)
        for r in range(4):
            w1, w2 = w_s.at[r, 0], w_s.at[r, 1]
            a = dot(x, w1[...])
            a2 = a * a
            th = jnp.tanh(0.7978845608028654 * a * (1.0 + 0.044715 * a2))
            half = 0.5 * (1.0 + th)
            hid = (a * half).astype(BF16)
            slope = half + 0.5 * a * (1.0 - th * th) * (0.7978845608028654 * (1.0 + 3 * 0.044715 * a2))
            da = (dot(g_rows, w2[...]) * slope).astype(BF16)
            y = y + dot_nt(hid, w2[...])
            dx = dx + dot_nt(da, w1[...])
            hid_s[slot, 0, :, r * FFS : (r + 1) * FFS] = da
            hid_s[slot, 1, :, r * FFS : (r + 1) * FFS] = hid
        at = pl.ds(pl.multiple_of(first, TILE), TILE)
        pltpu.make_async_copy(rows_s.at[slot], rows_out.at[:, at], row_sem.at[slot]).start()
        pltpu.make_async_copy(hid_s.at[slot], hid_out.at[:, at], hid_sem.at[slot]).start()
        dgate = jnp.sum(dys[...] * y, axis=1, keepdims=True)
        y_low = (y * gcol).astype(BF16)
        dx_low = dx.astype(BF16)

        def give(b, carry):
            @pl.when(meets(b, first))
            def _():
                hit = place(b, first)
                p = hit.astype(F32).astype(BF16)
                y_t[b] = y_t[b] + dot_tn(p, y_low).astype(BF16)
                dx_t[b] = dx_t[b] + dot_tn(p, dx_low).astype(BF16)
                dgate_s[pl.ds(b, 1), :] += jnp.sum(jnp.where(hit, dgate, 0.0), axis=0, keepdims=True)

            return carry

        lax.fori_loop(0, nb, give, 0)
        return carry

    lax.fori_loop(0, tiles, step, 0)
    for back in (1, 2):

        @pl.when(tiles >= back)
        def _():
            s = lax.rem(tiles - back, 2)
            pltpu.make_async_copy(rows_s.at[s], rows_out.at[:, pl.ds(0, TILE)], row_sem.at[s]).wait()
            pltpu.make_async_copy(hid_s.at[s], hid_out.at[:, pl.ds(0, TILE)], hid_sem.at[s]).wait()

    for b in range(nb):
        tail = dx_t[b, PAD - 16 : PAD, :].astype(F32)
        line = jnp.concatenate([dgate_s[b : b + 1, :], jnp.zeros((1, D - PAD), F32)], axis=1)
        dx_t[b, PAD - 16 : PAD, :] = (tail + jnp.where(row16 == 8 + me, line, 0.0)).astype(BF16)
    stores = [
        pltpu.make_async_copy(dx_t, dx_out, out_sem.at[0]),
        pltpu.make_async_copy(y_t, y_out, out_sem.at[1]),
    ]
    for copy in stores:
        copy.start()
    for copy in stores:
        copy.wait()


def expert_rows(nb):
    return -(-nb * SEQ // TILE) * TILE


def experts(member, h_all, dy_all, weights):
    nb = h_all.shape[0]
    rows = expert_rows(nb)
    hbm = pl.BlockSpec(memory_space=pl.ANY)
    sm = pl.BlockSpec(memory_space=pltpu.SMEM)
    table = jax.ShapeDtypeStruct((nb, PAD, D), BF16)
    return pl.pallas_call(
        functools.partial(expert_kernel, nb),
        out_shape=[
            table,
            table,
            jax.ShapeDtypeStruct((2, rows, D), BF16),
            jax.ShapeDtypeStruct((2, rows, 4 * FFS), BF16),
            jax.ShapeDtypeStruct((1,), jnp.int32),
        ],
        in_specs=[sm, hbm, hbm, hbm],
        out_specs=[hbm] * 4 + [sm],
        scratch_shapes=[
            pltpu.VMEM((nb, PAD, D), BF16),
            pltpu.VMEM((nb, PAD, D), BF16),
            pltpu.VMEM((nb, PAD, D), BF16),
            pltpu.VMEM((nb, PAD, D), BF16),
            pltpu.VMEM((4, 2, D, FFS), BF16),
            pltpu.VMEM((nb, PAD), F32),
            pltpu.VMEM((nb, PAD), jnp.int32),
            pltpu.VMEM((nb, PAD), F32),
            pltpu.VMEM((TILE, D), F32),
            pltpu.VMEM((TILE, D), F32),
            pltpu.VMEM((2, 2, TILE, 4 * FFS), BF16),
            pltpu.VMEM((2, 2, TILE, D), BF16),
            pltpu.SMEM((nb,), jnp.int32),
            pltpu.SMEM((nb,), jnp.int32),
            pltpu.SemaphoreType.DMA((2,)),
            pltpu.SemaphoreType.DMA((2,)),
            pltpu.SemaphoreType.DMA((2,)),
            pltpu.SemaphoreType.DMA((2,)),
            pltpu.SemaphoreType.DMA((4, E)),
        ],
        compiler_params=pltpu.CompilerParams(vmem_limit_bytes=VMEM_LIMIT),
        cost_estimate=pl.CostEstimate(flops=30 * 10**9, bytes_accessed=4 * 10**7, transcendentals=4 * 10**6),
        name="experts",
    )(member.reshape(1), h_all, dy_all, weights)


def expert_grad_kernel(tiles_ref, rows_ref, hid_ref, out_ref, acc):
    acc[...] = jnp.zeros_like(acc)

    def step(t, carry):
        at = pl.ds(pl.multiple_of(t * TILE, TILE), TILE)
        acc[...] += dot_tn(rows_ref[0, at, :], hid_ref[0, at, :])
        return carry

    lax.fori_loop(0, tiles_ref[0], step, 0)
    out_ref[0] = acc[...].astype(BF16)


def expert_grads(tiles, rows, hid, kind, base):
    n = rows.shape[1]
    return pl.pallas_call(
        expert_grad_kernel,
        grid_spec=pltpu.PrefetchScalarGridSpec(
            num_scalar_prefetch=1,
            grid=(2,),
            in_specs=[
                pl.BlockSpec((1, n, D), lambda s, _: (kind, 0, 0)),
                pl.BlockSpec((1, n, FFS), lambda s, _: (kind, 0, base + s)),
            ],
            out_specs=pl.BlockSpec((1, D, FFS), lambda s, _: (s, 0, 0)),
            scratch_shapes=[pltpu.VMEM((D, FFS), F32)],
        ),
        out_shape=jax.ShapeDtypeStruct((2, D, FFS), BF16),
        compiler_params=pltpu.CompilerParams(vmem_limit_bytes=VMEM_LIMIT),
        cost_estimate=pl.CostEstimate(flops=4 * 10**9, bytes_accessed=15 * 10**6, transcendentals=0),
        name="expert_grads",
    )(tiles, rows, hid)


def unpack_kernel(who_ref, *refs):
    blocks, (in_ref, out_ref) = refs[:E], refs[E:]
    for by in range(E):
        in_ref[who_ref[by]] = blocks[by][0].astype(F32)
        out_ref[who_ref[by]] = blocks[by][1].astype(F32)


def unpack(who, blocks):
    vm = pl.BlockSpec(memory_space=pltpu.VMEM)
    whole = jax.ShapeDtypeStruct((E,) + blocks[0].shape[1:], F32)
    return pl.pallas_call(
        unpack_kernel,
        out_shape=(whole, whole),
        in_specs=[pl.BlockSpec(memory_space=pltpu.SMEM)] + [vm] * E,
        out_specs=(vm, vm),
        compiler_params=pltpu.CompilerParams(vmem_limit_bytes=VMEM_LIMIT),
        cost_estimate=pl.CostEstimate(flops=10**6, bytes_accessed=7 * 10**6, transcendentals=0),
        name="unpack",
    )(who, *blocks)


def lay_out_kernel(imgs, at_ref, *refs):
    parts, out_ref, held, sem = refs[:4], refs[4], refs[5], refs[6]
    copies = [pltpu.make_async_copy(parts[s], held.at[s], sem.at[s]) for s in range(4)]
    for copy in copies:
        copy.start()
    for copy in copies:
        copy.wait()
    for i in range(4 * imgs):
        out_ref[i * SEQ : (i + 1) * SEQ, :] = held[at_ref[i // imgs], i % imgs, :SEQ, :]


def lay_out(at, parts):
    imgs = parts[0].shape[0]
    hbm = pl.BlockSpec(memory_space=pl.ANY)
    return pl.pallas_call(
        functools.partial(lay_out_kernel, imgs),
        out_shape=jax.ShapeDtypeStruct((4 * imgs * SEQ, D), BF16),
        in_specs=[pl.BlockSpec(memory_space=pltpu.SMEM)] + [hbm] * 4,
        out_specs=pl.BlockSpec(memory_space=pltpu.VMEM),
        scratch_shapes=[pltpu.VMEM((4, imgs, PAD, D), BF16), pltpu.SemaphoreType.DMA((4,))],
        compiler_params=pltpu.CompilerParams(vmem_limit_bytes=VMEM_LIMIT),
        cost_estimate=pl.CostEstimate(flops=10**6, bytes_accessed=5 * 10**6, transcendentals=0),
        name="lay_out",
    )(at, *parts)


class Backward:
    def __init__(self, imgs, dh_of, saved, w_ref, dx1_s, low_s, h1_s, dh1_s, dqkv_s, o_s):
        self.imgs, self.dh_of, self.saved, self.w_ref = imgs, dh_of, saved, w_ref
        self.dx1_s, self.low_s, self.h1_s, self.dh1_s, self.dqkv_s, self.o_s = dx1_s, low_s, h1_s, dh1_s, dqkv_s, o_s
        self.par = params_of(w_ref[0])
        self.row_ok = iota((PAD, 1), 0) < SEQ
        self.started = False

    def span(self, c):
        return slice(c * PAD, (c + 1) * PAD)

    def first(self):
        x1_in, x_in, dy_in, probs_in = self.saved[:4]
        par, row_ok = self.par, self.row_ok
        lane_ok = iota((E, PAD), 1) < SEQ
        router = par[8:16].astype(BF16)
        gain = jnp.zeros((1, D), F32)
        bias = jnp.zeros((1, D), F32)
        g_router = jnp.zeros((E, D), F32)
        for c in range(self.imgs):
            arrived = self.dh_of(c).astype(F32)
            dgate = arrived[PAD - 8 :, :PAD]
            probs = probs_in[c]
            dlogits = probs * (dgate - jnp.sum(probs * dgate, axis=0, keepdims=True))
            dlogits = jnp.where(lane_ok, dlogits, 0.0).astype(BF16)
            unit, scale = normalise(x1_in[c])
            h2 = (unit * par[2:3] + par[3:4]).astype(BF16)
            g_router = g_router + dot(dlogits, h2)
            dh2 = jnp.where(row_ok, arrived + dot_tn(dlogits, router), 0.0)
            gain = gain + jnp.sum(dh2 * unit, axis=0, keepdims=True)
            bias = bias + jnp.sum(dh2, axis=0, keepdims=True)
            dx1 = dy_in[c].astype(F32) + norm_back(dh2, unit, scale, par[2:3])
            self.dx1_s[self.span(c), :] = dx1
            self.low_s[self.span(c), :] = dx1.astype(BF16)
            unit1, _ = normalise(x_in[c].astype(F32))
            self.h1_s[self.span(c), :] = (unit1 * par[0:1] + par[1:2]).astype(BF16)
        self.small2 = [gain, bias, jnp.zeros((4, D), F32), g_router]

    def heads(self, r):
        qkv_in, o_in, lse_in = self.saved[4:]
        key_ok = iota((PAD, PAD), 1) < SEQ
        low, h1, w = self.low_s[...], self.h1_s[...], self.w_ref[r]
        dout = dot(low, w[:, 9 * HD : D]).astype(BF16)
        for c in range(self.imgs):
            qkv = qkv_in[c, r]
            lse = lse_in[c]
            self.o_s[self.span(c), :] = o_in[c, r]
            dqs, dks, dvs = [], [], []
            for h in range(3):
                q = qkv[:, h * HD : (h + 1) * HD]
                k = qkv[:, (3 + h) * HD : (4 + h) * HD]
                v = qkv[:, (6 + h) * HD : (7 + h) * HD]
                do = dout[self.span(c), h * HD : (h + 1) * HD]
                s = dot_nt(q, k) * HD ** (-0.5)
                p = jnp.where(key_ok, jnp.exp(s - lse[:, 3 * r + h : 3 * r + h + 1]), 0.0)
                dvs.append(dot_tn(p.astype(BF16), do).astype(BF16))
                dp = dot_nt(do, v)
                ds = (p * (dp - jnp.sum(p * dp, axis=-1, keepdims=True))).astype(BF16)
                dqs.append((dot(ds, k) * HD ** (-0.5)).astype(BF16))
                dks.append((dot_tn(ds, q) * HD ** (-0.5)).astype(BF16))
            self.dqkv_s[self.span(c), :] = jnp.concatenate(dqs + dks + dvs, axis=1)
        dqkv = self.dqkv_s[...]
        part = dot_nt(dqkv, w[:, : 9 * HD])
        self.dh1_s[...] = self.dh1_s[...] + part if self.started else part
        self.started = True
        return jnp.concatenate([dot_tn(h1, dqkv), dot_tn(low, self.o_s[...])], axis=1).astype(BF16)

    def last(self, dtok_ref):
        x_in = self.saved[1]
        gain = jnp.zeros((1, D), F32)
        bias = jnp.zeros((1, D), F32)
        for c in range(self.imgs):
            dh1 = jnp.where(self.row_ok, self.dh1_s[self.span(c), :], 0.0)
            unit, scale = normalise(x_in[c].astype(F32))
            gain = gain + jnp.sum(dh1 * unit, axis=0, keepdims=True)
            bias = bias + jnp.sum(dh1, axis=0, keepdims=True)
            dtok_ref[c] = (self.dx1_s[self.span(c), :] + norm_back(dh1, unit, scale, self.par[0:1])).astype(BF16)
        return jnp.concatenate([gain, bias] + self.small2, axis=0)


def small_block(small, i, d_own):
    line = jnp.concatenate([small[:, i * d_own : (i + 1) * d_own], jnp.zeros((16, D - d_own), F32)], axis=1)
    return line.astype(BF16)


def backward_scratch(imgs):
    rows = imgs * PAD
    return [
        pltpu.VMEM((rows, D), F32),
        pltpu.VMEM((rows, D), BF16),
        pltpu.VMEM((rows, D), BF16),
        pltpu.VMEM((rows, D), F32),
        pltpu.VMEM((rows, 9 * HD), BF16),
        pltpu.VMEM((rows, 3 * HD), BF16),
    ]


def attn_backward_kernel(imgs, *refs):
    dh_in, saved, w_ref = refs[:imgs], refs[imgs : imgs + 7], refs[imgs + 7]
    packs, dtok_ref = refs[imgs + 8 : imgs + 11], refs[imgs + 11]
    n_dp, d_own = packs[0].shape[0], packs[0].shape[1] - 16
    back = Backward(imgs, lambda c: dh_in[c][...], saved, w_ref, *refs[imgs + 12 :])

    def pack_of(r):
        return packs[r] if r < 2 else packs[2].at[:, r - 2]

    back.first()
    for r in range(4):
        grad = back.heads(r)
        for i in range(n_dp):
            pack_of(r)[i, :d_own, :] = grad[i * d_own : (i + 1) * d_own]
    small = back.last(dtok_ref)
    for i in range(n_dp):
        for r in range(4):
            pack_of(r)[i, d_own:, :] = small_block(small, i, d_own)


def attn_backward(dh, saved, w, n_dp):
    imgs = len(dh)
    pack = (n_dp, D // n_dp + 16, D)
    vm = pl.BlockSpec(memory_space=pltpu.VMEM)
    return pl.pallas_call(
        functools.partial(attn_backward_kernel, imgs),
        out_shape=(
            jax.ShapeDtypeStruct(pack, BF16),
            jax.ShapeDtypeStruct(pack, BF16),
            jax.ShapeDtypeStruct((n_dp, 2) + pack[1:], BF16),
            jax.ShapeDtypeStruct((imgs, PAD, D), BF16),
        ),
        in_specs=[vm] * (imgs + 8),
        out_specs=(vm,) * 4,
        scratch_shapes=backward_scratch(imgs),
        compiler_params=pltpu.CompilerParams(vmem_limit_bytes=VMEM_LIMIT),
        cost_estimate=pl.CostEstimate(flops=12 * 10**9, bytes_accessed=2 * 10**7, transcendentals=2 * 10**6),
        name="attn_backward",
    )(*dh, *saved, w)


HOMES = ((0,), (1, 2), (3,), (4,), (5, 6), (7,), ())


def back_kernel(
    imgs, g_low, y_ref, yf_ref, dh_ref, x1_ref, x_ref, dy_ref, probs_ref, qkv_ref, o_ref, lse_ref, w_ref,
    out_all, dtok_all, g_out, total_ref,
    ga_s, gc_s, gx_s, pk_s, pkc_s, pkr_s, sm_s, smr_s, cs_s, cr_s, fs_s, fr_s, or_s, dt_s, y_s, yr_s,
    dx1_s, low_s, h1_s, dh1_s, dqkv_s, o_s,
    gc_ss, gc_r, gx_ss, gx_r, ga_ss, ga_r, pk_ss, pk_r, sm_ss, sm_r, c_ss, c_r, f_ss, f_r, row_ss, row_r, y_ss, y_r, local,
):
    peers = Peers()
    member = peers.member
    tensor = lax.axis_index("tensor")
    d_own = g_low.shape[3]
    peers.meet()
    loads = []

    def here(src, dst):
        copy = pltpu.make_async_copy(src, dst, local.at[len(loads)])
        copy.start()
        loads.append(copy)
        return copy

    def give_rows(kind, src, whole):
        here(src, whole.at[tensor])
        across = peers.send(src, whole.at[tensor], (row_ss, row_r), (kind, 0), peers.across)
        core = peers.send(src, whole.at[tensor], (row_ss, row_r), (kind, 1), peers.core)

        def onwards():
            across.wait_recv()
            other = lax.rem(tensor + 2, 4)
            copy = peers.send(whole.at[other], whole.at[other], (row_ss, row_r), (kind, 2), peers.core)
            return core, copy

        return onwards

    y_load = here(y_ref, y_s)
    yf_load = here(yf_ref, yr_s.at[0])
    y_sent = {}

    def y_hop(k):
        for c in range(imgs):
            if k > 2:
                y_sent[c, k - 1].wait_recv()
            src = yr_s.at[k - 2, c]
            src[...] = (src[...].astype(F32) + y_s[k, c].astype(F32)).astype(BF16)
            y_sent[c, k] = peers.send(src, yr_s.at[k - 1, c], (y_ss, y_r), (c, k - 1), peers.next[c % 2])

    def y_last():
        for c in range(imgs):
            y_sent[c, E - 1].wait_recv()
            total = yr_s[E - 2, c].astype(F32) + y_s[0, c].astype(F32)
            or_s[c] = (x1_ref[c] + total).astype(BF16)

    g_core = [
        peers.send(g_low.at[2 + s], gc_s.at[s], (gc_ss, gc_r), s, peers.core) for s in (1, 0)
    ][::-1]
    g_load = [here(g_low.at[s], ga_s.at[s]) for s in (1, 0)][::-1]
    y_load.wait()
    yf_load.wait()
    y_hop(2)
    order = (4, 3, 5, 2, 6, 1, 7, 0)
    gx = {}

    def pass_across():
        g_core[1].wait_recv()
        g_load[1].wait()
        for by in order:
            to = peers.ahead(by)
            ga_s[1, to] = (ga_s[1, to].astype(F32) + gc_s[1, to].astype(F32)).astype(BF16)
            gx[by] = peers.send(ga_s.at[1, to], gx_s.at[to], (gx_ss, gx_r), by, peers.across)
        g_core[0].wait_recv()
        g_load[0].wait()

    ga = {}

    def pass_home(by):
        gx[by].wait_recv()
        to = peers.ahead(by)
        part = ga_s[0, to].astype(F32) + gc_s[0, to].astype(F32)
        ga_s[0, to] = (part + gx_s[to].astype(F32)).astype(BF16)
        if by:
            device = {"dp": peers.base + to}
            ga[by] = peers.send(ga_s.at[0, to], g_out.at[member], (ga_ss, ga_r), by, device)
        else:
            here(ga_s.at[0, to], g_out.at[member])

    def homes(at):
        for number in HOMES[at]:
            pass_home(order[number])

    saved = (x1_ref, x_ref, dy_ref, probs_ref, qkv_ref, o_ref, lse_ref)
    back = Backward(imgs, lambda c: dh_ref[c], saved, w_ref, dx1_s, low_s, h1_s, dh1_s, dqkv_s, o_s)
    back.first()
    for r in (2, 3):
        grad = back.heads(r)
        for i in range(E):
            pkc_s[i, r - 2] = grad[i * d_own : (i + 1) * d_own]
        y_hop(r + 1)
        if r == 2:
            pass_across()
    pk_core = peers.send(pkc_s, pkr_s, (pk_ss, pk_r), 0, peers.core)
    for r in (0, 1):
        grad = back.heads(r)
        for i in range(E):
            pk_s[i, r, :d_own] = grad[i * d_own : (i + 1) * d_own]
        y_hop(5 + r)
        homes(r)
    small = back.last(dt_s)
    dtok_rows = give_rows(1, dt_s, dtok_all)
    for i in range(E):
        sm_s[i] = small_block(small, i, d_own)
    sm_core = peers.send(sm_s, smr_s, (sm_ss, sm_r), 0, peers.core)
    pk_core.wait_recv()
    sm_core.wait_recv()

    def term(of):
        weights = pk_s[of, :, :d_own].astype(F32) + pkr_s[of].astype(F32)
        both = sm_s[of].astype(F32) + smr_s[of].astype(F32)
        return jnp.concatenate([weights, jnp.broadcast_to(both[None], (2,) + both.shape)], axis=1)

    steps = (E // 2, E // 2 - 1)
    hops = {}

    def hop(way, i):
        value = term(peers.behind(1 - way, steps[way] - i))
        if i:
            hops[way, i - 1].wait_recv()
            value = value + cr_s[way, i - 1].astype(F32)
        cs_s[way, i] = value.astype(BF16)
        hops[way, i] = peers.send(cs_s.at[way, i], cr_s.at[way, i], (c_ss, c_r), (way, i), peers.next[way])

    for i in range(E // 2):
        hop(0, i)
        if i < steps[1]:
            hop(1, i)
        if i == 0:
            y_hop(7)
        if i == 1:
            y_last()
            out_rows = give_rows(0, or_s, out_all)
        homes(2 + i)
    hops[1, steps[1] - 1].wait_recv()
    hops[0, steps[0] - 1].wait_recv()
    total = term(member) + cr_s[0, steps[0] - 1].astype(F32) + cr_s[1, steps[1] - 1].astype(F32)
    fs_s[...] = total[1].astype(BF16)
    final = peers.send(fs_s, fr_s, (f_ss, f_r), 0, peers.across)
    homes(6)
    dtok_rows = dtok_rows()
    out_rows = out_rows()
    final.wait_recv()
    total_ref[...] = total[0] + fr_s[...].astype(F32)
    for by in range(1, E):
        ga[by].wait_recv()
    for copy in (*out_rows, *dtok_rows):
        copy.wait_recv()
    for copy in loads:
        if all(copy is not other for other in (y_load, yf_load, *g_load)):
            copy.wait()
    for copy in peers.sends:
        copy.wait_send()


def back(g_low, y, y_first, dh, saved, w):
    imgs = dh.shape[0]
    d_own = g_low.shape[3]
    vm = pl.BlockSpec(memory_space=pltpu.VMEM)
    hbm = pl.BlockSpec(memory_space=pl.ANY)
    dma = pltpu.SemaphoreType.DMA
    part = (E, 2, d_own, D)
    rows = (imgs, PAD, D)
    hop = (2, E // 2, 2, d_own + 16, D)
    return pl.pallas_call(
        functools.partial(back_kernel, imgs),
        out_shape=(
            jax.ShapeDtypeStruct((4,) + rows, BF16),
            jax.ShapeDtypeStruct((4,) + rows, BF16),
            jax.ShapeDtypeStruct(part, BF16),
            jax.ShapeDtypeStruct((d_own + 16, D), F32),
        ),
        in_specs=[hbm, hbm, hbm] + [vm] * 9,
        out_specs=(hbm, hbm, hbm, vm),
        scratch_shapes=[
            pltpu.VMEM((2,) + part, BF16),
            pltpu.VMEM((2,) + part, BF16),
            pltpu.VMEM(part, BF16),
            pltpu.VMEM((E, 2, d_own + 16, D), BF16),
            pltpu.VMEM(part, BF16),
            pltpu.VMEM(part, BF16),
            pltpu.VMEM((E, 16, D), BF16),
            pltpu.VMEM((E, 16, D), BF16),
            pltpu.VMEM(hop, BF16),
            pltpu.VMEM(hop, BF16),
            pltpu.VMEM((d_own + 16, D), BF16),
            pltpu.VMEM((d_own + 16, D), BF16),
            pltpu.VMEM(rows, BF16),
            pltpu.VMEM(rows, BF16),
            pltpu.VMEM((E,) + rows, BF16),
            pltpu.VMEM((E - 1,) + rows, BF16),
            *backward_scratch(imgs),
            dma((2,)), dma((2,)), dma((E,)), dma((E,)), dma((E,)), dma((E,)), dma((1,)), dma((1,)),
            dma((1,)), dma((1,)), dma((2, E // 2)), dma((2, E // 2)), dma((1,)), dma((1,)), dma((2, 3)), dma((2, 3)),
            dma((imgs, E - 1)), dma((imgs, E - 1)), dma((7,)),
        ],
        compiler_params=pltpu.CompilerParams(
            vmem_limit_bytes=VMEM_LIMIT, collective_id=1, has_side_effects=True
        ),
        cost_estimate=pl.CostEstimate(flops=12 * 10**9, bytes_accessed=10**8, transcendentals=2 * 10**6),
        name="back",
    )(g_low, y, y_first, dh, *saved, w)


def eye_of(n, lanes):
    return (iota((n, lanes), 0) == iota((n, lanes), 1)).astype(F32).astype(BF16)


def prepare_kernel(
    imgs, tensor_ref, tok_ref, cot_ref, qkv_ref, wo_ref, v0_ref, v1_ref, v2_ref, v3_ref, router_ref, win_ref, wout_ref, noise_ref, routes_ref,
    pack_ref, ew_ref, x_ref, dy_ref, keep_out, noise_out, keep_s,
):
    tensor = tensor_ref[0]
    d_own = wo_ref.shape[1]
    wo = dot_tn(wo_ref[...].astype(BF16), eye_of(3 * HD, 3 * HD)).astype(BF16)
    vectors = [ref[...] for ref in (v0_ref, v1_ref, v2_ref, v3_ref)]
    lines = jnp.concatenate(vectors + [jnp.zeros((4, d_own), F32), router_ref[...]], axis=0).astype(BF16)
    lines = dot_tn(lines, eye_of(16, 128)).astype(BF16)
    pack_ref[...] = jnp.concatenate([qkv_ref[i].astype(BF16) for i in range(3)] + [wo, lines], axis=1)
    for e in range(E):
        ew_ref[e, 0] = win_ref[e].astype(BF16)
        ew_ref[e, 1] = wout_ref[e].astype(BF16)
    count = routes_ref.shape[1]
    earlier = (iota((count, count), 0) <= iota((count, count), 1)).astype(F32).astype(BF16)
    experts_ = iota((E, count), 0)
    before = jnp.zeros((E, 1), F32)
    keep = jnp.zeros((E, count), F32)
    for choice in range(TOP):
        named = experts_ == routes_ref[choice : choice + 1, :]
        upto = before + dot(named.astype(F32).astype(BF16), earlier)
        keep = keep + jnp.where(named & (upto <= CAP), 1.0, 0.0)
        before = upto[:, count - 1 :]
    keep_s[...] = keep
    for t in range(4):

        @pl.when(tensor == t)
        def _():
            for c in range(imgs):
                at = (t * imgs + c) * SEQ
                for src, dst in ((tok_ref, x_ref), (cot_ref, dy_ref)):
                    dst[c, :SEQ, :] = src[at : at + SEQ, :]
                    dst[c, SEQ:, :] = jnp.zeros((PAD - SEQ, D), BF16)
                for src, dst in ((keep_s, keep_out), (noise_ref, noise_out)):
                    dst[c] = jnp.concatenate([src[:, at : at + SEQ], jnp.zeros((E, PAD - SEQ), F32)], axis=1)


def prepare(tensor, imgs, tokens, cotangent, w_qkv, w_attn_out, vectors, router, w_in, w_out, noise, routes):
    vm = pl.BlockSpec(memory_space=pltpu.VMEM)
    d_own = w_attn_out.shape[1]
    rows = jax.ShapeDtypeStruct((imgs, PAD, D), BF16)
    lanes = jax.ShapeDtypeStruct((imgs, E, PAD), F32)
    return pl.pallas_call(
        functools.partial(prepare_kernel, imgs),
        out_shape=(
            jax.ShapeDtypeStruct((d_own, D + 128), BF16),
            jax.ShapeDtypeStruct((E, 2, d_own, FFS), BF16),
            rows,
            rows,
            lanes,
            lanes,
        ),
        in_specs=[pl.BlockSpec(memory_space=pltpu.SMEM)] + [vm] * 13,
        out_specs=(vm,) * 6,
        scratch_shapes=[pltpu.VMEM((E, tokens.shape[0]), F32)],
        compiler_params=pltpu.CompilerParams(vmem_limit_bytes=VMEM_LIMIT),
        cost_estimate=pl.CostEstimate(flops=10**8, bytes_accessed=15 * 10**6, transcendentals=0),
        name="prepare",
    )(tensor.reshape(1), tokens, cotangent, w_qkv, w_attn_out, *vectors, router, w_in, w_out, noise, routes)


def finish_kernel(imgs, out_in, dtok_in, g_in, total_ref, out_ref, dtok_ref, gi_ref, go_ref, qkv_ref, wo_ref, s0_ref, s1_ref, s2_ref, s3_ref, router_ref, rows_s, g_s, sem):
    loads = [pltpu.make_async_copy(src, rows_s.at[i], sem.at[i]) for i, src in enumerate((out_in, dtok_in))]
    loads.append(pltpu.make_async_copy(g_in, g_s, sem.at[2]))
    for copy in loads:
        copy.start()
    d_own = gi_ref.shape[1]
    total = total_ref[...]
    for i in range(3):
        qkv_ref[i] = total[:d_own, i * 3 * HD : (i + 1) * 3 * HD]
    wo_ref[...] = jnp.transpose(total[:d_own, 9 * HD :])
    for i, ref in enumerate((s0_ref, s1_ref, s2_ref, s3_ref)):
        ref[...] = total[d_own + i : d_own + i + 1, :d_own]
    router_ref[...] = total[d_own + 8 :, :d_own]
    for which, dst in ((0, out_ref), (1, dtok_ref)):
        loads[which].wait()
        for i in range(4 * imgs):
            dst[i * SEQ : (i + 1) * SEQ, :] = rows_s[which, i // imgs, i % imgs, :SEQ, :]
    loads[2].wait()
    for e in range(E):
        gi_ref[e] = g_s[e, 0].astype(F32)
        go_ref[e] = g_s[e, 1].astype(F32)


def finish(out_all, dtok_all, g_exp, total):
    imgs = out_all.shape[1]
    d_own = g_exp.shape[2]
    vm = pl.BlockSpec(memory_space=pltpu.VMEM)
    hbm = pl.BlockSpec(memory_space=pl.ANY)
    rows = jax.ShapeDtypeStruct((4 * imgs * SEQ, D), BF16)
    grad = jax.ShapeDtypeStruct((E, d_own, FFS), F32)
    return pl.pallas_call(
        functools.partial(finish_kernel, imgs),
        out_shape=(
            rows,
            rows,
            grad,
            grad,
            jax.ShapeDtypeStruct((3, d_own, 3 * HD), F32),
            jax.ShapeDtypeStruct((3 * HD, d_own), F32),
            *[jax.ShapeDtypeStruct((1, d_own), F32)] * 4,
            jax.ShapeDtypeStruct((E, d_own), F32),
        ),
        in_specs=[hbm, hbm, hbm, vm],
        out_specs=(vm,) * 11,
        scratch_shapes=[
            pltpu.VMEM((2, 4, imgs, PAD, D), BF16),
            pltpu.VMEM(g_exp.shape, BF16),
            pltpu.SemaphoreType.DMA((3,)),
        ],
        compiler_params=pltpu.CompilerParams(vmem_limit_bytes=VMEM_LIMIT),
        cost_estimate=pl.CostEstimate(flops=10**6, bytes_accessed=18 * 10**6, transcendentals=0),
        name="finish",
    )(out_all, dtok_all, g_exp, total)


RING = (0, 2, 4, 6, 7, 5, 3, 1)


class Mover:
    def __init__(self, n_dp):
        self.n_dp = n_dp
        self.groups = n_dp // E
        self.me = lax.axis_index("dp")
        self.member = lax.rem(self.me, E)
        self.group = lax.div(self.me, E)
        self.tensor = lax.axis_index("tensor")
        self.place = ring_place(self.member)
        bases = range(0, n_dp, E)
        self.ring = (
            [(b + RING[i], b + RING[(i + 1) % E]) for b in bases for i in range(E)],
            [(b + RING[(i + 1) % E], b + RING[i]) for b in bases for i in range(E)],
        )

    def along(self, value, way):
        return lax.ppermute(value, "dp", self.ring[way])

    def shift(self, value, by):
        perm = [(b + i, b + (i + by) % E) for b in range(0, self.n_dp, E) for i in range(E)]
        return lax.ppermute(value, "dp", perm)

    def shift_group(self, value, by):
        return lax.ppermute(value, "dp", [(k, (k + by * E) % self.n_dp) for k in range(self.n_dp)])

    def other(self, value, mask):
        return lax.ppermute(value, "tensor", [(k, k ^ mask) for k in range(4)])

    def behind(self, way, k):
        step = -k if way == 0 else k
        return ring_member(lax.rem(self.place + step + E, E))

    def group_lists(self):
        if self.groups == 1:
            return None
        return [[b + i for i in range(E)] for b in range(0, self.n_dp, E)]

    def gather(self, value):
        return lax.all_gather(value, "dp", axis=0, tiled=False, axis_index_groups=self.group_lists())

    def scatter_sum(self, value):
        return lax.psum_scatter(
            value, "dp", scatter_dimension=0, tiled=False, axis_index_groups=self.group_lists()
        )

    def front(self, pack, ew, dy, x, noise, keep):
        own = lax.all_gather(pack, "dp", axis=0, tiled=True)
        two = jnp.stack([own, self.other(own, 2)])
        w = jnp.concatenate([two, self.other(two, 1)], axis=0)
        blocks = jnp.zeros((2, E * pack.shape[0], FFS), BF16)
        for by in range(E):
            to = lax.rem(self.member + by, E)
            block = lax.dynamic_index_in_dim(ew, to, 0, False)
            came = lax.rem(self.member - by + E, E)
            block = self.shift(block, by) if by else block
            blocks = lax.dynamic_update_slice_in_dim(blocks, block, came * pack.shape[0], 1)
        blocks = self.all_groups(blocks, 1)
        blocks = jnp.swapaxes(blocks.reshape(2, E, D // E, FFS), 0, 1)
        two = jnp.stack([blocks, self.other(blocks, 2)])
        weights = jnp.concatenate([two, self.other(two, 1)], axis=0)
        chunk, *saved = attn_forward(x, w, noise, keep)
        table = (E * x.shape[0], PAD, D)
        dh, y, rows, hid, tiles = experts(
            self.member, self.gather(chunk).reshape(table), self.gather(dy).reshape(table), weights
        )
        sums = [self.scatter_sum(t.reshape((E,) + chunk.shape)) for t in (dh, y)]
        g = [jnp.concatenate([expert_grads(tiles, rows, hid, kind, base) for base in (0, 2)]) for kind in (0, 1)]
        g = jnp.stack([part.reshape(4, E, D // E, FFS) for part in g], axis=2)
        return g, jnp.stack(sums), w, *saved

    def back(self, g_low, sums, saved, x, dy, w):
        x1, qkv, o, lse, probs = saved
        dh_sum, y_sum = sums[0], sums[1]
        imgs, d_own = x.shape[0], D // self.n_dp
        passed = self.other(g_low[2:], 1)
        pair = [(g_low[s].astype(F32) + passed[s].astype(F32)).astype(BF16) for s in range(2)]
        total = (pair[0].astype(F32) + self.other(pair[1], 2).astype(F32)).astype(BF16)
        if self.groups > 1:
            total = jnp.swapaxes(total, 1, 2).reshape(D, 2, FFS)
            total = jnp.swapaxes(self.sum_groups(total, 0).reshape(E, d_own, 2, FFS), 1, 2)
        g_exp = []
        for by in range(E):
            to = lax.rem(self.member + by, E)
            block = lax.dynamic_index_in_dim(total, to, 0, False)
            g_exp.append(self.shift(block, by) if by else block)

        pack0, pack1, packs, d_tok = attn_backward(
            [dh_sum[c] for c in range(imgs)], (x1, x, dy, probs, qkv, o, lse), w, self.n_dp
        )
        passed = self.other(packs, 1)
        if self.groups > 1:
            pack0 = self.sum_groups((pack0.astype(F32) + passed[:, 0].astype(F32)).astype(BF16), 0)
            pack1 = self.sum_groups((pack1.astype(F32) + passed[:, 1].astype(F32)).astype(BF16), 0)
            passed = jnp.zeros((E, 2) + pack0.shape[1:], BF16)

        def pack_for(member):
            one, two = (lax.dynamic_index_in_dim(p, member, 0, False).astype(F32) for p in (pack0, pack1))
            came = lax.dynamic_index_in_dim(passed, member, 0, False).astype(F32)
            return one + came[0] + self.other((two + came[1]).astype(BF16), 2).astype(F32)

        total = self.sum_both_ways(pack_for)
        at = jnp.stack([_slot(self.tensor, t) for t in range(4)])

        def all_rows(own):
            across = self.other(own, 2)
            return lay_out(at, [own, across, self.other(own, 1), self.other(across, 1)])

        d_tokens = all_rows(d_tok)
        output = all_rows((x1 + y_sum.astype(F32)).astype(BF16))
        came = jnp.stack([lax.rem(self.member - by + E, E) for by in range(E)])
        return output, d_tokens, *unpack(came, g_exp), total

    def sum_both_ways(self, block_for):
        def chain(way, steps):
            total = block_for(self.behind(1 - way, steps)).astype(BF16)
            for k in range(steps - 1, -1, -1):
                total = self.along(total, way)
                if k:
                    total = (total.astype(F32) + block_for(self.behind(1 - way, k)).astype(F32)).astype(BF16)
            return total

        ahead = chain(0, E // 2)
        back = chain(1, E // 2 - 1)
        return ahead.astype(F32) + back.astype(F32) + block_for(self.member).astype(F32)

    def all_groups(self, part, dim):
        if self.groups == 1:
            return part
        size = part.shape[dim]
        shape = part.shape[:dim] + (size * self.groups,) + part.shape[dim + 1 :]
        whole = lax.dynamic_update_slice_in_dim(jnp.zeros(shape, part.dtype), part, self.group * size, dim)
        for by in range(1, self.groups):
            came = lax.rem(self.group - by + self.groups, self.groups)
            whole = lax.dynamic_update_slice_in_dim(whole, self.shift_group(part, by), came * size, dim)
        return whole

    def sum_groups(self, whole, dim):
        if self.groups == 1:
            return whole
        size = whole.shape[dim] // self.groups
        total = lax.dynamic_slice_in_dim(whole, self.group * size, size, dim).astype(F32)
        for by in range(1, self.groups):
            to = lax.rem(self.group + by, self.groups)
            part = lax.dynamic_slice_in_dim(whole, to * size, size, dim)
            total = total + self.shift_group(part, by).astype(F32)
        return total.astype(whole.dtype)


def after(value, *first):
    return lax.optimization_barrier((value, first))[0]


def _slot(tensor, t):
    apart = lax.bitwise_xor(tensor, t)
    return lax.div(apart, 2) + 2 * lax.rem(apart, 2)


def image_blocks(rows, tensor, imgs):
    first = tensor * (imgs * SEQ)
    return [
        jnp.pad(lax.dynamic_slice_in_dim(rows, first + c * SEQ, SEQ, 0), ((0, PAD - SEQ), (0, 0)))
        for c in range(imgs)
    ]


def image_lanes(lanes, tensor, imgs):
    first = tensor * (imgs * SEQ)
    return [
        jnp.pad(lax.dynamic_slice_in_dim(lanes, first + c * SEQ, SEQ, 1), ((0, 0), (0, PAD - SEQ)))
        for c in range(imgs)
    ]


def kept_pairs(routes):
    chosen = jnp.transpose(routes).reshape(1, -1)
    named = (chosen == jnp.arange(E, dtype=jnp.int32)[:, None]).astype(jnp.int32)
    kept = named * (jnp.cumsum(named, axis=1) <= CAP)
    return jnp.sum(kept.reshape(E, TOP, -1), axis=1).astype(F32)


def body(
    n_dp,
    tokens,
    ln1_gain,
    ln1_bias,
    w_qkv,
    w_attn_out,
    ln2_gain,
    ln2_bias,
    router_weight,
    w_in,
    w_expert_out,
    router_noise,
    routes,
    cotangent,
):
    move = Mover(n_dp)
    token_count = tokens.shape[0]
    imgs = token_count // SEQ // 4
    d_own = w_qkv.shape[0]
    ways = [c % 2 for c in range(imgs)]

    w_out = jnp.transpose(w_expert_out, (0, 2, 1))
    if move.groups == 1:
        pack, ew, x, dy, keep, noise = prepare(
            move.tensor, imgs, tokens, cotangent, jnp.transpose(w_qkv, (1, 0, 2)), w_attn_out,
            [v.reshape(1, d_own) for v in (ln1_gain, ln1_bias, ln2_gain, ln2_bias)], jnp.transpose(router_weight),
            w_in, w_out, jnp.transpose(router_noise), jnp.transpose(routes),
        )
        _, _, _, y, y_first, g_low, dh, w, *saved = front(pack, ew, dy, x, noise, keep)
        x1, qkv, o, lse, probs = saved
        output, d_tokens, g_in, g_out, g_qkv, g_attn_out, *g_vectors, g_router = finish(
            *back(g_low, y, y_first, dh, (x1, x, dy, probs, qkv, o, lse), w)
        )
        g_vectors = [v.reshape(d_own) for v in g_vectors]
        g_qkv = jnp.transpose(g_qkv, (1, 0, 2))
    else:
        vectors = jnp.stack([ln1_gain, ln1_bias, ln2_gain, ln2_bias] + [jnp.zeros_like(ln1_gain)] * 4, axis=1)
        pack = jnp.concatenate(
            [w_qkv[:, 0], w_qkv[:, 1], w_qkv[:, 2], jnp.transpose(w_attn_out), vectors, router_weight], axis=1
        )
        pack = jnp.pad(pack, ((0, 0), (0, 128 - 16))).astype(BF16)
        ew = jnp.stack([w_in, jnp.transpose(w_expert_out, (0, 2, 1))], axis=1).astype(BF16)
        x = jnp.stack(image_blocks(tokens, move.tensor, imgs))
        dy = jnp.stack(image_blocks(cotangent, move.tensor, imgs))
        keep = jnp.stack(image_lanes(kept_pairs(routes), move.tensor, imgs))
        noise = jnp.stack(image_lanes(jnp.transpose(router_noise), move.tensor, imgs))
        g_low, sums, w, *saved = move.front(pack, ew, dy, x, noise, keep)
        output, d_tokens, g_in, g_out, total = move.back(g_low, sums, saved, x, dy, w)
        g_qkv = total[:d_own, : 9 * HD].reshape(d_own, 3, 3 * HD)
        g_attn_out = jnp.transpose(total[:d_own, 9 * HD :])
        g_vectors = [total[d_own + i, :d_own] for i in range(4)]
        g_router = total[d_own + 8 :, :d_own]
    return (
        output,
        d_tokens,
        g_vectors[0],
        g_vectors[1],
        g_qkv,
        g_attn_out,
        g_vectors[2],
        g_vectors[3],
        jnp.transpose(g_router),
        g_in,
        jnp.transpose(g_out, (0, 2, 1)),
    )


def solution(mesh):
    in_specs = (
        P("dp", None),
        P("dp"),
        P("dp"),
        P("dp", None, "tensor"),
        P("tensor", "dp"),
        P("dp"),
        P("dp"),
        P("dp", None),
        P(None, "dp", "tensor"),
        P(None, "tensor", "dp"),
        P("dp", None),
        P("dp", None),
        P("dp", None),
    )
    out_specs = (
        P("dp", None),
        P("dp", None),
        P("dp"),
        P("dp"),
        P("dp", None, "tensor"),
        P("tensor", "dp"),
        P("dp"),
        P("dp"),
        P("dp", None),
        P(None, "dp", "tensor"),
        P(None, "tensor", "dp"),
    )
    return jax.shard_map(
        functools.partial(body, mesh.shape["dp"]),
        mesh=mesh,
        in_specs=in_specs,
        out_specs=out_specs,
        check_vma=False,
    )
```

```python
import functools

import jax
import jax.numpy as jnp
from jax import lax
from jax.experimental import pallas as pl
from jax.experimental.pallas import tpu as pltpu
from jax.sharding import PartitionSpec as P

D = 768
HD = 64
E = 8
TOP = 2
SEQ = 197
CAP = 689
PAD = 208
META = 200
TILE = 256
FFS = 768
EPS = 1e-06
VMEM_LIMIT = 62 * 1024 * 1024

F32 = jnp.float32
BF16 = jnp.bfloat16


def dot(a, b):
    return jnp.dot(a, b, preferred_element_type=F32)


def dot_nt(a, b):
    return lax.dot_general(a, b, (((1,), (1,)), ((), ())), preferred_element_type=F32)


def dot_tn(a, b):
    return lax.dot_general(a, b, (((0,), (0,)), ((), ())), preferred_element_type=F32)


def iota(shape, dim):
    return lax.broadcasted_iota(jnp.int32, shape, dim)


def normalise(values):
    centred = values - jnp.mean(values, axis=-1, keepdims=True)
    scale = lax.rsqrt(jnp.mean(centred * centred, axis=-1, keepdims=True) + EPS)
    return centred * scale, scale


def norm_back(grad, unit, scale, gain):
    g = grad * gain
    return scale * (
        g - jnp.mean(g, axis=-1, keepdims=True) - unit * jnp.mean(g * unit, axis=-1, keepdims=True)
    )


def params_of(w_own):
    return jnp.transpose(w_own[:, D:].astype(F32))[:16]


def attend(x, par, w_of, noise, keep, chunk_ref, x1_ref, qkv_ref, o_ref, lse_ref, probs_ref):
    x = x.astype(F32)
    unit, _ = normalise(x)
    h1 = (unit * par[0:1] + par[1:2]).astype(BF16)
    acc = x
    lse = jnp.zeros((PAD, 128), F32)
    key_ok = iota((PAD, PAD), 1) < SEQ
    lane = iota((PAD, 128), 1)
    for r in range(4):
        w = w_of(r)
        qkv = dot(h1, w[:, : 9 * HD]).astype(BF16)
        qkv_ref[r] = qkv
        outs = []
        for h in range(3):
            q = qkv[:, h * HD : (h + 1) * HD]
            k = qkv[:, (3 + h) * HD : (4 + h) * HD]
            v = qkv[:, (6 + h) * HD : (7 + h) * HD]
            s = jnp.where(key_ok, dot_nt(q, k) * HD ** (-0.5), -1e30)
            top = jnp.max(s, axis=-1, keepdims=True)
            p = jnp.exp(s - top)
            total = jnp.sum(p, axis=-1, keepdims=True)
            outs.append(dot((p * (1.0 / total)).astype(BF16), v).astype(BF16))
            lse = jnp.where(lane == 3 * r + h, top + jnp.log(total), lse)
        o = jnp.concatenate(outs, axis=1)
        o_ref[r] = o
        acc = acc + dot_nt(o, w[:, 9 * HD : D])
    lse_ref[...] = lse
    x1_ref[...] = acc
    unit2, _ = normalise(acc)
    h2 = (unit2 * par[2:3] + par[3:4]).astype(BF16)
    logits = dot_nt(par[8:16].astype(BF16), h2) + noise
    e = jnp.exp(logits - jnp.max(logits, axis=0, keepdims=True))
    probs = e / jnp.sum(e, axis=0, keepdims=True)
    probs_ref[...] = probs
    gates = jnp.where(keep > 0, probs, -1.0)
    chunk_ref[...] = h2
    tail = jnp.concatenate([gates, jnp.zeros((8, D - PAD), F32)], axis=1)
    low = h2[PAD - 16 :, :].astype(F32)
    chunk_ref[PAD - 16 :, :] = jnp.concatenate([low[:8], tail], axis=0).astype(BF16)


def attn_shapes(imgs):
    return (
        jax.ShapeDtypeStruct((imgs, PAD, D), F32),
        jax.ShapeDtypeStruct((imgs, 4, PAD, 9 * HD), BF16),
        jax.ShapeDtypeStruct((imgs, 4, PAD, 3 * HD), BF16),
        jax.ShapeDtypeStruct((imgs, PAD, 128), F32),
        jax.ShapeDtypeStruct((imgs, E, PAD), F32),
    )


def attn_forward_kernel(imgs, x_ref, w_ref, noise_ref, keep_ref, chunk_ref, *saved):
    par = params_of(w_ref[0])
    for c in range(imgs):
        attend(
            x_ref[c], par, lambda r: w_ref[r], noise_ref[c], keep_ref[c],
            chunk_ref.at[c], *(ref.at[c] for ref in saved),
        )


def attn_forward(x, w, noise, keep):
    imgs = x.shape[0]
    vm = pl.BlockSpec(memory_space=pltpu.VMEM)
    return pl.pallas_call(
        functools.partial(attn_forward_kernel, imgs),
        out_shape=(jax.ShapeDtypeStruct((imgs, PAD, D), BF16),) + attn_shapes(imgs),
        in_specs=[vm] * 4,
        out_specs=(vm,) * 6,
        compiler_params=pltpu.CompilerParams(vmem_limit_bytes=VMEM_LIMIT),
        cost_estimate=pl.CostEstimate(flops=6 * 10**9, bytes_accessed=10**7, transcendentals=2 * 10**6),
        name="attn_forward",
    )(x, w, noise, keep)


def ring_place(member):
    odd = lax.rem(member, 2)
    half = lax.div(member, 2)
    return half + odd * (E - 1 - 2 * half)


def ring_member(place):
    late = lax.div(place, E // 2)
    return 2 * place + late * (2 * E - 1 - 4 * place)


class Peers:
    def __init__(self):
        dp = lax.axis_index("dp")
        tensor = lax.axis_index("tensor")
        self.member = lax.rem(dp, E)
        self.base = dp - self.member
        self.place = ring_place(self.member)
        self.across = {"tensor": lax.rem(tensor + 2, 4)}
        self.core = {"tensor": tensor + 1 - 2 * lax.rem(tensor, 2)}
        self.next = ({"dp": self.base + self.behind(1, 1)}, {"dp": self.base + self.behind(0, 1)})
        self.sends = []

    def behind(self, way, k):
        step = E - k if way == 0 else k
        return ring_member(lax.rem(self.place + step, E))

    def ahead(self, by):
        return lax.rem(self.member + by, E)

    def came(self, by):
        return lax.rem(self.member + E - by, E)

    def meet(self):
        barrier = pltpu.get_barrier_semaphore()
        others = [{"dp": self.base + self.ahead(by)} for by in range(1, E)] + [self.across, self.core]
        for device in others:
            pl.semaphore_signal(barrier, inc=1, device_id=device, device_id_type=pl.DeviceIdType.MESH)
        pl.semaphore_wait(barrier, len(others))

    def send(self, src, dst, sems, at, device):
        copy = pltpu.make_async_remote_copy(
            src_ref=src,
            dst_ref=dst,
            send_sem=sems[0].at[at],
            recv_sem=sems[1].at[at],
            device_id=device,
            device_id_type=pl.DeviceIdType.MESH,
        )
        copy.start()
        self.sends.append(copy)
        return copy


def expert_step(x, dy, gate, w_ref, g_ref, y_ref, dx_ref, meanwhile):
    weight = jnp.maximum(gate, 0.0)
    d_rows = (dy.astype(F32) * weight).astype(BF16)

    def hidden(i, carry):
        r = 2 * lax.rem(i, 2) + lax.div(i, 2)
        w1 = w_ref[r, :, 0].reshape(D, FFS)
        w2 = w_ref[r, :, 1].reshape(D, FFS)
        a = dot(x, w1)
        a2 = a * a
        th = jnp.tanh(0.7978845608028654 * a * (1.0 + 0.044715 * a2))
        half = 0.5 * (1.0 + th)
        hid = (a * half).astype(BF16)
        slope = half + 0.5 * a * (1.0 - th * th) * (0.7978845608028654 * (1.0 + 3 * 0.044715 * a2))
        da = (dot(d_rows, w2) * slope).astype(BF16)
        y_ref[...] += dot_nt(hid, w2)
        dx_ref[...] += dot_nt(da, w1)
        g_ref[r, 0] += dot_tn(x, da)
        g_ref[r, 1] += dot_tn(d_rows, hid)
        meanwhile(i)
        return carry

    y_ref[...] = jnp.zeros_like(y_ref)
    dx_ref[...] = jnp.zeros_like(dx_ref)
    lax.fori_loop(0, 4, hidden, 0)
    y = y_ref[...]
    dgate = jnp.where(gate >= 0, jnp.sum(dy.astype(F32) * y, axis=1, keepdims=True), 0.0)
    return (y * weight).astype(BF16), dx_ref[...], dgate


GIVEN, PASSED, DY_AT = (1, 2, 4, 6, 7), (1, 3), 3
HOP0, PASSED_EX = 5, 4
NEXT_AT, SUMS_AT, Y_AT = 0, 2, 5
HOPS_AT = ()


def front_kernel(
    imgs, pack_ref, ew_ref, dy_ref, x_ref, noise_ref, keep_ref,
    h_out, dy_out, t_in, y_out, y_first, y_second, g_out, sum_out, w_out, x1_ref, qkv_ref, o_ref, lse_ref, probs_ref,
    w_s, chunk_s, we_s, g_s, xs, dys, y_s, dx_s, t_s, own_s, y_low, pass_s, g_low,
    p_s, p_r, px_s, px_r, pc_s, pc_r, d_s, d_r, h_s, h_r, e_s, e_r, ex_s, ex_r, ec_s, ec_r, t_ss, t_r, local, stage, y_sem, g_sem, yf_s, yf_r,
):
    peers = Peers()
    member = peers.member
    d_own = pack_ref.shape[0]
    half = E // 2
    peers.meet()

    def rows(of):
        return pl.ds(pl.multiple_of(of * d_own, 16), d_own)

    own_pack = pltpu.make_async_copy(pack_ref, w_s.at[0, rows(member)], local.at[0])
    own_pack.start()

    ring, px, pc = {}, {}, {}

    def pass_pack(number, of, src, way=None, k=None):
        if way is not None:
            ring[way, k] = peers.send(src, w_s.at[0, rows(of)], (p_s, p_r), (way, k), peers.next[way])
        px[number] = peers.send(src, w_s.at[1, rows(of)], (px_s, px_r), number, peers.across)
        pc[0, number] = peers.send(src, w_s.at[2, rows(of)], (pc_s, pc_r), (0, number), peers.core)

    arrivals = [(0, k) if i == 0 else (1, k) for k in range(1, half + 1) for i in range(2 if k < half else 1)]
    owners = [member] + [peers.behind(way, k) for way, k in arrivals]

    def pass_x(number):
        px[number].wait_recv()
        at = rows(owners[number])
        pc[1, number] = peers.send(w_s.at[1, at], w_s.at[3, at], (pc_s, pc_r), (1, number), peers.core)

    far = (1, 7, 2, 6, 3, 5, 4)
    e_copy, ex, ec = {}, {}, {}

    def give_e(part):
        for by in part:
            to = peers.ahead(by)
            e_copy[by] = peers.send(ew_ref.at[to], we_s.at[0, member], (e_s, e_r), by, {"dp": peers.base + to})

    def pass_e(by):
        if by:
            e_copy[by].wait_recv()
        of = peers.came(by)
        src = we_s.at[0, of] if by else ew_ref.at[member]
        ex[by] = peers.send(src, we_s.at[1, of], (ex_s, ex_r), by, peers.across)
        ec[0, by] = peers.send(src, we_s.at[2, of], (ec_s, ec_r), (0, by), peers.core)

    def slice_copy(to, of, sent, got, at, device):
        return pltpu.make_async_remote_copy(
            src_ref=we_s.at[0 if to == 1 else 1, of],
            dst_ref=we_s.at[to, of],
            send_sem=sent.at[at],
            recv_sem=got.at[at],
            device_id=device,
            device_id_type=pl.DeviceIdType.MESH,
        )

    def ex_core(by):
        return slice_copy(3, peers.came(by), ec_s, ec_r, (1, by), peers.core)

    def pass_ex(by):
        of = peers.came(by)
        slice_copy(1, of, ex_s, ex_r, by, peers.across).wait_recv()
        ex_core(by).start()

    def block_at(c, k):
        return peers.behind(c % 2, k) * imgs + c

    def row_copy(out, sems, c, k, src=None):
        at = block_at(c, k)
        return pltpu.make_async_remote_copy(
            src_ref=out.at[at] if src is None else src,
            dst_ref=out.at[at],
            send_sem=sems[0].at[c, k],
            recv_sem=sems[1].at[c, k],
            device_id=peers.next[c % 2],
            device_id_type=pl.DeviceIdType.MESH,
        )

    h_sems, d_sems = (h_s, h_r), (d_s, d_r)

    def row_hop(k):
        for c in range(imgs):
            for out, sems in ((h_out, h_sems), (dy_out, d_sems)):
                row_copy(out, sems, c, k - 1).wait_recv()
                row_copy(out, sems, c, k).start()

    def give_dy():
        for c in range(imgs):
            row_copy(dy_out, d_sems, c, 0, dy_ref.at[c]).start()

    ring[0, 0] = peers.send(pack_ref, w_s.at[0, rows(member)], (p_s, p_r), (0, 0), peers.next[0])
    pass_pack(0, member, pack_ref, 1, 0)
    give_e(far[:GIVEN[0]])
    pass_e(0)
    if DY_AT == 0:
        give_dy()
    keepers = [
        pltpu.make_async_copy(ew_ref.at[member], we_s.at[0, member], local.at[2]),
    ] + [
        pltpu.make_async_copy(dy_ref.at[c], dy_out.at[member * imgs + c], local.at[3 + c]) for c in range(imgs)
    ]
    for copy in keepers:
        copy.start()
    for number, (way, k) in enumerate(arrivals, 1):
        ring[way, k - 1].wait_recv()
        of = owners[number]
        last = half if way == 0 else half - 1
        pass_pack(number, of, w_s.at[0, rows(of)], way if k < last else None, k)
        if number >= 2:
            pass_x(number - 2)
        if number == 4:
            give_e(far[GIVEN[0]:GIVEN[1]])
    give_e(far[GIVEN[1]:GIVEN[2]])
    if DY_AT == 1:
        give_dy()
    for number in range(len(arrivals) - 1, len(arrivals) + 1):
        pass_x(number)
    for number in range(E):
        pc[0, number].wait_recv()
        pc[1, number].wait_recv()
    own_pack.wait()
    keepers.append(pltpu.make_async_copy(w_s, w_out, local.at[1]))
    keepers[-1].start()

    par = params_of(w_s[0])
    done = 0
    for c in range(imgs):
        for by in far[done : PASSED[c]]:
            pass_e(by)
            pass_ex((0, *far)[done])
            done += 1
        attend(
            x_ref[c], par, lambda r: w_s[r], noise_ref[c], keep_ref[c],
            chunk_s.at[c], *(ref.at[c] for ref in (x1_ref, qkv_ref, o_ref, lse_ref, probs_ref)),
        )
        if HOP0 == 0:
            row_copy(h_out, h_sems, c, 0, chunk_s.at[c]).start()
        keepers.append(
            pltpu.make_async_copy(chunk_s.at[c], h_out.at[member * imgs + c], local.at[3 + imgs + c])
        )
        keepers[-1].start()
        give_e(far[GIVEN[2 + c]:GIVEN[3 + c]])
    if DY_AT == 2:
        give_dy()

    def first_hops():
        for c in range(imgs):
            row_copy(h_out, h_sems, c, 0, chunk_s.at[c]).start()
        if DY_AT == 3:
            give_dy()

    for i, by in enumerate(far):
        if i >= done:
            pass_e(by)
            if i <= PASSED_EX:
                pass_ex((0, *far)[i])
        if HOP0 and i == HOP0:
            first_hops()
        if i in HOPS_AT:
            row_hop(1 + HOPS_AT.index(i))
    g_s[...] = jnp.zeros_like(g_s)
    for by in range(E):
        ec[0, by].wait_recv()
    for copy in keepers:
        copy.wait()

    row16 = iota((16, D), 0)
    eye = iota((PAD, PAD), 0) == iota((PAD, PAD), 1)

    def sum_copy(c, k):
        return pltpu.make_async_remote_copy(
            src_ref=pass_s.at[lax.rem(k, 2), c],
            dst_ref=t_in.at[k - 1, c],
            send_sem=t_ss.at[c, k - 1],
            recv_sem=t_r.at[c, k - 1],
            device_id=peers.next[c % 2],
            device_id_type=pl.DeviceIdType.MESH,
        )

    def sums_to_hand(k):
        return [pltpu.make_async_copy(t_in.at[k - 2, c], t_s.at[c], stage.at[2, c]) for c in range(imgs)]

    def rows_to_hand(k):
        slot = lax.rem(k, 2)
        return [
            pltpu.make_async_copy(out.at[block_at(c, k)], held.at[slot, c], stage.at[i, c])
            for c in range(imgs)
            for i, (out, held) in enumerate(((h_out, xs), (dy_out, dys)))
        ]

    def start(copies):
        for copy in copies:
            copy.start()

    def finish(copies):
        for copy in copies:
            copy.wait()

    def y_copy(c, hop):
        return pltpu.make_async_remote_copy(
            src_ref=y_out.at[1, c] if hop == 0 else xs.at[0, c],
            dst_ref=y_first.at[c] if hop == 0 else y_second.at[c],
            send_sem=yf_s.at[hop, c],
            recv_sem=yf_r.at[hop, c],
            device_id=peers.next[c % 2],
            device_id_type=pl.DeviceIdType.MESH,
        )

    def keep_y(k):
        return pltpu.make_async_copy(y_low, y_out.at[k], y_sem)

    def step(k, carry):
        slot = lax.rem(k, 2)
        finish(rows_to_hand(k))

        def meanwhile(r):
            @pl.when((r == 0) & (k == 0))
            def _():
                for by in far[PASSED_EX:]:
                    pass_ex(by)

            @pl.when((r == 1) & (k == 0))
            def _():
                for by in range(E):
                    ex_core(by).wait_recv()

            for c in range(imgs):
                for out, sems in ((h_out, h_sems), (dy_out, d_sems)):

                    @pl.when((r == NEXT_AT) & (k >= len(HOPS_AT)) & (k < E - 1))
                    def _():
                        row_copy(out, sems, c, k).wait_recv()

                    @pl.when((r == NEXT_AT) & (k >= len(HOPS_AT)) & (k < E - 2))
                    def _():
                        row_copy(out, sems, c, k + 1).start()

            @pl.when((r == NEXT_AT) & (k < E - 1))
            def _():
                start(rows_to_hand(k + 1))

            @pl.when((r == SUMS_AT) & (k >= 2))
            def _():
                for c in range(imgs):
                    sum_copy(c, k - 1).wait_recv()
                start(sums_to_hand(k))

        columns = []
        for c in range(imgs):
            meta = xs[slot, c, PAD - 16 :, :].astype(F32)
            line = jnp.sum(jnp.where(row16 == 8 + member, meta, 0.0), axis=0, keepdims=True)[:, :PAD]
            columns.append(jnp.sum(jnp.where(eye, line, 0.0), axis=1, keepdims=True))
        y, dx, dgate = expert_step(
            xs[slot].reshape(imgs * PAD, D), dys[slot].reshape(imgs * PAD, D), jnp.concatenate(columns, axis=0),
            we_s, g_s, y_s, dx_s, meanwhile,
        )

        @pl.when(k >= 3)
        def _():
            for c in range(imgs):
                sum_copy(c, k - 2).wait_send()

        @pl.when(k >= 1)
        def _():
            keep_y(k - 1).wait()

        for c in range(imgs):
            span = slice(c * PAD, (c + 1) * PAD)
            line = jnp.sum(jnp.where(eye, dgate[span], 0.0), axis=0, keepdims=True)
            line = jnp.concatenate([line, jnp.zeros((1, D - PAD), F32)], axis=1)
            tail = dx[span][PAD - 16 :] + jnp.where(row16 == 8 + member, line, 0.0)
            pass_s[slot, c] = jnp.concatenate([dx[span][: PAD - 16], tail], axis=0).astype(BF16)
            y_low[c] = y[span]

        keep_y(k).start()

        @pl.when(k == 0)
        def _():
            own_s[...] = pass_s[0]

        @pl.when(k >= 2)
        def _():
            finish(sums_to_hand(k))
            pass_s[slot] = (pass_s[slot].astype(F32) + t_s[...].astype(F32)).astype(BF16)

        @pl.when(k >= 1)
        def _():
            for c in range(imgs):
                sum_copy(c, k).start()

        @pl.when(k == Y_AT)
        def _():
            for c in range(imgs):
                y_copy(c, 0).start()

        return carry

    start(rows_to_hand(0))
    lax.fori_loop(0, E, step, 0)

    for c in range(imgs):
        y_copy(c, 0).wait()
    y_loads = [pltpu.make_async_copy(y_first, xs.at[0], stage.at[0, 0]), pltpu.make_async_copy(y_out.at[2], dys.at[0], stage.at[1, 0])]
    start(y_loads)
    for i in range(8):
        if i == 2:
            finish(y_loads)
            xs[0] = (xs[0].astype(F32) + dys[0].astype(F32)).astype(BF16)
            for c in range(imgs):
                y_copy(c, 1).start()
        r, kind = i // 2, i % 2
        if i >= 2:
            pltpu.make_async_copy(g_low.at[i % 2], g_out.at[r, :, kind], g_sem.at[i % 2]).wait()
        g_low[i % 2] = g_s[r, kind].astype(BF16).reshape(E, d_own, FFS)
        pltpu.make_async_copy(g_low.at[i % 2], g_out.at[r, :, kind], g_sem.at[i % 2]).start()
    for c in range(imgs):
        sum_copy(c, E - 1).wait_recv()
    start(sums_to_hand(E))
    finish(sums_to_hand(E))
    sum_out[...] = (own_s[...].astype(F32) + t_s[...].astype(F32)).astype(BF16)
    keep_y(E - 1).wait()
    for c in range(imgs):
        y_copy(c, 1).wait()
    for i in range(2):
        pltpu.make_async_copy(g_low.at[i], g_out.at[3, :, i], g_sem.at[i]).wait()
    for c in range(imgs):
        sum_copy(c, E - 2).wait_send()
        sum_copy(c, E - 1).wait_send()
        for k in range(E - 1):
            row_copy(h_out, h_sems, c, k).wait_send()
            row_copy(dy_out, d_sems, c, k).wait_send()
    for by in range(E):
        ex_core(by).wait_send()
    for copy in peers.sends:
        copy.wait_send()


def front(pack, ew, dy, x, noise, keep):
    imgs = x.shape[0]
    d_own = pack.shape[0]
    vm = pl.BlockSpec(memory_space=pltpu.VMEM)
    hbm = pl.BlockSpec(memory_space=pl.ANY)
    table = jax.ShapeDtypeStruct((E * imgs, PAD, D), BF16)
    dma = pltpu.SemaphoreType.DMA
    rows = (imgs, PAD, D)
    return pl.pallas_call(
        functools.partial(front_kernel, imgs),
        out_shape=(
            table,
            table,
            jax.ShapeDtypeStruct((E - 1,) + rows, BF16),
            jax.ShapeDtypeStruct((E,) + rows, BF16),
            jax.ShapeDtypeStruct(rows, BF16),
            jax.ShapeDtypeStruct(rows, BF16),
            jax.ShapeDtypeStruct((4, E, 2, d_own, FFS), BF16),
            jax.ShapeDtypeStruct(rows, BF16),
            jax.ShapeDtypeStruct((4, E * d_own, D + 128), BF16),
        )
        + attn_shapes(imgs),
        in_specs=[vm, hbm, hbm, vm, vm, vm],
        out_specs=(hbm,) * 7 + (vm, hbm) + (vm,) * 5,
        scratch_shapes=[
            pltpu.VMEM((4, E * d_own, D + 128), BF16),
            pltpu.VMEM((imgs, PAD, D), BF16),
            pltpu.VMEM((4, E, 2, d_own, FFS), BF16),
            pltpu.VMEM((4, 2, D, FFS), F32),
            pltpu.VMEM((2, imgs, PAD, D), BF16),
            pltpu.VMEM((2, imgs, PAD, D), BF16),
            pltpu.VMEM((imgs * PAD, D), F32),
            pltpu.VMEM((imgs * PAD, D), F32),
            pltpu.VMEM(rows, BF16),
            pltpu.VMEM(rows, BF16),
            pltpu.VMEM(rows, BF16),
            pltpu.VMEM((2,) + rows, BF16),
            pltpu.VMEM((2, E, d_own, FFS), BF16),
            dma((2, 4)), dma((2, 4)), dma((E,)), dma((E,)), dma((2, E)), dma((2, E)),
            dma((imgs, E - 1)), dma((imgs, E - 1)), dma((imgs, E - 1)), dma((imgs, E - 1)),
            dma((E,)), dma((E,)), dma((E,)), dma((E,)), dma((2, E)), dma((2, E)),
            dma((imgs, E - 1)), dma((imgs, E - 1)),
            dma((3 + 2 * imgs,)), dma((3, imgs)), dma(()), dma((2,)), dma((2, imgs)), dma((2, imgs)),
        ],
        compiler_params=pltpu.CompilerParams(
            vmem_limit_bytes=VMEM_LIMIT, collective_id=0, has_side_effects=True
        ),
        cost_estimate=pl.CostEstimate(flops=10**11, bytes_accessed=10**8, transcendentals=2 * 10**7),
        name="front",
    )(pack, ew, dy, x, noise, keep)


def expert_kernel(nb, who_ref, *refs):
    h_in, dy_in, w_in = refs[:3]
    outs = refs[3:]
    dx_out, y_out, rows_out, hid_out, tiles_ref = outs[:5]
    (h, dy, y_t, dx_t, w_s, gate_s, slot_s, dgate_s, xs, dys, hid_s, rows_s, lo_s, hi_s, in_sem, out_sem, row_sem, hid_sem, w_sem) = outs[5:]
    me = who_ref[0]
    loads = [
        pltpu.make_async_copy(h_in, h, in_sem.at[0]),
        pltpu.make_async_copy(dy_in, dy, in_sem.at[1]),
    ]
    for b in range(E):
        at = pl.ds(b * (D // E), D // E)
        for r in range(4):
            loads.append(pltpu.make_async_copy(w_in.at[r, b], w_s.at[r, :, at], w_sem.at[r, b]))
    for copy in loads:
        copy.start()
    y_t[...] = jnp.zeros_like(y_t)
    dx_t[...] = jnp.zeros_like(dx_t)
    dgate_s[...] = jnp.zeros_like(dgate_s)
    for copy in loads:
        copy.wait()

    row16 = iota((16, D), 0)
    for b in range(nb):
        meta = h[b, PAD - 16 : PAD, :].astype(F32)
        gate_s[b : b + 1, :] = jnp.sum(jnp.where(row16 == 8 + me, meta, 0.0), axis=0, keepdims=True)[:, :PAD]
    gates = gate_s[...]
    named = (gates >= 0) & (iota((nb, PAD), 1) < SEQ)
    ones = named.astype(F32).astype(BF16)
    upto = dot(ones, (iota((PAD, PAD), 0) <= iota((PAD, PAD), 1)).astype(F32).astype(BF16))
    count = dot(ones, jnp.ones((PAD, PAD), BF16)).astype(BF16)
    before = dot((iota((nb, nb), 0) > iota((nb, nb), 1)).astype(F32).astype(BF16), count)
    slot_s[...] = jnp.where(named, before + upto - 1.0, -1.0).astype(jnp.int32)
    ends = jnp.where(named, before + upto, before)
    for b in range(nb):
        lo_s[b] = jnp.max(before[b : b + 1, :]).astype(jnp.int32)
        hi_s[b] = jnp.max(ends[b : b + 1, :]).astype(jnp.int32)
    tiles = lax.div(hi_s[nb - 1] + TILE - 1, TILE)
    tiles_ref[0] = tiles

    def meets(b, first):
        return (lo_s[b] < first + TILE) & (hi_s[b] > first) & (hi_s[b] > lo_s[b])

    def place(b, first):
        return iota((TILE, PAD), 0) + first == slot_s[pl.ds(b, 1), :]

    def step(t, carry):
        first = t * TILE
        slot = lax.rem(t, 2)
        xs[...] = jnp.zeros_like(xs)
        dys[...] = jnp.zeros_like(dys)

        def collect(b, gcol):
            def one(gcol):
                hit = place(b, first)
                p = hit.astype(F32).astype(BF16)
                xs[...] += dot(p, h[b])
                dys[...] += dot(p, dy[b])
                return gcol + jnp.sum(jnp.where(hit, gate_s[pl.ds(b, 1), :], 0.0), axis=1, keepdims=True)

            return lax.cond(meets(b, first), one, lambda g: g, gcol)

        gcol = lax.fori_loop(0, nb, collect, jnp.zeros((TILE, 1), F32))

        def drain(s):
            pltpu.make_async_copy(rows_s.at[s], rows_out.at[:, pl.ds(0, TILE)], row_sem.at[s]).wait()
            pltpu.make_async_copy(hid_s.at[s], hid_out.at[:, pl.ds(0, TILE)], hid_sem.at[s]).wait()

        @pl.when(t >= 2)
        def _():
            drain(slot)

        x = xs[...].astype(BF16)
        g_rows = (dys[...] * gcol).astype(BF16)
        rows_s[slot, 0] = x
        rows_s[slot, 1] = g_rows
        y = jnp.zeros((TILE, D), F32)
        dx = jnp.zeros((TILE, D), F32)
        for r in range(4):
            w1, w2 = w_s.at[r, 0], w_s.at[r, 1]
            a = dot(x, w1[...])
            a2 = a * a
            th = jnp.tanh(0.7978845608028654 * a * (1.0 + 0.044715 * a2))
            half = 0.5 * (1.0 + th)
            hid = (a * half).astype(BF16)
            slope = half + 0.5 * a * (1.0 - th * th) * (0.7978845608028654 * (1.0 + 3 * 0.044715 * a2))
            da = (dot(g_rows, w2[...]) * slope).astype(BF16)
            y = y + dot_nt(hid, w2[...])
            dx = dx + dot_nt(da, w1[...])
            hid_s[slot, 0, :, r * FFS : (r + 1) * FFS] = da
            hid_s[slot, 1, :, r * FFS : (r + 1) * FFS] = hid
        at = pl.ds(pl.multiple_of(first, TILE), TILE)
        pltpu.make_async_copy(rows_s.at[slot], rows_out.at[:, at], row_sem.at[slot]).start()
        pltpu.make_async_copy(hid_s.at[slot], hid_out.at[:, at], hid_sem.at[slot]).start()
        dgate = jnp.sum(dys[...] * y, axis=1, keepdims=True)
        y_low = (y * gcol).astype(BF16)
        dx_low = dx.astype(BF16)

        def give(b, carry):
            @pl.when(meets(b, first))
            def _():
                hit = place(b, first)
                p = hit.astype(F32).astype(BF16)
                y_t[b] = y_t[b] + dot_tn(p, y_low).astype(BF16)
                dx_t[b] = dx_t[b] + dot_tn(p, dx_low).astype(BF16)
                dgate_s[pl.ds(b, 1), :] += jnp.sum(jnp.where(hit, dgate, 0.0), axis=0, keepdims=True)

            return carry

        lax.fori_loop(0, nb, give, 0)
        return carry

    lax.fori_loop(0, tiles, step, 0)
    for back in (1, 2):

        @pl.when(tiles >= back)
        def _():
            s = lax.rem(tiles - back, 2)
            pltpu.make_async_copy(rows_s.at[s], rows_out.at[:, pl.ds(0, TILE)], row_sem.at[s]).wait()
            pltpu.make_async_copy(hid_s.at[s], hid_out.at[:, pl.ds(0, TILE)], hid_sem.at[s]).wait()

    for b in range(nb):
        tail = dx_t[b, PAD - 16 : PAD, :].astype(F32)
        line = jnp.concatenate([dgate_s[b : b + 1, :], jnp.zeros((1, D - PAD), F32)], axis=1)
        dx_t[b, PAD - 16 : PAD, :] = (tail + jnp.where(row16 == 8 + me, line, 0.0)).astype(BF16)
    stores = [
        pltpu.make_async_copy(dx_t, dx_out, out_sem.at[0]),
        pltpu.make_async_copy(y_t, y_out, out_sem.at[1]),
    ]
    for copy in stores:
        copy.start()
    for copy in stores:
        copy.wait()


def expert_rows(nb):
    return -(-nb * SEQ // TILE) * TILE


def experts(member, h_all, dy_all, weights):
    nb = h_all.shape[0]
    rows = expert_rows(nb)
    hbm = pl.BlockSpec(memory_space=pl.ANY)
    sm = pl.BlockSpec(memory_space=pltpu.SMEM)
    table = jax.ShapeDtypeStruct((nb, PAD, D), BF16)
    return pl.pallas_call(
        functools.partial(expert_kernel, nb),
        out_shape=[
            table,
            table,
            jax.ShapeDtypeStruct((2, rows, D), BF16),
            jax.ShapeDtypeStruct((2, rows, 4 * FFS), BF16),
            jax.ShapeDtypeStruct((1,), jnp.int32),
        ],
        in_specs=[sm, hbm, hbm, hbm],
        out_specs=[hbm] * 4 + [sm],
        scratch_shapes=[
            pltpu.VMEM((nb, PAD, D), BF16),
            pltpu.VMEM((nb, PAD, D), BF16),
            pltpu.VMEM((nb, PAD, D), BF16),
            pltpu.VMEM((nb, PAD, D), BF16),
            pltpu.VMEM((4, 2, D, FFS), BF16),
            pltpu.VMEM((nb, PAD), F32),
            pltpu.VMEM((nb, PAD), jnp.int32),
            pltpu.VMEM((nb, PAD), F32),
            pltpu.VMEM((TILE, D), F32),
            pltpu.VMEM((TILE, D), F32),
            pltpu.VMEM((2, 2, TILE, 4 * FFS), BF16),
            pltpu.VMEM((2, 2, TILE, D), BF16),
            pltpu.SMEM((nb,), jnp.int32),
            pltpu.SMEM((nb,), jnp.int32),
            pltpu.SemaphoreType.DMA((2,)),
            pltpu.SemaphoreType.DMA((2,)),
            pltpu.SemaphoreType.DMA((2,)),
            pltpu.SemaphoreType.DMA((2,)),
            pltpu.SemaphoreType.DMA((4, E)),
        ],
        compiler_params=pltpu.CompilerParams(vmem_limit_bytes=VMEM_LIMIT),
        cost_estimate=pl.CostEstimate(flops=30 * 10**9, bytes_accessed=4 * 10**7, transcendentals=4 * 10**6),
        name="experts",
    )(member.reshape(1), h_all, dy_all, weights)


def expert_grad_kernel(tiles_ref, rows_ref, hid_ref, out_ref, acc):
    acc[...] = jnp.zeros_like(acc)

    def step(t, carry):
        at = pl.ds(pl.multiple_of(t * TILE, TILE), TILE)
        acc[...] += dot_tn(rows_ref[0, at, :], hid_ref[0, at, :])
        return carry

    lax.fori_loop(0, tiles_ref[0], step, 0)
    out_ref[0] = acc[...].astype(BF16)


def expert_grads(tiles, rows, hid, kind, base):
    n = rows.shape[1]
    return pl.pallas_call(
        expert_grad_kernel,
        grid_spec=pltpu.PrefetchScalarGridSpec(
            num_scalar_prefetch=1,
            grid=(2,),
            in_specs=[
                pl.BlockSpec((1, n, D), lambda s, _: (kind, 0, 0)),
                pl.BlockSpec((1, n, FFS), lambda s, _: (kind, 0, base + s)),
            ],
            out_specs=pl.BlockSpec((1, D, FFS), lambda s, _: (s, 0, 0)),
            scratch_shapes=[pltpu.VMEM((D, FFS), F32)],
        ),
        out_shape=jax.ShapeDtypeStruct((2, D, FFS), BF16),
        compiler_params=pltpu.CompilerParams(vmem_limit_bytes=VMEM_LIMIT),
        cost_estimate=pl.CostEstimate(flops=4 * 10**9, bytes_accessed=15 * 10**6, transcendentals=0),
        name="expert_grads",
    )(tiles, rows, hid)


def unpack_kernel(who_ref, *refs):
    blocks, (in_ref, out_ref) = refs[:E], refs[E:]
    for by in range(E):
        in_ref[who_ref[by]] = blocks[by][0].astype(F32)
        out_ref[who_ref[by]] = blocks[by][1].astype(F32)


def unpack(who, blocks):
    vm = pl.BlockSpec(memory_space=pltpu.VMEM)
    whole = jax.ShapeDtypeStruct((E,) + blocks[0].shape[1:], F32)
    return pl.pallas_call(
        unpack_kernel,
        out_shape=(whole, whole),
        in_specs=[pl.BlockSpec(memory_space=pltpu.SMEM)] + [vm] * E,
        out_specs=(vm, vm),
        compiler_params=pltpu.CompilerParams(vmem_limit_bytes=VMEM_LIMIT),
        cost_estimate=pl.CostEstimate(flops=10**6, bytes_accessed=7 * 10**6, transcendentals=0),
        name="unpack",
    )(who, *blocks)


def lay_out_kernel(imgs, at_ref, *refs):
    parts, out_ref, held, sem = refs[:4], refs[4], refs[5], refs[6]
    copies = [pltpu.make_async_copy(parts[s], held.at[s], sem.at[s]) for s in range(4)]
    for copy in copies:
        copy.start()
    for copy in copies:
        copy.wait()
    for i in range(4 * imgs):
        out_ref[i * SEQ : (i + 1) * SEQ, :] = held[at_ref[i // imgs], i % imgs, :SEQ, :]


def lay_out(at, parts):
    imgs = parts[0].shape[0]
    hbm = pl.BlockSpec(memory_space=pl.ANY)
    return pl.pallas_call(
        functools.partial(lay_out_kernel, imgs),
        out_shape=jax.ShapeDtypeStruct((4 * imgs * SEQ, D), BF16),
        in_specs=[pl.BlockSpec(memory_space=pltpu.SMEM)] + [hbm] * 4,
        out_specs=pl.BlockSpec(memory_space=pltpu.VMEM),
        scratch_shapes=[pltpu.VMEM((4, imgs, PAD, D), BF16), pltpu.SemaphoreType.DMA((4,))],
        compiler_params=pltpu.CompilerParams(vmem_limit_bytes=VMEM_LIMIT),
        cost_estimate=pl.CostEstimate(flops=10**6, bytes_accessed=5 * 10**6, transcendentals=0),
        name="lay_out",
    )(at, *parts)


class Backward:
    def __init__(self, imgs, dh_of, saved, w_ref, dx1_s, low_s, h1_s, dh1_s, dqkv_s, o_s):
        self.imgs, self.dh_of, self.saved, self.w_ref = imgs, dh_of, saved, w_ref
        self.dx1_s, self.low_s, self.h1_s, self.dh1_s, self.dqkv_s, self.o_s = dx1_s, low_s, h1_s, dh1_s, dqkv_s, o_s
        self.par = params_of(w_ref[0])
        self.row_ok = iota((PAD, 1), 0) < SEQ
        self.started = False

    def span(self, c):
        return slice(c * PAD, (c + 1) * PAD)

    def first(self):
        x1_in, x_in, dy_in, probs_in = self.saved[:4]
        par, row_ok = self.par, self.row_ok
        lane_ok = iota((E, PAD), 1) < SEQ
        router = par[8:16].astype(BF16)
        gain = jnp.zeros((1, D), F32)
        bias = jnp.zeros((1, D), F32)
        g_router = jnp.zeros((E, D), F32)
        for c in range(self.imgs):
            arrived = self.dh_of(c).astype(F32)
            dgate = arrived[PAD - 8 :, :PAD]
            probs = probs_in[c]
            dlogits = probs * (dgate - jnp.sum(probs * dgate, axis=0, keepdims=True))
            dlogits = jnp.where(lane_ok, dlogits, 0.0).astype(BF16)
            unit, scale = normalise(x1_in[c])
            h2 = (unit * par[2:3] + par[3:4]).astype(BF16)
            g_router = g_router + dot(dlogits, h2)
            dh2 = jnp.where(row_ok, arrived + dot_tn(dlogits, router), 0.0)
            gain = gain + jnp.sum(dh2 * unit, axis=0, keepdims=True)
            bias = bias + jnp.sum(dh2, axis=0, keepdims=True)
            dx1 = dy_in[c].astype(F32) + norm_back(dh2, unit, scale, par[2:3])
            self.dx1_s[self.span(c), :] = dx1
            self.low_s[self.span(c), :] = dx1.astype(BF16)
            unit1, _ = normalise(x_in[c].astype(F32))
            self.h1_s[self.span(c), :] = (unit1 * par[0:1] + par[1:2]).astype(BF16)
        self.small2 = [gain, bias, jnp.zeros((4, D), F32), g_router]

    def heads(self, r):
        qkv_in, o_in, lse_in = self.saved[4:]
        key_ok = iota((PAD, PAD), 1) < SEQ
        low, h1, w = self.low_s[...], self.h1_s[...], self.w_ref[r]
        dout = dot(low, w[:, 9 * HD : D]).astype(BF16)
        for c in range(self.imgs):
            qkv = qkv_in[c, r]
            lse = lse_in[c]
            self.o_s[self.span(c), :] = o_in[c, r]
            dqs, dks, dvs = [], [], []
            for h in range(3):
                q = qkv[:, h * HD : (h + 1) * HD]
                k = qkv[:, (3 + h) * HD : (4 + h) * HD]
                v = qkv[:, (6 + h) * HD : (7 + h) * HD]
                do = dout[self.span(c), h * HD : (h + 1) * HD]
                s = dot_nt(q, k) * HD ** (-0.5)
                p = jnp.where(key_ok, jnp.exp(s - lse[:, 3 * r + h : 3 * r + h + 1]), 0.0)
                dvs.append(dot_tn(p.astype(BF16), do).astype(BF16))
                dp = dot_nt(do, v)
                ds = (p * (dp - jnp.sum(p * dp, axis=-1, keepdims=True))).astype(BF16)
                dqs.append((dot(ds, k) * HD ** (-0.5)).astype(BF16))
                dks.append((dot_tn(ds, q) * HD ** (-0.5)).astype(BF16))
            self.dqkv_s[self.span(c), :] = jnp.concatenate(dqs + dks + dvs, axis=1)
        dqkv = self.dqkv_s[...]
        part = dot_nt(dqkv, w[:, : 9 * HD])
        self.dh1_s[...] = self.dh1_s[...] + part if self.started else part
        self.started = True
        return jnp.concatenate([dot_tn(h1, dqkv), dot_tn(low, self.o_s[...])], axis=1).astype(BF16)

    def last(self, dtok_ref):
        x_in = self.saved[1]
        gain = jnp.zeros((1, D), F32)
        bias = jnp.zeros((1, D), F32)
        for c in range(self.imgs):
            dh1 = jnp.where(self.row_ok, self.dh1_s[self.span(c), :], 0.0)
            unit, scale = normalise(x_in[c].astype(F32))
            gain = gain + jnp.sum(dh1 * unit, axis=0, keepdims=True)
            bias = bias + jnp.sum(dh1, axis=0, keepdims=True)
            dtok_ref[c] = (self.dx1_s[self.span(c), :] + norm_back(dh1, unit, scale, self.par[0:1])).astype(BF16)
        return jnp.concatenate([gain, bias] + self.small2, axis=0)


def small_block(small, i, d_own):
    line = jnp.concatenate([small[:, i * d_own : (i + 1) * d_own], jnp.zeros((16, D - d_own), F32)], axis=1)
    return line.astype(BF16)


def backward_scratch(imgs):
    rows = imgs * PAD
    return [
        pltpu.VMEM((rows, D), F32),
        pltpu.VMEM((rows, D), BF16),
        pltpu.VMEM((rows, D), BF16),
        pltpu.VMEM((rows, D), F32),
        pltpu.VMEM((rows, 9 * HD), BF16),
        pltpu.VMEM((rows, 3 * HD), BF16),
    ]


def attn_backward_kernel(imgs, *refs):
    dh_in, saved, w_ref = refs[:imgs], refs[imgs : imgs + 7], refs[imgs + 7]
    packs, dtok_ref = refs[imgs + 8 : imgs + 11], refs[imgs + 11]
    n_dp, d_own = packs[0].shape[0], packs[0].shape[1] - 16
    back = Backward(imgs, lambda c: dh_in[c][...], saved, w_ref, *refs[imgs + 12 :])

    def pack_of(r):
        return packs[r] if r < 2 else packs[2].at[:, r - 2]

    back.first()
    for r in range(4):
        grad = back.heads(r)
        for i in range(n_dp):
            pack_of(r)[i, :d_own, :] = grad[i * d_own : (i + 1) * d_own]
    small = back.last(dtok_ref)
    for i in range(n_dp):
        for r in range(4):
            pack_of(r)[i, d_own:, :] = small_block(small, i, d_own)


def attn_backward(dh, saved, w, n_dp):
    imgs = len(dh)
    pack = (n_dp, D // n_dp + 16, D)
    vm = pl.BlockSpec(memory_space=pltpu.VMEM)
    return pl.pallas_call(
        functools.partial(attn_backward_kernel, imgs),
        out_shape=(
            jax.ShapeDtypeStruct(pack, BF16),
            jax.ShapeDtypeStruct(pack, BF16),
            jax.ShapeDtypeStruct((n_dp, 2) + pack[1:], BF16),
            jax.ShapeDtypeStruct((imgs, PAD, D), BF16),
        ),
        in_specs=[vm] * (imgs + 8),
        out_specs=(vm,) * 4,
        scratch_shapes=backward_scratch(imgs),
        compiler_params=pltpu.CompilerParams(vmem_limit_bytes=VMEM_LIMIT),
        cost_estimate=pl.CostEstimate(flops=12 * 10**9, bytes_accessed=2 * 10**7, transcendentals=2 * 10**6),
        name="attn_backward",
    )(*dh, *saved, w)


HOMES = ((), (0,), (1, 2), (3,), (4, 5), (6, 7), ())


def back_kernel(
    imgs, g_low, y_ref, yf_ref, dh_ref, x1_ref, x_ref, dy_ref, probs_ref, qkv_ref, o_ref, lse_ref, w_ref,
    out_all, dtok_all, g_out, total_ref,
    ga_s, gc_s, gx_s, pk_s, pkc_s, pkr_s, sm_s, smr_s, cs_s, cr_s, fs_s, fr_s, or_s, dt_s, y_s, yr_s,
    dx1_s, low_s, h1_s, dh1_s, dqkv_s, o_s,
    gc_ss, gc_r, gx_ss, gx_r, ga_ss, ga_r, pk_ss, pk_r, sm_ss, sm_r, c_ss, c_r, f_ss, f_r, row_ss, row_r, y_ss, y_r, local,
):
    peers = Peers()
    member = peers.member
    tensor = lax.axis_index("tensor")
    d_own = g_low.shape[3]
    peers.meet()
    loads = []

    def here(src, dst):
        copy = pltpu.make_async_copy(src, dst, local.at[len(loads)])
        copy.start()
        loads.append(copy)
        return copy

    def give_rows(kind, src, whole):
        here(src, whole.at[tensor])
        across = peers.send(src, whole.at[tensor], (row_ss, row_r), (kind, 0), peers.across)
        core = peers.send(src, whole.at[tensor], (row_ss, row_r), (kind, 1), peers.core)

        def onwards():
            across.wait_recv()
            other = lax.rem(tensor + 2, 4)
            copy = peers.send(whole.at[other], whole.at[other], (row_ss, row_r), (kind, 2), peers.core)
            return core, copy

        return onwards

    y_load = here(y_ref, y_s)
    yf_load = here(yf_ref, yr_s.at[1])
    y_sent = {}

    def y_hop(k):
        for c in range(imgs):
            if k > 3:
                y_sent[c, k - 1].wait_recv()
            src = yr_s.at[k - 2, c]
            src[...] = (src[...].astype(F32) + y_s[k, c].astype(F32)).astype(BF16)
            y_sent[c, k] = peers.send(src, yr_s.at[k - 1, c], (y_ss, y_r), (c, k - 1), peers.next[c % 2])

    def y_last():
        for c in range(imgs):
            y_sent[c, E - 1].wait_recv()
            total = yr_s[E - 2, c].astype(F32) + y_s[0, c].astype(F32)
            or_s[c] = (x1_ref[c] + total).astype(BF16)

    g_core = [
        peers.send(g_low.at[2 + s], gc_s.at[s], (gc_ss, gc_r), s, peers.core) for s in (1, 0)
    ][::-1]
    g_load = [here(g_low.at[s], ga_s.at[s]) for s in (1, 0)][::-1]
    y_load.wait()
    yf_load.wait()
    y_hop(3)
    order = (4, 3, 5, 2, 6, 1, 7, 0)
    gx = {}

    def pass_across():
        g_core[1].wait_recv()
        g_load[1].wait()
        for by in order:
            to = peers.ahead(by)
            ga_s[1, to] = (ga_s[1, to].astype(F32) + gc_s[1, to].astype(F32)).astype(BF16)
            gx[by] = peers.send(ga_s.at[1, to], gx_s.at[to], (gx_ss, gx_r), by, peers.across)
        g_core[0].wait_recv()
        g_load[0].wait()

    ga = {}

    def pass_home(by):
        gx[by].wait_recv()
        to = peers.ahead(by)
        part = ga_s[0, to].astype(F32) + gc_s[0, to].astype(F32)
        ga_s[0, to] = (part + gx_s[to].astype(F32)).astype(BF16)
        if by:
            device = {"dp": peers.base + to}
            ga[by] = peers.send(ga_s.at[0, to], g_out.at[member], (ga_ss, ga_r), by, device)
        else:
            here(ga_s.at[0, to], g_out.at[member])

    def homes(at):
        for number in HOMES[at]:
            pass_home(order[number])

    saved = (x1_ref, x_ref, dy_ref, probs_ref, qkv_ref, o_ref, lse_ref)
    back = Backward(imgs, lambda c: dh_ref[c], saved, w_ref, dx1_s, low_s, h1_s, dh1_s, dqkv_s, o_s)
    back.first()
    for r in (2, 3):
        grad = back.heads(r)
        for i in range(E):
            pkc_s[i, r - 2] = grad[i * d_own : (i + 1) * d_own]
        y_hop(r + 2)
        if r == 2:
            pass_across()
    pk_core = peers.send(pkc_s, pkr_s, (pk_ss, pk_r), 0, peers.core)
    for r in (0, 1):
        grad = back.heads(r)
        for i in range(E):
            pk_s[i, r, :d_own] = grad[i * d_own : (i + 1) * d_own]
        y_hop(6 + r)
        homes(r)
    small = back.last(dt_s)
    dtok_rows = give_rows(1, dt_s, dtok_all)
    for i in range(E):
        sm_s[i] = small_block(small, i, d_own)
    sm_core = peers.send(sm_s, smr_s, (sm_ss, sm_r), 0, peers.core)
    pk_core.wait_recv()
    sm_core.wait_recv()

    def term(of):
        weights = pk_s[of, :, :d_own].astype(F32) + pkr_s[of].astype(F32)
        both = sm_s[of].astype(F32) + smr_s[of].astype(F32)
        return jnp.concatenate([weights, jnp.broadcast_to(both[None], (2,) + both.shape)], axis=1)

    steps = (E // 2, E // 2 - 1)
    hops = {}

    def hop(way, i):
        value = term(peers.behind(1 - way, steps[way] - i))
        if i:
            hops[way, i - 1].wait_recv()
            value = value + cr_s[way, i - 1].astype(F32)
        cs_s[way, i] = value.astype(BF16)
        hops[way, i] = peers.send(cs_s.at[way, i], cr_s.at[way, i], (c_ss, c_r), (way, i), peers.next[way])

    for i in range(E // 2):
        hop(0, i)
        if i < steps[1]:
            hop(1, i)
        if i == 0:
            y_last()
            out_rows = give_rows(0, or_s, out_all)
        homes(2 + i)
    hops[1, steps[1] - 1].wait_recv()
    hops[0, steps[0] - 1].wait_recv()
    total = term(member) + cr_s[0, steps[0] - 1].astype(F32) + cr_s[1, steps[1] - 1].astype(F32)
    fs_s[...] = total[1].astype(BF16)
    final = peers.send(fs_s, fr_s, (f_ss, f_r), 0, peers.across)
    homes(6)
    dtok_rows = dtok_rows()
    out_rows = out_rows()
    final.wait_recv()
    total_ref[...] = total[0] + fr_s[...].astype(F32)
    for by in range(1, E):
        ga[by].wait_recv()
    for copy in (*out_rows, *dtok_rows):
        copy.wait_recv()
    for copy in loads:
        if all(copy is not other for other in (y_load, yf_load, *g_load)):
            copy.wait()
    for copy in peers.sends:
        copy.wait_send()


def back(g_low, y, y_begun, dh, saved, w):
    imgs = dh.shape[0]
    d_own = g_low.shape[3]
    vm = pl.BlockSpec(memory_space=pltpu.VMEM)
    hbm = pl.BlockSpec(memory_space=pl.ANY)
    dma = pltpu.SemaphoreType.DMA
    part = (E, 2, d_own, D)
    rows = (imgs, PAD, D)
    hop = (2, E // 2, 2, d_own + 16, D)
    return pl.pallas_call(
        functools.partial(back_kernel, imgs),
        out_shape=(
            jax.ShapeDtypeStruct((4,) + rows, BF16),
            jax.ShapeDtypeStruct((4,) + rows, BF16),
            jax.ShapeDtypeStruct(part, BF16),
            jax.ShapeDtypeStruct((d_own + 16, D), F32),
        ),
        in_specs=[hbm, hbm, hbm] + [vm] * 9,
        out_specs=(hbm, hbm, hbm, vm),
        scratch_shapes=[
            pltpu.VMEM((2,) + part, BF16),
            pltpu.VMEM((2,) + part, BF16),
            pltpu.VMEM(part, BF16),
            pltpu.VMEM((E, 2, d_own + 16, D), BF16),
            pltpu.VMEM(part, BF16),
            pltpu.VMEM(part, BF16),
            pltpu.VMEM((E, 16, D), BF16),
            pltpu.VMEM((E, 16, D), BF16),
            pltpu.VMEM(hop, BF16),
            pltpu.VMEM(hop, BF16),
            pltpu.VMEM((d_own + 16, D), BF16),
            pltpu.VMEM((d_own + 16, D), BF16),
            pltpu.VMEM(rows, BF16),
            pltpu.VMEM(rows, BF16),
            pltpu.VMEM((E,) + rows, BF16),
            pltpu.VMEM((E - 1,) + rows, BF16),
            *backward_scratch(imgs),
            dma((2,)), dma((2,)), dma((E,)), dma((E,)), dma((E,)), dma((E,)), dma((1,)), dma((1,)),
            dma((1,)), dma((1,)), dma((2, E // 2)), dma((2, E // 2)), dma((1,)), dma((1,)), dma((2, 3)), dma((2, 3)),
            dma((imgs, E - 1)), dma((imgs, E - 1)), dma((7,)),
        ],
        compiler_params=pltpu.CompilerParams(
            vmem_limit_bytes=VMEM_LIMIT, collective_id=1, has_side_effects=True
        ),
        cost_estimate=pl.CostEstimate(flops=12 * 10**9, bytes_accessed=10**8, transcendentals=2 * 10**6),
        name="back",
    )(g_low, y, y_begun, dh, *saved, w)


def eye_of(n, lanes):
    return (iota((n, lanes), 0) == iota((n, lanes), 1)).astype(F32).astype(BF16)


def prepare_kernel(
    imgs, tensor_ref, tok_ref, cot_ref, qkv_ref, wo_ref, v0_ref, v1_ref, v2_ref, v3_ref, router_ref, win_ref, wout_ref, noise_ref, routes_ref,
    pack_ref, ew_ref, x_ref, dy_ref, keep_out, noise_out, keep_s,
):
    tensor = tensor_ref[0]
    d_own = wo_ref.shape[1]
    wo = dot_tn(wo_ref[...].astype(BF16), eye_of(3 * HD, 3 * HD)).astype(BF16)
    vectors = [ref[...] for ref in (v0_ref, v1_ref, v2_ref, v3_ref)]
    lines = jnp.concatenate(vectors + [jnp.zeros((4, d_own), F32), router_ref[...]], axis=0).astype(BF16)
    lines = dot_tn(lines, eye_of(16, 128)).astype(BF16)
    pack_ref[...] = jnp.concatenate([qkv_ref[i].astype(BF16) for i in range(3)] + [wo, lines], axis=1)
    for e in range(E):
        ew_ref[e, 0] = win_ref[e].astype(BF16)
        ew_ref[e, 1] = wout_ref[e].astype(BF16)
    count = routes_ref.shape[1]
    earlier = (iota((count, count), 0) <= iota((count, count), 1)).astype(F32).astype(BF16)
    experts_ = iota((E, count), 0)
    before = jnp.zeros((E, 1), F32)
    keep = jnp.zeros((E, count), F32)
    for choice in range(TOP):
        named = experts_ == routes_ref[choice : choice + 1, :]
        upto = before + dot(named.astype(F32).astype(BF16), earlier)
        keep = keep + jnp.where(named & (upto <= CAP), 1.0, 0.0)
        before = upto[:, count - 1 :]
    keep_s[...] = keep
    for t in range(4):

        @pl.when(tensor == t)
        def _():
            for c in range(imgs):
                at = (t * imgs + c) * SEQ
                for src, dst in ((tok_ref, x_ref), (cot_ref, dy_ref)):
                    dst[c, :SEQ, :] = src[at : at + SEQ, :]
                    dst[c, SEQ:, :] = jnp.zeros((PAD - SEQ, D), BF16)
                for src, dst in ((keep_s, keep_out), (noise_ref, noise_out)):
                    dst[c] = jnp.concatenate([src[:, at : at + SEQ], jnp.zeros((E, PAD - SEQ), F32)], axis=1)


def prepare(tensor, imgs, tokens, cotangent, w_qkv, w_attn_out, vectors, router, w_in, w_out, noise, routes):
    vm = pl.BlockSpec(memory_space=pltpu.VMEM)
    d_own = w_attn_out.shape[1]
    rows = jax.ShapeDtypeStruct((imgs, PAD, D), BF16)
    lanes = jax.ShapeDtypeStruct((imgs, E, PAD), F32)
    return pl.pallas_call(
        functools.partial(prepare_kernel, imgs),
        out_shape=(
            jax.ShapeDtypeStruct((d_own, D + 128), BF16),
            jax.ShapeDtypeStruct((E, 2, d_own, FFS), BF16),
            rows,
            rows,
            lanes,
            lanes,
        ),
        in_specs=[pl.BlockSpec(memory_space=pltpu.SMEM)] + [vm] * 13,
        out_specs=(vm,) * 6,
        scratch_shapes=[pltpu.VMEM((E, tokens.shape[0]), F32)],
        compiler_params=pltpu.CompilerParams(vmem_limit_bytes=VMEM_LIMIT),
        cost_estimate=pl.CostEstimate(flops=10**8, bytes_accessed=15 * 10**6, transcendentals=0),
        name="prepare",
    )(tensor.reshape(1), tokens, cotangent, w_qkv, w_attn_out, *vectors, router, w_in, w_out, noise, routes)


def finish_kernel(imgs, out_in, dtok_in, g_in, total_ref, out_ref, dtok_ref, gi_ref, go_ref, qkv_ref, wo_ref, s0_ref, s1_ref, s2_ref, s3_ref, router_ref, rows_s, g_s, sem):
    loads = [pltpu.make_async_copy(src, rows_s.at[i], sem.at[i]) for i, src in enumerate((out_in, dtok_in))]
    loads.append(pltpu.make_async_copy(g_in, g_s, sem.at[2]))
    for copy in loads:
        copy.start()
    d_own = gi_ref.shape[1]
    total = total_ref[...]
    for i in range(3):
        qkv_ref[i] = total[:d_own, i * 3 * HD : (i + 1) * 3 * HD]
    wo_ref[...] = jnp.transpose(total[:d_own, 9 * HD :])
    for i, ref in enumerate((s0_ref, s1_ref, s2_ref, s3_ref)):
        ref[...] = total[d_own + i : d_own + i + 1, :d_own]
    router_ref[...] = total[d_own + 8 :, :d_own]
    for which, dst in ((0, out_ref), (1, dtok_ref)):
        loads[which].wait()
        for i in range(4 * imgs):
            dst[i * SEQ : (i + 1) * SEQ, :] = rows_s[which, i // imgs, i % imgs, :SEQ, :]
    loads[2].wait()
    for e in range(E):
        gi_ref[e] = g_s[e, 0].astype(F32)
        go_ref[e] = g_s[e, 1].astype(F32)


def finish(out_all, dtok_all, g_exp, total):
    imgs = out_all.shape[1]
    d_own = g_exp.shape[2]
    vm = pl.BlockSpec(memory_space=pltpu.VMEM)
    hbm = pl.BlockSpec(memory_space=pl.ANY)
    rows = jax.ShapeDtypeStruct((4 * imgs * SEQ, D), BF16)
    grad = jax.ShapeDtypeStruct((E, d_own, FFS), F32)
    return pl.pallas_call(
        functools.partial(finish_kernel, imgs),
        out_shape=(
            rows,
            rows,
            grad,
            grad,
            jax.ShapeDtypeStruct((3, d_own, 3 * HD), F32),
            jax.ShapeDtypeStruct((3 * HD, d_own), F32),
            *[jax.ShapeDtypeStruct((1, d_own), F32)] * 4,
            jax.ShapeDtypeStruct((E, d_own), F32),
        ),
        in_specs=[hbm, hbm, hbm, vm],
        out_specs=(vm,) * 11,
        scratch_shapes=[
            pltpu.VMEM((2, 4, imgs, PAD, D), BF16),
            pltpu.VMEM(g_exp.shape, BF16),
            pltpu.SemaphoreType.DMA((3,)),
        ],
        compiler_params=pltpu.CompilerParams(vmem_limit_bytes=VMEM_LIMIT),
        cost_estimate=pl.CostEstimate(flops=10**6, bytes_accessed=18 * 10**6, transcendentals=0),
        name="finish",
    )(out_all, dtok_all, g_exp, total)


RING = (0, 2, 4, 6, 7, 5, 3, 1)


class Mover:
    def __init__(self, n_dp):
        self.n_dp = n_dp
        self.groups = n_dp // E
        self.me = lax.axis_index("dp")
        self.member = lax.rem(self.me, E)
        self.group = lax.div(self.me, E)
        self.tensor = lax.axis_index("tensor")
        self.place = ring_place(self.member)
        bases = range(0, n_dp, E)
        self.ring = (
            [(b + RING[i], b + RING[(i + 1) % E]) for b in bases for i in range(E)],
            [(b + RING[(i + 1) % E], b + RING[i]) for b in bases for i in range(E)],
        )

    def along(self, value, way):
        return lax.ppermute(value, "dp", self.ring[way])

    def shift(self, value, by):
        perm = [(b + i, b + (i + by) % E) for b in range(0, self.n_dp, E) for i in range(E)]
        return lax.ppermute(value, "dp", perm)

    def shift_group(self, value, by):
        return lax.ppermute(value, "dp", [(k, (k + by * E) % self.n_dp) for k in range(self.n_dp)])

    def other(self, value, mask):
        return lax.ppermute(value, "tensor", [(k, k ^ mask) for k in range(4)])

    def behind(self, way, k):
        step = -k if way == 0 else k
        return ring_member(lax.rem(self.place + step + E, E))

    def group_lists(self):
        if self.groups == 1:
            return None
        return [[b + i for i in range(E)] for b in range(0, self.n_dp, E)]

    def gather(self, value):
        return lax.all_gather(value, "dp", axis=0, tiled=False, axis_index_groups=self.group_lists())

    def scatter_sum(self, value):
        return lax.psum_scatter(
            value, "dp", scatter_dimension=0, tiled=False, axis_index_groups=self.group_lists()
        )

    def front(self, pack, ew, dy, x, noise, keep):
        own = lax.all_gather(pack, "dp", axis=0, tiled=True)
        two = jnp.stack([own, self.other(own, 2)])
        w = jnp.concatenate([two, self.other(two, 1)], axis=0)
        blocks = jnp.zeros((2, E * pack.shape[0], FFS), BF16)
        for by in range(E):
            to = lax.rem(self.member + by, E)
            block = lax.dynamic_index_in_dim(ew, to, 0, False)
            came = lax.rem(self.member - by + E, E)
            block = self.shift(block, by) if by else block
            blocks = lax.dynamic_update_slice_in_dim(blocks, block, came * pack.shape[0], 1)
        blocks = self.all_groups(blocks, 1)
        blocks = jnp.swapaxes(blocks.reshape(2, E, D // E, FFS), 0, 1)
        two = jnp.stack([blocks, self.other(blocks, 2)])
        weights = jnp.concatenate([two, self.other(two, 1)], axis=0)
        chunk, *saved = attn_forward(x, w, noise, keep)
        table = (E * x.shape[0], PAD, D)
        dh, y, rows, hid, tiles = experts(
            self.member, self.gather(chunk).reshape(table), self.gather(dy).reshape(table), weights
        )
        sums = [self.scatter_sum(t.reshape((E,) + chunk.shape)) for t in (dh, y)]
        g = [jnp.concatenate([expert_grads(tiles, rows, hid, kind, base) for base in (0, 2)]) for kind in (0, 1)]
        g = jnp.stack([part.reshape(4, E, D // E, FFS) for part in g], axis=2)
        return g, jnp.stack(sums), w, *saved

    def back(self, g_low, sums, saved, x, dy, w):
        x1, qkv, o, lse, probs = saved
        dh_sum, y_sum = sums[0], sums[1]
        imgs, d_own = x.shape[0], D // self.n_dp
        passed = self.other(g_low[2:], 1)
        pair = [(g_low[s].astype(F32) + passed[s].astype(F32)).astype(BF16) for s in range(2)]
        total = (pair[0].astype(F32) + self.other(pair[1], 2).astype(F32)).astype(BF16)
        if self.groups > 1:
            total = jnp.swapaxes(total, 1, 2).reshape(D, 2, FFS)
            total = jnp.swapaxes(self.sum_groups(total, 0).reshape(E, d_own, 2, FFS), 1, 2)
        g_exp = []
        for by in range(E):
            to = lax.rem(self.member + by, E)
            block = lax.dynamic_index_in_dim(total, to, 0, False)
            g_exp.append(self.shift(block, by) if by else block)

        pack0, pack1, packs, d_tok = attn_backward(
            [dh_sum[c] for c in range(imgs)], (x1, x, dy, probs, qkv, o, lse), w, self.n_dp
        )
        passed = self.other(packs, 1)
        if self.groups > 1:
            pack0 = self.sum_groups((pack0.astype(F32) + passed[:, 0].astype(F32)).astype(BF16), 0)
            pack1 = self.sum_groups((pack1.astype(F32) + passed[:, 1].astype(F32)).astype(BF16), 0)
            passed = jnp.zeros((E, 2) + pack0.shape[1:], BF16)

        def pack_for(member):
            one, two = (lax.dynamic_index_in_dim(p, member, 0, False).astype(F32) for p in (pack0, pack1))
            came = lax.dynamic_index_in_dim(passed, member, 0, False).astype(F32)
            return one + came[0] + self.other((two + came[1]).astype(BF16), 2).astype(F32)

        total = self.sum_both_ways(pack_for)
        at = jnp.stack([_slot(self.tensor, t) for t in range(4)])

        def all_rows(own):
            across = self.other(own, 2)
            return lay_out(at, [own, across, self.other(own, 1), self.other(across, 1)])

        d_tokens = all_rows(d_tok)
        output = all_rows((x1 + y_sum.astype(F32)).astype(BF16))
        came = jnp.stack([lax.rem(self.member - by + E, E) for by in range(E)])
        return output, d_tokens, *unpack(came, g_exp), total

    def sum_both_ways(self, block_for):
        def chain(way, steps):
            total = block_for(self.behind(1 - way, steps)).astype(BF16)
            for k in range(steps - 1, -1, -1):
                total = self.along(total, way)
                if k:
                    total = (total.astype(F32) + block_for(self.behind(1 - way, k)).astype(F32)).astype(BF16)
            return total

        ahead = chain(0, E // 2)
        back = chain(1, E // 2 - 1)
        return ahead.astype(F32) + back.astype(F32) + block_for(self.member).astype(F32)

    def all_groups(self, part, dim):
        if self.groups == 1:
            return part
        size = part.shape[dim]
        shape = part.shape[:dim] + (size * self.groups,) + part.shape[dim + 1 :]
        whole = lax.dynamic_update_slice_in_dim(jnp.zeros(shape, part.dtype), part, self.group * size, dim)
        for by in range(1, self.groups):
            came = lax.rem(self.group - by + self.groups, self.groups)
            whole = lax.dynamic_update_slice_in_dim(whole, self.shift_group(part, by), came * size, dim)
        return whole

    def sum_groups(self, whole, dim):
        if self.groups == 1:
            return whole
        size = whole.shape[dim] // self.groups
        total = lax.dynamic_slice_in_dim(whole, self.group * size, size, dim).astype(F32)
        for by in range(1, self.groups):
            to = lax.rem(self.group + by, self.groups)
            part = lax.dynamic_slice_in_dim(whole, to * size, size, dim)
            total = total + self.shift_group(part, by).astype(F32)
        return total.astype(whole.dtype)


def after(value, *first):
    return lax.optimization_barrier((value, first))[0]


def _slot(tensor, t):
    apart = lax.bitwise_xor(tensor, t)
    return lax.div(apart, 2) + 2 * lax.rem(apart, 2)


def image_blocks(rows, tensor, imgs):
    first = tensor * (imgs * SEQ)
    return [
        jnp.pad(lax.dynamic_slice_in_dim(rows, first + c * SEQ, SEQ, 0), ((0, PAD - SEQ), (0, 0)))
        for c in range(imgs)
    ]


def image_lanes(lanes, tensor, imgs):
    first = tensor * (imgs * SEQ)
    return [
        jnp.pad(lax.dynamic_slice_in_dim(lanes, first + c * SEQ, SEQ, 1), ((0, 0), (0, PAD - SEQ)))
        for c in range(imgs)
    ]


def kept_pairs(routes):
    chosen = jnp.transpose(routes).reshape(1, -1)
    named = (chosen == jnp.arange(E, dtype=jnp.int32)[:, None]).astype(jnp.int32)
    kept = named * (jnp.cumsum(named, axis=1) <= CAP)
    return jnp.sum(kept.reshape(E, TOP, -1), axis=1).astype(F32)


def body(
    n_dp,
    tokens,
    ln1_gain,
    ln1_bias,
    w_qkv,
    w_attn_out,
    ln2_gain,
    ln2_bias,
    router_weight,
    w_in,
    w_expert_out,
    router_noise,
    routes,
    cotangent,
):
    move = Mover(n_dp)
    token_count = tokens.shape[0]
    imgs = token_count // SEQ // 4
    d_own = w_qkv.shape[0]
    ways = [c % 2 for c in range(imgs)]

    w_out = jnp.transpose(w_expert_out, (0, 2, 1))
    if move.groups == 1:
        pack, ew, x, dy, keep, noise = prepare(
            move.tensor, imgs, tokens, cotangent, jnp.transpose(w_qkv, (1, 0, 2)), w_attn_out,
            [v.reshape(1, d_own) for v in (ln1_gain, ln1_bias, ln2_gain, ln2_bias)], jnp.transpose(router_weight),
            w_in, w_out, jnp.transpose(router_noise), jnp.transpose(routes),
        )
        _, _, _, y, _, y_begun, g_low, dh, w, *saved = front(pack, ew, dy, x, noise, keep)
        x1, qkv, o, lse, probs = saved
        output, d_tokens, g_in, g_out, g_qkv, g_attn_out, *g_vectors, g_router = finish(
            *back(g_low, y, y_begun, dh, (x1, x, dy, probs, qkv, o, lse), w)
        )
        g_vectors = [v.reshape(d_own) for v in g_vectors]
        g_qkv = jnp.transpose(g_qkv, (1, 0, 2))
    else:
        vectors = jnp.stack([ln1_gain, ln1_bias, ln2_gain, ln2_bias] + [jnp.zeros_like(ln1_gain)] * 4, axis=1)
        pack = jnp.concatenate(
            [w_qkv[:, 0], w_qkv[:, 1], w_qkv[:, 2], jnp.transpose(w_attn_out), vectors, router_weight], axis=1
        )
        pack = jnp.pad(pack, ((0, 0), (0, 128 - 16))).astype(BF16)
        ew = jnp.stack([w_in, jnp.transpose(w_expert_out, (0, 2, 1))], axis=1).astype(BF16)
        x = jnp.stack(image_blocks(tokens, move.tensor, imgs))
        dy = jnp.stack(image_blocks(cotangent, move.tensor, imgs))
        keep = jnp.stack(image_lanes(kept_pairs(routes), move.tensor, imgs))
        noise = jnp.stack(image_lanes(jnp.transpose(router_noise), move.tensor, imgs))
        g_low, sums, w, *saved = move.front(pack, ew, dy, x, noise, keep)
        output, d_tokens, g_in, g_out, total = move.back(g_low, sums, saved, x, dy, w)
        g_qkv = total[:d_own, : 9 * HD].reshape(d_own, 3, 3 * HD)
        g_attn_out = jnp.transpose(total[:d_own, 9 * HD :])
        g_vectors = [total[d_own + i, :d_own] for i in range(4)]
        g_router = total[d_own + 8 :, :d_own]
    return (
        output,
        d_tokens,
        g_vectors[0],
        g_vectors[1],
        g_qkv,
        g_attn_out,
        g_vectors[2],
        g_vectors[3],
        jnp.transpose(g_router),
        g_in,
        jnp.transpose(g_out, (0, 2, 1)),
    )


def solution(mesh):
    in_specs = (
        P("dp", None),
        P("dp"),
        P("dp"),
        P("dp", None, "tensor"),
        P("tensor", "dp"),
        P("dp"),
        P("dp"),
        P("dp", None),
        P(None, "dp", "tensor"),
        P(None, "tensor", "dp"),
        P("dp", None),
        P("dp", None),
        P("dp", None),
    )
    out_specs = (
        P("dp", None),
        P("dp", None),
        P("dp"),
        P("dp"),
        P("dp", None, "tensor"),
        P("tensor", "dp"),
        P("dp"),
        P("dp"),
        P("dp", None),
        P(None, "dp", "tensor"),
        P(None, "tensor", "dp"),
    )
    return jax.shard_map(
        functools.partial(body, mesh.shape["dp"]),
        mesh=mesh,
        in_specs=in_specs,
        out_specs=out_specs,
        check_vma=False,
    )
```

```python
import functools

import jax
import jax.numpy as jnp
from jax import lax
from jax.experimental import pallas as pl
from jax.experimental.pallas import tpu as pltpu
from jax.sharding import PartitionSpec as P

D = 768
HD = 64
E = 8
TOP = 2
SEQ = 197
CAP = 689
PAD = 208
META = 200
TILE = 256
FFS = 768
EPS = 1e-06
VMEM_LIMIT = 62 * 1024 * 1024

F32 = jnp.float32
BF16 = jnp.bfloat16


def dot(a, b):
    return jnp.dot(a, b, preferred_element_type=F32)


def dot_nt(a, b):
    return lax.dot_general(a, b, (((1,), (1,)), ((), ())), preferred_element_type=F32)


def dot_tn(a, b):
    return lax.dot_general(a, b, (((0,), (0,)), ((), ())), preferred_element_type=F32)


def iota(shape, dim):
    return lax.broadcasted_iota(jnp.int32, shape, dim)


def normalise(values):
    centred = values - jnp.mean(values, axis=-1, keepdims=True)
    scale = lax.rsqrt(jnp.mean(centred * centred, axis=-1, keepdims=True) + EPS)
    return centred * scale, scale


def norm_back(grad, unit, scale, gain):
    g = grad * gain
    return scale * (
        g - jnp.mean(g, axis=-1, keepdims=True) - unit * jnp.mean(g * unit, axis=-1, keepdims=True)
    )


def params_of(w_own):
    return jnp.transpose(w_own[:, D:].astype(F32))[:16]


def attend(x, par, w_of, noise, keep, chunk_ref, x1_ref, qkv_ref, o_ref, lse_ref, probs_ref):
    x = x.astype(F32)
    unit, _ = normalise(x)
    h1 = (unit * par[0:1] + par[1:2]).astype(BF16)
    acc = x
    lse = jnp.zeros((PAD, 128), F32)
    key_ok = iota((PAD, PAD), 1) < SEQ
    lane = iota((PAD, 128), 1)
    for r in range(4):
        w = w_of(r)
        qkv = dot(h1, w[:, : 9 * HD]).astype(BF16)
        qkv_ref[r] = qkv
        outs = []
        for h in range(3):
            q = qkv[:, h * HD : (h + 1) * HD]
            k = qkv[:, (3 + h) * HD : (4 + h) * HD]
            v = qkv[:, (6 + h) * HD : (7 + h) * HD]
            s = jnp.where(key_ok, dot_nt(q, k) * HD ** (-0.5), -1e30)
            top = jnp.max(s, axis=-1, keepdims=True)
            p = jnp.exp(s - top)
            total = jnp.sum(p, axis=-1, keepdims=True)
            outs.append(dot((p * (1.0 / total)).astype(BF16), v).astype(BF16))
            lse = jnp.where(lane == 3 * r + h, top + jnp.log(total), lse)
        o = jnp.concatenate(outs, axis=1)
        o_ref[r] = o
        acc = acc + dot_nt(o, w[:, 9 * HD : D])
    lse_ref[...] = lse
    x1_ref[...] = acc
    unit2, _ = normalise(acc)
    h2 = (unit2 * par[2:3] + par[3:4]).astype(BF16)
    logits = dot_nt(par[8:16].astype(BF16), h2) + noise
    e = jnp.exp(logits - jnp.max(logits, axis=0, keepdims=True))
    probs = e / jnp.sum(e, axis=0, keepdims=True)
    probs_ref[...] = probs
    gates = jnp.where(keep > 0, probs, -1.0)
    chunk_ref[...] = h2
    tail = jnp.concatenate([gates, jnp.zeros((8, D - PAD), F32)], axis=1)
    low = h2[PAD - 16 :, :].astype(F32)
    chunk_ref[PAD - 16 :, :] = jnp.concatenate([low[:8], tail], axis=0).astype(BF16)


def attn_shapes(imgs):
    return (
        jax.ShapeDtypeStruct((imgs, PAD, D), F32),
        jax.ShapeDtypeStruct((imgs, 4, PAD, 9 * HD), BF16),
        jax.ShapeDtypeStruct((imgs, 4, PAD, 3 * HD), BF16),
        jax.ShapeDtypeStruct((imgs, PAD, 128), F32),
        jax.ShapeDtypeStruct((imgs, E, PAD), F32),
    )


def attn_forward_kernel(imgs, x_ref, w_ref, noise_ref, keep_ref, chunk_ref, *saved):
    par = params_of(w_ref[0])
    for c in range(imgs):
        attend(
            x_ref[c], par, lambda r: w_ref[r], noise_ref[c], keep_ref[c],
            chunk_ref.at[c], *(ref.at[c] for ref in saved),
        )


def attn_forward(x, w, noise, keep):
    imgs = x.shape[0]
    vm = pl.BlockSpec(memory_space=pltpu.VMEM)
    return pl.pallas_call(
        functools.partial(attn_forward_kernel, imgs),
        out_shape=(jax.ShapeDtypeStruct((imgs, PAD, D), BF16),) + attn_shapes(imgs),
        in_specs=[vm] * 4,
        out_specs=(vm,) * 6,
        compiler_params=pltpu.CompilerParams(vmem_limit_bytes=VMEM_LIMIT),
        cost_estimate=pl.CostEstimate(flops=6 * 10**9, bytes_accessed=10**7, transcendentals=2 * 10**6),
        name="attn_forward",
    )(x, w, noise, keep)


def ring_place(member):
    odd = lax.rem(member, 2)
    half = lax.div(member, 2)
    return half + odd * (E - 1 - 2 * half)


def ring_member(place):
    late = lax.div(place, E // 2)
    return 2 * place + late * (2 * E - 1 - 4 * place)


class Peers:
    def __init__(self):
        dp = lax.axis_index("dp")
        tensor = lax.axis_index("tensor")
        self.member = lax.rem(dp, E)
        self.base = dp - self.member
        self.place = ring_place(self.member)
        self.across = {"tensor": lax.rem(tensor + 2, 4)}
        self.core = {"tensor": tensor + 1 - 2 * lax.rem(tensor, 2)}
        self.next = ({"dp": self.base + self.behind(1, 1)}, {"dp": self.base + self.behind(0, 1)})
        self.sends = []

    def behind(self, way, k):
        step = E - k if way == 0 else k
        return ring_member(lax.rem(self.place + step, E))

    def ahead(self, by):
        return lax.rem(self.member + by, E)

    def came(self, by):
        return lax.rem(self.member + E - by, E)

    def meet(self):
        barrier = pltpu.get_barrier_semaphore()
        others = [{"dp": self.base + self.ahead(by)} for by in range(1, E)] + [self.across, self.core]
        for device in others:
            pl.semaphore_signal(barrier, inc=1, device_id=device, device_id_type=pl.DeviceIdType.MESH)
        pl.semaphore_wait(barrier, len(others))

    def send(self, src, dst, sems, at, device):
        copy = pltpu.make_async_remote_copy(
            src_ref=src,
            dst_ref=dst,
            send_sem=sems[0].at[at],
            recv_sem=sems[1].at[at],
            device_id=device,
            device_id_type=pl.DeviceIdType.MESH,
        )
        copy.start()
        self.sends.append(copy)
        return copy


def expert_step(x, dy, gate, w_ref, g_ref, y_ref, dx_ref, meanwhile):
    weight = jnp.maximum(gate, 0.0)
    d_rows = (dy.astype(F32) * weight).astype(BF16)

    def hidden(i, carry):
        r = 2 * lax.rem(i, 2) + lax.div(i, 2)
        w1 = w_ref[r, :, 0].reshape(D, FFS)
        w2 = w_ref[r, :, 1].reshape(D, FFS)
        a = dot(x, w1)
        a2 = a * a
        th = jnp.tanh(0.7978845608028654 * a * (1.0 + 0.044715 * a2))
        half = 0.5 * (1.0 + th)
        hid = (a * half).astype(BF16)
        slope = half + 0.5 * a * (1.0 - th * th) * (0.7978845608028654 * (1.0 + 3 * 0.044715 * a2))
        da = (dot(d_rows, w2) * slope).astype(BF16)
        y_ref[...] += dot_nt(hid, w2)
        dx_ref[...] += dot_nt(da, w1)
        g_ref[r, 0] += dot_tn(x, da)
        g_ref[r, 1] += dot_tn(d_rows, hid)
        meanwhile(i)
        return carry

    y_ref[...] = jnp.zeros_like(y_ref)
    dx_ref[...] = jnp.zeros_like(dx_ref)
    lax.fori_loop(0, 4, hidden, 0)
    y = y_ref[...]
    dgate = jnp.where(gate >= 0, jnp.sum(dy.astype(F32) * y, axis=1, keepdims=True), 0.0)
    return (y * weight).astype(BF16), dx_ref[...], dgate


GIVEN, PASSED, DY_AT = (1, 2, 4, 6, 7), (1, 3), 3
HOP0, PASSED_EX = 5, 4
NEXT_AT, SUMS_AT, Y_AT = 0, 2, 5
HOPS_AT = ()


def front_kernel(
    imgs, pack_ref, ew_ref, dy_ref, x_ref, noise_ref, keep_ref,
    h_out, dy_out, t_in, y_out, y_first, y_second, g_out, sum_out, w_out, x1_ref, qkv_ref, o_ref, lse_ref, probs_ref,
    w_s, chunk_s, we_s, g_s, xs, dys, y_s, dx_s, t_s, own_s, y_low, pass_s, g_low,
    p_s, p_r, px_s, px_r, pc_s, pc_r, d_s, d_r, h_s, h_r, e_s, e_r, ex_s, ex_r, ec_s, ec_r, t_ss, t_r, local, stage, y_sem, g_sem, yf_s, yf_r,
):
    peers = Peers()
    member = peers.member
    d_own = pack_ref.shape[0]
    half = E // 2
    peers.meet()

    def rows(of):
        return pl.ds(pl.multiple_of(of * d_own, 16), d_own)

    own_pack = pltpu.make_async_copy(pack_ref, w_s.at[0, rows(member)], local.at[0])
    own_pack.start()

    ring, px, pc = {}, {}, {}

    def pass_pack(number, of, src, way=None, k=None):
        if way is not None:
            ring[way, k] = peers.send(src, w_s.at[0, rows(of)], (p_s, p_r), (way, k), peers.next[way])
        px[number] = peers.send(src, w_s.at[1, rows(of)], (px_s, px_r), number, peers.across)
        pc[0, number] = peers.send(src, w_s.at[2, rows(of)], (pc_s, pc_r), (0, number), peers.core)

    arrivals = [(0, k) if i == 0 else (1, k) for k in range(1, half + 1) for i in range(2 if k < half else 1)]
    owners = [member] + [peers.behind(way, k) for way, k in arrivals]

    def pass_x(number):
        px[number].wait_recv()
        at = rows(owners[number])
        pc[1, number] = peers.send(w_s.at[1, at], w_s.at[3, at], (pc_s, pc_r), (1, number), peers.core)

    far = (1, 7, 2, 6, 3, 5, 4)
    e_copy, ex, ec = {}, {}, {}

    def give_e(part):
        for by in part:
            to = peers.ahead(by)
            e_copy[by] = peers.send(ew_ref.at[to], we_s.at[0, member], (e_s, e_r), by, {"dp": peers.base + to})

    def pass_e(by):
        if by:
            e_copy[by].wait_recv()
        of = peers.came(by)
        src = we_s.at[0, of] if by else ew_ref.at[member]
        ex[by] = peers.send(src, we_s.at[1, of], (ex_s, ex_r), by, peers.across)
        ec[0, by] = peers.send(src, we_s.at[2, of], (ec_s, ec_r), (0, by), peers.core)

    def slice_copy(to, of, sent, got, at, device):
        return pltpu.make_async_remote_copy(
            src_ref=we_s.at[0 if to == 1 else 1, of],
            dst_ref=we_s.at[to, of],
            send_sem=sent.at[at],
            recv_sem=got.at[at],
            device_id=device,
            device_id_type=pl.DeviceIdType.MESH,
        )

    def ex_core(by):
        return slice_copy(3, peers.came(by), ec_s, ec_r, (1, by), peers.core)

    def pass_ex(by):
        of = peers.came(by)
        slice_copy(1, of, ex_s, ex_r, by, peers.across).wait_recv()
        ex_core(by).start()

    def block_at(c, k):
        return peers.behind(c % 2, k) * imgs + c

    def row_copy(out, sems, c, k, src=None):
        at = block_at(c, k)
        return pltpu.make_async_remote_copy(
            src_ref=out.at[at] if src is None else src,
            dst_ref=out.at[at],
            send_sem=sems[0].at[c, k],
            recv_sem=sems[1].at[c, k],
            device_id=peers.next[c % 2],
            device_id_type=pl.DeviceIdType.MESH,
        )

    h_sems, d_sems = (h_s, h_r), (d_s, d_r)

    def row_hop(k):
        for c in range(imgs):
            for out, sems in ((h_out, h_sems), (dy_out, d_sems)):
                row_copy(out, sems, c, k - 1).wait_recv()
                row_copy(out, sems, c, k).start()

    def give_dy():
        for c in range(imgs):
            row_copy(dy_out, d_sems, c, 0, dy_ref.at[c]).start()

    ring[0, 0] = peers.send(pack_ref, w_s.at[0, rows(member)], (p_s, p_r), (0, 0), peers.next[0])
    pass_pack(0, member, pack_ref, 1, 0)
    give_e(far[:GIVEN[0]])
    pass_e(0)
    if DY_AT == 0:
        give_dy()
    keepers = [
        pltpu.make_async_copy(ew_ref.at[member], we_s.at[0, member], local.at[2]),
    ] + [
        pltpu.make_async_copy(dy_ref.at[c], dy_out.at[member * imgs + c], local.at[3 + c]) for c in range(imgs)
    ]
    for copy in keepers:
        copy.start()
    for number, (way, k) in enumerate(arrivals, 1):
        ring[way, k - 1].wait_recv()
        of = owners[number]
        last = half if way == 0 else half - 1
        pass_pack(number, of, w_s.at[0, rows(of)], way if k < last else None, k)
        if number >= 2:
            pass_x(number - 2)
        if number == 4:
            give_e(far[GIVEN[0]:GIVEN[1]])
    give_e(far[GIVEN[1]:GIVEN[2]])
    if DY_AT == 1:
        give_dy()
    for number in range(len(arrivals) - 1, len(arrivals) + 1):
        pass_x(number)
    for number in range(E):
        pc[0, number].wait_recv()
        pc[1, number].wait_recv()
    own_pack.wait()
    keepers.append(pltpu.make_async_copy(w_s, w_out, local.at[1]))
    keepers[-1].start()

    par = params_of(w_s[0])
    done = 0
    for c in range(imgs):
        for by in far[done : PASSED[c]]:
            pass_e(by)
            pass_ex((0, *far)[done])
            done += 1
        attend(
            x_ref[c], par, lambda r: w_s[r], noise_ref[c], keep_ref[c],
            chunk_s.at[c], *(ref.at[c] for ref in (x1_ref, qkv_ref, o_ref, lse_ref, probs_ref)),
        )
        if HOP0 == 0:
            row_copy(h_out, h_sems, c, 0, chunk_s.at[c]).start()
        keepers.append(
            pltpu.make_async_copy(chunk_s.at[c], h_out.at[member * imgs + c], local.at[3 + imgs + c])
        )
        keepers[-1].start()
        give_e(far[GIVEN[2 + c]:GIVEN[3 + c]])
    if DY_AT == 2:
        give_dy()

    def first_hops():
        for c in range(imgs):
            row_copy(h_out, h_sems, c, 0, chunk_s.at[c]).start()
        if DY_AT == 3:
            give_dy()

    for i, by in enumerate(far):
        if i >= done:
            pass_e(by)
            if i <= PASSED_EX:
                pass_ex((0, *far)[i])
        if HOP0 and i == HOP0:
            first_hops()
        if i in HOPS_AT:
            row_hop(1 + HOPS_AT.index(i))
    g_s[...] = jnp.zeros_like(g_s)
    for by in range(E):
        ec[0, by].wait_recv()
    for copy in keepers:
        copy.wait()

    row16 = iota((16, D), 0)
    eye = iota((PAD, PAD), 0) == iota((PAD, PAD), 1)

    def sum_copy(c, k):
        return pltpu.make_async_remote_copy(
            src_ref=pass_s.at[lax.rem(k, 2), c],
            dst_ref=t_in.at[k - 1, c],
            send_sem=t_ss.at[c, k - 1],
            recv_sem=t_r.at[c, k - 1],
            device_id=peers.next[c % 2],
            device_id_type=pl.DeviceIdType.MESH,
        )

    def sums_to_hand(k):
        return [pltpu.make_async_copy(t_in.at[k - 2, c], t_s.at[c], stage.at[2, c]) for c in range(imgs)]

    def rows_to_hand(k):
        slot = lax.rem(k, 2)
        return [
            pltpu.make_async_copy(out.at[block_at(c, k)], held.at[slot, c], stage.at[i, c])
            for c in range(imgs)
            for i, (out, held) in enumerate(((h_out, xs), (dy_out, dys)))
        ]

    def start(copies):
        for copy in copies:
            copy.start()

    def finish(copies):
        for copy in copies:
            copy.wait()

    def y_copy(c, hop):
        return pltpu.make_async_remote_copy(
            src_ref=y_out.at[1, c] if hop == 0 else xs.at[0, c],
            dst_ref=y_first.at[c] if hop == 0 else y_second.at[c],
            send_sem=yf_s.at[hop, c],
            recv_sem=yf_r.at[hop, c],
            device_id=peers.next[c % 2],
            device_id_type=pl.DeviceIdType.MESH,
        )

    def keep_y(k):
        return pltpu.make_async_copy(y_low, y_out.at[k], y_sem)

    def step(k, carry):
        slot = lax.rem(k, 2)
        finish(rows_to_hand(k))

        def meanwhile(r):
            @pl.when((r == 0) & (k == 0))
            def _():
                for by in far[PASSED_EX:]:
                    pass_ex(by)

            @pl.when((r == 1) & (k == 0))
            def _():
                for by in range(E):
                    ex_core(by).wait_recv()

            for c in range(imgs):
                for out, sems in ((h_out, h_sems), (dy_out, d_sems)):

                    @pl.when((r == NEXT_AT) & (k >= len(HOPS_AT)) & (k < E - 1))
                    def _():
                        row_copy(out, sems, c, k).wait_recv()

                    @pl.when((r == NEXT_AT) & (k >= len(HOPS_AT)) & (k < E - 2))
                    def _():
                        row_copy(out, sems, c, k + 1).start()

            @pl.when((r == NEXT_AT) & (k < E - 1))
            def _():
                start(rows_to_hand(k + 1))

            @pl.when((r == SUMS_AT) & (k >= 2))
            def _():
                for c in range(imgs):
                    sum_copy(c, k - 1).wait_recv()
                start(sums_to_hand(k))

        columns = []
        for c in range(imgs):
            meta = xs[slot, c, PAD - 16 :, :].astype(F32)
            line = jnp.sum(jnp.where(row16 == 8 + member, meta, 0.0), axis=0, keepdims=True)[:, :PAD]
            columns.append(jnp.sum(jnp.where(eye, line, 0.0), axis=1, keepdims=True))
        y, dx, dgate = expert_step(
            xs[slot].reshape(imgs * PAD, D), dys[slot].reshape(imgs * PAD, D), jnp.concatenate(columns, axis=0),
            we_s, g_s, y_s, dx_s, meanwhile,
        )

        @pl.when(k >= 3)
        def _():
            for c in range(imgs):
                sum_copy(c, k - 2).wait_send()

        @pl.when(k >= 1)
        def _():
            keep_y(k - 1).wait()

        for c in range(imgs):
            span = slice(c * PAD, (c + 1) * PAD)
            line = jnp.sum(jnp.where(eye, dgate[span], 0.0), axis=0, keepdims=True)
            line = jnp.concatenate([line, jnp.zeros((1, D - PAD), F32)], axis=1)
            tail = dx[span][PAD - 16 :] + jnp.where(row16 == 8 + member, line, 0.0)
            pass_s[slot, c] = jnp.concatenate([dx[span][: PAD - 16], tail], axis=0).astype(BF16)
            y_low[c] = y[span]

        keep_y(k).start()

        @pl.when(k == 0)
        def _():
            own_s[...] = pass_s[0]

        @pl.when(k >= 2)
        def _():
            finish(sums_to_hand(k))
            pass_s[slot] = (pass_s[slot].astype(F32) + t_s[...].astype(F32)).astype(BF16)

        @pl.when(k >= 1)
        def _():
            for c in range(imgs):
                sum_copy(c, k).start()

        @pl.when(k == Y_AT)
        def _():
            for c in range(imgs):
                y_copy(c, 0).start()

        return carry

    start(rows_to_hand(0))
    lax.fori_loop(0, E, step, 0)

    for c in range(imgs):
        y_copy(c, 0).wait()
    y_loads = [pltpu.make_async_copy(y_first, xs.at[0], stage.at[0, 0]), pltpu.make_async_copy(y_out.at[2], dys.at[0], stage.at[1, 0])]
    start(y_loads)
    for i in range(8):
        if i == 2:
            finish(y_loads)
            xs[0] = (xs[0].astype(F32) + dys[0].astype(F32)).astype(BF16)
            for c in range(imgs):
                y_copy(c, 1).start()
        r, kind = i // 2, i % 2
        if i >= 2:
            pltpu.make_async_copy(g_low.at[i % 2], g_out.at[r, :, kind], g_sem.at[i % 2]).wait()
        g_low[i % 2] = g_s[r, kind].astype(BF16).reshape(E, d_own, FFS)
        pltpu.make_async_copy(g_low.at[i % 2], g_out.at[r, :, kind], g_sem.at[i % 2]).start()
    for c in range(imgs):
        sum_copy(c, E - 1).wait_recv()
    start(sums_to_hand(E))
    finish(sums_to_hand(E))
    sum_out[...] = (own_s[...].astype(F32) + t_s[...].astype(F32)).astype(BF16)
    keep_y(E - 1).wait()
    for c in range(imgs):
        y_copy(c, 1).wait()
    for i in range(2):
        pltpu.make_async_copy(g_low.at[i], g_out.at[3, :, i], g_sem.at[i]).wait()
    for c in range(imgs):
        sum_copy(c, E - 2).wait_send()
        sum_copy(c, E - 1).wait_send()
        for k in range(E - 1):
            row_copy(h_out, h_sems, c, k).wait_send()
            row_copy(dy_out, d_sems, c, k).wait_send()
    for by in range(E):
        ex_core(by).wait_send()
    for copy in peers.sends:
        copy.wait_send()


def front(pack, ew, dy, x, noise, keep):
    imgs = x.shape[0]
    d_own = pack.shape[0]
    vm = pl.BlockSpec(memory_space=pltpu.VMEM)
    hbm = pl.BlockSpec(memory_space=pl.ANY)
    table = jax.ShapeDtypeStruct((E * imgs, PAD, D), BF16)
    dma = pltpu.SemaphoreType.DMA
    rows = (imgs, PAD, D)
    return pl.pallas_call(
        functools.partial(front_kernel, imgs),
        out_shape=(
            table,
            table,
            jax.ShapeDtypeStruct((E - 1,) + rows, BF16),
            jax.ShapeDtypeStruct((E,) + rows, BF16),
            jax.ShapeDtypeStruct(rows, BF16),
            jax.ShapeDtypeStruct(rows, BF16),
            jax.ShapeDtypeStruct((4, E, 2, d_own, FFS), BF16),
            jax.ShapeDtypeStruct(rows, BF16),
            jax.ShapeDtypeStruct((4, E * d_own, D + 128), BF16),
        )
        + attn_shapes(imgs),
        in_specs=[vm, hbm, hbm, vm, vm, vm],
        out_specs=(hbm,) * 7 + (vm, hbm) + (vm,) * 5,
        scratch_shapes=[
            pltpu.VMEM((4, E * d_own, D + 128), BF16),
            pltpu.VMEM((imgs, PAD, D), BF16),
            pltpu.VMEM((4, E, 2, d_own, FFS), BF16),
            pltpu.VMEM((4, 2, D, FFS), F32),
            pltpu.VMEM((2, imgs, PAD, D), BF16),
            pltpu.VMEM((2, imgs, PAD, D), BF16),
            pltpu.VMEM((imgs * PAD, D), F32),
            pltpu.VMEM((imgs * PAD, D), F32),
            pltpu.VMEM(rows, BF16),
            pltpu.VMEM(rows, BF16),
            pltpu.VMEM(rows, BF16),
            pltpu.VMEM((2,) + rows, BF16),
            pltpu.VMEM((2, E, d_own, FFS), BF16),
            dma((2, 4)), dma((2, 4)), dma((E,)), dma((E,)), dma((2, E)), dma((2, E)),
            dma((imgs, E - 1)), dma((imgs, E - 1)), dma((imgs, E - 1)), dma((imgs, E - 1)),
            dma((E,)), dma((E,)), dma((E,)), dma((E,)), dma((2, E)), dma((2, E)),
            dma((imgs, E - 1)), dma((imgs, E - 1)),
            dma((3 + 2 * imgs,)), dma((3, imgs)), dma(()), dma((2,)), dma((2, imgs)), dma((2, imgs)),
        ],
        compiler_params=pltpu.CompilerParams(
            vmem_limit_bytes=VMEM_LIMIT, collective_id=0, has_side_effects=True
        ),
        cost_estimate=pl.CostEstimate(flops=10**11, bytes_accessed=10**8, transcendentals=2 * 10**7),
        name="front",
    )(pack, ew, dy, x, noise, keep)


def expert_kernel(nb, who_ref, *refs):
    h_in, dy_in, w_in = refs[:3]
    outs = refs[3:]
    dx_out, y_out, rows_out, hid_out, tiles_ref = outs[:5]
    (h, dy, y_t, dx_t, w_s, gate_s, slot_s, dgate_s, xs, dys, hid_s, rows_s, lo_s, hi_s, in_sem, out_sem, row_sem, hid_sem, w_sem) = outs[5:]
    me = who_ref[0]
    loads = [
        pltpu.make_async_copy(h_in, h, in_sem.at[0]),
        pltpu.make_async_copy(dy_in, dy, in_sem.at[1]),
    ]
    for b in range(E):
        at = pl.ds(b * (D // E), D // E)
        for r in range(4):
            loads.append(pltpu.make_async_copy(w_in.at[r, b], w_s.at[r, :, at], w_sem.at[r, b]))
    for copy in loads:
        copy.start()
    y_t[...] = jnp.zeros_like(y_t)
    dx_t[...] = jnp.zeros_like(dx_t)
    dgate_s[...] = jnp.zeros_like(dgate_s)
    for copy in loads:
        copy.wait()

    row16 = iota((16, D), 0)
    for b in range(nb):
        meta = h[b, PAD - 16 : PAD, :].astype(F32)
        gate_s[b : b + 1, :] = jnp.sum(jnp.where(row16 == 8 + me, meta, 0.0), axis=0, keepdims=True)[:, :PAD]
    gates = gate_s[...]
    named = (gates >= 0) & (iota((nb, PAD), 1) < SEQ)
    ones = named.astype(F32).astype(BF16)
    upto = dot(ones, (iota((PAD, PAD), 0) <= iota((PAD, PAD), 1)).astype(F32).astype(BF16))
    count = dot(ones, jnp.ones((PAD, PAD), BF16)).astype(BF16)
    before = dot((iota((nb, nb), 0) > iota((nb, nb), 1)).astype(F32).astype(BF16), count)
    slot_s[...] = jnp.where(named, before + upto - 1.0, -1.0).astype(jnp.int32)
    ends = jnp.where(named, before + upto, before)
    for b in range(nb):
        lo_s[b] = jnp.max(before[b : b + 1, :]).astype(jnp.int32)
        hi_s[b] = jnp.max(ends[b : b + 1, :]).astype(jnp.int32)
    tiles = lax.div(hi_s[nb - 1] + TILE - 1, TILE)
    tiles_ref[0] = tiles

    def meets(b, first):
        return (lo_s[b] < first + TILE) & (hi_s[b] > first) & (hi_s[b] > lo_s[b])

    def place(b, first):
        return iota((TILE, PAD), 0) + first == slot_s[pl.ds(b, 1), :]

    def step(t, carry):
        first = t * TILE
        slot = lax.rem(t, 2)
        xs[...] = jnp.zeros_like(xs)
        dys[...] = jnp.zeros_like(dys)

        def collect(b, gcol):
            def one(gcol):
                hit = place(b, first)
                p = hit.astype(F32).astype(BF16)
                xs[...] += dot(p, h[b])
                dys[...] += dot(p, dy[b])
                return gcol + jnp.sum(jnp.where(hit, gate_s[pl.ds(b, 1), :], 0.0), axis=1, keepdims=True)

            return lax.cond(meets(b, first), one, lambda g: g, gcol)

        gcol = lax.fori_loop(0, nb, collect, jnp.zeros((TILE, 1), F32))

        def drain(s):
            pltpu.make_async_copy(rows_s.at[s], rows_out.at[:, pl.ds(0, TILE)], row_sem.at[s]).wait()
            pltpu.make_async_copy(hid_s.at[s], hid_out.at[:, pl.ds(0, TILE)], hid_sem.at[s]).wait()

        @pl.when(t >= 2)
        def _():
            drain(slot)

        x = xs[...].astype(BF16)
        g_rows = (dys[...] * gcol).astype(BF16)
        rows_s[slot, 0] = x
        rows_s[slot, 1] = g_rows
        y = jnp.zeros((TILE, D), F32)
        dx = jnp.zeros((TILE, D), F32)
        for r in range(4):
            w1, w2 = w_s.at[r, 0], w_s.at[r, 1]
            a = dot(x, w1[...])
            a2 = a * a
            th = jnp.tanh(0.7978845608028654 * a * (1.0 + 0.044715 * a2))
            half = 0.5 * (1.0 + th)
            hid = (a * half).astype(BF16)
            slope = half + 0.5 * a * (1.0 - th * th) * (0.7978845608028654 * (1.0 + 3 * 0.044715 * a2))
            da = (dot(g_rows, w2[...]) * slope).astype(BF16)
            y = y + dot_nt(hid, w2[...])
            dx = dx + dot_nt(da, w1[...])
            hid_s[slot, 0, :, r * FFS : (r + 1) * FFS] = da
            hid_s[slot, 1, :, r * FFS : (r + 1) * FFS] = hid
        at = pl.ds(pl.multiple_of(first, TILE), TILE)
        pltpu.make_async_copy(rows_s.at[slot], rows_out.at[:, at], row_sem.at[slot]).start()
        pltpu.make_async_copy(hid_s.at[slot], hid_out.at[:, at], hid_sem.at[slot]).start()
        dgate = jnp.sum(dys[...] * y, axis=1, keepdims=True)
        y_low = (y * gcol).astype(BF16)
        dx_low = dx.astype(BF16)

        def give(b, carry):
            @pl.when(meets(b, first))
            def _():
                hit = place(b, first)
                p = hit.astype(F32).astype(BF16)
                y_t[b] = y_t[b] + dot_tn(p, y_low).astype(BF16)
                dx_t[b] = dx_t[b] + dot_tn(p, dx_low).astype(BF16)
                dgate_s[pl.ds(b, 1), :] += jnp.sum(jnp.where(hit, dgate, 0.0), axis=0, keepdims=True)

            return carry

        lax.fori_loop(0, nb, give, 0)
        return carry

    lax.fori_loop(0, tiles, step, 0)
    for back in (1, 2):

        @pl.when(tiles >= back)
        def _():
            s = lax.rem(tiles - back, 2)
            pltpu.make_async_copy(rows_s.at[s], rows_out.at[:, pl.ds(0, TILE)], row_sem.at[s]).wait()
            pltpu.make_async_copy(hid_s.at[s], hid_out.at[:, pl.ds(0, TILE)], hid_sem.at[s]).wait()

    for b in range(nb):
        tail = dx_t[b, PAD - 16 : PAD, :].astype(F32)
        line = jnp.concatenate([dgate_s[b : b + 1, :], jnp.zeros((1, D - PAD), F32)], axis=1)
        dx_t[b, PAD - 16 : PAD, :] = (tail + jnp.where(row16 == 8 + me, line, 0.0)).astype(BF16)
    stores = [
        pltpu.make_async_copy(dx_t, dx_out, out_sem.at[0]),
        pltpu.make_async_copy(y_t, y_out, out_sem.at[1]),
    ]
    for copy in stores:
        copy.start()
    for copy in stores:
        copy.wait()


def expert_rows(nb):
    return -(-nb * SEQ // TILE) * TILE


def experts(member, h_all, dy_all, weights):
    nb = h_all.shape[0]
    rows = expert_rows(nb)
    hbm = pl.BlockSpec(memory_space=pl.ANY)
    sm = pl.BlockSpec(memory_space=pltpu.SMEM)
    table = jax.ShapeDtypeStruct((nb, PAD, D), BF16)
    return pl.pallas_call(
        functools.partial(expert_kernel, nb),
        out_shape=[
            table,
            table,
            jax.ShapeDtypeStruct((2, rows, D), BF16),
            jax.ShapeDtypeStruct((2, rows, 4 * FFS), BF16),
            jax.ShapeDtypeStruct((1,), jnp.int32),
        ],
        in_specs=[sm, hbm, hbm, hbm],
        out_specs=[hbm] * 4 + [sm],
        scratch_shapes=[
            pltpu.VMEM((nb, PAD, D), BF16),
            pltpu.VMEM((nb, PAD, D), BF16),
            pltpu.VMEM((nb, PAD, D), BF16),
            pltpu.VMEM((nb, PAD, D), BF16),
            pltpu.VMEM((4, 2, D, FFS), BF16),
            pltpu.VMEM((nb, PAD), F32),
            pltpu.VMEM((nb, PAD), jnp.int32),
            pltpu.VMEM((nb, PAD), F32),
            pltpu.VMEM((TILE, D), F32),
            pltpu.VMEM((TILE, D), F32),
            pltpu.VMEM((2, 2, TILE, 4 * FFS), BF16),
            pltpu.VMEM((2, 2, TILE, D), BF16),
            pltpu.SMEM((nb,), jnp.int32),
            pltpu.SMEM((nb,), jnp.int32),
            pltpu.SemaphoreType.DMA((2,)),
            pltpu.SemaphoreType.DMA((2,)),
            pltpu.SemaphoreType.DMA((2,)),
            pltpu.SemaphoreType.DMA((2,)),
            pltpu.SemaphoreType.DMA((4, E)),
        ],
        compiler_params=pltpu.CompilerParams(vmem_limit_bytes=VMEM_LIMIT),
        cost_estimate=pl.CostEstimate(flops=30 * 10**9, bytes_accessed=4 * 10**7, transcendentals=4 * 10**6),
        name="experts",
    )(member.reshape(1), h_all, dy_all, weights)


def expert_grad_kernel(tiles_ref, rows_ref, hid_ref, out_ref, acc):
    acc[...] = jnp.zeros_like(acc)

    def step(t, carry):
        at = pl.ds(pl.multiple_of(t * TILE, TILE), TILE)
        acc[...] += dot_tn(rows_ref[0, at, :], hid_ref[0, at, :])
        return carry

    lax.fori_loop(0, tiles_ref[0], step, 0)
    out_ref[0] = acc[...].astype(BF16)


def expert_grads(tiles, rows, hid, kind, base):
    n = rows.shape[1]
    return pl.pallas_call(
        expert_grad_kernel,
        grid_spec=pltpu.PrefetchScalarGridSpec(
            num_scalar_prefetch=1,
            grid=(2,),
            in_specs=[
                pl.BlockSpec((1, n, D), lambda s, _: (kind, 0, 0)),
                pl.BlockSpec((1, n, FFS), lambda s, _: (kind, 0, base + s)),
            ],
            out_specs=pl.BlockSpec((1, D, FFS), lambda s, _: (s, 0, 0)),
            scratch_shapes=[pltpu.VMEM((D, FFS), F32)],
        ),
        out_shape=jax.ShapeDtypeStruct((2, D, FFS), BF16),
        compiler_params=pltpu.CompilerParams(vmem_limit_bytes=VMEM_LIMIT),
        cost_estimate=pl.CostEstimate(flops=4 * 10**9, bytes_accessed=15 * 10**6, transcendentals=0),
        name="expert_grads",
    )(tiles, rows, hid)


def unpack_kernel(who_ref, *refs):
    blocks, (in_ref, out_ref) = refs[:E], refs[E:]
    for by in range(E):
        in_ref[who_ref[by]] = blocks[by][0].astype(F32)
        out_ref[who_ref[by]] = blocks[by][1].astype(F32)


def unpack(who, blocks):
    vm = pl.BlockSpec(memory_space=pltpu.VMEM)
    whole = jax.ShapeDtypeStruct((E,) + blocks[0].shape[1:], F32)
    return pl.pallas_call(
        unpack_kernel,
        out_shape=(whole, whole),
        in_specs=[pl.BlockSpec(memory_space=pltpu.SMEM)] + [vm] * E,
        out_specs=(vm, vm),
        compiler_params=pltpu.CompilerParams(vmem_limit_bytes=VMEM_LIMIT),
        cost_estimate=pl.CostEstimate(flops=10**6, bytes_accessed=7 * 10**6, transcendentals=0),
        name="unpack",
    )(who, *blocks)


def lay_out_kernel(imgs, at_ref, *refs):
    parts, out_ref, held, sem = refs[:4], refs[4], refs[5], refs[6]
    copies = [pltpu.make_async_copy(parts[s], held.at[s], sem.at[s]) for s in range(4)]
    for copy in copies:
        copy.start()
    for copy in copies:
        copy.wait()
    for i in range(4 * imgs):
        out_ref[i * SEQ : (i + 1) * SEQ, :] = held[at_ref[i // imgs], i % imgs, :SEQ, :]


def lay_out(at, parts):
    imgs = parts[0].shape[0]
    hbm = pl.BlockSpec(memory_space=pl.ANY)
    return pl.pallas_call(
        functools.partial(lay_out_kernel, imgs),
        out_shape=jax.ShapeDtypeStruct((4 * imgs * SEQ, D), BF16),
        in_specs=[pl.BlockSpec(memory_space=pltpu.SMEM)] + [hbm] * 4,
        out_specs=pl.BlockSpec(memory_space=pltpu.VMEM),
        scratch_shapes=[pltpu.VMEM((4, imgs, PAD, D), BF16), pltpu.SemaphoreType.DMA((4,))],
        compiler_params=pltpu.CompilerParams(vmem_limit_bytes=VMEM_LIMIT),
        cost_estimate=pl.CostEstimate(flops=10**6, bytes_accessed=5 * 10**6, transcendentals=0),
        name="lay_out",
    )(at, *parts)


class Backward:
    def __init__(self, imgs, dh_of, saved, w_ref, dx1_s, low_s, h1_s, dh1_s, dqkv_s, o_s):
        self.imgs, self.dh_of, self.saved, self.w_ref = imgs, dh_of, saved, w_ref
        self.dx1_s, self.low_s, self.h1_s, self.dh1_s, self.dqkv_s, self.o_s = dx1_s, low_s, h1_s, dh1_s, dqkv_s, o_s
        self.par = params_of(w_ref[0])
        self.row_ok = iota((PAD, 1), 0) < SEQ
        self.started = False

    def span(self, c):
        return slice(c * PAD, (c + 1) * PAD)

    def first(self):
        x1_in, x_in, dy_in, probs_in = self.saved[:4]
        par, row_ok = self.par, self.row_ok
        lane_ok = iota((E, PAD), 1) < SEQ
        router = par[8:16].astype(BF16)
        gain = jnp.zeros((1, D), F32)
        bias = jnp.zeros((1, D), F32)
        g_router = jnp.zeros((E, D), F32)
        for c in range(self.imgs):
            arrived = self.dh_of(c).astype(F32)
            dgate = arrived[PAD - 8 :, :PAD]
            probs = probs_in[c]
            dlogits = probs * (dgate - jnp.sum(probs * dgate, axis=0, keepdims=True))
            dlogits = jnp.where(lane_ok, dlogits, 0.0).astype(BF16)
            unit, scale = normalise(x1_in[c])
            h2 = (unit * par[2:3] + par[3:4]).astype(BF16)
            g_router = g_router + dot(dlogits, h2)
            dh2 = jnp.where(row_ok, arrived + dot_tn(dlogits, router), 0.0)
            gain = gain + jnp.sum(dh2 * unit, axis=0, keepdims=True)
            bias = bias + jnp.sum(dh2, axis=0, keepdims=True)
            dx1 = dy_in[c].astype(F32) + norm_back(dh2, unit, scale, par[2:3])
            self.dx1_s[self.span(c), :] = dx1
            self.low_s[self.span(c), :] = dx1.astype(BF16)
            unit1, _ = normalise(x_in[c].astype(F32))
            self.h1_s[self.span(c), :] = (unit1 * par[0:1] + par[1:2]).astype(BF16)
        self.small2 = [gain, bias, jnp.zeros((4, D), F32), g_router]

    def heads(self, r):
        qkv_in, o_in, lse_in = self.saved[4:]
        key_ok = iota((PAD, PAD), 1) < SEQ
        low, h1, w = self.low_s[...], self.h1_s[...], self.w_ref[r]
        dout = dot(low, w[:, 9 * HD : D]).astype(BF16)
        for c in range(self.imgs):
            qkv = qkv_in[c, r]
            lse = lse_in[c]
            self.o_s[self.span(c), :] = o_in[c, r]
            dqs, dks, dvs = [], [], []
            for h in range(3):
                q = qkv[:, h * HD : (h + 1) * HD]
                k = qkv[:, (3 + h) * HD : (4 + h) * HD]
                v = qkv[:, (6 + h) * HD : (7 + h) * HD]
                do = dout[self.span(c), h * HD : (h + 1) * HD]
                s = dot_nt(q, k) * HD ** (-0.5)
                p = jnp.where(key_ok, jnp.exp(s - lse[:, 3 * r + h : 3 * r + h + 1]), 0.0)
                dvs.append(dot_tn(p.astype(BF16), do).astype(BF16))
                dp = dot_nt(do, v)
                ds = (p * (dp - jnp.sum(p * dp, axis=-1, keepdims=True))).astype(BF16)
                dqs.append((dot(ds, k) * HD ** (-0.5)).astype(BF16))
                dks.append((dot_tn(ds, q) * HD ** (-0.5)).astype(BF16))
            self.dqkv_s[self.span(c), :] = jnp.concatenate(dqs + dks + dvs, axis=1)
        dqkv = self.dqkv_s[...]
        part = dot_nt(dqkv, w[:, : 9 * HD])
        self.dh1_s[...] = self.dh1_s[...] + part if self.started else part
        self.started = True
        return jnp.concatenate([dot_tn(h1, dqkv), dot_tn(low, self.o_s[...])], axis=1).astype(BF16)

    def last(self, dtok_ref):
        x_in = self.saved[1]
        gain = jnp.zeros((1, D), F32)
        bias = jnp.zeros((1, D), F32)
        for c in range(self.imgs):
            dh1 = jnp.where(self.row_ok, self.dh1_s[self.span(c), :], 0.0)
            unit, scale = normalise(x_in[c].astype(F32))
            gain = gain + jnp.sum(dh1 * unit, axis=0, keepdims=True)
            bias = bias + jnp.sum(dh1, axis=0, keepdims=True)
            dtok_ref[c] = (self.dx1_s[self.span(c), :] + norm_back(dh1, unit, scale, self.par[0:1])).astype(BF16)
        return jnp.concatenate([gain, bias] + self.small2, axis=0)


def small_block(small, i, d_own):
    line = jnp.concatenate([small[:, i * d_own : (i + 1) * d_own], jnp.zeros((16, D - d_own), F32)], axis=1)
    return line.astype(BF16)


def backward_scratch(imgs):
    rows = imgs * PAD
    return [
        pltpu.VMEM((rows, D), F32),
        pltpu.VMEM((rows, D), BF16),
        pltpu.VMEM((rows, D), BF16),
        pltpu.VMEM((rows, D), F32),
        pltpu.VMEM((rows, 9 * HD), BF16),
        pltpu.VMEM((rows, 3 * HD), BF16),
    ]


def attn_backward_kernel(imgs, *refs):
    dh_in, saved, w_ref = refs[:imgs], refs[imgs : imgs + 7], refs[imgs + 7]
    packs, dtok_ref = refs[imgs + 8 : imgs + 11], refs[imgs + 11]
    n_dp, d_own = packs[0].shape[0], packs[0].shape[1] - 16
    back = Backward(imgs, lambda c: dh_in[c][...], saved, w_ref, *refs[imgs + 12 :])

    def pack_of(r):
        return packs[r] if r < 2 else packs[2].at[:, r - 2]

    back.first()
    for r in range(4):
        grad = back.heads(r)
        for i in range(n_dp):
            pack_of(r)[i, :d_own, :] = grad[i * d_own : (i + 1) * d_own]
    small = back.last(dtok_ref)
    for i in range(n_dp):
        for r in range(4):
            pack_of(r)[i, d_own:, :] = small_block(small, i, d_own)


def attn_backward(dh, saved, w, n_dp):
    imgs = len(dh)
    pack = (n_dp, D // n_dp + 16, D)
    vm = pl.BlockSpec(memory_space=pltpu.VMEM)
    return pl.pallas_call(
        functools.partial(attn_backward_kernel, imgs),
        out_shape=(
            jax.ShapeDtypeStruct(pack, BF16),
            jax.ShapeDtypeStruct(pack, BF16),
            jax.ShapeDtypeStruct((n_dp, 2) + pack[1:], BF16),
            jax.ShapeDtypeStruct((imgs, PAD, D), BF16),
        ),
        in_specs=[vm] * (imgs + 8),
        out_specs=(vm,) * 4,
        scratch_shapes=backward_scratch(imgs),
        compiler_params=pltpu.CompilerParams(vmem_limit_bytes=VMEM_LIMIT),
        cost_estimate=pl.CostEstimate(flops=12 * 10**9, bytes_accessed=2 * 10**7, transcendentals=2 * 10**6),
        name="attn_backward",
    )(*dh, *saved, w)


HOMES = ((), (0,), (1, 2), (3,), (4, 5), (6, 7), ())


def back_kernel(
    imgs, g_low, y_ref, yf_ref, dh_ref, x1_ref, x_ref, dy_ref, probs_ref, qkv_ref, o_ref, lse_ref, w_ref,
    out_all, dtok_all, g_out, total_ref,
    ga_s, gc_s, gx_s, pk_s, pkc_s, pkr_s, sm_s, smr_s, cs_s, cr_s, fs_s, fr_s, or_s, dt_s, y_s, yr_s,
    dx1_s, low_s, h1_s, dh1_s, dqkv_s, o_s,
    gc_ss, gc_r, gx_ss, gx_r, ga_ss, ga_r, pk_ss, pk_r, sm_ss, sm_r, c_ss, c_r, f_ss, f_r, row_ss, row_r, y_ss, y_r, local,
):
    peers = Peers()
    member = peers.member
    tensor = lax.axis_index("tensor")
    d_own = g_low.shape[3]
    peers.meet()
    loads = []

    def here(src, dst):
        copy = pltpu.make_async_copy(src, dst, local.at[len(loads)])
        copy.start()
        loads.append(copy)
        return copy

    def give_rows(kind, src, whole):
        here(src, whole.at[tensor])
        across = peers.send(src, whole.at[tensor], (row_ss, row_r), (kind, 0), peers.across)
        core = peers.send(src, whole.at[tensor], (row_ss, row_r), (kind, 1), peers.core)

        def onwards():
            across.wait_recv()
            other = lax.rem(tensor + 2, 4)
            copy = peers.send(whole.at[other], whole.at[other], (row_ss, row_r), (kind, 2), peers.core)
            return core, copy

        return onwards

    y_load = here(y_ref, y_s)
    yf_load = here(yf_ref, yr_s.at[1])
    y_sent = {}

    def y_hop(k):
        for c in range(imgs):
            if k > 3:
                y_sent[c, k - 1].wait_recv()
            src = yr_s.at[k - 2, c]
            src[...] = (src[...].astype(F32) + y_s[k, c].astype(F32)).astype(BF16)
            y_sent[c, k] = peers.send(src, yr_s.at[k - 1, c], (y_ss, y_r), (c, k - 1), peers.next[c % 2])

    def y_last():
        for c in range(imgs):
            y_sent[c, E - 1].wait_recv()
            total = yr_s[E - 2, c].astype(F32) + y_s[0, c].astype(F32)
            or_s[c] = (x1_ref[c] + total).astype(BF16)

    g_core = [
        peers.send(g_low.at[2 + s], gc_s.at[s], (gc_ss, gc_r), s, peers.core) for s in (1, 0)
    ][::-1]
    g_load = [here(g_low.at[s], ga_s.at[s]) for s in (1, 0)][::-1]
    y_load.wait()
    yf_load.wait()
    y_hop(3)
    order = (4, 3, 5, 2, 6, 1, 7, 0)
    gx = {}

    def pass_across():
        g_core[1].wait_recv()
        g_load[1].wait()
        for by in order:
            to = peers.ahead(by)
            ga_s[1, to] = (ga_s[1, to].astype(F32) + gc_s[1, to].astype(F32)).astype(BF16)
            gx[by] = peers.send(ga_s.at[1, to], gx_s.at[to], (gx_ss, gx_r), by, peers.across)
        g_core[0].wait_recv()
        g_load[0].wait()

    ga = {}

    def pass_home(by):
        gx[by].wait_recv()
        to = peers.ahead(by)
        part = ga_s[0, to].astype(F32) + gc_s[0, to].astype(F32)
        ga_s[0, to] = (part + gx_s[to].astype(F32)).astype(BF16)
        if by:
            device = {"dp": peers.base + to}
            ga[by] = peers.send(ga_s.at[0, to], g_out.at[member], (ga_ss, ga_r), by, device)
        else:
            here(ga_s.at[0, to], g_out.at[member])

    def homes(at):
        for number in HOMES[at]:
            pass_home(order[number])

    saved = (x1_ref, x_ref, dy_ref, probs_ref, qkv_ref, o_ref, lse_ref)
    back = Backward(imgs, lambda c: dh_ref[c], saved, w_ref, dx1_s, low_s, h1_s, dh1_s, dqkv_s, o_s)
    back.first()
    for r in (2, 3):
        grad = back.heads(r)
        for i in range(E):
            pkc_s[i, r - 2] = grad[i * d_own : (i + 1) * d_own]
        y_hop(r + 2)
        if r == 2:
            pass_across()
    pk_core = peers.send(pkc_s, pkr_s, (pk_ss, pk_r), 0, peers.core)
    for r in (0, 1):
        grad = back.heads(r)
        for i in range(E):
            pk_s[i, r, :d_own] = grad[i * d_own : (i + 1) * d_own]
        y_hop(6 + r)
        homes(r)
    small = back.last(dt_s)
    dtok_rows = give_rows(1, dt_s, dtok_all)
    for i in range(E):
        sm_s[i] = small_block(small, i, d_own)
    sm_core = peers.send(sm_s, smr_s, (sm_ss, sm_r), 0, peers.core)
    pk_core.wait_recv()
    sm_core.wait_recv()

    def term(of):
        weights = pk_s[of, :, :d_own].astype(F32) + pkr_s[of].astype(F32)
        both = sm_s[of].astype(F32) + smr_s[of].astype(F32)
        return jnp.concatenate([weights, jnp.broadcast_to(both[None], (2,) + both.shape)], axis=1)

    steps = (E // 2, E // 2 - 1)
    hops = {}

    def hop(way, i):
        value = term(peers.behind(1 - way, steps[way] - i))
        if i:
            hops[way, i - 1].wait_recv()
            value = value + cr_s[way, i - 1].astype(F32)
        cs_s[way, i] = value.astype(BF16)
        hops[way, i] = peers.send(cs_s.at[way, i], cr_s.at[way, i], (c_ss, c_r), (way, i), peers.next[way])

    for i in range(E // 2):
        hop(0, i)
        if i < steps[1]:
            hop(1, i)
        if i == 0:
            y_last()
            out_rows = give_rows(0, or_s, out_all)
        homes(2 + i)
    dtok_rows = dtok_rows()
    hops[1, steps[1] - 1].wait_recv()
    hops[0, steps[0] - 1].wait_recv()
    total = term(member) + cr_s[0, steps[0] - 1].astype(F32) + cr_s[1, steps[1] - 1].astype(F32)
    fs_s[...] = total[1].astype(BF16)
    final = peers.send(fs_s, fr_s, (f_ss, f_r), 0, peers.across)
    homes(6)
    out_rows = out_rows()
    final.wait_recv()
    total_ref[...] = total[0] + fr_s[...].astype(F32)
    for by in range(1, E):
        ga[by].wait_recv()
    for copy in (*out_rows, *dtok_rows):
        copy.wait_recv()
    for copy in loads:
        if all(copy is not other for other in (y_load, yf_load, *g_load)):
            copy.wait()
    for copy in peers.sends:
        copy.wait_send()


def back(g_low, y, y_begun, dh, saved, w):
    imgs = dh.shape[0]
    d_own = g_low.shape[3]
    vm = pl.BlockSpec(memory_space=pltpu.VMEM)
    hbm = pl.BlockSpec(memory_space=pl.ANY)
    dma = pltpu.SemaphoreType.DMA
    part = (E, 2, d_own, D)
    rows = (imgs, PAD, D)
    hop = (2, E // 2, 2, d_own + 16, D)
    return pl.pallas_call(
        functools.partial(back_kernel, imgs),
        out_shape=(
            jax.ShapeDtypeStruct((4,) + rows, BF16),
            jax.ShapeDtypeStruct((4,) + rows, BF16),
            jax.ShapeDtypeStruct(part, BF16),
            jax.ShapeDtypeStruct((d_own + 16, D), F32),
        ),
        in_specs=[hbm, hbm, hbm] + [vm] * 9,
        out_specs=(hbm, hbm, hbm, vm),
        scratch_shapes=[
            pltpu.VMEM((2,) + part, BF16),
            pltpu.VMEM((2,) + part, BF16),
            pltpu.VMEM(part, BF16),
            pltpu.VMEM((E, 2, d_own + 16, D), BF16),
            pltpu.VMEM(part, BF16),
            pltpu.VMEM(part, BF16),
            pltpu.VMEM((E, 16, D), BF16),
            pltpu.VMEM((E, 16, D), BF16),
            pltpu.VMEM(hop, BF16),
            pltpu.VMEM(hop, BF16),
            pltpu.VMEM((d_own + 16, D), BF16),
            pltpu.VMEM((d_own + 16, D), BF16),
            pltpu.VMEM(rows, BF16),
            pltpu.VMEM(rows, BF16),
            pltpu.VMEM((E,) + rows, BF16),
            pltpu.VMEM((E - 1,) + rows, BF16),
            *backward_scratch(imgs),
            dma((2,)), dma((2,)), dma((E,)), dma((E,)), dma((E,)), dma((E,)), dma((1,)), dma((1,)),
            dma((1,)), dma((1,)), dma((2, E // 2)), dma((2, E // 2)), dma((1,)), dma((1,)), dma((2, 3)), dma((2, 3)),
            dma((imgs, E - 1)), dma((imgs, E - 1)), dma((7,)),
        ],
        compiler_params=pltpu.CompilerParams(
            vmem_limit_bytes=VMEM_LIMIT, collective_id=1, has_side_effects=True
        ),
        cost_estimate=pl.CostEstimate(flops=12 * 10**9, bytes_accessed=10**8, transcendentals=2 * 10**6),
        name="back",
    )(g_low, y, y_begun, dh, *saved, w)


def eye_of(n, lanes):
    return (iota((n, lanes), 0) == iota((n, lanes), 1)).astype(F32).astype(BF16)


def prepare_kernel(
    imgs, tensor_ref, tok_ref, cot_ref, qkv_ref, wo_ref, v0_ref, v1_ref, v2_ref, v3_ref, router_ref, win_ref, wout_ref, noise_ref, routes_ref,
    pack_ref, ew_ref, x_ref, dy_ref, keep_out, noise_out, keep_s,
):
    tensor = tensor_ref[0]
    d_own = wo_ref.shape[1]
    wo = dot_tn(wo_ref[...].astype(BF16), eye_of(3 * HD, 3 * HD)).astype(BF16)
    vectors = [ref[...] for ref in (v0_ref, v1_ref, v2_ref, v3_ref)]
    lines = jnp.concatenate(vectors + [jnp.zeros((4, d_own), F32), router_ref[...]], axis=0).astype(BF16)
    lines = dot_tn(lines, eye_of(16, 128)).astype(BF16)
    pack_ref[...] = jnp.concatenate([qkv_ref[i].astype(BF16) for i in range(3)] + [wo, lines], axis=1)
    for e in range(E):
        ew_ref[e, 0] = win_ref[e].astype(BF16)
        ew_ref[e, 1] = wout_ref[e].astype(BF16)
    count = routes_ref.shape[1]
    earlier = (iota((count, count), 0) <= iota((count, count), 1)).astype(F32).astype(BF16)
    experts_ = iota((E, count), 0)
    before = jnp.zeros((E, 1), F32)
    keep = jnp.zeros((E, count), F32)
    for choice in range(TOP):
        named = experts_ == routes_ref[choice : choice + 1, :]
        upto = before + dot(named.astype(F32).astype(BF16), earlier)
        keep = keep + jnp.where(named & (upto <= CAP), 1.0, 0.0)
        before = upto[:, count - 1 :]
    keep_s[...] = keep
    for t in range(4):

        @pl.when(tensor == t)
        def _():
            for c in range(imgs):
                at = (t * imgs + c) * SEQ
                for src, dst in ((tok_ref, x_ref), (cot_ref, dy_ref)):
                    dst[c, :SEQ, :] = src[at : at + SEQ, :]
                    dst[c, SEQ:, :] = jnp.zeros((PAD - SEQ, D), BF16)
                for src, dst in ((keep_s, keep_out), (noise_ref, noise_out)):
                    dst[c] = jnp.concatenate([src[:, at : at + SEQ], jnp.zeros((E, PAD - SEQ), F32)], axis=1)


def prepare(tensor, imgs, tokens, cotangent, w_qkv, w_attn_out, vectors, router, w_in, w_out, noise, routes):
    vm = pl.BlockSpec(memory_space=pltpu.VMEM)
    d_own = w_attn_out.shape[1]
    rows = jax.ShapeDtypeStruct((imgs, PAD, D), BF16)
    lanes = jax.ShapeDtypeStruct((imgs, E, PAD), F32)
    return pl.pallas_call(
        functools.partial(prepare_kernel, imgs),
        out_shape=(
            jax.ShapeDtypeStruct((d_own, D + 128), BF16),
            jax.ShapeDtypeStruct((E, 2, d_own, FFS), BF16),
            rows,
            rows,
            lanes,
            lanes,
        ),
        in_specs=[pl.BlockSpec(memory_space=pltpu.SMEM)] + [vm] * 13,
        out_specs=(vm,) * 6,
        scratch_shapes=[pltpu.VMEM((E, tokens.shape[0]), F32)],
        compiler_params=pltpu.CompilerParams(vmem_limit_bytes=VMEM_LIMIT),
        cost_estimate=pl.CostEstimate(flops=10**8, bytes_accessed=15 * 10**6, transcendentals=0),
        name="prepare",
    )(tensor.reshape(1), tokens, cotangent, w_qkv, w_attn_out, *vectors, router, w_in, w_out, noise, routes)


def finish_kernel(imgs, out_in, dtok_in, g_in, total_ref, out_ref, dtok_ref, gi_ref, go_ref, qkv_ref, wo_ref, s0_ref, s1_ref, s2_ref, s3_ref, router_ref, rows_s, g_s, sem):
    loads = [pltpu.make_async_copy(src, rows_s.at[i], sem.at[i]) for i, src in enumerate((out_in, dtok_in))]
    loads.append(pltpu.make_async_copy(g_in, g_s, sem.at[2]))
    for copy in loads:
        copy.start()
    d_own = gi_ref.shape[1]
    total = total_ref[...]
    for i in range(3):
        qkv_ref[i] = total[:d_own, i * 3 * HD : (i + 1) * 3 * HD]
    wo_ref[...] = jnp.transpose(total[:d_own, 9 * HD :])
    for i, ref in enumerate((s0_ref, s1_ref, s2_ref, s3_ref)):
        ref[...] = total[d_own + i : d_own + i + 1, :d_own]
    router_ref[...] = total[d_own + 8 :, :d_own]
    for which, dst in ((0, out_ref), (1, dtok_ref)):
        loads[which].wait()
        for i in range(4 * imgs):
            dst[i * SEQ : (i + 1) * SEQ, :] = rows_s[which, i // imgs, i % imgs, :SEQ, :]
    loads[2].wait()
    for e in range(E):
        gi_ref[e] = g_s[e, 0].astype(F32)
        go_ref[e] = g_s[e, 1].astype(F32)


def finish(out_all, dtok_all, g_exp, total):
    imgs = out_all.shape[1]
    d_own = g_exp.shape[2]
    vm = pl.BlockSpec(memory_space=pltpu.VMEM)
    hbm = pl.BlockSpec(memory_space=pl.ANY)
    rows = jax.ShapeDtypeStruct((4 * imgs * SEQ, D), BF16)
    grad = jax.ShapeDtypeStruct((E, d_own, FFS), F32)
    return pl.pallas_call(
        functools.partial(finish_kernel, imgs),
        out_shape=(
            rows,
            rows,
            grad,
            grad,
            jax.ShapeDtypeStruct((3, d_own, 3 * HD), F32),
            jax.ShapeDtypeStruct((3 * HD, d_own), F32),
            *[jax.ShapeDtypeStruct((1, d_own), F32)] * 4,
            jax.ShapeDtypeStruct((E, d_own), F32),
        ),
        in_specs=[hbm, hbm, hbm, vm],
        out_specs=(vm,) * 11,
        scratch_shapes=[
            pltpu.VMEM((2, 4, imgs, PAD, D), BF16),
            pltpu.VMEM(g_exp.shape, BF16),
            pltpu.SemaphoreType.DMA((3,)),
        ],
        compiler_params=pltpu.CompilerParams(vmem_limit_bytes=VMEM_LIMIT),
        cost_estimate=pl.CostEstimate(flops=10**6, bytes_accessed=18 * 10**6, transcendentals=0),
        name="finish",
    )(out_all, dtok_all, g_exp, total)


RING = (0, 2, 4, 6, 7, 5, 3, 1)


class Mover:
    def __init__(self, n_dp):
        self.n_dp = n_dp
        self.groups = n_dp // E
        self.me = lax.axis_index("dp")
        self.member = lax.rem(self.me, E)
        self.group = lax.div(self.me, E)
        self.tensor = lax.axis_index("tensor")
        self.place = ring_place(self.member)
        bases = range(0, n_dp, E)
        self.ring = (
            [(b + RING[i], b + RING[(i + 1) % E]) for b in bases for i in range(E)],
            [(b + RING[(i + 1) % E], b + RING[i]) for b in bases for i in range(E)],
        )

    def along(self, value, way):
        return lax.ppermute(value, "dp", self.ring[way])

    def shift(self, value, by):
        perm = [(b + i, b + (i + by) % E) for b in range(0, self.n_dp, E) for i in range(E)]
        return lax.ppermute(value, "dp", perm)

    def shift_group(self, value, by):
        return lax.ppermute(value, "dp", [(k, (k + by * E) % self.n_dp) for k in range(self.n_dp)])

    def other(self, value, mask):
        return lax.ppermute(value, "tensor", [(k, k ^ mask) for k in range(4)])

    def behind(self, way, k):
        step = -k if way == 0 else k
        return ring_member(lax.rem(self.place + step + E, E))

    def group_lists(self):
        if self.groups == 1:
            return None
        return [[b + i for i in range(E)] for b in range(0, self.n_dp, E)]

    def gather(self, value):
        return lax.all_gather(value, "dp", axis=0, tiled=False, axis_index_groups=self.group_lists())

    def scatter_sum(self, value):
        return lax.psum_scatter(
            value, "dp", scatter_dimension=0, tiled=False, axis_index_groups=self.group_lists()
        )

    def front(self, pack, ew, dy, x, noise, keep):
        own = lax.all_gather(pack, "dp", axis=0, tiled=True)
        two = jnp.stack([own, self.other(own, 2)])
        w = jnp.concatenate([two, self.other(two, 1)], axis=0)
        blocks = jnp.zeros((2, E * pack.shape[0], FFS), BF16)
        for by in range(E):
            to = lax.rem(self.member + by, E)
            block = lax.dynamic_index_in_dim(ew, to, 0, False)
            came = lax.rem(self.member - by + E, E)
            block = self.shift(block, by) if by else block
            blocks = lax.dynamic_update_slice_in_dim(blocks, block, came * pack.shape[0], 1)
        blocks = self.all_groups(blocks, 1)
        blocks = jnp.swapaxes(blocks.reshape(2, E, D // E, FFS), 0, 1)
        two = jnp.stack([blocks, self.other(blocks, 2)])
        weights = jnp.concatenate([two, self.other(two, 1)], axis=0)
        chunk, *saved = attn_forward(x, w, noise, keep)
        table = (E * x.shape[0], PAD, D)
        dh, y, rows, hid, tiles = experts(
            self.member, self.gather(chunk).reshape(table), self.gather(dy).reshape(table), weights
        )
        sums = [self.scatter_sum(t.reshape((E,) + chunk.shape)) for t in (dh, y)]
        g = [jnp.concatenate([expert_grads(tiles, rows, hid, kind, base) for base in (0, 2)]) for kind in (0, 1)]
        g = jnp.stack([part.reshape(4, E, D // E, FFS) for part in g], axis=2)
        return g, jnp.stack(sums), w, *saved

    def back(self, g_low, sums, saved, x, dy, w):
        x1, qkv, o, lse, probs = saved
        dh_sum, y_sum = sums[0], sums[1]
        imgs, d_own = x.shape[0], D // self.n_dp
        passed = self.other(g_low[2:], 1)
        pair = [(g_low[s].astype(F32) + passed[s].astype(F32)).astype(BF16) for s in range(2)]
        total = (pair[0].astype(F32) + self.other(pair[1], 2).astype(F32)).astype(BF16)
        if self.groups > 1:
            total = jnp.swapaxes(total, 1, 2).reshape(D, 2, FFS)
            total = jnp.swapaxes(self.sum_groups(total, 0).reshape(E, d_own, 2, FFS), 1, 2)
        g_exp = []
        for by in range(E):
            to = lax.rem(self.member + by, E)
            block = lax.dynamic_index_in_dim(total, to, 0, False)
            g_exp.append(self.shift(block, by) if by else block)

        pack0, pack1, packs, d_tok = attn_backward(
            [dh_sum[c] for c in range(imgs)], (x1, x, dy, probs, qkv, o, lse), w, self.n_dp
        )
        passed = self.other(packs, 1)
        if self.groups > 1:
            pack0 = self.sum_groups((pack0.astype(F32) + passed[:, 0].astype(F32)).astype(BF16), 0)
            pack1 = self.sum_groups((pack1.astype(F32) + passed[:, 1].astype(F32)).astype(BF16), 0)
            passed = jnp.zeros((E, 2) + pack0.shape[1:], BF16)

        def pack_for(member):
            one, two = (lax.dynamic_index_in_dim(p, member, 0, False).astype(F32) for p in (pack0, pack1))
            came = lax.dynamic_index_in_dim(passed, member, 0, False).astype(F32)
            return one + came[0] + self.other((two + came[1]).astype(BF16), 2).astype(F32)

        total = self.sum_both_ways(pack_for)
        at = jnp.stack([_slot(self.tensor, t) for t in range(4)])

        def all_rows(own):
            across = self.other(own, 2)
            return lay_out(at, [own, across, self.other(own, 1), self.other(across, 1)])

        d_tokens = all_rows(d_tok)
        output = all_rows((x1 + y_sum.astype(F32)).astype(BF16))
        came = jnp.stack([lax.rem(self.member - by + E, E) for by in range(E)])
        return output, d_tokens, *unpack(came, g_exp), total

    def sum_both_ways(self, block_for):
        def chain(way, steps):
            total = block_for(self.behind(1 - way, steps)).astype(BF16)
            for k in range(steps - 1, -1, -1):
                total = self.along(total, way)
                if k:
                    total = (total.astype(F32) + block_for(self.behind(1 - way, k)).astype(F32)).astype(BF16)
            return total

        ahead = chain(0, E // 2)
        back = chain(1, E // 2 - 1)
        return ahead.astype(F32) + back.astype(F32) + block_for(self.member).astype(F32)

    def all_groups(self, part, dim):
        if self.groups == 1:
            return part
        size = part.shape[dim]
        shape = part.shape[:dim] + (size * self.groups,) + part.shape[dim + 1 :]
        whole = lax.dynamic_update_slice_in_dim(jnp.zeros(shape, part.dtype), part, self.group * size, dim)
        for by in range(1, self.groups):
            came = lax.rem(self.group - by + self.groups, self.groups)
            whole = lax.dynamic_update_slice_in_dim(whole, self.shift_group(part, by), came * size, dim)
        return whole

    def sum_groups(self, whole, dim):
        if self.groups == 1:
            return whole
        size = whole.shape[dim] // self.groups
        total = lax.dynamic_slice_in_dim(whole, self.group * size, size, dim).astype(F32)
        for by in range(1, self.groups):
            to = lax.rem(self.group + by, self.groups)
            part = lax.dynamic_slice_in_dim(whole, to * size, size, dim)
            total = total + self.shift_group(part, by).astype(F32)
        return total.astype(whole.dtype)


def after(value, *first):
    return lax.optimization_barrier((value, first))[0]


def _slot(tensor, t):
    apart = lax.bitwise_xor(tensor, t)
    return lax.div(apart, 2) + 2 * lax.rem(apart, 2)


def image_blocks(rows, tensor, imgs):
    first = tensor * (imgs * SEQ)
    return [
        jnp.pad(lax.dynamic_slice_in_dim(rows, first + c * SEQ, SEQ, 0), ((0, PAD - SEQ), (0, 0)))
        for c in range(imgs)
    ]


def image_lanes(lanes, tensor, imgs):
    first = tensor * (imgs * SEQ)
    return [
        jnp.pad(lax.dynamic_slice_in_dim(lanes, first + c * SEQ, SEQ, 1), ((0, 0), (0, PAD - SEQ)))
        for c in range(imgs)
    ]


def kept_pairs(routes):
    chosen = jnp.transpose(routes).reshape(1, -1)
    named = (chosen == jnp.arange(E, dtype=jnp.int32)[:, None]).astype(jnp.int32)
    kept = named * (jnp.cumsum(named, axis=1) <= CAP)
    return jnp.sum(kept.reshape(E, TOP, -1), axis=1).astype(F32)


def body(
    n_dp,
    tokens,
    ln1_gain,
    ln1_bias,
    w_qkv,
    w_attn_out,
    ln2_gain,
    ln2_bias,
    router_weight,
    w_in,
    w_expert_out,
    router_noise,
    routes,
    cotangent,
):
    move = Mover(n_dp)
    token_count = tokens.shape[0]
    imgs = token_count // SEQ // 4
    d_own = w_qkv.shape[0]
    ways = [c % 2 for c in range(imgs)]

    w_out = jnp.transpose(w_expert_out, (0, 2, 1))
    if move.groups == 1:
        pack, ew, x, dy, keep, noise = prepare(
            move.tensor, imgs, tokens, cotangent, jnp.transpose(w_qkv, (1, 0, 2)), w_attn_out,
            [v.reshape(1, d_own) for v in (ln1_gain, ln1_bias, ln2_gain, ln2_bias)], jnp.transpose(router_weight),
            w_in, w_out, jnp.transpose(router_noise), jnp.transpose(routes),
        )
        _, _, _, y, _, y_begun, g_low, dh, w, *saved = front(pack, ew, dy, x, noise, keep)
        x1, qkv, o, lse, probs = saved
        output, d_tokens, g_in, g_out, g_qkv, g_attn_out, *g_vectors, g_router = finish(
            *back(g_low, y, y_begun, dh, (x1, x, dy, probs, qkv, o, lse), w)
        )
        g_vectors = [v.reshape(d_own) for v in g_vectors]
        g_qkv = jnp.transpose(g_qkv, (1, 0, 2))
    else:
        vectors = jnp.stack([ln1_gain, ln1_bias, ln2_gain, ln2_bias] + [jnp.zeros_like(ln1_gain)] * 4, axis=1)
        pack = jnp.concatenate(
            [w_qkv[:, 0], w_qkv[:, 1], w_qkv[:, 2], jnp.transpose(w_attn_out), vectors, router_weight], axis=1
        )
        pack = jnp.pad(pack, ((0, 0), (0, 128 - 16))).astype(BF16)
        ew = jnp.stack([w_in, jnp.transpose(w_expert_out, (0, 2, 1))], axis=1).astype(BF16)
        x = jnp.stack(image_blocks(tokens, move.tensor, imgs))
        dy = jnp.stack(image_blocks(cotangent, move.tensor, imgs))
        keep = jnp.stack(image_lanes(kept_pairs(routes), move.tensor, imgs))
        noise = jnp.stack(image_lanes(jnp.transpose(router_noise), move.tensor, imgs))
        g_low, sums, w, *saved = move.front(pack, ew, dy, x, noise, keep)
        output, d_tokens, g_in, g_out, total = move.back(g_low, sums, saved, x, dy, w)
        g_qkv = total[:d_own, : 9 * HD].reshape(d_own, 3, 3 * HD)
        g_attn_out = jnp.transpose(total[:d_own, 9 * HD :])
        g_vectors = [total[d_own + i, :d_own] for i in range(4)]
        g_router = total[d_own + 8 :, :d_own]
    return (
        output,
        d_tokens,
        g_vectors[0],
        g_vectors[1],
        g_qkv,
        g_attn_out,
        g_vectors[2],
        g_vectors[3],
        jnp.transpose(g_router),
        g_in,
        jnp.transpose(g_out, (0, 2, 1)),
    )


def solution(mesh):
    in_specs = (
        P("dp", None),
        P("dp"),
        P("dp"),
        P("dp", None, "tensor"),
        P("tensor", "dp"),
        P("dp"),
        P("dp"),
        P("dp", None),
        P(None, "dp", "tensor"),
        P(None, "tensor", "dp"),
        P("dp", None),
        P("dp", None),
        P("dp", None),
    )
    out_specs = (
        P("dp", None),
        P("dp", None),
        P("dp"),
        P("dp"),
        P("dp", None, "tensor"),
        P("tensor", "dp"),
        P("dp"),
        P("dp"),
        P("dp", None),
        P(None, "dp", "tensor"),
        P(None, "tensor", "dp"),
    )
    return jax.shard_map(
        functools.partial(body, mesh.shape["dp"]),
        mesh=mesh,
        in_specs=in_specs,
        out_specs=out_specs,
        check_vma=False,
    )
```
